32 devices in a mesh: grp: 16 (over z, y, core), shard: 2 (over x).
Axes of the slice: x: 2, y: 2, z: 4, core: 2. Of those that a mesh axis runs over, the one named last changes fastest.
Arguments:
- latents: bfloat16 [32, 128, 1024], P('grp'), may hold values from -6 to 6
- inputs: bfloat16 [32, 1568, 1024], P('grp', 'shard'), may hold values from -6 to 6
- latent_segment: int32 [32, 128], P('grp'), may hold values from 0 to 3
- input_segment: int32 [32, 1568], P('grp', 'shard'), may hold values from 0 to 3, as said below
- cross_query: bfloat16 [1024, 1024], P('shard'), may hold values from -0.1875 to 0.1875
- cross_key: bfloat16 [1024, 1024], P('shard'), may hold values from -0.1875 to 0.1875
- cross_value: bfloat16 [1024, 1024], P('shard'), may hold values from -0.1875 to 0.1875
- cross_output: bfloat16 [1024, 1024], P('shard'), may hold values from -3 to 3
- mlp_up: bfloat16 [1024, 4096], P(None, 'shard'), may hold values from -0.1875 to 0.1875
- mlp_down: bfloat16 [4096, 1024], P('shard'), may hold values from -0.09375 to 0.09375
- self_query: bfloat16 [1024, 1024], P(None, 'shard'), may hold values from -0.1875 to 0.1875
- self_key: bfloat16 [1024, 1024], P(None, 'shard'), may hold values from -0.1875 to 0.1875
- self_value: bfloat16 [1024, 1024], P(None, 'shard'), may hold values from -0.1875 to 0.1875
- self_output: bfloat16 [1024, 1024], P('shard'), may hold values from -1.5 to 1.5
- latent_gain: bfloat16 [1024], P('shard'), may hold values from 0.5 to 1.5
- latent_bias: bfloat16 [1024], P('shard'), may hold values from -2 to 2
- input_gain: bfloat16 [1024], P('shard'), may hold values from 0.5 to 1.5
- input_bias: bfloat16 [1024], P('shard'), may hold values from -2 to 2
- mlp_gain: bfloat16 [1024], P('shard'), may hold values from 0.5 to 1.5
- mlp_bias: bfloat16 [1024], P('shard'), may hold values from -2 to 2
- self_gain: bfloat16 [1024], P('shard'), may hold values from 0.5 to 1.5
- self_bias: bfloat16 [1024], P('shard'), may hold values from -2 to 2
- cotangent: bfloat16 [32, 128, 1024], P('grp'), may hold values from -6 to 6
Outputs:
- new_latents: bfloat16 [32, 128, 1024], P('grp')
- grad_latents: bfloat16 [32, 128, 1024], P('grp')
- grad_inputs: bfloat16 [32, 1568, 1024], P('grp', 'shard')
- grad_cross_query: float32 [1024, 1024], P('shard')
- grad_cross_key: float32 [1024, 1024], P('shard')
- grad_cross_value: float32 [1024, 1024], P('shard')
- grad_cross_output: float32 [1024, 1024], P('shard')
- grad_mlp_up: float32 [1024, 4096], P(None, 'shard')
- grad_mlp_down: float32 [4096, 1024], P('shard')
- grad_self_query: float32 [1024, 1024], P(None, 'shard')
- grad_self_key: float32 [1024, 1024], P(None, 'shard')
- grad_self_value: float32 [1024, 1024], P(None, 'shard')
- grad_self_output: float32 [1024, 1024], P('shard')
- grad_latent_gain: float32 [1024], P('shard')
- grad_latent_bias: float32 [1024], P('shard')
- grad_input_gain: float32 [1024], P('shard')
- grad_input_bias: float32 [1024], P('shard')
- grad_mlp_gain: float32 [1024], P('shard')
- grad_mlp_bias: float32 [1024], P('shard')
- grad_self_gain: float32 [1024], P('shard')
- grad_self_bias: float32 [1024], P('shard')
The draws below stay inside these ranges and needn't reach their ends.
Inputs may be any that keep to these rules, and one draw needn't show every extreme that they name: `input_segment`: within every group the ids never fall along the 1568 inputs, and each of the values 0 to 3 occurs.
All inputs are finite; a program needn't handle non-finite values.
Results may differ from the reference program's by a relative error of at most 0.025.
Values may be sent and summed in bfloat16 or wider, within the bound.
A program may use at most 256 MiB of HBM per device.

```python
import jax
import jax.numpy as jnp
from jax import lax

D = 1024
FF = 4096
HEADS = 8
HEAD_DIM = 128
LATENTS = 128
INPUTS = 1568
GROUPS = 32


def draw_input_segment(key, part):
    key = jax.random.fold_in(key, 7)
    key_one, key_two, key_three = jax.random.split(key, 3)
    start_long = jax.random.randint(key_one, (GROUPS, 1), 1, INPUTS // 16)
    end_long = jax.random.randint(key_two, (GROUPS, 1), INPUTS - INPUTS // 16, INPUTS - INPUTS // 32)
    start_last = jax.random.randint(key_three, (GROUPS, 1), end_long + 1, INPUTS)
    places = jnp.arange(INPUTS, dtype=jnp.int32)[None, :]
    return (places >= start_long).astype(jnp.int32) + (places >= end_long).astype(jnp.int32) + (places >= start_last).astype(jnp.int32)


def with_ends(values, rng, least, high):
    longest = values.shape.index(max(values.shape))
    spots = []
    for shift in (0, 1):
        where = [jax.random.randint(jax.random.fold_in(rng, axis), (), 0, length) for axis, length in enumerate(values.shape)]
        where[longest] = (where[longest] + shift) % values.shape[longest]
        spots.append(tuple(where))
    return values.at[spots[0]].set(least).at[spots[1]].set(high)


def block_levels(rng, dims, cuts, low, high):
    level = 1.0
    for axis_at, shards_of in cuts:
        heights = jax.random.uniform(jax.random.fold_in(jax.random.fold_in(rng, 6), axis_at), (shards_of,), jnp.float32, low / len(cuts), high / len(cuts))
        level = level * jnp.repeat(jnp.exp(heights), dims[axis_at] // shards_of).reshape((-1,) + (1,) * (len(dims) - 1 - axis_at))
    return level


def gaussian(stream_key, dims, deviation, reach, cuts=(), kind=jnp.bfloat16):
    entries = deviation * jax.random.normal(stream_key, dims, jnp.float32)
    if cuts:
        entries = entries * block_levels(stream_key, dims, cuts, -0.22, 0.18)
    return jnp.clip(entries, -reach, reach).astype(kind)


def setup_inputs(seed: int = 0) -> dict:
    key_list = jax.random.split(jax.random.key(seed), 24)
    return {
        "latents": gaussian(key_list[0], (GROUPS, LATENTS, D), 1.0, 6.0, ((0, 16),)),
        "inputs": gaussian(key_list[1], (GROUPS, INPUTS, D), 1.0, 6.0, ((0, 16), (1, 2))),
        "latent_segment": with_ends(jax.random.randint(key_list[2], (GROUPS, LATENTS), 0, 4), jax.random.fold_in(key_list[2], 1), 0, 3).astype(jnp.int32),
        "input_segment": draw_input_segment(jax.random.fold_in(key_list[23], 71), 0),
        "cross_query": gaussian(key_list[4], (D, D), D ** -0.5, 0.1875, ((0, 2),)),
        "cross_key": gaussian(key_list[5], (D, D), D ** -0.5, 0.1875, ((0, 2),)),
        "cross_value": gaussian(key_list[6], (D, D), D ** -0.5, 0.1875, ((0, 2),)),
        "cross_output": gaussian(key_list[7], (D, D), 0.5, 3.0, ((0, 2),)),
        "mlp_up": gaussian(key_list[8], (D, FF), D ** -0.5, 0.1875, ((1, 2),)),
        "mlp_down": gaussian(key_list[9], (FF, D), FF ** -0.5, 0.09375, ((0, 2),)),
        "self_query": gaussian(key_list[10], (D, D), D ** -0.5, 0.1875, ((1, 2),)),
        "self_key": gaussian(key_list[11], (D, D), D ** -0.5, 0.1875, ((1, 2),)),
        "self_value": gaussian(key_list[12], (D, D), D ** -0.5, 0.1875, ((1, 2),)),
        "self_output": gaussian(key_list[13], (D, D), 0.25, 1.5, ((0, 2),)),
        "latent_gain": jnp.clip(1.0 + 0.1 * jax.random.normal(key_list[14], (D,), jnp.float32), 0.5, 1.5).astype(jnp.bfloat16),
        "latent_bias": gaussian(key_list[15], (D,), 0.3, 2.0, ((0, 2),)),
        "input_gain": jnp.clip(1.0 + 0.1 * jax.random.normal(key_list[16], (D,), jnp.float32), 0.5, 1.5).astype(jnp.bfloat16),
        "input_bias": gaussian(key_list[17], (D,), 0.3, 2.0, ((0, 2),)),
        "mlp_gain": jnp.clip(1.0 + 0.1 * jax.random.normal(key_list[18], (D,), jnp.float32), 0.5, 1.5).astype(jnp.bfloat16),
        "mlp_bias": gaussian(key_list[19], (D,), 0.3, 2.0, ((0, 2),)),
        "self_gain": jnp.clip(1.0 + 0.1 * jax.random.normal(key_list[20], (D,), jnp.float32), 0.5, 1.5).astype(jnp.bfloat16),
        "self_bias": gaussian(key_list[21], (D,), 0.3, 2.0, ((0, 2),)),
        "cotangent": gaussian(key_list[22], (GROUPS, LATENTS, D), 1.0, 6.0, ((0, 16),)),
    }


EPSILON = 1e-05
NEGATIVE = -1e+30

@jax.custom_vjp
def low(v):
    return lax.optimization_barrier(v.astype(jnp.bfloat16)).astype(jnp.float32)

@jax.custom_vjp
def low_back(v):
    return v

def low_keep(v):
    return (low(v), None)

def low_pass(kept, grad):
    return (grad,)

def back_keep(v):
    return (v, None)

def back_low(kept, grad):
    return (low(grad),)
low.defvjp(low_keep, low_pass)
low_back.defvjp(back_keep, back_low)

def layer_norm(values, gain, shift):
    centred = values - lax.optimization_barrier(jnp.mean(values, axis=-1, keepdims=True))
    spread = lax.optimization_barrier(jnp.mean(centred * centred, axis=-1, keepdims=True))
    return centred * lax.rsqrt(spread + EPSILON) * gain + shift

def product(left, right):
    return jnp.dot(left, right, preferred_element_type=jnp.float32, precision=lax.Precision.HIGHEST)

def heads_of(values):
    return values.reshape(values.shape[0], HEADS, HEAD_DIM)

def attention(queries, key_rows, value_rows, allowed):
    scores = low_back(jnp.einsum('lhd,nhd->hln', queries, key_rows, precision=lax.Precision.HIGHEST) * HEAD_DIM ** (-0.5))
    scores = jnp.where(allowed, scores, NEGATIVE)
    weights = low(jax.nn.softmax(scores, axis=-1))
    mixed = jnp.einsum('hln,nhd->lhd', weights, value_rows, precision=lax.Precision.HIGHEST)
    return mixed.reshape(mixed.shape[0], HEADS * HEAD_DIM)

def group_forward(weights, lat_val, inp_val, lat_seg, inp_seg):
    cross_q, cross_k, cross_v, cross_o, weight_up, weight_down, self_q, self_k, self_v, self_o, gain_lat, bias_lat, gain_inp, bias_inp, gain_mlp, bias_mlp, gain_self, bias_self = weights
    lat_in = low(layer_norm(lat_val, gain_lat, bias_lat))
    inp_in = low(layer_norm(inp_val, gain_inp, bias_inp))
    queries = heads_of(low(low_back(product(lat_in, cross_q))))
    key_rows = heads_of(low(low_back(product(inp_in, cross_k))))
    value_rows = heads_of(low(low_back(product(inp_in, cross_v))))
    allowed = (lat_seg[:, None] == inp_seg[None, :])[None]
    attended = low(low_back(attention(queries, key_rows, value_rows, allowed)))
    h_one = lat_val + low_back(product(attended, cross_o))
    mlp_in = low(layer_norm(h_one, gain_mlp, bias_mlp))
    hidden = low(jax.nn.gelu(low_back(product(mlp_in, weight_up))))
    h_two = h_one + low_back(product(hidden, weight_down))
    self_in = low(layer_norm(h_two, gain_self, bias_self))
    self_queries = heads_of(low(low_back(product(self_in, self_q))))
    self_keys = heads_of(low(low_back(product(self_in, self_k))))
    self_values = heads_of(low(low_back(product(self_in, self_v))))
    mixed = low(low_back(attention(self_queries, self_keys, self_values, True)))
    return h_two + low_back(product(mixed, self_o))

def reference(latents, inputs, latent_segment, input_segment, cross_query, cross_key, cross_value, cross_output, mlp_up, mlp_down, self_query, self_key, self_value, self_output, latent_gain, latent_bias, input_gain, input_bias, mlp_gain, mlp_bias, self_gain, self_bias, cotangent):
    params = tuple((piece.astype(jnp.float32) for piece in (cross_query, cross_key, cross_value, cross_output, mlp_up, mlp_down, self_query, self_key, self_value, self_output, latent_gain, latent_bias, input_gain, input_bias, mlp_gain, mlp_bias, self_gain, self_bias)))

    def one_group(totals, group_items):
        lat_one, inp_one, lat_seg, inp_seg, cot_one = group_items

        def forward(weights, lat_val, inp_val):
            return group_forward(weights, lat_val, inp_val, lat_seg, inp_seg)
        result, pull_back = jax.vjp(forward, params, lat_one.astype(jnp.float32), inp_one.astype(jnp.float32))
        grad_weights, grad_lat, grad_inp = pull_back(cot_one.astype(jnp.float32))
        totals = jax.tree.map(lambda left, right: left + right, totals, grad_weights)
        return (totals, (result.astype(jnp.bfloat16), grad_lat.astype(jnp.bfloat16), grad_inp.astype(jnp.bfloat16)))
    zero_grads = jax.tree.map(jnp.zeros_like, params)
    totals, outputs = lax.scan(one_group, zero_grads, (latents, inputs, latent_segment, input_segment, cotangent))
    new_latents, grad_latents, grad_inputs = outputs
    return (new_latents, grad_latents, grad_inputs, totals[0], totals[1], totals[2], totals[3], totals[4], totals[5], totals[6], totals[7], totals[8], totals[9], totals[10], totals[11], totals[12], totals[13], totals[14], totals[15], totals[16], totals[17])
```

```python
import jax
import jax.numpy as jnp
from jax import lax
from jax.experimental import pallas as pl
from jax.experimental.pallas import tpu as pltpu
from jax.sharding import PartitionSpec as P

HEADS = 8
HEAD_DIM = 128


EPSILON = 1e-05
NEGATIVE = -1e30

BF = jnp.bfloat16
F32 = jnp.float32
MESH = pl.DeviceIdType.MESH
LAT = 128
INP = 784
D = 1024
HALF = 512
HID = 2048
ROWS = 2 * LAT
NROWS = 2 * INP
SCALE = HEAD_DIM ** (-0.5)
MIB = 1 << 20


def nn(a, b):
    return lax.dot_general(a, b, (((1,), (0,)), ((), ())), preferred_element_type=F32)


def nt(a, b):
    return lax.dot_general(a, b, (((1,), (1,)), ((), ())), preferred_element_type=F32)


def tn(a, b):
    return lax.dot_general(a, b, (((0,), (0,)), ((), ())), preferred_element_type=F32)


def place():
    g = lax.axis_index("grp")
    x = lax.axis_index("shard")
    c = lax.rem(g, 2)
    y = lax.rem(g // 2, 2)
    a = lax.rem(g // 4, 2)
    b = g // 8
    return dict(
        x=x, c=c, y=y, a=a, b=b,
        xp=(g, 1 - x),
        cp=(g + 1 - 2 * c, x),
        yp=(g + 2 - 4 * y, x),
        ap=(g + 4 - 8 * a, x),
        bp=(g + 8 - 16 * b, x),
    )


def greet(partners):
    barrier = pltpu.get_barrier_semaphore()
    for partner in partners:
        pl.semaphore_signal(barrier, inc=1, device_id=partner, device_id_type=MESH)
    pl.semaphore_wait(barrier, len(partners))


def remote(src, dst, send, recv, partner):
    return pltpu.make_async_remote_copy(
        src_ref=src, dst_ref=dst, send_sem=send, recv_sem=recv,
        device_id=partner, device_id_type=MESH,
    )


def norm(v, gain, shift):
    cen = v - jnp.mean(v, axis=-1, keepdims=True)
    inv = lax.rsqrt(jnp.mean(cen * cen, axis=-1, keepdims=True) + EPSILON)
    return cen * inv * gain + shift


def vec_row(vecs, i):
    return jnp.concatenate([vecs[0, i:i + 1, :], vecs[1, i:i + 1, :]], axis=1)


def loop(n, body):
    lax.fori_loop(0, n, lambda i, carry: (body(i), carry)[1], 0)


def first_kernel(
    lat_h, inp_h, seglat, seginp, vec_h, wk_h, wv_h, wq_h, wo_h, up_h, down_h,
    sq_h, sk_h, sv_h, so_h, cot_h,
    wf_o, ck_o, cv_o, inin_o, latin_o, cq_o, att_o, st_o, vec_o, hone_o, htwo_o,
    mlpin_o, selfin_o, pre_o, hid_o, ds_o, slow_o, mask_o,
    wf, inp, inin, ck, cv, lat, latin, cq, mask, segs, axb, stx, att, st, vecs,
    hone, htwo, mlpin, pre, hid, xm, selfin, wup, wdown, wself, wso, cot, qkv, dself,
    ds, slow, lsem, osem, xs, xr, ys, yr, c0s, c0r, c1s, c1r, ms, mr,
):
    me = place()
    x, y, c = me["x"], me["y"], me["c"]
    xp, yp, cp = me["xp"], me["yp"], me["cp"]
    nlocal = [0]
    nout = [0]

    def load(src, dst):
        copy = pltpu.make_async_copy(src, dst, lsem.at[nlocal[0]])
        nlocal[0] += 1
        copy.start()
        return copy

    outs = []

    def store(src, dst):
        copy = pltpu.make_async_copy(src, dst, osem.at[nout[0]])
        nout[0] += 1
        copy.start()
        outs.append(copy)

    own = pl.ds(pl.multiple_of(x * HALF, HALF), HALF)
    in_inp = load(inp_h, inp)
    in_vec = load(vec_h, vecs.at[x])
    in_lat = load(lat_h, lat)
    in_cot = load(cot_h, cot)
    in_so = load(so_h, wso)
    greet((xp, yp, cp))
    vec_move = remote(vec_h, vecs.at[x], xs.at[4], xr.at[4], xp)
    vec_move.start()
    weights = (wk_h, wv_h, wq_h, wo_h)
    quarter = 2 * y + c

    def part(w, side, q):
        return wf.at[w, pl.ds(pl.multiple_of(side * HALF + q * 128, 128), 128)]

    x_moves = []
    for w in range(4):
        src = weights[w].at[pl.ds(pl.multiple_of(quarter * 128, 128), 128)]
        move = remote(src, part(w, x, quarter), xs.at[w], xr.at[w], xp)
        move.start()
        x_moves.append(move)
    in_w = [load(weights[w], wf.at[w, own]) for w in range(4)]
    in_self = [load(h, wself.at[i]) for i, h in enumerate((sq_h, sk_h, sv_h))]
    in_up = load(up_h, wup)
    in_down = load(down_h, wdown)
    pending = []

    def forward_x(w):
        x_moves[w].wait()
        for sems, partner in (((ys, yr), yp), ((c0s, c0r), cp)):
            block = part(w, 1 - x, quarter)
            move = remote(block, block, sems[0].at[w], sems[1].at[w], partner)
            move.start()
            pending.append(move)

    def forward_y(w):
        block = part(w, 1 - x, quarter)
        remote(block, block, ys.at[w], yr.at[w], yp).wait_recv()
        block = part(w, 1 - x, 2 * (1 - y) + c)
        move = remote(block, block, c1s.at[w], c1r.at[w], cp)
        move.start()
        pending.append(move)

    def whole(w):
        block = part(w, 1 - x, quarter)
        remote(block, block, c0s.at[w], c0r.at[w], cp).wait_recv()
        remote(block, block, c1s.at[w], c1r.at[w], cp).wait_recv()
        in_w[w].wait()
        store(wf.at[w], wf_o.at[w])

    segs[...] = jnp.zeros_like(segs)
    segs[0:2, 0:INP] = seginp[...].astype(F32)
    for g in range(2):
        lat_row = seglat[g:g + 1, :].astype(F32)
        for j in range(7):
            count = min(128, INP - j * 128)
            col = jnp.broadcast_to(segs[g:g + 1, j * 128:(j + 1) * 128], (128, 128)).T
            mask[g * INP + j * 128:g * INP + j * 128 + count, :] = jnp.where(
                col[:count] == lat_row, 0.0, NEGATIVE
            ).astype(BF)
    store(mask, mask_o)
    in_cot.wait()
    in_so.wait()
    dself[...] = nt(cot[...], wso[...]).astype(BF)
    in_inp.wait()
    in_vec.wait()
    vec_move.wait()
    store(vecs, vec_o)
    gain_inp, bias_inp = vec_row(vecs, 2), vec_row(vecs, 3)

    def norm_rows(i):
        rows = pl.ds(pl.multiple_of(i * 112, 16), 112)
        inin[rows, :] = norm(inp[rows, :].astype(F32), gain_inp, bias_inp).astype(BF)

    loop(14, norm_rows)
    store(inin, inin_o)
    in_lat.wait()
    latin[...] = norm(lat[...].astype(F32), vec_row(vecs, 0), vec_row(vecs, 1)).astype(BF)
    store(latin, latin_o)

    def project(target, w, first, last):
        def body(i):
            rows = pl.ds(pl.multiple_of(i * 112, 16), 112)
            target[rows, :] = nn(inin[rows, :], wf[w]).astype(BF)

        lax.fori_loop(first, last, lambda i, carry: (body(i), carry)[1], 0)

    forward_x(0)
    forward_x(1)
    forward_y(0)
    whole(0)
    project(ck, 0, 0, 7)
    forward_x(2)
    forward_y(1)
    project(ck, 0, 7, 14)
    store(ck, ck_o)
    whole(1)
    forward_x(3)
    forward_y(2)
    project(cv, 1, 0, 14)
    store(cv, cv_o)
    whole(2)
    cq[...] = nn(latin[...], wf[2]).astype(BF)
    store(cq, cq_o)
    forward_y(3)

    def head(g, h):
        cols = pl.ds(pl.multiple_of(h * HEAD_DIM, HEAD_DIM), HEAD_DIM)
        n_rows = slice(g * INP, (g + 1) * INP)
        s = nt(ck[n_rows, cols], cq[g * LAT:(g + 1) * LAT, cols]) * SCALE + mask[n_rows, :].astype(F32)
        top = jnp.maximum(jnp.max(s, axis=0, keepdims=True), 0.1 * NEGATIVE)
        e = jnp.exp(s - top)
        total = jnp.sum(e, axis=0, keepdims=True)
        out = tn(cv[n_rows, cols], e.astype(BF))
        out = out * jnp.where(total > 0.0, 1.0 / total, 0.0)
        axb[x, pl.ds(pl.multiple_of(g * D + h * HEAD_DIM, HEAD_DIM), HEAD_DIM), :] = out.astype(BF)
        stx[x, g, pl.ds(h, 1), :] = top
        stx[x, g, pl.ds(HEADS + h, 1), :] = total

    a_moves = []
    for g in range(2):
        def pair(i, g=g):
            head(g, 2 * i)
            head(g, 2 * i + 1)

        loop(HEADS // 2, pair)
        block = axb.at[x, pl.ds(g * D, D)]
        for src, k in ((block, 0), (stx.at[x, g], 1)):
            move = remote(src, src, ms.at[2 * g + k], mr.at[2 * g + k], xp)
            move.start()
            a_moves.append(move)
    whole(3)
    for g in range(2):
        a_moves[2 * g].wait()
        a_moves[2 * g + 1].wait()
        for h in range(HEADS):
            m0, m1 = stx[0, g, h:h + 1, :], stx[1, g, h:h + 1, :]
            top = jnp.maximum(m0, m1)
            w0 = stx[0, g, HEADS + h:HEADS + h + 1, :] * jnp.exp(m0 - top)
            w1 = stx[1, g, HEADS + h:HEADS + h + 1, :] * jnp.exp(m1 - top)
            inv = 1.0 / (w0 + w1)
            rows = slice(g * D + h * HEAD_DIM, g * D + (h + 1) * HEAD_DIM)
            mixed = axb[0, rows, :].astype(F32) * (w0 * inv) + axb[1, rows, :].astype(F32) * (w1 * inv)
            att[rows, :] = mixed.astype(BF)
            st[g, h:h + 1, :] = top
            st[g, HEADS + h:HEADS + h + 1, :] = inv
        lrows = slice(g * LAT, (g + 1) * LAT)
        hone[lrows, :] = lat[lrows, :].astype(F32) + tn(att[g * D:(g + 1) * D, :], wf[3])
    store(att, att_o)
    store(st, st_o)
    store(hone, hone_o)
    mlpin[...] = norm(hone[...], vec_row(vecs, 4), vec_row(vecs, 5)).astype(BF)
    store(mlpin, mlpin_o)
    in_up.wait()
    for j in range(4):
        cols = slice(j * HALF, (j + 1) * HALF)
        u = nn(mlpin[...], wup[:, cols])
        pre[:, cols] = u
        hid[:, cols] = jax.nn.gelu(u).astype(BF)
    store(pre, pre_o)
    store(hid, hid_o)
    in_down.wait()
    m_moves = []
    for j in range(2):
        xm[x, j] = nn(hid[...], wdown[:, j * HALF:(j + 1) * HALF]).astype(BF)
        move = remote(xm.at[x, j], xm.at[x, j], ms.at[4 + j], mr.at[4 + j], xp)
        move.start()
        m_moves.append(move)
    for copy in in_self:
        copy.wait()
    for j in range(2):
        m_moves[j].wait()
        cols = slice(j * HALF, (j + 1) * HALF)
        htwo[:, cols] = hone[:, cols] + (xm[0, j].astype(F32) + xm[1, j].astype(F32))
    store(htwo, htwo_o)
    selfin[...] = norm(htwo[...], vec_row(vecs, 6), vec_row(vecs, 7)).astype(BF)
    store(selfin, selfin_o)
    for i in range(3):
        qkv[i] = nn(selfin[...], wself[i]).astype(BF)

    def self_group(g):
        rows = pl.ds(pl.multiple_of(g * LAT, LAT), LAT)
        for h in range(4):
            cols = slice(h * HEAD_DIM, (h + 1) * HEAD_DIM)
            q, k, v = qkv[0, rows, cols], qkv[1, rows, cols], qkv[2, rows, cols]
            do = dself[rows, cols]
            s = nt(q, k) * SCALE
            e = jnp.exp(s - jnp.max(s, axis=1, keepdims=True))
            p = e / jnp.sum(e, axis=1, keepdims=True)
            p_low = p.astype(BF)
            o = nn(p_low, v)
            slow[rows, cols] = o.astype(BF)
            delta = jnp.sum(do.astype(F32) * o, axis=1, keepdims=True)
            dp = nt(do, v)
            dsc = (p * (dp - delta)).astype(BF)
            ds[0, rows, cols] = (nn(dsc, k) * SCALE).astype(BF)
            ds[1, rows, cols] = (tn(dsc, q) * SCALE).astype(BF)
            ds[2, rows, cols] = tn(p_low, do).astype(BF)

    loop(2, self_group)
    store(ds, ds_o)
    store(slow, slow_o)
    for move in pending:
        move.wait_send()
    for copy in outs:
        copy.wait()


def run_first(args):
    any_spec = pl.BlockSpec(memory_space=pl.ANY)
    vmem_spec = pl.BlockSpec(memory_space=pltpu.VMEM)
    outs = [
        ((4, D, D), BF), ((NROWS, D), BF), ((NROWS, D), BF), ((NROWS, D), BF),
        ((ROWS, D), BF), ((ROWS, D), BF), ((2 * D, LAT), BF), ((2, 16, LAT), F32),
        ((2, 8, HALF), F32), ((ROWS, D), F32), ((ROWS, D), F32), ((ROWS, D), BF),
        ((ROWS, D), BF), ((ROWS, HID), F32), ((ROWS, HID), BF), ((3, ROWS, HALF), BF),
        ((ROWS, HALF), BF), ((NROWS, LAT), BF),
    ]
    scratch = [
        ((4, D, D), BF), ((NROWS, D), BF), ((NROWS, D), BF), ((NROWS, D), BF), ((NROWS, D), BF),
        ((ROWS, D), BF), ((ROWS, D), BF), ((ROWS, D), BF), ((NROWS, LAT), BF), ((8, 896), F32),
        ((2, 2 * D, LAT), BF), ((2, 2, 16, LAT), F32), ((2 * D, LAT), BF), ((2, 16, LAT), F32),
        ((2, 8, HALF), F32), ((ROWS, D), F32), ((ROWS, D), F32), ((ROWS, D), BF),
        ((ROWS, HID), F32), ((ROWS, HID), BF), ((2, 2, ROWS, HALF), BF), ((ROWS, D), BF),
        ((D, HID), BF), ((HID, D), BF), ((3, D, HALF), BF), ((HALF, D), BF), ((ROWS, D), BF),
        ((3, ROWS, HALF), BF), ((ROWS, HALF), BF), ((3, ROWS, HALF), BF), ((ROWS, HALF), BF),
    ]
    dma = pltpu.SemaphoreType.DMA
    return pl.pallas_call(
        first_kernel,
        out_shape=[jax.ShapeDtypeStruct(*o) for o in outs],
        in_specs=[any_spec, any_spec, vmem_spec, vmem_spec] + [any_spec] * 12,
        out_specs=[any_spec] * len(outs),
        scratch_shapes=[pltpu.VMEM(*s) for s in scratch]
        + [dma((16,)), dma((24,))] + [dma((5,))] * 2 + [dma((4,))] * 6 + [dma((6,))] * 2,
        compiler_params=pltpu.CompilerParams(
            collective_id=0, has_side_effects=True, vmem_limit_bytes=58 * MIB
        ),
        name="forward",
    )(*args)


def norm_back(v, dy, gain):
    cen = v - jnp.mean(v, axis=-1, keepdims=True)
    inv = lax.rsqrt(jnp.mean(cen * cen, axis=-1, keepdims=True) + EPSILON)
    n = cen * inv
    t = dy * gain
    dv = inv * (t - jnp.mean(t, axis=-1, keepdims=True) - n * jnp.mean(t * n, axis=-1, keepdims=True))
    return (
        dv,
        jnp.sum(dy * n, axis=0, keepdims=True),
        jnp.sum(dy, axis=0, keepdims=True),
    )


def gelu_slope(u):
    root = (2.0 / jnp.pi) ** 0.5
    t = jnp.tanh(root * (u + 0.044715 * u * u * u))
    return 0.5 * (1.0 + t) + 0.5 * u * (1.0 - t * t) * root * (1.0 + 3.0 * 0.044715 * u * u)


CHUNKS = 16
SLOTS = 3


def second_kernel(
    wf_h, ck_h, cv_h, inin_h, latin_h, cq_h, att_h, st_h, vec_h, hone_h, htwo_h,
    mlpin_h, selfin_h, pre_h, hid_h, ds_h, slow_h, mask_h,
    lat_h, inp_h, up_h, down_h, sq_h, sk_h, sv_h, so_h, cot_h,
    newlat_o, glat_o, ginp_o, gq_o, gk_o, gv_o, go_o, gup_o, gdown_o, gsq_o, gsk_o,
    gsv_o, gso_o, gvec_o,
    z, wf, latin, cq, att, st, vecs, hone, htwo, etwo, mlpin, selfin, pre, hid, ds,
    slow, mask, lat, cot, elow2, elow1, dpre, dcr, xb, grad, other, t0, t1, t2, t3,
    tk, xk, gvec, gvr,
    lsem, osem, gs, gr, xs, xr, vs, vr,
):
    me = place()
    x, c = me["x"], me["c"]
    xp, yp, cp, ap, bp = me["xp"], me["yp"], me["cp"], me["ap"], me["bp"]
    counts = [0, 0]
    outs = []

    def load(src, dst):
        copy = pltpu.make_async_copy(src, dst, lsem.at[counts[0]])
        counts[0] += 1
        copy.start()
        return copy

    def store(src, dst):
        copy = pltpu.make_async_copy(src, dst, osem.at[counts[1]])
        counts[1] += 1
        copy.start()
        outs.append(copy)

    in_ds = load(ds_h, ds)
    in_self = [
        load(sq_h, z.at[pl.ds(4096, D), pl.ds(0, HALF)]),
        load(sk_h, z.at[pl.ds(4096, D), pl.ds(HALF, HALF)]),
        load(sv_h, z.at[pl.ds(5120, D), pl.ds(0, HALF)]),
    ]
    in_early = [load(slow_h, slow), load(cot_h, cot), load(selfin_h, selfin)] + [
        load(so_h.at[:, pl.ds(j * HALF, HALF)], z.at[pl.ds(5120 + j * HALF, HALF), pl.ds(HALF, HALF)])
        for j in range(2)
    ]
    in_two = [load(htwo_h, htwo), load(vec_h, vecs)]
    in_mlp = [
        load(pre_h, pre), load(down_h, z.at[pl.ds(0, HID)]),
        load(up_h.at[:, pl.ds(0, D)], z.at[pl.ds(HID, D)]),
        load(up_h.at[:, pl.ds(D, D)], z.at[pl.ds(HID + D, D)]),
    ]
    in_mid = [load(hid_h, hid), load(mlpin_h, mlpin), load(hone_h, hone)]
    in_cross = [
        load(wf_h, wf), load(att_h, att), load(st_h, st), load(cq_h, cq), load(mask_h, mask),
        load(latin_h, latin), load(lat_h, lat),
    ]
    greet((xp, yp, cp, ap, bp))

    def wait_all(copies):
        for copy in copies:
            copy.wait()

    moves = {}

    def block(k, off, size, core):
        return grad.at[
            pl.ds(pl.multiple_of(k * HALF + off, 16), size),
            pl.ds(pl.multiple_of(core * HALF, HALF), HALF),
        ]

    def add_in(k, off, size, temp):
        cols = pl.ds(pl.multiple_of(c * HALF, HALF), HALF)

        def body(i):
            rows = pl.ds(pl.multiple_of(k * HALF + off + i * 64, 64), 64)
            part = temp[pl.ds(pl.multiple_of(i * 64, 64), 64), :]
            grad[rows, cols] = (grad[rows, cols].astype(F32) + part.astype(F32)).astype(BF)

        loop(size // 64, body)

    def path(k):
        one, two = (me["y"], yp), (me["a"], ap)
        if k % 4 == 3:
            one, two = two, one
        return one, two, (me["b"], bp)

    def offsets(k):
        (b1, _), (b2, _), _ = path(k)
        o1 = b1 * 256
        return o1, o1 + b2 * 128

    def result(k, off, size, core):
        rows = pl.ds(pl.multiple_of(core * HALF + off, 16), size)
        if 1 <= k <= 3:
            return (gsq_o, gsk_o, gsv_o)[k - 1].at[rows]
        if 8 <= k <= 11:
            return gup_o.at[rows, pl.ds((k - 8) * HALF, HALF)]
        cols = pl.ds(pl.multiple_of(core * HALF, HALF), HALF)
        if 4 <= k <= 7:
            return gdown_o.at[pl.ds(pl.multiple_of((k - 4) * HALF + off, 16), size), cols]
        target = {0: gso_o, 12: go_o, 13: gq_o, 14: gk_o, 15: gv_o}[k]
        return target.at[pl.ds(pl.multiple_of(off, 16), size), cols]

    def send(k, stage, src, dst, partner):
        move = remote(src, dst, gs.at[k * 8 + stage], gr.at[k * 8 + stage], partner)
        move.start()
        moves[k, stage] = move

    def event(k, s):
        slot = k % SLOTS
        (b1, p1), (b2, p2), (_, p3) = path(k)
        o1, o2 = offsets(k)
        if s == 0:
            send(k, 0, block(k, 0, HALF, 1 - c), t0.at[slot], cp)
            return
        moves[k, s - 1].wait()
        if s == 1:
            add_in(k, 0, HALF, t0.at[slot])
            if k >= 14:
                finish_x(k - 14)
            send(k, 1, block(k, (1 - b1) * 256, 256, c), t1.at[slot], p1)
        elif s == 2:
            add_in(k, o1, 256, t1.at[slot])
            send(k, 2, block(k, o1 + (1 - b2) * 128, 128, c), t2.at[slot], p2)
        elif s == 3:
            add_in(k, o2, 128, t2.at[slot])
            send(k, 3, block(k, o2, 128, c), t3.at[slot], p3)
        elif s == 4:
            add_in(k, o2, 128, t3.at[slot])
            own = block(k, o2, 128, c)
            target = result(k, o2, 128, c)
            send(k, 4, own, target, p2)
            copy = pltpu.make_async_copy(own, target, osem.at[16 + k])
            copy.start()
            moves[k, "own"] = copy
        elif s == 5:
            moves[k, "own"].wait()
            part = result(k, o1, 256, c)
            send(k, 5, part, part, p1)
        elif s == 6:
            part = result(k, 0, HALF, c)
            send(k, 6, part, part, cp)

    def tick(t):
        for s in range(7, -1, -1):
            if 0 <= t - s < CHUNKS:
                event(t - s, s)

    k_moves = {}

    def start_core(w):
        src = other.at[w, :, pl.ds(pl.multiple_of((1 - c) * HALF, HALF), HALF)]
        move = remote(src, tk.at[w], xs.at[8 + w], xr.at[8 + w], cp)
        move.start()
        k_moves[w, 0] = move

    def start_x(w):
        k_moves[w, 0].wait()
        cols = pl.ds(pl.multiple_of(c * HALF, HALF), HALF)

        def body(i):
            rows = pl.ds(pl.multiple_of(i * 64, 64), 64)
            other[w, rows, cols] = (
                other[w, rows, cols].astype(F32) + tk[w, rows, :].astype(F32)
            ).astype(BF)

        loop(HALF // 64, body)
        move = remote(other.at[w, :, cols], xk.at[w], xs.at[10 + w], xr.at[10 + w], xp)
        move.start()
        k_moves[w, 1] = move

    def finish_x(w):
        k_moves[w, 1].wait()
        add_in(14 + w, 0, HALF, xk.at[w])

    def exchange(n, part, index):
        move = remote(
            xb.at[(n, x) + part], xb.at[(n, x) + part], xs.at[index], xr.at[index], xp
        )
        move.start()
        return move

    def both(n, rows):
        return xb[n, 0, rows, :].astype(F32) + xb[n, 1, rows, :].astype(F32)

    def fill(k, half, value):
        grad[k * HALF:(k + 1) * HALF, half * HALF:(half + 1) * HALF] = value.astype(BF)

    gvec[...] = jnp.zeros_like(gvec)

    in_ds.wait()
    wait_all(in_self)
    m_self = []
    for j in range(2):
        cols = slice(j * HALF, (j + 1) * HALF)
        a_rows = slice(4096 + j * HALF, 4096 + (j + 1) * HALF)
        b_rows = slice(5120 + j * HALF, 5120 + (j + 1) * HALF)
        xb[0, x, :, cols] = (
            nt(ds[0], z[a_rows, 0:HALF]) + nt(ds[1], z[a_rows, HALF:D]) + nt(ds[2], z[b_rows, 0:HALF])
        ).astype(BF)
        m_self.append(exchange(0, (slice(None), pl.ds(j * HALF, HALF)), j))
    wait_all(in_early)
    for j in range(2):
        fill(0, j, tn(slow[...], cot[:, j * HALF:(j + 1) * HALF]))
    tick(0)
    for i in range(3):
        for j in range(2):
            fill(1 + i, j, tn(selfin[:, j * HALF:(j + 1) * HALF], ds[i]))
        tick(1 + i)
    m_new = []
    for j in range(2):
        cols = slice(j * HALF, (j + 1) * HALF)
        xb[1, x, :, cols] = nn(slow[...], z[5120 + j * HALF:5120 + (j + 1) * HALF, HALF:D]).astype(BF)
        m_new.append(exchange(1, (slice(None), pl.ds(j * HALF, HALF)), 2 + j))
    wait_all(in_two)
    wait_all(m_self)
    gain_self = vec_row(vecs, 6)

    def two_rows(i):
        rows = pl.ds(pl.multiple_of(i * 64, 64), 64)
        dv, dg, db = norm_back(htwo[rows, :], both(0, rows), gain_self)
        e = cot[rows, :].astype(F32) + dv
        etwo[rows, :] = e
        elow2[rows, :] = e.astype(BF)
        gvec[6:7, :] += dg
        gvec[7:8, :] += db

    loop(4, two_rows)
    wait_all(in_mlp)
    for j in range(4):
        cols = slice(j * HALF, (j + 1) * HALF)
        gh = nt(elow2[...], z[cols, :])
        dpre[:, cols] = (gh * gelu_slope(pre[:, cols])).astype(BF)
    m_mlp = []
    for j in range(2):
        cols = slice(j * HALF, (j + 1) * HALF)
        xb[2, x, :, cols] = (
            nt(dpre[:, 0:D], z[HID + j * HALF:HID + (j + 1) * HALF, :])
            + nt(dpre[:, D:HID], z[HID + D + j * HALF:HID + D + (j + 1) * HALF, :])
        ).astype(BF)
        m_mlp.append(exchange(2, (slice(None), pl.ds(j * HALF, HALF)), 4 + j))
    ck, cv = z.at[pl.ds(0, NROWS)], z.at[pl.ds(NROWS, NROWS)]
    inin, inp = z.at[pl.ds(2 * NROWS, NROWS)], z.at[pl.ds(3 * NROWS, NROWS)]
    in_keys = [load(ck_h, ck), load(cv_h, cv)]
    in_late = [load(inin_h, inin), load(inp_h, inp)]
    wait_all(in_mid)

    def fill_down(j):
        for i in range(2):
            fill(4 + j, i, tn(hid[:, j * HALF:(j + 1) * HALF], elow2[:, i * HALF:(i + 1) * HALF]))

    def fill_up(j):
        for i in range(2):
            fill(8 + j, i, tn(mlpin[:, i * HALF:(i + 1) * HALF], dpre[:, j * HALF:(j + 1) * HALF]))

    fill_down(0)
    tick(4)
    fill_down(1)
    tick(5)
    wait_all(m_mlp)
    gain_mlp = vec_row(vecs, 4)

    def one_rows(i):
        rows = pl.ds(pl.multiple_of(i * 64, 64), 64)
        dv, dg, db = norm_back(hone[rows, :], both(2, rows), gain_mlp)
        e = etwo[rows, :] + dv
        hone[rows, :] = e
        elow1[rows, :] = e.astype(BF)
        gvec[4:5, :] += dg
        gvec[5:6, :] += db

    loop(4, one_rows)
    wait_all(in_cross)
    for g in range(2):
        dcr[g * D:(g + 1) * D, :] = nt(wf[3], elow1[g * LAT:(g + 1) * LAT, :]).astype(BF)

    wait_all(m_new)

    def new_rows(i):
        rows = pl.ds(pl.multiple_of(i * 64, 64), 64)
        selfin[rows, :] = (htwo[rows, :] + both(1, rows)).astype(BF)

    loop(4, new_rows)
    store(selfin, newlat_o)
    wait_all(in_keys)

    def head(g, h):
        cols = pl.ds(pl.multiple_of(h * HEAD_DIM, HEAD_DIM), HEAD_DIM)
        n_rows = slice(g * INP, (g + 1) * INP)
        l_rows = slice(g * LAT, (g + 1) * LAT)
        t_rows = pl.ds(pl.multiple_of(g * D + h * HEAD_DIM, HEAD_DIM), HEAD_DIM)
        k, v, q = ck[n_rows, cols], cv[n_rows, cols], cq[l_rows, cols]
        s = nt(k, q) * SCALE + mask[n_rows, :].astype(F32)
        p = jnp.exp(s - st[g, pl.ds(h, 1), :]) * st[g, pl.ds(HEADS + h, 1), :]
        do = dcr[t_rows, :]
        delta = jnp.sum(do.astype(F32) * att[t_rows, :].astype(F32), axis=0, keepdims=True)
        dsc = (p * (nn(v, do) - delta)).astype(BF)
        cv[n_rows, cols] = nt(p.astype(BF), do).astype(BF)
        ck[n_rows, cols] = (nn(dsc, q) * SCALE).astype(BF)
        xb[0, x, l_rows, cols] = (tn(dsc, k) * SCALE).astype(BF)

    fills = [lambda: fill_down(2), lambda: fill_down(3), lambda: fill_up(0), lambda: fill_up(1)]
    m_query = []
    for g in range(2):
        for part in range(2):
            def heads(i, g=g, part=part):
                head(g, 4 * part + 2 * i)
                head(g, 4 * part + 2 * i + 1)

            loop(2, heads)
            fills[2 * g + part]()
            tick(6 + 2 * g + part)
        m_query.append(exchange(0, (pl.ds(g * LAT, LAT),), 6 + g))
    wait_all(in_late)

    def weight_grad(w, source):
        def body(i):
            rows = pl.ds(pl.multiple_of(i * 256, 256), 256)
            mine = pl.ds(pl.multiple_of(x * HALF + i * 256, 256), 256)
            theirs = pl.ds(pl.multiple_of((1 - x) * HALF + i * 256, 256), 256)
            for j in range(2):
                cols = slice(j * HALF, (j + 1) * HALF)
                other[w, rows, cols] = tn(inin[:, theirs], source[:, cols]).astype(BF)
                grad[pl.ds(pl.multiple_of((14 + w) * HALF + i * 256, 256), 256), cols] = tn(
                    inin[:, mine], source[:, cols]
                ).astype(BF)

        loop(2, body)

    weight_grad(0, ck)
    start_core(0)
    fill_up(2)
    tick(10)
    weight_grad(1, cv)
    start_x(0)
    start_core(1)
    fill_up(3)
    tick(11)
    for j in range(2):
        value = 0.0
        for g in range(2):
            rows = pl.ds(pl.multiple_of(g * D + x * HALF, HALF), HALF)
            value = value + nn(
                att[rows, :], elow1[g * LAT:(g + 1) * LAT, j * HALF:(j + 1) * HALF]
            )
        fill(12, j, value)
    start_x(1)
    tick(12)
    wait_all(m_query)
    dcq = elow2

    def query_rows(i):
        rows = pl.ds(pl.multiple_of(i * 64, 64), 64)
        dcq[rows, :] = both(0, rows).astype(BF)

    loop(4, query_rows)
    for j in range(2):
        mine = pl.ds(pl.multiple_of(x * HALF, HALF), HALF)
        fill(13, j, tn(latin[:, mine], dcq[:, j * HALF:(j + 1) * HALF]))
    tick(13)
    gain_lat = vec_row(vecs, 0)

    def lat_rows(i):
        rows = pl.ds(pl.multiple_of(i * 128, 128), 128)
        dv, dg, db = norm_back(lat[rows, :].astype(F32), nt(dcq[rows, :], wf[2]), gain_lat)
        lat[rows, :] = (hone[rows, :] + dv).astype(BF)
        gvec[0:1, :] += dg
        gvec[1:2, :] += db

    loop(2, lat_rows)
    store(lat, glat_o)
    gain_inp = vec_row(vecs, 2)

    def inp_rows(i):
        rows = pl.ds(pl.multiple_of(i * 224, 16), 224)
        dy = nt(ck[rows, :], wf[0]) + nt(cv[rows, :], wf[1])
        dv, dg, db = norm_back(inp[rows, :].astype(F32), dy, gain_inp)
        inp[rows, :] = dv.astype(BF)
        gvec[2:3, :] += dg
        gvec[3:4, :] += db

    lax.fori_loop(0, 4, lambda i, carry: (inp_rows(i), carry)[1], 0)
    tick(14)
    lax.fori_loop(4, 7, lambda i, carry: (inp_rows(i), carry)[1], 0)
    store(inp, ginp_o)
    tick(15)
    col = lax.broadcasted_iota(jnp.int32, (8, D), 1) // HALF
    row = lax.broadcasted_iota(jnp.int32, (8, D), 0)
    keep = (col == x) | (row == 2) | (row == 3)
    gvec[...] = jnp.where(keep, gvec[...], 0.0)
    v_partners = (xp, cp, yp, ap, bp)
    v_moves = []

    def vec_event(s):
        if s > 0:
            v_moves[s - 1].wait()
            gvec[...] += gvr[s - 1]
        if s < 5:
            move = remote(gvec, gvr.at[s], vs.at[s], vr.at[s], v_partners[s])
            move.start()
            v_moves.append(move)
        else:
            store(gvec, gvec_o)

    for t in range(16, 23):
        tick(t)
        if t - 16 <= 5:
            vec_event(t - 16)
    wait_all(outs)


def run_second(args):
    any_spec = pl.BlockSpec(memory_space=pl.ANY)
    outs = [
        ((ROWS, D), BF), ((ROWS, D), BF), ((NROWS, D), BF), ((HALF, D), BF), ((HALF, D), BF),
        ((HALF, D), BF), ((HALF, D), BF), ((D, HID), BF), ((HID, D), BF), ((D, HALF), BF),
        ((D, HALF), BF), ((D, HALF), BF), ((HALF, D), BF), ((8, D), F32),
    ]
    scratch = [
        ((4 * NROWS, D), BF), ((4, D, D), BF), ((ROWS, D), BF), ((ROWS, D), BF),
        ((2 * D, LAT), BF), ((2, 16, LAT), F32), ((2, 8, HALF), F32), ((ROWS, D), F32),
        ((ROWS, D), F32), ((ROWS, D), F32), ((ROWS, D), BF), ((ROWS, D), BF), ((ROWS, HID), F32),
        ((ROWS, HID), BF), ((3, ROWS, HALF), BF), ((ROWS, HALF), BF), ((NROWS, LAT), BF),
        ((ROWS, D), BF), ((ROWS, D), BF), ((ROWS, D), BF), ((ROWS, D), BF), ((ROWS, HID), BF),
        ((2 * D, LAT), BF), ((3, 2, ROWS, D), BF), ((CHUNKS * HALF, D), BF),
        ((2, HALF, D), BF), ((SLOTS, HALF, HALF), BF), ((SLOTS, 256, HALF), BF),
        ((SLOTS, 128, HALF), BF), ((SLOTS, 128, HALF), BF), ((2, HALF, HALF), BF),
        ((2, HALF, HALF), BF), ((8, D), F32), ((5, 8, D), F32),
    ]
    dma = pltpu.SemaphoreType.DMA
    return pl.pallas_call(
        second_kernel,
        out_shape=[jax.ShapeDtypeStruct(*o) for o in outs],
        in_specs=[any_spec] * len(args),
        out_specs=[any_spec] * len(outs),
        scratch_shapes=[pltpu.VMEM(*s) for s in scratch]
        + [dma((32,)), dma((32,))] + [dma((CHUNKS * 8,))] * 2 + [dma((12,))] * 2 + [dma((5,))] * 2,
        compiler_params=pltpu.CompilerParams(
            collective_id=1, has_side_effects=True, vmem_limit_bytes=63 * MIB
        ),
        name="backward",
    )(*args)


def per_device_pair(
    latents, inputs, latent_segment, input_segment, cross_query, cross_key, cross_value,
    cross_output, mlp_up, mlp_down, self_query, self_key, self_value, self_output,
    latent_gain, latent_bias, input_gain, input_bias, mlp_gain, mlp_bias, self_gain,
    self_bias, cotangent,
):
    vec = jnp.stack([
        latent_gain, latent_bias, input_gain, input_bias, mlp_gain, mlp_bias, self_gain, self_bias
    ]).astype(F32)
    lat = latents.reshape(ROWS, D)
    inp = inputs.reshape(NROWS, D)
    cot = cotangent.reshape(ROWS, D)
    kept = run_first((
        lat, inp, latent_segment, input_segment, vec, cross_key, cross_value, cross_query,
        cross_output, mlp_up, mlp_down, self_query, self_key, self_value, self_output, cot,
    ))
    (new, glat, ginp, gq, gk, gv, go, gup, gdown, gsq, gsk, gsv, gso, gvec) = run_second(
        tuple(kept) + (
            lat, inp, mlp_up, mlp_down, self_query, self_key, self_value, self_output, cot
        )
    )
    grads = [a.astype(F32) for a in (gq, gk, gv, go, gup, gdown, gsq, gsk, gsv, gso)]
    x = lax.axis_index("shard")
    small = lax.dynamic_slice_in_dim(gvec, x * HALF, HALF, 1)
    return (
        new.reshape(latents.shape), glat.reshape(latents.shape), ginp.reshape(inputs.shape),
        *grads, *[small[i] for i in range(8)],
    )


def norm_forward(values, gain, shift):
    centred = values - jnp.mean(values, axis=-1, keepdims=True)
    inv_std = lax.rsqrt(jnp.mean(centred * centred, axis=-1, keepdims=True) + EPSILON)
    normed = centred * inv_std
    return (normed * gain + shift, normed, inv_std)


def norm_backward(grad_out, normed, inv_std, gain):
    scaled = grad_out * gain
    first_mean = jnp.mean(scaled, axis=-1, keepdims=True)
    second_mean = jnp.mean(scaled * normed, axis=-1, keepdims=True)
    grad_in = inv_std * (scaled - first_mean - normed * second_mean)
    return (grad_in, jnp.sum(grad_out * normed, axis=0), jnp.sum(grad_out, axis=0))


def product(left, right):
    return jnp.dot(left, right, preferred_element_type=jnp.float32)


def inner_rows(left, right):
    return lax.dot_general(
        left, right, (((0,), (0,)), ((), ())), preferred_element_type=jnp.float32
    )


def outer_cols(left, right):
    return lax.dot_general(
        left, right, (((1,), (1,)), ((), ())), preferred_element_type=jnp.float32
    )


def forward_total(term):
    return lax.psum(term.astype(jnp.bfloat16), "shard").astype(jnp.float32)


def backward_total(term):
    return lax.psum(term.astype(jnp.bfloat16), "shard").astype(jnp.float32)


def per_device(
    latents,
    inputs,
    latent_segment,
    input_segment,
    cross_query,
    cross_key,
    cross_value,
    cross_output,
    mlp_up,
    mlp_down,
    self_query,
    self_key,
    self_value,
    self_output,
    latent_gain,
    latent_bias,
    input_gain,
    input_bias,
    mlp_gain,
    mlp_bias,
    self_gain,
    self_bias,
    cotangent,
):
    shards = lax.axis_size("shard")
    groups, lat_len, width = latents.shape
    inp_len = inputs.shape[1]
    width_part = width // shards
    column_start = lax.axis_index("shard") * width_part
    rows = groups * lat_len
    scale = HEAD_DIM ** (-0.5)
    gathered = (
        lax.all_gather(cross_query, "shard", axis=0, tiled=True),
        lax.all_gather(cross_key, "shard", axis=0, tiled=True),
        lax.all_gather(cross_value, "shard", axis=0, tiled=True),
        lax.all_gather(cross_output, "shard", axis=0, tiled=True),
        lax.all_gather(latent_gain, "shard", axis=0, tiled=True),
        lax.all_gather(latent_bias, "shard", axis=0, tiled=True),
        lax.all_gather(input_gain, "shard", axis=0, tiled=True),
        lax.all_gather(input_bias, "shard", axis=0, tiled=True),
        lax.all_gather(mlp_gain, "shard", axis=0, tiled=True),
        lax.all_gather(mlp_bias, "shard", axis=0, tiled=True),
        lax.all_gather(self_gain, "shard", axis=0, tiled=True),
        lax.all_gather(self_bias, "shard", axis=0, tiled=True),
    )
    full_query, full_key, full_value, full_output = (
        gathered[0],
        gathered[1],
        gathered[2],
        gathered[3],
    )
    gain_lat, bias_lat, gain_inp, bias_inp, gain_mlp, bias_mlp, gain_self, bias_self = [
        piece.astype(jnp.float32) for piece in gathered[4:]
    ]
    lat_rows = latents.astype(jnp.float32).reshape(rows, width)
    inp_rows = inputs.astype(jnp.float32).reshape(groups * inp_len, width)
    lat_value, lat_normed, lat_inv = norm_forward(lat_rows, gain_lat, bias_lat)
    lat_in = lat_value.astype(jnp.bfloat16)
    inp_value, inp_normed, inp_inv = norm_forward(inp_rows, gain_inp, bias_inp)
    inp_in = inp_value.astype(jnp.bfloat16)
    cross_q = (
        product(lat_in, full_query).astype(jnp.bfloat16).reshape(groups, lat_len, HEADS, HEAD_DIM)
    )
    cross_k = (
        product(inp_in, full_key).astype(jnp.bfloat16).reshape(groups, inp_len, HEADS, HEAD_DIM)
    )
    cross_v = (
        product(inp_in, full_value).astype(jnp.bfloat16).reshape(groups, inp_len, HEADS, HEAD_DIM)
    )
    allowed = latent_segment[:, None, :, None] == input_segment[:, None, None, :]
    scores = (
        jnp.einsum("glhd,gnhd->ghln", cross_q, cross_k, preferred_element_type=jnp.float32) * scale
    )
    masked = jnp.where(allowed, scores, NEGATIVE)
    part_max = jnp.max(masked, axis=-1)
    top = lax.pmax(part_max, "shard")
    total = lax.psum(
        jnp.sum(jnp.where(allowed, jnp.exp(masked - top[..., None]), 0.0), axis=-1), "shard"
    )
    cross_prob = jnp.where(allowed, jnp.exp(masked - top[..., None]), 0.0) / total[..., None]
    cross_prob_low = cross_prob.astype(jnp.bfloat16)
    part_out = jnp.einsum(
        "ghln,gnhd->glhd", cross_prob_low, cross_v, preferred_element_type=jnp.float32
    )
    attended = lax.psum(part_out.astype(jnp.bfloat16), "shard").astype(jnp.float32)
    attended_in = attended.reshape(rows, width).astype(jnp.bfloat16)
    h_one = lat_rows + product(attended_in, full_output)
    mlp_value, mlp_normed, mlp_inv = norm_forward(h_one, gain_mlp, bias_mlp)
    mlp_in = mlp_value.astype(jnp.bfloat16)
    pre_act = product(mlp_in, mlp_up)
    hidden_in = jax.nn.gelu(pre_act).astype(jnp.bfloat16)
    h_two = h_one + forward_total(product(hidden_in, mlp_down))
    self_value_n, self_normed, self_inv = norm_forward(h_two, gain_self, bias_self)
    self_in = self_value_n.astype(jnp.bfloat16)
    local_heads = self_query.shape[1] // HEAD_DIM
    local_width = local_heads * HEAD_DIM
    self_q = (
        product(self_in, self_query)
        .astype(jnp.bfloat16)
        .reshape(groups, lat_len, local_heads, HEAD_DIM)
    )
    self_k = (
        product(self_in, self_key)
        .astype(jnp.bfloat16)
        .reshape(groups, lat_len, local_heads, HEAD_DIM)
    )
    self_v = (
        product(self_in, self_value)
        .astype(jnp.bfloat16)
        .reshape(groups, lat_len, local_heads, HEAD_DIM)
    )
    self_scores = (
        jnp.einsum("glhd,gmhd->ghlm", self_q, self_k, preferred_element_type=jnp.float32) * scale
    )
    self_prob = jax.nn.softmax(self_scores, axis=-1)
    self_prob_low = self_prob.astype(jnp.bfloat16)
    self_att = jnp.einsum(
        "ghlm,gmhd->glhd", self_prob_low, self_v, preferred_element_type=jnp.float32
    )
    self_att_in = self_att.reshape(rows, local_width).astype(jnp.bfloat16)
    result = h_two + forward_total(product(self_att_in, self_output))
    new_latents = result.reshape(groups, lat_len, width).astype(jnp.bfloat16)
    grad_out = cotangent.astype(jnp.float32).reshape(rows, width)
    grad_branch = grad_out.astype(jnp.bfloat16)
    grad_self_output = inner_rows(self_att_in, grad_branch)
    grad_att = (
        outer_cols(grad_branch, self_output)
        .astype(jnp.bfloat16)
        .reshape(groups, lat_len, local_heads, HEAD_DIM)
    )
    delta = jnp.sum(grad_att.astype(jnp.float32) * self_att, axis=-1).transpose(0, 2, 1)
    grad_prob = jnp.einsum("glhd,gmhd->ghlm", grad_att, self_v, preferred_element_type=jnp.float32)
    grad_sv = jnp.einsum(
        "ghlm,glhd->gmhd", self_prob_low, grad_att, preferred_element_type=jnp.float32
    )
    grad_scores = (self_prob * (grad_prob - delta[..., None])).astype(jnp.bfloat16)
    grad_sq = (
        jnp.einsum("ghlm,gmhd->glhd", grad_scores, self_k, preferred_element_type=jnp.float32)
        * scale
    )
    grad_sk = (
        jnp.einsum("ghlm,glhd->gmhd", grad_scores, self_q, preferred_element_type=jnp.float32)
        * scale
    )
    grad_sq = grad_sq.astype(jnp.bfloat16).reshape(rows, local_width)
    grad_sk = grad_sk.astype(jnp.bfloat16).reshape(rows, local_width)
    grad_sv = grad_sv.astype(jnp.bfloat16).reshape(rows, local_width)
    grad_self_query = inner_rows(self_in, grad_sq)
    grad_self_key = inner_rows(self_in, grad_sk)
    grad_self_value = inner_rows(self_in, grad_sv)
    grad_self_in = backward_total(
        outer_cols(grad_sq, self_query)
        + outer_cols(grad_sk, self_key)
        + outer_cols(grad_sv, self_value)
    )
    grad_norm, gain_full, bias_full = norm_backward(grad_self_in, self_normed, self_inv, gain_self)
    grad_two = grad_out + grad_norm
    grad_self_gain = lax.dynamic_slice_in_dim(gain_full, column_start, width_part)
    grad_self_bias = lax.dynamic_slice_in_dim(bias_full, column_start, width_part)
    grad_mlp_branch = grad_two.astype(jnp.bfloat16)
    grad_mlp_down = inner_rows(hidden_in, grad_mlp_branch)
    grad_hidden = outer_cols(grad_mlp_branch, mlp_down)
    gelu_value, gelu_pull = jax.vjp(jax.nn.gelu, pre_act)
    grad_pre = gelu_pull(grad_hidden)[0].astype(jnp.bfloat16)
    grad_mlp_up = inner_rows(mlp_in, grad_pre)
    grad_mlp_in = backward_total(outer_cols(grad_pre, mlp_up))
    grad_norm, gain_full, bias_full = norm_backward(grad_mlp_in, mlp_normed, mlp_inv, gain_mlp)
    grad_one = grad_two + grad_norm
    grad_mlp_gain = lax.dynamic_slice_in_dim(gain_full, column_start, width_part)
    grad_mlp_bias = lax.dynamic_slice_in_dim(bias_full, column_start, width_part)
    grad_cross_branch = grad_one.astype(jnp.bfloat16)
    grad_cross_output = inner_rows(
        lax.dynamic_slice_in_dim(attended_in, column_start, width_part, 1), grad_cross_branch
    )
    grad_ca = (
        outer_cols(grad_cross_branch, full_output)
        .astype(jnp.bfloat16)
        .reshape(groups, lat_len, HEADS, HEAD_DIM)
    )
    cross_delta = jnp.sum(grad_ca.astype(jnp.float32) * attended, axis=-1).transpose(0, 2, 1)
    grad_cp = jnp.einsum("glhd,gnhd->ghln", grad_ca, cross_v, preferred_element_type=jnp.float32)
    grad_cv = jnp.einsum(
        "ghln,glhd->gnhd", cross_prob_low, grad_ca, preferred_element_type=jnp.float32
    )
    grad_cs = (cross_prob * (grad_cp - cross_delta[..., None])).astype(jnp.bfloat16)
    grad_cq_part = (
        jnp.einsum("ghln,gnhd->glhd", grad_cs, cross_k, preferred_element_type=jnp.float32) * scale
    )
    grad_ck = (
        jnp.einsum("ghln,glhd->gnhd", grad_cs, cross_q, preferred_element_type=jnp.float32) * scale
    )
    grad_cq = backward_total(grad_cq_part.reshape(rows, width)).astype(jnp.bfloat16)
    grad_ck = grad_ck.astype(jnp.bfloat16).reshape(groups * inp_len, width)
    grad_cv = grad_cv.astype(jnp.bfloat16).reshape(groups * inp_len, width)
    grad_cross_query = inner_rows(
        lax.dynamic_slice_in_dim(lat_in, column_start, width_part, 1), grad_cq
    )
    grad_lat_in = outer_cols(grad_cq, full_query)
    grad_norm, gain_full, bias_full = norm_backward(grad_lat_in, lat_normed, lat_inv, gain_lat)
    grad_latents = (grad_one + grad_norm).reshape(groups, lat_len, width).astype(jnp.bfloat16)
    grad_latent_gain = lax.dynamic_slice_in_dim(gain_full, column_start, width_part)
    grad_latent_bias = lax.dynamic_slice_in_dim(bias_full, column_start, width_part)
    key_term = inner_rows(inp_in, grad_ck)
    value_term = inner_rows(inp_in, grad_cv)
    grad_inp_in = outer_cols(grad_ck, full_key) + outer_cols(grad_cv, full_value)
    grad_inp, inp_gain_full, inp_bias_full = norm_backward(
        grad_inp_in, inp_normed, inp_inv, gain_inp
    )
    grad_inputs = grad_inp.reshape(groups, inp_len, width).astype(jnp.bfloat16)
    grad_cross_key, grad_cross_value, grad_input_gain, grad_input_bias = (
        lax.psum_scatter(
            key_term.astype(jnp.bfloat16), "shard", scatter_dimension=0, tiled=True
        ).astype(jnp.float32),
        lax.psum_scatter(
            value_term.astype(jnp.bfloat16), "shard", scatter_dimension=0, tiled=True
        ).astype(jnp.float32),
        lax.psum_scatter(
            inp_gain_full.astype(jnp.bfloat16), "shard", scatter_dimension=0, tiled=True
        ).astype(jnp.float32),
        lax.psum_scatter(
            inp_bias_full.astype(jnp.bfloat16), "shard", scatter_dimension=0, tiled=True
        ).astype(jnp.float32),
    )
    (
        grad_cross_query,
        grad_cross_key,
        grad_cross_value,
        grad_cross_output,
        grad_mlp_up,
        grad_mlp_down,
        grad_self_query,
        grad_self_key,
        grad_self_value,
        grad_self_output,
        grad_latent_gain,
        grad_latent_bias,
        grad_input_gain,
        grad_input_bias,
        grad_mlp_gain,
        grad_mlp_bias,
        grad_self_gain,
        grad_self_bias,
    ) = (
        lax.psum(grad_cross_query.astype(jnp.bfloat16), "grp").astype(jnp.float32),
        lax.psum(grad_cross_key.astype(jnp.bfloat16), "grp").astype(jnp.float32),
        lax.psum(grad_cross_value.astype(jnp.bfloat16), "grp").astype(jnp.float32),
        lax.psum(grad_cross_output.astype(jnp.bfloat16), "grp").astype(jnp.float32),
        lax.psum(grad_mlp_up.astype(jnp.bfloat16), "grp").astype(jnp.float32),
        lax.psum(grad_mlp_down.astype(jnp.bfloat16), "grp").astype(jnp.float32),
        lax.psum(grad_self_query.astype(jnp.bfloat16), "grp").astype(jnp.float32),
        lax.psum(grad_self_key.astype(jnp.bfloat16), "grp").astype(jnp.float32),
        lax.psum(grad_self_value.astype(jnp.bfloat16), "grp").astype(jnp.float32),
        lax.psum(grad_self_output.astype(jnp.bfloat16), "grp").astype(jnp.float32),
        lax.psum(grad_latent_gain.astype(jnp.bfloat16), "grp").astype(jnp.float32),
        lax.psum(grad_latent_bias.astype(jnp.bfloat16), "grp").astype(jnp.float32),
        lax.psum(grad_input_gain.astype(jnp.bfloat16), "grp").astype(jnp.float32),
        lax.psum(grad_input_bias.astype(jnp.bfloat16), "grp").astype(jnp.float32),
        lax.psum(grad_mlp_gain.astype(jnp.bfloat16), "grp").astype(jnp.float32),
        lax.psum(grad_mlp_bias.astype(jnp.bfloat16), "grp").astype(jnp.float32),
        lax.psum(grad_self_gain.astype(jnp.bfloat16), "grp").astype(jnp.float32),
        lax.psum(grad_self_bias.astype(jnp.bfloat16), "grp").astype(jnp.float32),
    )
    return (
        new_latents,
        grad_latents,
        grad_inputs,
        grad_cross_query,
        grad_cross_key,
        grad_cross_value,
        grad_cross_output,
        grad_mlp_up,
        grad_mlp_down,
        grad_self_query,
        grad_self_key,
        grad_self_value,
        grad_self_output,
        grad_latent_gain,
        grad_latent_bias,
        grad_input_gain,
        grad_input_bias,
        grad_mlp_gain,
        grad_mlp_bias,
        grad_self_gain,
        grad_self_bias,
    )


def solution(mesh):
    laid_out = mesh.shape["shard"] == 2 and mesh.shape["grp"] == 16
    return jax.shard_map(
        per_device_pair if laid_out else per_device,
        mesh=mesh,
        in_specs=(
            P("grp", None, None),
            P("grp", "shard", None),
            P("grp", None),
            P("grp", "shard"),
            P("shard", None),
            P("shard", None),
            P("shard", None),
            P("shard", None),
            P(None, "shard"),
            P("shard", None),
            P(None, "shard"),
            P(None, "shard"),
            P(None, "shard"),
            P("shard", None),
            P("shard"),
            P("shard"),
            P("shard"),
            P("shard"),
            P("shard"),
            P("shard"),
            P("shard"),
            P("shard"),
            P("grp", None, None),
        ),
        out_specs=(
            P("grp", None, None),
            P("grp", None, None),
            P("grp", "shard", None),
            P("shard", None),
            P("shard", None),
            P("shard", None),
            P("shard", None),
            P(None, "shard"),
            P("shard", None),
            P(None, "shard"),
            P(None, "shard"),
            P(None, "shard"),
            P("shard", None),
            P("shard"),
            P("shard"),
            P("shard"),
            P("shard"),
            P("shard"),
            P("shard"),
            P("shard"),
            P("shard"),
        ),
        check_vma=False,
    )
```

```python
import jax
import jax.numpy as jnp
from jax import lax
from jax.experimental import pallas as pl
from jax.experimental.pallas import tpu as pltpu
from jax.sharding import PartitionSpec as P

HEADS = 8
HEAD_DIM = 128


EPSILON = 1e-05
NEGATIVE = -1e30

BF = jnp.bfloat16
F32 = jnp.float32
MESH = pl.DeviceIdType.MESH
LAT = 128
INP = 784
D = 1024
HALF = 512
HID = 2048
ROWS = 2 * LAT
NROWS = 2 * INP
SCALE = HEAD_DIM ** (-0.5)
MIB = 1 << 20


def nn(a, b):
    return lax.dot_general(a, b, (((1,), (0,)), ((), ())), preferred_element_type=F32)


def nt(a, b):
    return lax.dot_general(a, b, (((1,), (1,)), ((), ())), preferred_element_type=F32)


def tn(a, b):
    return lax.dot_general(a, b, (((0,), (0,)), ((), ())), preferred_element_type=F32)


def place():
    g = lax.axis_index("grp")
    x = lax.axis_index("shard")
    c = lax.rem(g, 2)
    y = lax.rem(g // 2, 2)
    a = lax.rem(g // 4, 2)
    b = g // 8
    return dict(
        x=x, c=c, y=y, a=a, b=b,
        xp=(g, 1 - x),
        cp=(g + 1 - 2 * c, x),
        yp=(g + 2 - 4 * y, x),
        ap=(g + 4 - 8 * a, x),
        bp=(g + 8 - 16 * b, x),
    )


def greet(partners):
    barrier = pltpu.get_barrier_semaphore()
    for partner in partners:
        pl.semaphore_signal(barrier, inc=1, device_id=partner, device_id_type=MESH)
    pl.semaphore_wait(barrier, len(partners))


def remote(src, dst, send, recv, partner):
    return pltpu.make_async_remote_copy(
        src_ref=src, dst_ref=dst, send_sem=send, recv_sem=recv,
        device_id=partner, device_id_type=MESH,
    )


def norm(v, gain, shift):
    cen = v - jnp.mean(v, axis=-1, keepdims=True)
    inv = lax.rsqrt(jnp.mean(cen * cen, axis=-1, keepdims=True) + EPSILON)
    return cen * inv * gain + shift


def vec_row(vecs, i):
    return jnp.concatenate([vecs[0, i:i + 1, :], vecs[1, i:i + 1, :]], axis=1)


def loop(n, body):
    lax.fori_loop(0, n, lambda i, carry: (body(i), carry)[1], 0)


def first_kernel(
    lat_h, inp_h, seglat, seginp, v0, v1, v2, v3, v4, v5, v6, v7, wk_h, wv_h, wq_h, wo_h, up_h, down_h,
    sq_h, sk_h, sv_h, so_h, cot_h,
    wf_o, ck_o, cv_o, inin_o, latin_o, cq_o, att_o, st_o, vec_o, hone_o, htwo_o,
    mlpin_o, selfin_o, pre_o, hid_o, ds_o, slow_o, mask_o,
    wf, inp, inin, ck, cv, lat, latin, cq, mask, segs, axb, stx, att, st, vecs,
    hone, htwo, mlpin, pre, hid, xm, selfin, wup, wdown, wself, wso, cot, qkv, dself,
    ds, slow, lsem, osem, xs, xr, ys, yr, c0s, c0r, c1s, c1r, ms, mr,
):
    me = place()
    x, y, c = me["x"], me["y"], me["c"]
    xp, yp, cp = me["xp"], me["yp"], me["cp"]
    nlocal = [0]
    nout = [0]

    def load(src, dst):
        copy = pltpu.make_async_copy(src, dst, lsem.at[nlocal[0]])
        nlocal[0] += 1
        copy.start()
        return copy

    outs = []

    def store(src, dst):
        copy = pltpu.make_async_copy(src, dst, osem.at[nout[0]])
        nout[0] += 1
        copy.start()
        outs.append(copy)

    own = pl.ds(pl.multiple_of(x * HALF, HALF), HALF)
    in_inp = load(inp_h, inp)
    in_lat = load(lat_h, lat)
    in_cot = load(cot_h, cot)
    in_so = load(so_h, wso)
    greet((xp, yp, cp))
    for i, v in enumerate((v0, v1, v2, v3, v4, v5, v6, v7)):
        vecs[x, i:i + 1, :] = v[...].astype(F32).reshape(1, HALF)
    vec_move = remote(vecs.at[x], vecs.at[x], xs.at[4], xr.at[4], xp)
    vec_move.start()
    weights = (wk_h, wv_h, wq_h, wo_h)
    quarter = 2 * y + c

    def part(w, side, q):
        return wf.at[w, pl.ds(pl.multiple_of(side * HALF + q * 128, 128), 128)]

    x_moves = []
    for w in range(4):
        src = weights[w].at[pl.ds(pl.multiple_of(quarter * 128, 128), 128)]
        move = remote(src, part(w, x, quarter), xs.at[w], xr.at[w], xp)
        move.start()
        x_moves.append(move)
    in_w = [load(weights[w], wf.at[w, own]) for w in range(4)]
    in_self = [load(h, wself.at[i]) for i, h in enumerate((sq_h, sk_h, sv_h))]
    in_up = load(up_h, wup)
    in_down = load(down_h, wdown)
    pending = []

    def forward_x(w):
        x_moves[w].wait()
        for sems, partner in (((ys, yr), yp), ((c0s, c0r), cp)):
            block = part(w, 1 - x, quarter)
            move = remote(block, block, sems[0].at[w], sems[1].at[w], partner)
            move.start()
            pending.append(move)

    def forward_y(w):
        block = part(w, 1 - x, quarter)
        remote(block, block, ys.at[w], yr.at[w], yp).wait_recv()
        block = part(w, 1 - x, 2 * (1 - y) + c)
        move = remote(block, block, c1s.at[w], c1r.at[w], cp)
        move.start()
        pending.append(move)

    def whole(w):
        block = part(w, 1 - x, quarter)
        remote(block, block, c0s.at[w], c0r.at[w], cp).wait_recv()
        remote(block, block, c1s.at[w], c1r.at[w], cp).wait_recv()
        in_w[w].wait()
        store(wf.at[w], wf_o.at[w])

    segs[...] = jnp.zeros_like(segs)
    segs[0:2, 0:INP] = seginp[...].astype(F32)
    for g in range(2):
        lat_row = seglat[g:g + 1, :].astype(F32)
        for j in range(7):
            count = min(128, INP - j * 128)
            col = jnp.broadcast_to(segs[g:g + 1, j * 128:(j + 1) * 128], (128, 128)).T
            mask[g * INP + j * 128:g * INP + j * 128 + count, :] = jnp.where(
                col[:count] == lat_row, 0.0, NEGATIVE
            ).astype(BF)
    store(mask, mask_o)
    in_cot.wait()
    in_so.wait()
    dself[...] = nt(cot[...], wso[...]).astype(BF)
    in_inp.wait()
    vec_move.wait()
    store(vecs, vec_o)
    gain_inp, bias_inp = vec_row(vecs, 2), vec_row(vecs, 3)

    def norm_rows(i):
        rows = pl.ds(pl.multiple_of(i * 112, 16), 112)
        inin[rows, :] = norm(inp[rows, :].astype(F32), gain_inp, bias_inp).astype(BF)

    loop(14, norm_rows)
    store(inin, inin_o)
    in_lat.wait()
    latin[...] = norm(lat[...].astype(F32), vec_row(vecs, 0), vec_row(vecs, 1)).astype(BF)
    store(latin, latin_o)

    def project(target, w, first, last):
        def body(i):
            rows = pl.ds(pl.multiple_of(i * 112, 16), 112)
            target[rows, :] = nn(inin[rows, :], wf[w]).astype(BF)

        lax.fori_loop(first, last, lambda i, carry: (body(i), carry)[1], 0)

    forward_x(0)
    forward_x(1)
    forward_y(0)
    whole(0)
    project(ck, 0, 0, 7)
    forward_x(2)
    forward_y(1)
    project(ck, 0, 7, 14)
    store(ck, ck_o)
    whole(1)
    forward_x(3)
    forward_y(2)
    project(cv, 1, 0, 14)
    store(cv, cv_o)
    whole(2)
    cq[...] = nn(latin[...], wf[2]).astype(BF)
    store(cq, cq_o)
    forward_y(3)

    def head(g, h):
        cols = pl.ds(pl.multiple_of(h * HEAD_DIM, HEAD_DIM), HEAD_DIM)
        n_rows = slice(g * INP, (g + 1) * INP)
        s = nt(ck[n_rows, cols], cq[g * LAT:(g + 1) * LAT, cols]) * SCALE + mask[n_rows, :].astype(F32)
        top = jnp.maximum(jnp.max(s, axis=0, keepdims=True), 0.1 * NEGATIVE)
        e = jnp.exp(s - top)
        total = jnp.sum(e, axis=0, keepdims=True)
        out = tn(cv[n_rows, cols], e.astype(BF))
        out = out * jnp.where(total > 0.0, 1.0 / total, 0.0)
        axb[x, pl.ds(pl.multiple_of(g * D + h * HEAD_DIM, HEAD_DIM), HEAD_DIM), :] = out.astype(BF)
        stx[x, g, pl.ds(h, 1), :] = top
        stx[x, g, pl.ds(HEADS + h, 1), :] = total

    a_moves = []
    for g in range(2):
        def pair(i, g=g):
            head(g, 2 * i)
            head(g, 2 * i + 1)

        loop(HEADS // 2, pair)
        block = axb.at[x, pl.ds(g * D, D)]
        for src, k in ((block, 0), (stx.at[x, g], 1)):
            move = remote(src, src, ms.at[2 * g + k], mr.at[2 * g + k], xp)
            move.start()
            a_moves.append(move)
    whole(3)
    for g in range(2):
        a_moves[2 * g].wait()
        a_moves[2 * g + 1].wait()
        for h in range(HEADS):
            m0, m1 = stx[0, g, h:h + 1, :], stx[1, g, h:h + 1, :]
            top = jnp.maximum(m0, m1)
            w0 = stx[0, g, HEADS + h:HEADS + h + 1, :] * jnp.exp(m0 - top)
            w1 = stx[1, g, HEADS + h:HEADS + h + 1, :] * jnp.exp(m1 - top)
            inv = 1.0 / (w0 + w1)
            rows = slice(g * D + h * HEAD_DIM, g * D + (h + 1) * HEAD_DIM)
            mixed = axb[0, rows, :].astype(F32) * (w0 * inv) + axb[1, rows, :].astype(F32) * (w1 * inv)
            att[rows, :] = mixed.astype(BF)
            st[g, h:h + 1, :] = top
            st[g, HEADS + h:HEADS + h + 1, :] = inv
        lrows = slice(g * LAT, (g + 1) * LAT)
        hone[lrows, :] = lat[lrows, :].astype(F32) + tn(att[g * D:(g + 1) * D, :], wf[3])
    store(att, att_o)
    store(st, st_o)
    store(hone, hone_o)
    mlpin[...] = norm(hone[...], vec_row(vecs, 4), vec_row(vecs, 5)).astype(BF)
    store(mlpin, mlpin_o)
    in_up.wait()
    for j in range(4):
        cols = slice(j * HALF, (j + 1) * HALF)
        u = nn(mlpin[...], wup[:, cols])
        pre[:, cols] = u
        hid[:, cols] = jax.nn.gelu(u).astype(BF)
    store(pre, pre_o)
    store(hid, hid_o)
    in_down.wait()
    m_moves = []
    for j in range(2):
        xm[x, j] = nn(hid[...], wdown[:, j * HALF:(j + 1) * HALF]).astype(BF)
        move = remote(xm.at[x, j], xm.at[x, j], ms.at[4 + j], mr.at[4 + j], xp)
        move.start()
        m_moves.append(move)
    for copy in in_self:
        copy.wait()
    for j in range(2):
        m_moves[j].wait()
        cols = slice(j * HALF, (j + 1) * HALF)
        htwo[:, cols] = hone[:, cols] + (xm[0, j].astype(F32) + xm[1, j].astype(F32))
    store(htwo, htwo_o)
    selfin[...] = norm(htwo[...], vec_row(vecs, 6), vec_row(vecs, 7)).astype(BF)
    store(selfin, selfin_o)
    for i in range(3):
        qkv[i] = nn(selfin[...], wself[i]).astype(BF)

    def self_group(g):
        rows = pl.ds(pl.multiple_of(g * LAT, LAT), LAT)
        for h in range(4):
            cols = slice(h * HEAD_DIM, (h + 1) * HEAD_DIM)
            q, k, v = qkv[0, rows, cols], qkv[1, rows, cols], qkv[2, rows, cols]
            do = dself[rows, cols]
            s = nt(q, k) * SCALE
            e = jnp.exp(s - jnp.max(s, axis=1, keepdims=True))
            p = e / jnp.sum(e, axis=1, keepdims=True)
            p_low = p.astype(BF)
            o = nn(p_low, v)
            slow[rows, cols] = o.astype(BF)
            delta = jnp.sum(do.astype(F32) * o, axis=1, keepdims=True)
            dp = nt(do, v)
            dsc = (p * (dp - delta)).astype(BF)
            ds[0, rows, cols] = (nn(dsc, k) * SCALE).astype(BF)
            ds[1, rows, cols] = (tn(dsc, q) * SCALE).astype(BF)
            ds[2, rows, cols] = tn(p_low, do).astype(BF)

    loop(2, self_group)
    store(ds, ds_o)
    store(slow, slow_o)
    for move in pending:
        move.wait_send()
    for copy in outs:
        copy.wait()


def run_first(args):
    any_spec = pl.BlockSpec(memory_space=pl.ANY)
    vmem_spec = pl.BlockSpec(memory_space=pltpu.VMEM)
    outs = [
        ((4, D, D), BF), ((NROWS, D), BF), ((NROWS, D), BF), ((NROWS, D), BF),
        ((ROWS, D), BF), ((ROWS, D), BF), ((2 * D, LAT), BF), ((2, 16, LAT), F32),
        ((2, 8, HALF), F32), ((ROWS, D), F32), ((ROWS, D), F32), ((ROWS, D), BF),
        ((ROWS, D), BF), ((ROWS, HID), F32), ((ROWS, HID), BF), ((3, ROWS, HALF), BF),
        ((ROWS, HALF), BF), ((NROWS, LAT), BF),
    ]
    scratch = [
        ((4, D, D), BF), ((NROWS, D), BF), ((NROWS, D), BF), ((NROWS, D), BF), ((NROWS, D), BF),
        ((ROWS, D), BF), ((ROWS, D), BF), ((ROWS, D), BF), ((NROWS, LAT), BF), ((8, 896), F32),
        ((2, 2 * D, LAT), BF), ((2, 2, 16, LAT), F32), ((2 * D, LAT), BF), ((2, 16, LAT), F32),
        ((2, 8, HALF), F32), ((ROWS, D), F32), ((ROWS, D), F32), ((ROWS, D), BF),
        ((ROWS, HID), F32), ((ROWS, HID), BF), ((2, 2, ROWS, HALF), BF), ((ROWS, D), BF),
        ((D, HID), BF), ((HID, D), BF), ((3, D, HALF), BF), ((HALF, D), BF), ((ROWS, D), BF),
        ((3, ROWS, HALF), BF), ((ROWS, HALF), BF), ((3, ROWS, HALF), BF), ((ROWS, HALF), BF),
    ]
    dma = pltpu.SemaphoreType.DMA
    return pl.pallas_call(
        first_kernel,
        out_shape=[jax.ShapeDtypeStruct(*o) for o in outs],
        in_specs=[any_spec] * 2 + [vmem_spec] * 10 + [any_spec] * 11,
        out_specs=[any_spec] * len(outs),
        scratch_shapes=[pltpu.VMEM(*s) for s in scratch]
        + [dma((16,)), dma((24,))] + [dma((5,))] * 2 + [dma((4,))] * 6 + [dma((6,))] * 2,
        compiler_params=pltpu.CompilerParams(
            collective_id=0, has_side_effects=True, vmem_limit_bytes=58 * MIB
        ),
        name="forward",
    )(*args)


def norm_back(v, dy, gain):
    cen = v - jnp.mean(v, axis=-1, keepdims=True)
    inv = lax.rsqrt(jnp.mean(cen * cen, axis=-1, keepdims=True) + EPSILON)
    n = cen * inv
    t = dy * gain
    dv = inv * (t - jnp.mean(t, axis=-1, keepdims=True) - n * jnp.mean(t * n, axis=-1, keepdims=True))
    return (
        dv,
        jnp.sum(dy * n, axis=0, keepdims=True),
        jnp.sum(dy, axis=0, keepdims=True),
    )


def gelu_slope(u):
    root = (2.0 / jnp.pi) ** 0.5
    t = jnp.tanh(root * (u + 0.044715 * u * u * u))
    return 0.5 * (1.0 + t) + 0.5 * u * (1.0 - t * t) * root * (1.0 + 3.0 * 0.044715 * u * u)


CHUNKS = 16
OFFSETS = (0, 1, 4, 5, 6, 7, 10, 11)


def second_kernel(
    wf_h, ck_h, cv_h, inin_h, latin_h, cq_h, att_h, st_h, vec_h, hone_h, htwo_h,
    mlpin_h, selfin_h, pre_h, hid_h, ds_h, slow_h, mask_h,
    lat_h, inp_h, up_h, down_h, sq_h, sk_h, sv_h, so_h, cot_h,
    newlat_o, glat_o, ginp_o, gq_o, gk_o, gv_o, go_o, gup_o, gdown_o, gsq_o, gsk_o,
    gsv_o, gso_o, gvec_o,
    z, wf, latin, cq, att, st, vecs, hone, htwo, etwo, mlpin, selfin, pre, hid, ds,
    slow, mask, lat, cot, elow2, elow1, dpre, dcr, xb, grad, other, t0, t1, t2, t3,
    tk, xk, gvec, gvr,
    lsem, osem, gs, gr, xs, xr, vs, vr,
):
    me = place()
    x, c = me["x"], me["c"]
    xp, yp, cp, ap, bp = me["xp"], me["yp"], me["cp"], me["ap"], me["bp"]
    counts = [0, 0]
    outs = []

    def load(src, dst):
        copy = pltpu.make_async_copy(src, dst, lsem.at[counts[0]])
        counts[0] += 1
        copy.start()
        return copy

    def store(src, dst):
        copy = pltpu.make_async_copy(src, dst, osem.at[counts[1]])
        counts[1] += 1
        copy.start()
        outs.append(copy)

    in_ds = load(ds_h, ds)
    in_self = [
        load(sq_h, z.at[pl.ds(4096, D), pl.ds(0, HALF)]),
        load(sk_h, z.at[pl.ds(4096, D), pl.ds(HALF, HALF)]),
        load(sv_h, z.at[pl.ds(5120, D), pl.ds(0, HALF)]),
    ]
    in_early = [load(slow_h, slow), load(cot_h, cot), load(selfin_h, selfin)] + [
        load(so_h.at[:, pl.ds(j * HALF, HALF)], z.at[pl.ds(5120 + j * HALF, HALF), pl.ds(HALF, HALF)])
        for j in range(2)
    ]
    in_two = [load(htwo_h, htwo), load(vec_h, vecs)]
    in_mlp = [
        load(pre_h, pre), load(down_h, z.at[pl.ds(0, HID)]),
        load(up_h.at[:, pl.ds(0, D)], z.at[pl.ds(HID, D)]),
        load(up_h.at[:, pl.ds(D, D)], z.at[pl.ds(HID + D, D)]),
    ]
    in_mid = [load(hid_h, hid), load(mlpin_h, mlpin), load(hone_h, hone)]
    in_cross = [
        load(wf_h, wf), load(att_h, att), load(st_h, st), load(cq_h, cq), load(mask_h, mask),
        load(latin_h, latin), load(lat_h, lat),
    ]
    greet((xp, yp, cp, ap, bp))

    def wait_all(copies):
        for copy in copies:
            copy.wait()

    moves = {}

    def block(k, off, size, core):
        return grad.at[
            pl.ds(pl.multiple_of(k * HALF + off, 16), size),
            pl.ds(pl.multiple_of(core * HALF, HALF), HALF),
        ]

    def add_in(k, off, size, temp):
        cols = pl.ds(pl.multiple_of(c * HALF, HALF), HALF)

        def body(i):
            rows = pl.ds(pl.multiple_of(k * HALF + off + i * 64, 64), 64)
            part = temp[pl.ds(pl.multiple_of(i * 64, 64), 64), :]
            grad[rows, cols] = (grad[rows, cols].astype(F32) + part.astype(F32)).astype(BF)

        loop(size // 64, body)

    def path(k):
        one, two = (me["y"], yp), (me["a"], ap)
        if k % 4 == 3:
            one, two = two, one
        return one, two, (me["b"], bp)

    def slots(k):
        if k % 4 == 3:
            return 6 + (k // 4) % 2, 2, k % 2
        n = k - k // 4
        return n % 6, n % 2, k % 2

    def offsets(k):
        (b1, _), (b2, _), _ = path(k)
        o1 = b1 * 256
        return o1, o1 + b2 * 128

    def result(k, off, size, core):
        rows = pl.ds(pl.multiple_of(core * HALF + off, 16), size)
        if 1 <= k <= 3:
            return (gsq_o, gsk_o, gsv_o)[k - 1].at[rows]
        if 8 <= k <= 11:
            return gup_o.at[rows, pl.ds((k - 8) * HALF, HALF)]
        cols = pl.ds(pl.multiple_of(core * HALF, HALF), HALF)
        if 4 <= k <= 7:
            return gdown_o.at[pl.ds(pl.multiple_of((k - 4) * HALF + off, 16), size), cols]
        target = {0: gso_o, 12: go_o, 13: gq_o, 14: gk_o, 15: gv_o}[k]
        return target.at[pl.ds(pl.multiple_of(off, 16), size), cols]

    def send(k, stage, src, dst, partner):
        move = remote(src, dst, gs.at[k * 8 + stage], gr.at[k * 8 + stage], partner)
        move.start()
        moves[k, stage] = move

    def event(k, s):
        first, second, third = slots(k)
        (b1, p1), (b2, p2), (_, p3) = path(k)
        o1, o2 = offsets(k)
        if s == 0:
            send(k, 0, block(k, 0, HALF, 1 - c), t0.at[k % 2], cp)
            return
        moves[k, s - 1].wait()
        if s == 1:
            add_in(k, 0, HALF, t0.at[k % 2])
            if k >= 14:
                finish_x(k - 14)
            send(k, 1, block(k, (1 - b1) * 256, 256, c), t1.at[first], p1)
        elif s == 2:
            add_in(k, o1, 256, t1.at[first])
            send(k, 2, block(k, o1 + (1 - b2) * 128, 128, c), t2.at[second], p2)
        elif s == 3:
            add_in(k, o2, 128, t2.at[second])
            send(k, 3, block(k, o2, 128, c), t3.at[third], p3)
        elif s == 4:
            add_in(k, o2, 128, t3.at[third])
            own = block(k, o2, 128, c)
            target = result(k, o2, 128, c)
            send(k, 4, own, target, p2)
            copy = pltpu.make_async_copy(own, target, osem.at[16 + k])
            copy.start()
            moves[k, "own"] = copy
        elif s == 5:
            moves[k, "own"].wait()
            part = result(k, o1, 256, c)
            send(k, 5, part, part, p1)
        elif s == 6:
            part = result(k, 0, HALF, c)
            send(k, 6, part, part, cp)

    clock = [0]
    entered = {}

    def tick(chunk=None):
        now = clock[0]
        clock[0] += 1
        if chunk is not None:
            entered[chunk] = now
        for k in sorted(entered):
            if now - entered[k] in OFFSETS:
                event(k, OFFSETS.index(now - entered[k]))

    k_moves = {}

    def start_core(w):
        src = other.at[w, :, pl.ds(pl.multiple_of((1 - c) * HALF, HALF), HALF)]
        move = remote(src, tk.at[w], xs.at[8 + w], xr.at[8 + w], cp)
        move.start()
        k_moves[w, 0] = move

    def start_x(w):
        k_moves[w, 0].wait()
        cols = pl.ds(pl.multiple_of(c * HALF, HALF), HALF)

        def body(i):
            rows = pl.ds(pl.multiple_of(i * 64, 64), 64)
            other[w, rows, cols] = (
                other[w, rows, cols].astype(F32) + tk[w, rows, :].astype(F32)
            ).astype(BF)

        loop(HALF // 64, body)
        move = remote(other.at[w, :, cols], xk.at[w], xs.at[10 + w], xr.at[10 + w], xp)
        move.start()
        k_moves[w, 1] = move

    def finish_x(w):
        k_moves[w, 1].wait()
        add_in(14 + w, 0, HALF, xk.at[w])

    def exchange(n, part, index):
        move = remote(
            xb.at[(n, x) + part], xb.at[(n, x) + part], xs.at[index], xr.at[index], xp
        )
        move.start()
        return move

    def both(n, rows):
        return xb[n, 0, rows, :].astype(F32) + xb[n, 1, rows, :].astype(F32)

    def fill(k, half, value):
        grad[k * HALF:(k + 1) * HALF, half * HALF:(half + 1) * HALF] = value.astype(BF)

    gvec[...] = jnp.zeros_like(gvec)

    in_ds.wait()
    wait_all(in_self)
    m_self = []
    for j in range(2):
        cols = slice(j * HALF, (j + 1) * HALF)
        a_rows = slice(4096 + j * HALF, 4096 + (j + 1) * HALF)
        b_rows = slice(5120 + j * HALF, 5120 + (j + 1) * HALF)
        xb[0, x, :, cols] = (
            nt(ds[0], z[a_rows, 0:HALF]) + nt(ds[1], z[a_rows, HALF:D]) + nt(ds[2], z[b_rows, 0:HALF])
        ).astype(BF)
        m_self.append(exchange(0, (slice(None), pl.ds(j * HALF, HALF)), j))
    wait_all(in_early)
    for j in range(2):
        fill(0, j, tn(slow[...], cot[:, j * HALF:(j + 1) * HALF]))
    tick(0)
    for i in range(3):
        for j in range(2):
            fill(1 + i, j, tn(selfin[:, j * HALF:(j + 1) * HALF], ds[i]))
        tick(1 + i)
    m_new = []
    for j in range(2):
        cols = slice(j * HALF, (j + 1) * HALF)
        xb[1, x, :, cols] = nn(slow[...], z[5120 + j * HALF:5120 + (j + 1) * HALF, HALF:D]).astype(BF)
        m_new.append(exchange(1, (slice(None), pl.ds(j * HALF, HALF)), 2 + j))
    tick()
    wait_all(in_two)
    wait_all(m_self)
    gain_self = vec_row(vecs, 6)

    def two_rows(i):
        rows = pl.ds(pl.multiple_of(i * 64, 64), 64)
        dv, dg, db = norm_back(htwo[rows, :], both(0, rows), gain_self)
        e = cot[rows, :].astype(F32) + dv
        etwo[rows, :] = e
        elow2[rows, :] = e.astype(BF)
        gvec[6:7, :] += dg
        gvec[7:8, :] += db

    loop(4, two_rows)
    tick()
    wait_all(in_mlp)
    for j in range(4):
        cols = slice(j * HALF, (j + 1) * HALF)
        gh = nt(elow2[...], z[cols, :])
        dpre[:, cols] = (gh * gelu_slope(pre[:, cols])).astype(BF)
    m_mlp = []
    for j in range(2):
        cols = slice(j * HALF, (j + 1) * HALF)
        xb[2, x, :, cols] = (
            nt(dpre[:, 0:D], z[HID + j * HALF:HID + (j + 1) * HALF, :])
            + nt(dpre[:, D:HID], z[HID + D + j * HALF:HID + D + (j + 1) * HALF, :])
        ).astype(BF)
        m_mlp.append(exchange(2, (slice(None), pl.ds(j * HALF, HALF)), 4 + j))
    ck, cv = z.at[pl.ds(0, NROWS)], z.at[pl.ds(NROWS, NROWS)]
    inin, inp = z.at[pl.ds(2 * NROWS, NROWS)], z.at[pl.ds(3 * NROWS, NROWS)]
    in_keys = [load(ck_h, ck), load(cv_h, cv)]
    in_late = [load(inin_h, inin), load(inp_h, inp)]
    wait_all(in_mid)

    def fill_down(j):
        for i in range(2):
            fill(4 + j, i, tn(hid[:, j * HALF:(j + 1) * HALF], elow2[:, i * HALF:(i + 1) * HALF]))

    def fill_up(j):
        for i in range(2):
            fill(8 + j, i, tn(mlpin[:, i * HALF:(i + 1) * HALF], dpre[:, j * HALF:(j + 1) * HALF]))

    fill_down(0)
    tick(4)
    fill_down(1)
    tick(5)
    fill_down(2)
    tick(6)
    fill_down(3)
    tick(7)
    wait_all(m_mlp)
    gain_mlp = vec_row(vecs, 4)

    def one_rows(i):
        rows = pl.ds(pl.multiple_of(i * 64, 64), 64)
        dv, dg, db = norm_back(hone[rows, :], both(2, rows), gain_mlp)
        e = etwo[rows, :] + dv
        hone[rows, :] = e
        elow1[rows, :] = e.astype(BF)
        gvec[4:5, :] += dg
        gvec[5:6, :] += db

    loop(4, one_rows)
    wait_all(in_cross)
    for g in range(2):
        dcr[g * D:(g + 1) * D, :] = nt(wf[3], elow1[g * LAT:(g + 1) * LAT, :]).astype(BF)

    wait_all(m_new)

    def new_rows(i):
        rows = pl.ds(pl.multiple_of(i * 64, 64), 64)
        selfin[rows, :] = (htwo[rows, :] + both(1, rows)).astype(BF)

    loop(4, new_rows)
    store(selfin, newlat_o)
    wait_all(in_keys)

    def head(g, h):
        cols = pl.ds(pl.multiple_of(h * HEAD_DIM, HEAD_DIM), HEAD_DIM)
        n_rows = slice(g * INP, (g + 1) * INP)
        l_rows = slice(g * LAT, (g + 1) * LAT)
        t_rows = pl.ds(pl.multiple_of(g * D + h * HEAD_DIM, HEAD_DIM), HEAD_DIM)
        k, v, q = ck[n_rows, cols], cv[n_rows, cols], cq[l_rows, cols]
        s = nt(k, q) * SCALE + mask[n_rows, :].astype(F32)
        p = jnp.exp(s - st[g, pl.ds(h, 1), :]) * st[g, pl.ds(HEADS + h, 1), :]
        do = dcr[t_rows, :]
        delta = jnp.sum(do.astype(F32) * att[t_rows, :].astype(F32), axis=0, keepdims=True)
        dsc = (p * (nn(v, do) - delta)).astype(BF)
        cv[n_rows, cols] = nt(p.astype(BF), do).astype(BF)
        ck[n_rows, cols] = (nn(dsc, q) * SCALE).astype(BF)
        xb[0, x, l_rows, cols] = (tn(dsc, k) * SCALE).astype(BF)

    fills = [lambda j=j: fill_up(j) for j in range(4)]
    m_query = []
    for g in range(2):
        for part in range(2):
            def heads(i, g=g, part=part):
                head(g, 4 * part + 2 * i)
                head(g, 4 * part + 2 * i + 1)

            loop(2, heads)
            fills[2 * g + part]()
            tick(8 + 2 * g + part)
        m_query.append(exchange(0, (pl.ds(g * LAT, LAT),), 6 + g))
    wait_all(in_late)

    def weight_grad(w, source):
        def body(i):
            rows = pl.ds(pl.multiple_of(i * 256, 256), 256)
            mine = pl.ds(pl.multiple_of(x * HALF + i * 256, 256), 256)
            theirs = pl.ds(pl.multiple_of((1 - x) * HALF + i * 256, 256), 256)
            for j in range(2):
                cols = slice(j * HALF, (j + 1) * HALF)
                other[w, rows, cols] = tn(inin[:, theirs], source[:, cols]).astype(BF)
                grad[pl.ds(pl.multiple_of((14 + w) * HALF + i * 256, 256), 256), cols] = tn(
                    inin[:, mine], source[:, cols]
                ).astype(BF)

        loop(2, body)

    weight_grad(0, ck)
    start_core(0)
    tick()
    weight_grad(1, cv)
    start_x(0)
    start_core(1)
    for j in range(2):
        value = 0.0
        for g in range(2):
            rows = pl.ds(pl.multiple_of(g * D + x * HALF, HALF), HALF)
            value = value + nn(
                att[rows, :], elow1[g * LAT:(g + 1) * LAT, j * HALF:(j + 1) * HALF]
            )
        fill(12, j, value)
    start_x(1)
    tick(12)
    wait_all(m_query)
    dcq = elow2

    def query_rows(i):
        rows = pl.ds(pl.multiple_of(i * 64, 64), 64)
        dcq[rows, :] = both(0, rows).astype(BF)

    loop(4, query_rows)
    for j in range(2):
        mine = pl.ds(pl.multiple_of(x * HALF, HALF), HALF)
        fill(13, j, tn(latin[:, mine], dcq[:, j * HALF:(j + 1) * HALF]))
    tick(13)
    gain_lat = vec_row(vecs, 0)

    def lat_rows(i):
        rows = pl.ds(pl.multiple_of(i * 128, 128), 128)
        dv, dg, db = norm_back(lat[rows, :].astype(F32), nt(dcq[rows, :], wf[2]), gain_lat)
        lat[rows, :] = (hone[rows, :] + dv).astype(BF)
        gvec[0:1, :] += dg
        gvec[1:2, :] += db

    loop(2, lat_rows)
    store(lat, glat_o)
    gain_inp = vec_row(vecs, 2)

    def inp_rows(i):
        rows = pl.ds(pl.multiple_of(i * 224, 16), 224)
        dy = nt(ck[rows, :], wf[0]) + nt(cv[rows, :], wf[1])
        dv, dg, db = norm_back(inp[rows, :].astype(F32), dy, gain_inp)
        inp[rows, :] = dv.astype(BF)
        gvec[2:3, :] += dg
        gvec[3:4, :] += db

    lax.fori_loop(0, 4, lambda i, carry: (inp_rows(i), carry)[1], 0)
    tick(14)
    lax.fori_loop(4, 7, lambda i, carry: (inp_rows(i), carry)[1], 0)
    store(inp, ginp_o)
    tick(15)
    col = lax.broadcasted_iota(jnp.int32, (8, D), 1) // HALF
    row = lax.broadcasted_iota(jnp.int32, (8, D), 0)
    keep = (col == x) | (row == 2) | (row == 3)
    gvec[...] = jnp.where(keep, gvec[...], 0.0)
    v_partners = (xp, cp, yp, ap, bp)
    v_moves = []

    def vec_event(s):
        if s > 0:
            v_moves[s - 1].wait()
            gvec[...] += gvr[s - 1]
        if s < 5:
            move = remote(gvec, gvr.at[s], vs.at[s], vr.at[s], v_partners[s])
            move.start()
            v_moves.append(move)
        else:
            store(gvec, gvec_o)

    for t in range(OFFSETS[-1]):
        tick()
        if t <= 5:
            vec_event(t)
    wait_all(outs)


def run_second(args):
    any_spec = pl.BlockSpec(memory_space=pl.ANY)
    outs = [
        ((ROWS, D), BF), ((ROWS, D), BF), ((NROWS, D), BF), ((HALF, D), BF), ((HALF, D), BF),
        ((HALF, D), BF), ((HALF, D), BF), ((D, HID), BF), ((HID, D), BF), ((D, HALF), BF),
        ((D, HALF), BF), ((D, HALF), BF), ((HALF, D), BF), ((8, D), F32),
    ]
    scratch = [
        ((4 * NROWS, D), BF), ((4, D, D), BF), ((ROWS, D), BF), ((ROWS, D), BF),
        ((2 * D, LAT), BF), ((2, 16, LAT), F32), ((2, 8, HALF), F32), ((ROWS, D), F32),
        ((ROWS, D), F32), ((ROWS, D), F32), ((ROWS, D), BF), ((ROWS, D), BF), ((ROWS, HID), F32),
        ((ROWS, HID), BF), ((3, ROWS, HALF), BF), ((ROWS, HALF), BF), ((NROWS, LAT), BF),
        ((ROWS, D), BF), ((ROWS, D), BF), ((ROWS, D), BF), ((ROWS, D), BF), ((ROWS, HID), BF),
        ((2 * D, LAT), BF), ((3, 2, ROWS, D), BF), ((CHUNKS * HALF, D), BF),
        ((2, HALF, D), BF), ((2, HALF, HALF), BF), ((8, 256, HALF), BF),
        ((3, 128, HALF), BF), ((2, 128, HALF), BF), ((2, HALF, HALF), BF),
        ((2, HALF, HALF), BF), ((8, D), F32), ((5, 8, D), F32),
    ]
    dma = pltpu.SemaphoreType.DMA
    return pl.pallas_call(
        second_kernel,
        out_shape=[jax.ShapeDtypeStruct(*o) for o in outs],
        in_specs=[any_spec] * len(args),
        out_specs=[any_spec] * len(outs),
        scratch_shapes=[pltpu.VMEM(*s) for s in scratch]
        + [dma((32,)), dma((32,))] + [dma((CHUNKS * 8,))] * 2 + [dma((12,))] * 2 + [dma((5,))] * 2,
        compiler_params=pltpu.CompilerParams(
            collective_id=1, has_side_effects=True, vmem_limit_bytes=63 * MIB
        ),
        name="backward",
    )(*args)


def finish_kernel(*refs):
    srcs, refs = refs[:13], refs[13:]
    dsts, (low, wide, insem, outsem, passsem) = refs[:13], refs[13:]
    passes = []
    for i in range(3):
        copy = pltpu.make_async_copy(srcs[i], dsts[i], passsem.at[i])
        copy.start()
        passes.append(copy)
    tiles = []
    for i in range(3, 13):
        rows, cols = srcs[i].shape
        for r in range(0, rows, HALF):
            for q in range(0, cols, HALF):
                tiles.append((i, pl.ds(r, HALF), pl.ds(q, HALF)))
    depth = low.shape[0]
    ins, outs = {}, {}

    def start_in(n):
        i, rows, cols = tiles[n]
        ins[n] = pltpu.make_async_copy(srcs[i].at[rows, cols], low.at[n % depth], insem.at[n % depth])
        ins[n].start()

    for n in range(depth):
        start_in(n)
    for n in range(len(tiles)):
        slot = n % depth
        ins[n].wait()
        if n >= depth:
            outs[n - depth].wait()

        def body(i, slot=slot):
            rows = pl.ds(pl.multiple_of(i * 64, 64), 64)
            wide[slot, rows, :] = low[slot, rows, :].astype(F32)

        loop(HALF // 64, body)
        i, rows, cols = tiles[n]
        outs[n] = pltpu.make_async_copy(wide.at[slot], dsts[i].at[rows, cols], outsem.at[slot])
        outs[n].start()
        if n + depth < len(tiles):
            start_in(n + depth)
    for n in range(len(tiles) - depth, len(tiles)):
        outs[n].wait()
    for copy in passes:
        copy.wait()


def run_finish(args):
    any_spec = pl.BlockSpec(memory_space=pl.ANY)
    depth = 6
    return pl.pallas_call(
        finish_kernel,
        out_shape=[
            jax.ShapeDtypeStruct(a.shape, BF if i < 3 else F32) for i, a in enumerate(args)
        ],
        in_specs=[any_spec] * 13,
        out_specs=[any_spec] * 13,
        scratch_shapes=[
            pltpu.VMEM((depth, HALF, HALF), BF), pltpu.VMEM((depth, HALF, HALF), F32),
            pltpu.SemaphoreType.DMA((depth,)), pltpu.SemaphoreType.DMA((depth,)),
            pltpu.SemaphoreType.DMA((3,)),
        ],
        compiler_params=pltpu.CompilerParams(vmem_limit_bytes=40 * MIB),
        name="finish",
    )(*args)


def per_device_pair(
    latents, inputs, latent_segment, input_segment, cross_query, cross_key, cross_value,
    cross_output, mlp_up, mlp_down, self_query, self_key, self_value, self_output,
    latent_gain, latent_bias, input_gain, input_bias, mlp_gain, mlp_bias, self_gain,
    self_bias, cotangent,
):
    vec = (
        latent_gain, latent_bias, input_gain, input_bias, mlp_gain, mlp_bias, self_gain, self_bias
    )
    lat = latents.reshape(ROWS, D)
    inp = inputs.reshape(NROWS, D)
    cot = cotangent.reshape(ROWS, D)
    kept = run_first((
        lat, inp, latent_segment, input_segment, *vec, cross_key, cross_value, cross_query,
        cross_output, mlp_up, mlp_down, self_query, self_key, self_value, self_output, cot,
    ))
    (new, glat, ginp, gq, gk, gv, go, gup, gdown, gsq, gsk, gsv, gso, gvec) = run_second(
        tuple(kept) + (
            lat, inp, mlp_up, mlp_down, self_query, self_key, self_value, self_output, cot
        )
    )
    new, glat, ginp, *grads = run_finish(
        (new, glat, ginp, gq, gk, gv, go, gup, gdown, gsq, gsk, gsv, gso)
    )
    x = lax.axis_index("shard")
    small = lax.dynamic_slice_in_dim(gvec, x * HALF, HALF, 1)
    return (
        new.reshape(latents.shape), glat.reshape(latents.shape), ginp.reshape(inputs.shape),
        *grads, *[small[i] for i in range(8)],
    )


def norm_forward(values, gain, shift):
    centred = values - jnp.mean(values, axis=-1, keepdims=True)
    inv_std = lax.rsqrt(jnp.mean(centred * centred, axis=-1, keepdims=True) + EPSILON)
    normed = centred * inv_std
    return (normed * gain + shift, normed, inv_std)


def norm_backward(grad_out, normed, inv_std, gain):
    scaled = grad_out * gain
    first_mean = jnp.mean(scaled, axis=-1, keepdims=True)
    second_mean = jnp.mean(scaled * normed, axis=-1, keepdims=True)
    grad_in = inv_std * (scaled - first_mean - normed * second_mean)
    return (grad_in, jnp.sum(grad_out * normed, axis=0), jnp.sum(grad_out, axis=0))


def product(left, right):
    return jnp.dot(left, right, preferred_element_type=jnp.float32)


def inner_rows(left, right):
    return lax.dot_general(
        left, right, (((0,), (0,)), ((), ())), preferred_element_type=jnp.float32
    )


def outer_cols(left, right):
    return lax.dot_general(
        left, right, (((1,), (1,)), ((), ())), preferred_element_type=jnp.float32
    )


def forward_total(term):
    return lax.psum(term.astype(jnp.bfloat16), "shard").astype(jnp.float32)


def backward_total(term):
    return lax.psum(term.astype(jnp.bfloat16), "shard").astype(jnp.float32)


def per_device(
    latents,
    inputs,
    latent_segment,
    input_segment,
    cross_query,
    cross_key,
    cross_value,
    cross_output,
    mlp_up,
    mlp_down,
    self_query,
    self_key,
    self_value,
    self_output,
    latent_gain,
    latent_bias,
    input_gain,
    input_bias,
    mlp_gain,
    mlp_bias,
    self_gain,
    self_bias,
    cotangent,
):
    shards = lax.axis_size("shard")
    groups, lat_len, width = latents.shape
    inp_len = inputs.shape[1]
    width_part = width // shards
    column_start = lax.axis_index("shard") * width_part
    rows = groups * lat_len
    scale = HEAD_DIM ** (-0.5)
    gathered = (
        lax.all_gather(cross_query, "shard", axis=0, tiled=True),
        lax.all_gather(cross_key, "shard", axis=0, tiled=True),
        lax.all_gather(cross_value, "shard", axis=0, tiled=True),
        lax.all_gather(cross_output, "shard", axis=0, tiled=True),
        lax.all_gather(latent_gain, "shard", axis=0, tiled=True),
        lax.all_gather(latent_bias, "shard", axis=0, tiled=True),
        lax.all_gather(input_gain, "shard", axis=0, tiled=True),
        lax.all_gather(input_bias, "shard", axis=0, tiled=True),
        lax.all_gather(mlp_gain, "shard", axis=0, tiled=True),
        lax.all_gather(mlp_bias, "shard", axis=0, tiled=True),
        lax.all_gather(self_gain, "shard", axis=0, tiled=True),
        lax.all_gather(self_bias, "shard", axis=0, tiled=True),
    )
    full_query, full_key, full_value, full_output = (
        gathered[0],
        gathered[1],
        gathered[2],
        gathered[3],
    )
    gain_lat, bias_lat, gain_inp, bias_inp, gain_mlp, bias_mlp, gain_self, bias_self = [
        piece.astype(jnp.float32) for piece in gathered[4:]
    ]
    lat_rows = latents.astype(jnp.float32).reshape(rows, width)
    inp_rows = inputs.astype(jnp.float32).reshape(groups * inp_len, width)
    lat_value, lat_normed, lat_inv = norm_forward(lat_rows, gain_lat, bias_lat)
    lat_in = lat_value.astype(jnp.bfloat16)
    inp_value, inp_normed, inp_inv = norm_forward(inp_rows, gain_inp, bias_inp)
    inp_in = inp_value.astype(jnp.bfloat16)
    cross_q = (
        product(lat_in, full_query).astype(jnp.bfloat16).reshape(groups, lat_len, HEADS, HEAD_DIM)
    )
    cross_k = (
        product(inp_in, full_key).astype(jnp.bfloat16).reshape(groups, inp_len, HEADS, HEAD_DIM)
    )
    cross_v = (
        product(inp_in, full_value).astype(jnp.bfloat16).reshape(groups, inp_len, HEADS, HEAD_DIM)
    )
    allowed = latent_segment[:, None, :, None] == input_segment[:, None, None, :]
    scores = (
        jnp.einsum("glhd,gnhd->ghln", cross_q, cross_k, preferred_element_type=jnp.float32) * scale
    )
    masked = jnp.where(allowed, scores, NEGATIVE)
    part_max = jnp.max(masked, axis=-1)
    top = lax.pmax(part_max, "shard")
    total = lax.psum(
        jnp.sum(jnp.where(allowed, jnp.exp(masked - top[..., None]), 0.0), axis=-1), "shard"
    )
    cross_prob = jnp.where(allowed, jnp.exp(masked - top[..., None]), 0.0) / total[..., None]
    cross_prob_low = cross_prob.astype(jnp.bfloat16)
    part_out = jnp.einsum(
        "ghln,gnhd->glhd", cross_prob_low, cross_v, preferred_element_type=jnp.float32
    )
    attended = lax.psum(part_out.astype(jnp.bfloat16), "shard").astype(jnp.float32)
    attended_in = attended.reshape(rows, width).astype(jnp.bfloat16)
    h_one = lat_rows + product(attended_in, full_output)
    mlp_value, mlp_normed, mlp_inv = norm_forward(h_one, gain_mlp, bias_mlp)
    mlp_in = mlp_value.astype(jnp.bfloat16)
    pre_act = product(mlp_in, mlp_up)
    hidden_in = jax.nn.gelu(pre_act).astype(jnp.bfloat16)
    h_two = h_one + forward_total(product(hidden_in, mlp_down))
    self_value_n, self_normed, self_inv = norm_forward(h_two, gain_self, bias_self)
    self_in = self_value_n.astype(jnp.bfloat16)
    local_heads = self_query.shape[1] // HEAD_DIM
    local_width = local_heads * HEAD_DIM
    self_q = (
        product(self_in, self_query)
        .astype(jnp.bfloat16)
        .reshape(groups, lat_len, local_heads, HEAD_DIM)
    )
    self_k = (
        product(self_in, self_key)
        .astype(jnp.bfloat16)
        .reshape(groups, lat_len, local_heads, HEAD_DIM)
    )
    self_v = (
        product(self_in, self_value)
        .astype(jnp.bfloat16)
        .reshape(groups, lat_len, local_heads, HEAD_DIM)
    )
    self_scores = (
        jnp.einsum("glhd,gmhd->ghlm", self_q, self_k, preferred_element_type=jnp.float32) * scale
    )
    self_prob = jax.nn.softmax(self_scores, axis=-1)
    self_prob_low = self_prob.astype(jnp.bfloat16)
    self_att = jnp.einsum(
        "ghlm,gmhd->glhd", self_prob_low, self_v, preferred_element_type=jnp.float32
    )
    self_att_in = self_att.reshape(rows, local_width).astype(jnp.bfloat16)
    result = h_two + forward_total(product(self_att_in, self_output))
    new_latents = result.reshape(groups, lat_len, width).astype(jnp.bfloat16)
    grad_out = cotangent.astype(jnp.float32).reshape(rows, width)
    grad_branch = grad_out.astype(jnp.bfloat16)
    grad_self_output = inner_rows(self_att_in, grad_branch)
    grad_att = (
        outer_cols(grad_branch, self_output)
        .astype(jnp.bfloat16)
        .reshape(groups, lat_len, local_heads, HEAD_DIM)
    )
    delta = jnp.sum(grad_att.astype(jnp.float32) * self_att, axis=-1).transpose(0, 2, 1)
    grad_prob = jnp.einsum("glhd,gmhd->ghlm", grad_att, self_v, preferred_element_type=jnp.float32)
    grad_sv = jnp.einsum(
        "ghlm,glhd->gmhd", self_prob_low, grad_att, preferred_element_type=jnp.float32
    )
    grad_scores = (self_prob * (grad_prob - delta[..., None])).astype(jnp.bfloat16)
    grad_sq = (
        jnp.einsum("ghlm,gmhd->glhd", grad_scores, self_k, preferred_element_type=jnp.float32)
        * scale
    )
    grad_sk = (
        jnp.einsum("ghlm,glhd->gmhd", grad_scores, self_q, preferred_element_type=jnp.float32)
        * scale
    )
    grad_sq = grad_sq.astype(jnp.bfloat16).reshape(rows, local_width)
    grad_sk = grad_sk.astype(jnp.bfloat16).reshape(rows, local_width)
    grad_sv = grad_sv.astype(jnp.bfloat16).reshape(rows, local_width)
    grad_self_query = inner_rows(self_in, grad_sq)
    grad_self_key = inner_rows(self_in, grad_sk)
    grad_self_value = inner_rows(self_in, grad_sv)
    grad_self_in = backward_total(
        outer_cols(grad_sq, self_query)
        + outer_cols(grad_sk, self_key)
        + outer_cols(grad_sv, self_value)
    )
    grad_norm, gain_full, bias_full = norm_backward(grad_self_in, self_normed, self_inv, gain_self)
    grad_two = grad_out + grad_norm
    grad_self_gain = lax.dynamic_slice_in_dim(gain_full, column_start, width_part)
    grad_self_bias = lax.dynamic_slice_in_dim(bias_full, column_start, width_part)
    grad_mlp_branch = grad_two.astype(jnp.bfloat16)
    grad_mlp_down = inner_rows(hidden_in, grad_mlp_branch)
    grad_hidden = outer_cols(grad_mlp_branch, mlp_down)
    gelu_value, gelu_pull = jax.vjp(jax.nn.gelu, pre_act)
    grad_pre = gelu_pull(grad_hidden)[0].astype(jnp.bfloat16)
    grad_mlp_up = inner_rows(mlp_in, grad_pre)
    grad_mlp_in = backward_total(outer_cols(grad_pre, mlp_up))
    grad_norm, gain_full, bias_full = norm_backward(grad_mlp_in, mlp_normed, mlp_inv, gain_mlp)
    grad_one = grad_two + grad_norm
    grad_mlp_gain = lax.dynamic_slice_in_dim(gain_full, column_start, width_part)
    grad_mlp_bias = lax.dynamic_slice_in_dim(bias_full, column_start, width_part)
    grad_cross_branch = grad_one.astype(jnp.bfloat16)
    grad_cross_output = inner_rows(
        lax.dynamic_slice_in_dim(attended_in, column_start, width_part, 1), grad_cross_branch
    )
    grad_ca = (
        outer_cols(grad_cross_branch, full_output)
        .astype(jnp.bfloat16)
        .reshape(groups, lat_len, HEADS, HEAD_DIM)
    )
    cross_delta = jnp.sum(grad_ca.astype(jnp.float32) * attended, axis=-1).transpose(0, 2, 1)
    grad_cp = jnp.einsum("glhd,gnhd->ghln", grad_ca, cross_v, preferred_element_type=jnp.float32)
    grad_cv = jnp.einsum(
        "ghln,glhd->gnhd", cross_prob_low, grad_ca, preferred_element_type=jnp.float32
    )
    grad_cs = (cross_prob * (grad_cp - cross_delta[..., None])).astype(jnp.bfloat16)
    grad_cq_part = (
        jnp.einsum("ghln,gnhd->glhd", grad_cs, cross_k, preferred_element_type=jnp.float32) * scale
    )
    grad_ck = (
        jnp.einsum("ghln,glhd->gnhd", grad_cs, cross_q, preferred_element_type=jnp.float32) * scale
    )
    grad_cq = backward_total(grad_cq_part.reshape(rows, width)).astype(jnp.bfloat16)
    grad_ck = grad_ck.astype(jnp.bfloat16).reshape(groups * inp_len, width)
    grad_cv = grad_cv.astype(jnp.bfloat16).reshape(groups * inp_len, width)
    grad_cross_query = inner_rows(
        lax.dynamic_slice_in_dim(lat_in, column_start, width_part, 1), grad_cq
    )
    grad_lat_in = outer_cols(grad_cq, full_query)
    grad_norm, gain_full, bias_full = norm_backward(grad_lat_in, lat_normed, lat_inv, gain_lat)
    grad_latents = (grad_one + grad_norm).reshape(groups, lat_len, width).astype(jnp.bfloat16)
    grad_latent_gain = lax.dynamic_slice_in_dim(gain_full, column_start, width_part)
    grad_latent_bias = lax.dynamic_slice_in_dim(bias_full, column_start, width_part)
    key_term = inner_rows(inp_in, grad_ck)
    value_term = inner_rows(inp_in, grad_cv)
    grad_inp_in = outer_cols(grad_ck, full_key) + outer_cols(grad_cv, full_value)
    grad_inp, inp_gain_full, inp_bias_full = norm_backward(
        grad_inp_in, inp_normed, inp_inv, gain_inp
    )
    grad_inputs = grad_inp.reshape(groups, inp_len, width).astype(jnp.bfloat16)
    grad_cross_key, grad_cross_value, grad_input_gain, grad_input_bias = (
        lax.psum_scatter(
            key_term.astype(jnp.bfloat16), "shard", scatter_dimension=0, tiled=True
        ).astype(jnp.float32),
        lax.psum_scatter(
            value_term.astype(jnp.bfloat16), "shard", scatter_dimension=0, tiled=True
        ).astype(jnp.float32),
        lax.psum_scatter(
            inp_gain_full.astype(jnp.bfloat16), "shard", scatter_dimension=0, tiled=True
        ).astype(jnp.float32),
        lax.psum_scatter(
            inp_bias_full.astype(jnp.bfloat16), "shard", scatter_dimension=0, tiled=True
        ).astype(jnp.float32),
    )
    (
        grad_cross_query,
        grad_cross_key,
        grad_cross_value,
        grad_cross_output,
        grad_mlp_up,
        grad_mlp_down,
        grad_self_query,
        grad_self_key,
        grad_self_value,
        grad_self_output,
        grad_latent_gain,
        grad_latent_bias,
        grad_input_gain,
        grad_input_bias,
        grad_mlp_gain,
        grad_mlp_bias,
        grad_self_gain,
        grad_self_bias,
    ) = (
        lax.psum(grad_cross_query.astype(jnp.bfloat16), "grp").astype(jnp.float32),
        lax.psum(grad_cross_key.astype(jnp.bfloat16), "grp").astype(jnp.float32),
        lax.psum(grad_cross_value.astype(jnp.bfloat16), "grp").astype(jnp.float32),
        lax.psum(grad_cross_output.astype(jnp.bfloat16), "grp").astype(jnp.float32),
        lax.psum(grad_mlp_up.astype(jnp.bfloat16), "grp").astype(jnp.float32),
        lax.psum(grad_mlp_down.astype(jnp.bfloat16), "grp").astype(jnp.float32),
        lax.psum(grad_self_query.astype(jnp.bfloat16), "grp").astype(jnp.float32),
        lax.psum(grad_self_key.astype(jnp.bfloat16), "grp").astype(jnp.float32),
        lax.psum(grad_self_value.astype(jnp.bfloat16), "grp").astype(jnp.float32),
        lax.psum(grad_self_output.astype(jnp.bfloat16), "grp").astype(jnp.float32),
        lax.psum(grad_latent_gain.astype(jnp.bfloat16), "grp").astype(jnp.float32),
        lax.psum(grad_latent_bias.astype(jnp.bfloat16), "grp").astype(jnp.float32),
        lax.psum(grad_input_gain.astype(jnp.bfloat16), "grp").astype(jnp.float32),
        lax.psum(grad_input_bias.astype(jnp.bfloat16), "grp").astype(jnp.float32),
        lax.psum(grad_mlp_gain.astype(jnp.bfloat16), "grp").astype(jnp.float32),
        lax.psum(grad_mlp_bias.astype(jnp.bfloat16), "grp").astype(jnp.float32),
        lax.psum(grad_self_gain.astype(jnp.bfloat16), "grp").astype(jnp.float32),
        lax.psum(grad_self_bias.astype(jnp.bfloat16), "grp").astype(jnp.float32),
    )
    return (
        new_latents,
        grad_latents,
        grad_inputs,
        grad_cross_query,
        grad_cross_key,
        grad_cross_value,
        grad_cross_output,
        grad_mlp_up,
        grad_mlp_down,
        grad_self_query,
        grad_self_key,
        grad_self_value,
        grad_self_output,
        grad_latent_gain,
        grad_latent_bias,
        grad_input_gain,
        grad_input_bias,
        grad_mlp_gain,
        grad_mlp_bias,
        grad_self_gain,
        grad_self_bias,
    )


def solution(mesh):
    laid_out = mesh.shape["shard"] == 2 and mesh.shape["grp"] == 16
    return jax.shard_map(
        per_device_pair if laid_out else per_device,
        mesh=mesh,
        in_specs=(
            P("grp", None, None),
            P("grp", "shard", None),
            P("grp", None),
            P("grp", "shard"),
            P("shard", None),
            P("shard", None),
            P("shard", None),
            P("shard", None),
            P(None, "shard"),
            P("shard", None),
            P(None, "shard"),
            P(None, "shard"),
            P(None, "shard"),
            P("shard", None),
            P("shard"),
            P("shard"),
            P("shard"),
            P("shard"),
            P("shard"),
            P("shard"),
            P("shard"),
            P("shard"),
            P("grp", None, None),
        ),
        out_specs=(
            P("grp", None, None),
            P("grp", None, None),
            P("grp", "shard", None),
            P("shard", None),
            P("shard", None),
            P("shard", None),
            P("shard", None),
            P(None, "shard"),
            P("shard", None),
            P(None, "shard"),
            P(None, "shard"),
            P(None, "shard"),
            P("shard", None),
            P("shard"),
            P("shard"),
            P("shard"),
            P("shard"),
            P("shard"),
            P("shard"),
            P("shard"),
            P("shard"),
        ),
        check_vma=False,
    )
```

```python
import jax
import jax.numpy as jnp
from jax import lax
from jax.experimental import pallas as pl
from jax.experimental.pallas import tpu as pltpu
from jax.sharding import PartitionSpec as P

HEADS = 8
HEAD_DIM = 128


EPSILON = 1e-05
NEGATIVE = -1e30

BF = jnp.bfloat16
F32 = jnp.float32
MESH = pl.DeviceIdType.MESH
LAT = 128
INP = 784
D = 1024
HALF = 512
HID = 2048
ROWS = 2 * LAT
NROWS = 2 * INP
SCALE = HEAD_DIM ** (-0.5)
MIB = 1 << 20


def nn(a, b):
    return lax.dot_general(a, b, (((1,), (0,)), ((), ())), preferred_element_type=F32)


def nt(a, b):
    return lax.dot_general(a, b, (((1,), (1,)), ((), ())), preferred_element_type=F32)


def tn(a, b):
    return lax.dot_general(a, b, (((0,), (0,)), ((), ())), preferred_element_type=F32)


def place():
    g = lax.axis_index("grp")
    x = lax.axis_index("shard")
    c = lax.rem(g, 2)
    y = lax.rem(g // 2, 2)
    a = lax.rem(g // 4, 2)
    b = g // 8
    return dict(
        x=x, c=c, y=y, a=a, b=b,
        xp=(g, 1 - x),
        cp=(g + 1 - 2 * c, x),
        yp=(g + 2 - 4 * y, x),
        ap=(g + 4 - 8 * a, x),
        bp=(g + 8 - 16 * b, x),
    )


def greet(partners):
    barrier = pltpu.get_barrier_semaphore()
    for partner in partners:
        pl.semaphore_signal(barrier, inc=1, device_id=partner, device_id_type=MESH)
    pl.semaphore_wait(barrier, len(partners))


def remote(src, dst, send, recv, partner):
    return pltpu.make_async_remote_copy(
        src_ref=src, dst_ref=dst, send_sem=send, recv_sem=recv,
        device_id=partner, device_id_type=MESH,
    )


def norm(v, gain, shift):
    cen = v - jnp.mean(v, axis=-1, keepdims=True)
    inv = lax.rsqrt(jnp.mean(cen * cen, axis=-1, keepdims=True) + EPSILON)
    return cen * inv * gain + shift


def vec_row(vecs, i):
    return jnp.concatenate([vecs[0, i:i + 1, :], vecs[1, i:i + 1, :]], axis=1)


def span(first, last, body):
    lax.fori_loop(first, last, lambda i, carry: (body(i), carry)[1], 0)


def loop(n, body):
    span(0, n, body)


def first_kernel(
    lat_h, inp_h, seglat, seginp, v0, v1, v2, v3, v4, v5, v6, v7, wk_h, wv_h, wq_h, wo_h, up_h, down_h,
    sq_h, sk_h, sv_h, so_h, cot_h,
    wf_o, ck_o, cv_o, inin_o, latin_o, cq_o, att_o, st_o, vec_o, hone_o, htwo_o,
    mlpin_o, selfin_o, pre_o, hid_o, ds_o, slow_o, mask_o,
    wf, inp, inin, ck, cv, lat, latin, cq, mask, segs, axb, stx, att, st, vecs,
    hone, htwo, mlpin, pre, hid, xm, selfin, wup, wdown, wself, wso, cot, qkv, dself,
    ds, slow, lsem, osem, xs, xr, ys, yr, c0s, c0r, c1s, c1r, ms, mr,
):
    me = place()
    x, y, c = me["x"], me["y"], me["c"]
    xp, yp, cp = me["xp"], me["yp"], me["cp"]
    nlocal = [0]
    nout = [0]

    def load(src, dst):
        copy = pltpu.make_async_copy(src, dst, lsem.at[nlocal[0]])
        nlocal[0] += 1
        copy.start()
        return copy

    outs = []

    def store(src, dst):
        copy = pltpu.make_async_copy(src, dst, osem.at[nout[0]])
        nout[0] += 1
        copy.start()
        outs.append(copy)

    own = pl.ds(pl.multiple_of(x * HALF, HALF), HALF)
    in_inp = load(inp_h, inp)
    in_lat = load(lat_h, lat)
    in_cot = load(cot_h, cot)
    in_so = load(so_h, wso)
    greet((xp, yp, cp))
    for i, v in enumerate((v0, v1, v2, v3, v4, v5, v6, v7)):
        vecs[x, i:i + 1, :] = v[...].astype(F32).reshape(1, HALF)
    vec_move = remote(vecs.at[x], vecs.at[x], xs.at[4], xr.at[4], xp)
    vec_move.start()
    weights = (wk_h, wv_h, wq_h, wo_h)
    quarter = 2 * y + c

    def part(w, side, q):
        return wf.at[w, pl.ds(pl.multiple_of(side * HALF + q * 128, 128), 128)]

    x_moves = []
    for w in range(4):
        src = weights[w].at[pl.ds(pl.multiple_of(quarter * 128, 128), 128)]
        move = remote(src, part(w, x, quarter), xs.at[w], xr.at[w], xp)
        move.start()
        x_moves.append(move)
    in_w = [load(weights[w], wf.at[w, own]) for w in range(4)]
    in_self = [load(h, wself.at[i]) for i, h in enumerate((sq_h, sk_h, sv_h))]
    in_up = load(up_h, wup)
    in_down = load(down_h, wdown)
    pending = []

    def forward_x(w):
        x_moves[w].wait()
        for sems, partner in (((ys, yr), yp), ((c0s, c0r), cp)):
            block = part(w, 1 - x, quarter)
            move = remote(block, block, sems[0].at[w], sems[1].at[w], partner)
            move.start()
            pending.append(move)

    def forward_y(w):
        block = part(w, 1 - x, quarter)
        remote(block, block, ys.at[w], yr.at[w], yp).wait_recv()
        block = part(w, 1 - x, 2 * (1 - y) + c)
        move = remote(block, block, c1s.at[w], c1r.at[w], cp)
        move.start()
        pending.append(move)

    def whole(w):
        block = part(w, 1 - x, quarter)
        remote(block, block, c0s.at[w], c0r.at[w], cp).wait_recv()
        remote(block, block, c1s.at[w], c1r.at[w], cp).wait_recv()
        in_w[w].wait()
        store(wf.at[w], wf_o.at[w])

    segs[...] = jnp.zeros_like(segs)
    segs[0:2, 0:INP] = seginp[...].astype(F32)
    for g in range(2):
        lat_row = seglat[g:g + 1, :].astype(F32)
        for j in range(7):
            count = min(128, INP - j * 128)
            col = jnp.broadcast_to(segs[g:g + 1, j * 128:(j + 1) * 128], (128, 128)).T
            mask[g * INP + j * 128:g * INP + j * 128 + count, :] = jnp.where(
                col[:count] == lat_row, 0.0, NEGATIVE
            ).astype(BF)
    store(mask, mask_o)
    in_cot.wait()
    in_so.wait()
    dself[...] = nt(cot[...], wso[...]).astype(BF)
    in_inp.wait()
    vec_move.wait()
    store(vecs, vec_o)
    gain_inp, bias_inp = vec_row(vecs, 2), vec_row(vecs, 3)

    def norm_rows(i):
        rows = pl.ds(pl.multiple_of(i * 32, 32), 32)
        inin[rows, :] = norm(inp[rows, :].astype(F32), gain_inp, bias_inp).astype(BF)

    span(0, 24, norm_rows)
    forward_x(0)
    span(24, 49, norm_rows)
    store(inin, inin_o)
    forward_x(1)
    forward_y(0)
    in_lat.wait()
    latin[...] = norm(lat[...].astype(F32), vec_row(vecs, 0), vec_row(vecs, 1)).astype(BF)
    store(latin, latin_o)

    def project(target, w, half):
        cols = slice(half * HALF, (half + 1) * HALF)

        def body(i):
            rows = pl.ds(pl.multiple_of(i * INP, 16), INP)
            target[rows, cols] = nn(inin[rows, :], wf[w, :, cols]).astype(BF)

        loop(2, body)

    whole(0)
    project(ck, 0, 0)
    forward_x(2)
    forward_y(1)
    project(ck, 0, 1)
    store(ck, ck_o)
    whole(1)
    forward_x(3)
    forward_y(2)
    project(cv, 1, 0)
    project(cv, 1, 1)
    store(cv, cv_o)
    whole(2)
    cq[...] = nn(latin[...], wf[2]).astype(BF)
    store(cq, cq_o)
    forward_y(3)

    def head(g, h):
        cols = pl.ds(pl.multiple_of(h * HEAD_DIM, HEAD_DIM), HEAD_DIM)
        n_rows = slice(g * INP, (g + 1) * INP)
        s = nt(ck[n_rows, cols], cq[g * LAT:(g + 1) * LAT, cols]) * SCALE + mask[n_rows, :].astype(F32)
        top = jnp.maximum(jnp.max(s, axis=0, keepdims=True), 0.1 * NEGATIVE)
        e = jnp.exp(s - top)
        total = jnp.sum(e, axis=0, keepdims=True)
        out = tn(cv[n_rows, cols], e.astype(BF))
        out = out * jnp.where(total > 0.0, 1.0 / total, 0.0)
        axb[x, pl.ds(pl.multiple_of(g * D + h * HEAD_DIM, HEAD_DIM), HEAD_DIM), :] = out.astype(BF)
        stx[x, g, pl.ds(h, 1), :] = top
        stx[x, g, pl.ds(HEADS + h, 1), :] = total

    a_moves = []
    for g in range(2):
        def pair(i, g=g):
            head(g, 2 * i)
            head(g, 2 * i + 1)

        loop(HEADS // 2, pair)
        block = axb.at[x, pl.ds(g * D, D)]
        for src, k in ((block, 0), (stx.at[x, g], 1)):
            move = remote(src, src, ms.at[2 * g + k], mr.at[2 * g + k], xp)
            move.start()
            a_moves.append(move)
    whole(3)
    for g in range(2):
        a_moves[2 * g].wait()
        a_moves[2 * g + 1].wait()
        for h in range(HEADS):
            m0, m1 = stx[0, g, h:h + 1, :], stx[1, g, h:h + 1, :]
            top = jnp.maximum(m0, m1)
            w0 = stx[0, g, HEADS + h:HEADS + h + 1, :] * jnp.exp(m0 - top)
            w1 = stx[1, g, HEADS + h:HEADS + h + 1, :] * jnp.exp(m1 - top)
            inv = 1.0 / (w0 + w1)
            rows = slice(g * D + h * HEAD_DIM, g * D + (h + 1) * HEAD_DIM)
            mixed = axb[0, rows, :].astype(F32) * (w0 * inv) + axb[1, rows, :].astype(F32) * (w1 * inv)
            att[rows, :] = mixed.astype(BF)
            st[g, h:h + 1, :] = top
            st[g, HEADS + h:HEADS + h + 1, :] = inv
        lrows = slice(g * LAT, (g + 1) * LAT)
        hone[lrows, :] = lat[lrows, :].astype(F32) + tn(att[g * D:(g + 1) * D, :], wf[3])
    store(att, att_o)
    store(st, st_o)
    store(hone, hone_o)
    mlpin[...] = norm(hone[...], vec_row(vecs, 4), vec_row(vecs, 5)).astype(BF)
    store(mlpin, mlpin_o)
    in_up.wait()
    for j in range(4):
        cols = slice(j * HALF, (j + 1) * HALF)
        u = nn(mlpin[...], wup[:, cols])
        pre[:, cols] = u
        hid[:, cols] = jax.nn.gelu(u).astype(BF)
    store(pre, pre_o)
    store(hid, hid_o)
    in_down.wait()
    m_moves = []
    for j in range(2):
        xm[x, j] = nn(hid[...], wdown[:, j * HALF:(j + 1) * HALF]).astype(BF)
        move = remote(xm.at[x, j], xm.at[x, j], ms.at[4 + j], mr.at[4 + j], xp)
        move.start()
        m_moves.append(move)
    for copy in in_self:
        copy.wait()
    for j in range(2):
        m_moves[j].wait()
        cols = slice(j * HALF, (j + 1) * HALF)
        htwo[:, cols] = hone[:, cols] + (xm[0, j].astype(F32) + xm[1, j].astype(F32))
    store(htwo, htwo_o)
    selfin[...] = norm(htwo[...], vec_row(vecs, 6), vec_row(vecs, 7)).astype(BF)
    store(selfin, selfin_o)
    for i in range(3):
        qkv[i] = nn(selfin[...], wself[i]).astype(BF)

    def self_group(g):
        rows = pl.ds(pl.multiple_of(g * LAT, LAT), LAT)
        for h in range(4):
            cols = slice(h * HEAD_DIM, (h + 1) * HEAD_DIM)
            q, k, v = qkv[0, rows, cols], qkv[1, rows, cols], qkv[2, rows, cols]
            do = dself[rows, cols]
            s = nt(q, k) * SCALE
            e = jnp.exp(s - jnp.max(s, axis=1, keepdims=True))
            p = e / jnp.sum(e, axis=1, keepdims=True)
            p_low = p.astype(BF)
            o = nn(p_low, v)
            slow[rows, cols] = o.astype(BF)
            delta = jnp.sum(do.astype(F32) * o, axis=1, keepdims=True)
            dp = nt(do, v)
            dsc = (p * (dp - delta)).astype(BF)
            ds[0, rows, cols] = (nn(dsc, k) * SCALE).astype(BF)
            ds[1, rows, cols] = (tn(dsc, q) * SCALE).astype(BF)
            ds[2, rows, cols] = tn(p_low, do).astype(BF)

    loop(2, self_group)
    store(ds, ds_o)
    store(slow, slow_o)
    for move in pending:
        move.wait_send()
    for copy in outs:
        copy.wait()


def run_first(args):
    any_spec = pl.BlockSpec(memory_space=pl.ANY)
    vmem_spec = pl.BlockSpec(memory_space=pltpu.VMEM)
    outs = [
        ((4, D, D), BF), ((NROWS, D), BF), ((NROWS, D), BF), ((NROWS, D), BF),
        ((ROWS, D), BF), ((ROWS, D), BF), ((2 * D, LAT), BF), ((2, 16, LAT), F32),
        ((2, 8, HALF), F32), ((ROWS, D), F32), ((ROWS, D), F32), ((ROWS, D), BF),
        ((ROWS, D), BF), ((ROWS, HID), F32), ((ROWS, HID), BF), ((3, ROWS, HALF), BF),
        ((ROWS, HALF), BF), ((NROWS, LAT), BF),
    ]
    scratch = [
        ((4, D, D), BF), ((NROWS, D), BF), ((NROWS, D), BF), ((NROWS, D), BF), ((NROWS, D), BF),
        ((ROWS, D), BF), ((ROWS, D), BF), ((ROWS, D), BF), ((NROWS, LAT), BF), ((8, 896), F32),
        ((2, 2 * D, LAT), BF), ((2, 2, 16, LAT), F32), ((2 * D, LAT), BF), ((2, 16, LAT), F32),
        ((2, 8, HALF), F32), ((ROWS, D), F32), ((ROWS, D), F32), ((ROWS, D), BF),
        ((ROWS, HID), F32), ((ROWS, HID), BF), ((2, 2, ROWS, HALF), BF), ((ROWS, D), BF),
        ((D, HID), BF), ((HID, D), BF), ((3, D, HALF), BF), ((HALF, D), BF), ((ROWS, D), BF),
        ((3, ROWS, HALF), BF), ((ROWS, HALF), BF), ((3, ROWS, HALF), BF), ((ROWS, HALF), BF),
    ]
    dma = pltpu.SemaphoreType.DMA
    return pl.pallas_call(
        first_kernel,
        out_shape=[jax.ShapeDtypeStruct(*o) for o in outs],
        in_specs=[any_spec] * 2 + [vmem_spec] * 10 + [any_spec] * 11,
        out_specs=[any_spec] * len(outs),
        scratch_shapes=[pltpu.VMEM(*s) for s in scratch]
        + [dma((16,)), dma((24,))] + [dma((5,))] * 2 + [dma((4,))] * 6 + [dma((6,))] * 2,
        compiler_params=pltpu.CompilerParams(
            collective_id=0, has_side_effects=True, vmem_limit_bytes=58 * MIB
        ),
        name="forward",
    )(*args)


def norm_back(v, dy, gain):
    cen = v - jnp.mean(v, axis=-1, keepdims=True)
    inv = lax.rsqrt(jnp.mean(cen * cen, axis=-1, keepdims=True) + EPSILON)
    n = cen * inv
    t = dy * gain
    dv = inv * (t - jnp.mean(t, axis=-1, keepdims=True) - n * jnp.mean(t * n, axis=-1, keepdims=True))
    return (
        dv,
        jnp.sum(dy * n, axis=0, keepdims=True),
        jnp.sum(dy, axis=0, keepdims=True),
    )


def gelu_slope(u):
    root = (2.0 / jnp.pi) ** 0.5
    t = jnp.tanh(root * (u + 0.044715 * u * u * u))
    return 0.5 * (1.0 + t) + 0.5 * u * (1.0 - t * t) * root * (1.0 + 3.0 * 0.044715 * u * u)


CHUNKS = 16
OFFSETS = (0, 1, 4, 5, 6, 7, 10, 11)


def second_kernel(
    wf_h, ck_h, cv_h, inin_h, latin_h, cq_h, att_h, st_h, vec_h, hone_h, htwo_h,
    mlpin_h, selfin_h, pre_h, hid_h, ds_h, slow_h, mask_h,
    lat_h, inp_h, up_h, down_h, sq_h, sk_h, sv_h, so_h, cot_h,
    newlat_o, glat_o, ginp_o, grad_o, gvec_o,
    z, wf, latin, cq, att, st, vecs, hone, htwo, etwo, mlpin, selfin, pre, hid, ds,
    slow, mask, lat, cot, elow2, elow1, dpre, dcr, xb, grad, other, dyb,
    tk, xk, gvec,
    lsem, osem, xs, xr,
):
    me = place()
    x, c = me["x"], me["c"]
    xp, cp = me["xp"], me["cp"]
    counts = [0, 0]
    outs = []

    def load(src, dst):
        copy = pltpu.make_async_copy(src, dst, lsem.at[counts[0]])
        counts[0] += 1
        copy.start()
        return copy

    def store(src, dst):
        copy = pltpu.make_async_copy(src, dst, osem.at[counts[1]])
        counts[1] += 1
        copy.start()
        outs.append(copy)

    in_ds = load(ds_h, ds)
    in_self = [
        load(sq_h, z.at[pl.ds(4096, D), pl.ds(0, HALF)]),
        load(sk_h, z.at[pl.ds(4096, D), pl.ds(HALF, HALF)]),
        load(sv_h, z.at[pl.ds(5120, D), pl.ds(0, HALF)]),
    ]
    in_early = [load(slow_h, slow), load(cot_h, cot), load(selfin_h, selfin)] + [
        load(so_h.at[:, pl.ds(j * HALF, HALF)], z.at[pl.ds(5120 + j * HALF, HALF), pl.ds(HALF, HALF)])
        for j in range(2)
    ]
    in_two = [load(htwo_h, htwo), load(vec_h, vecs)]
    in_mlp = [
        load(pre_h, pre), load(down_h, z.at[pl.ds(0, HID)]),
        load(up_h.at[:, pl.ds(0, D)], z.at[pl.ds(HID, D)]),
        load(up_h.at[:, pl.ds(D, D)], z.at[pl.ds(HID + D, D)]),
    ]
    in_mid = [load(hid_h, hid), load(mlpin_h, mlpin), load(hone_h, hone)]
    in_cross = [
        load(wf_h, wf), load(att_h, att), load(st_h, st), load(cq_h, cq), load(mask_h, mask),
        load(latin_h, latin), load(lat_h, lat),
    ]
    greet((xp, cp))

    def wait_all(copies):
        for copy in copies:
            copy.wait()

    def add_in(k, off, size, temp):
        cols = pl.ds(pl.multiple_of(c * HALF, HALF), HALF)

        def body(i):
            rows = pl.ds(pl.multiple_of(k * HALF + off + i * 64, 64), 64)
            part = temp[pl.ds(pl.multiple_of(i * 64, 64), 64), :]
            grad[rows, cols] = (grad[rows, cols].astype(F32) + part.astype(F32)).astype(BF)

        loop(size // 64, body)

    def tick(chunk=None):
        if chunk is not None:
            store(grad.at[pl.ds(chunk * HALF, HALF)], grad_o.at[pl.ds(chunk * HALF, HALF)])

    k_moves = {}

    def start_core(w):
        src = other.at[w, :, pl.ds(pl.multiple_of((1 - c) * HALF, HALF), HALF)]
        move = remote(src, tk.at[w], xs.at[8 + w], xr.at[8 + w], cp)
        move.start()
        k_moves[w, 0] = move

    def start_x(w):
        k_moves[w, 0].wait()
        cols = pl.ds(pl.multiple_of(c * HALF, HALF), HALF)

        def body(i):
            rows = pl.ds(pl.multiple_of(i * 64, 64), 64)
            other[w, rows, cols] = (
                other[w, rows, cols].astype(F32) + tk[w, rows, :].astype(F32)
            ).astype(BF)

        loop(HALF // 64, body)
        move = remote(other.at[w, :, cols], xk.at[w], xs.at[10 + w], xr.at[10 + w], xp)
        move.start()
        k_moves[w, 1] = move

    def finish_x(w):
        k_moves[w, 1].wait()
        add_in(14 + w, 0, HALF, xk.at[w])

    def exchange(n, part, index):
        move = remote(
            xb.at[(n, x) + part], xb.at[(n, x) + part], xs.at[index], xr.at[index], xp
        )
        move.start()
        return move

    def both(n, rows):
        return xb[n, 0, rows, :].astype(F32) + xb[n, 1, rows, :].astype(F32)

    def fill(k, half, value):
        grad[k * HALF:(k + 1) * HALF, half * HALF:(half + 1) * HALF] = value.astype(BF)

    gvec[...] = jnp.zeros_like(gvec)

    in_ds.wait()
    wait_all(in_self)
    m_self = []
    for j in range(2):
        cols = slice(j * HALF, (j + 1) * HALF)
        a_rows = slice(4096 + j * HALF, 4096 + (j + 1) * HALF)
        b_rows = slice(5120 + j * HALF, 5120 + (j + 1) * HALF)
        xb[0, x, :, cols] = (
            nt(ds[0], z[a_rows, 0:HALF]) + nt(ds[1], z[a_rows, HALF:D]) + nt(ds[2], z[b_rows, 0:HALF])
        ).astype(BF)
        m_self.append(exchange(0, (slice(None), pl.ds(j * HALF, HALF)), j))
    wait_all(in_early)
    for j in range(2):
        fill(0, j, tn(slow[...], cot[:, j * HALF:(j + 1) * HALF]))
    tick(0)
    for i in range(3):
        for j in range(2):
            fill(1 + i, j, tn(selfin[:, j * HALF:(j + 1) * HALF], ds[i]))
        tick(1 + i)
    m_new = []
    for j in range(2):
        cols = slice(j * HALF, (j + 1) * HALF)
        xb[1, x, :, cols] = nn(slow[...], z[5120 + j * HALF:5120 + (j + 1) * HALF, HALF:D]).astype(BF)
        m_new.append(exchange(1, (slice(None), pl.ds(j * HALF, HALF)), 2 + j))
    tick()
    wait_all(in_two)
    wait_all(m_self)
    gain_self = vec_row(vecs, 6)

    def two_rows(i):
        rows = pl.ds(pl.multiple_of(i * 32, 32), 32)
        dv, dg, db = norm_back(htwo[rows, :], both(0, rows), gain_self)
        e = cot[rows, :].astype(F32) + dv
        etwo[rows, :] = e
        elow2[rows, :] = e.astype(BF)
        gvec[6:7, :] += dg
        gvec[7:8, :] += db

    loop(8, two_rows)
    tick()
    wait_all(in_mlp)
    for j in range(4):
        cols = slice(j * HALF, (j + 1) * HALF)
        gh = nt(elow2[...], z[cols, :])
        dpre[:, cols] = (gh * gelu_slope(pre[:, cols])).astype(BF)
    m_mlp = []
    for j in range(2):
        cols = slice(j * HALF, (j + 1) * HALF)
        xb[2, x, :, cols] = (
            nt(dpre[:, 0:D], z[HID + j * HALF:HID + (j + 1) * HALF, :])
            + nt(dpre[:, D:HID], z[HID + D + j * HALF:HID + D + (j + 1) * HALF, :])
        ).astype(BF)
        m_mlp.append(exchange(2, (slice(None), pl.ds(j * HALF, HALF)), 4 + j))
    ck, cv = z.at[pl.ds(0, NROWS)], z.at[pl.ds(NROWS, NROWS)]
    inin, inp = z.at[pl.ds(2 * NROWS, NROWS)], z.at[pl.ds(3 * NROWS, NROWS)]
    in_keys = [load(ck_h, ck), load(cv_h, cv)]
    in_late = [load(inin_h, inin), load(inp_h, inp)]
    wait_all(in_mid)

    def fill_down(j):
        for i in range(2):
            fill(4 + j, i, tn(hid[:, j * HALF:(j + 1) * HALF], elow2[:, i * HALF:(i + 1) * HALF]))

    def fill_up(j):
        for i in range(2):
            fill(8 + j, i, tn(mlpin[:, i * HALF:(i + 1) * HALF], dpre[:, j * HALF:(j + 1) * HALF]))

    fill_down(0)
    tick(4)
    fill_down(1)
    tick(5)
    fill_down(2)
    tick(6)
    fill_down(3)
    tick(7)
    wait_all(m_mlp)
    gain_mlp = vec_row(vecs, 4)

    def one_rows(i):
        rows = pl.ds(pl.multiple_of(i * 32, 32), 32)
        dv, dg, db = norm_back(hone[rows, :], both(2, rows), gain_mlp)
        e = etwo[rows, :] + dv
        hone[rows, :] = e
        elow1[rows, :] = e.astype(BF)
        gvec[4:5, :] += dg
        gvec[5:6, :] += db

    loop(8, one_rows)
    wait_all(in_cross)
    for g in range(2):
        dcr[g * D:(g + 1) * D, :] = nt(wf[3], elow1[g * LAT:(g + 1) * LAT, :]).astype(BF)

    wait_all(m_new)

    def new_rows(i):
        rows = pl.ds(pl.multiple_of(i * 64, 64), 64)
        selfin[rows, :] = (htwo[rows, :] + both(1, rows)).astype(BF)

    loop(4, new_rows)
    store(selfin, newlat_o)
    wait_all(in_keys)

    def head(g, h):
        cols = pl.ds(pl.multiple_of(h * HEAD_DIM, HEAD_DIM), HEAD_DIM)
        n_rows = slice(g * INP, (g + 1) * INP)
        l_rows = slice(g * LAT, (g + 1) * LAT)
        t_rows = pl.ds(pl.multiple_of(g * D + h * HEAD_DIM, HEAD_DIM), HEAD_DIM)
        k, v, q = ck[n_rows, cols], cv[n_rows, cols], cq[l_rows, cols]
        s = nt(k, q) * SCALE + mask[n_rows, :].astype(F32)
        p = jnp.exp(s - st[g, pl.ds(h, 1), :]) * st[g, pl.ds(HEADS + h, 1), :]
        do = dcr[t_rows, :]
        delta = jnp.sum(do.astype(F32) * att[t_rows, :].astype(F32), axis=0, keepdims=True)
        dsc = (p * (nn(v, do) - delta)).astype(BF)
        cv[n_rows, cols] = nt(p.astype(BF), do).astype(BF)
        ck[n_rows, cols] = (nn(dsc, q) * SCALE).astype(BF)
        xb[0, x, l_rows, cols] = (tn(dsc, k) * SCALE).astype(BF)

    fills = [lambda j=j: fill_up(j) for j in range(4)]
    m_query = []
    for g in range(2):
        for part in range(2):
            def heads(i, g=g, part=part):
                head(g, 4 * part + 2 * i)
                head(g, 4 * part + 2 * i + 1)

            loop(2, heads)
            fills[2 * g + part]()
            tick(8 + 2 * g + part)
        m_query.append(exchange(0, (pl.ds(g * LAT, LAT),), 6 + g))
    wait_all(in_late)

    def weight_grad(w, source):
        def body(i):
            rows = pl.ds(pl.multiple_of(i * 256, 256), 256)
            mine = pl.ds(pl.multiple_of(x * HALF + i * 256, 256), 256)
            theirs = pl.ds(pl.multiple_of((1 - x) * HALF + i * 256, 256), 256)
            other[w, rows, :] = tn(inin[:, theirs], source[...]).astype(BF)
            grad[pl.ds(pl.multiple_of((14 + w) * HALF + i * 256, 256), 256), :] = tn(
                inin[:, mine], source[...]
            ).astype(BF)

        loop(2, body)

    weight_grad(0, ck)
    start_core(0)
    tick()
    weight_grad(1, cv)
    start_x(0)
    start_core(1)
    for j in range(2):
        value = 0.0
        for g in range(2):
            rows = pl.ds(pl.multiple_of(g * D + x * HALF, HALF), HALF)
            value = value + nn(
                att[rows, :], elow1[g * LAT:(g + 1) * LAT, j * HALF:(j + 1) * HALF]
            )
        fill(12, j, value)
    start_x(1)
    tick(12)
    for w in range(2):
        finish_x(w)
    wait_all(m_query)
    dcq = elow2

    def query_rows(i):
        rows = pl.ds(pl.multiple_of(i * 64, 64), 64)
        dcq[rows, :] = both(0, rows).astype(BF)

    loop(4, query_rows)
    for j in range(2):
        mine = pl.ds(pl.multiple_of(x * HALF, HALF), HALF)
        fill(13, j, tn(latin[:, mine], dcq[:, j * HALF:(j + 1) * HALF]))
    tick(13)
    gain_lat = vec_row(vecs, 0)

    def lat_rows(i):
        rows = pl.ds(pl.multiple_of(i * 128, 128), 128)
        dv, dg, db = norm_back(lat[rows, :].astype(F32), nt(dcq[rows, :], wf[2]), gain_lat)
        lat[rows, :] = (hone[rows, :] + dv).astype(BF)
        gvec[0:1, :] += dg
        gvec[1:2, :] += db

    loop(2, lat_rows)
    store(lat, glat_o)
    gain_inp = vec_row(vecs, 2)

    def inp_rows(first):
        def body(i):
            rows = pl.ds(pl.multiple_of(first + i * 32, 16), 32)
            part = pl.ds(pl.multiple_of(i * 32, 32), 32)
            dv, dg, db = norm_back(inp[rows, :].astype(F32), dyb[part, :], gain_inp)
            inp[rows, :] = dv.astype(BF)
            gvec[2:3, :] += dg
            gvec[3:4, :] += db

        return body

    for first, count in ((0, 800), (800, 768)):
        rows = slice(first, first + count)
        for j in range(2):
            cols = slice(j * HALF, (j + 1) * HALF)
            dyb[0:count, cols] = nt(ck[rows, :], wf[0, cols, :]) + nt(cv[rows, :], wf[1, cols, :])
        loop(count // 32, inp_rows(first))
    tick(14)
    store(inp, ginp_o)
    tick(15)
    col = lax.broadcasted_iota(jnp.int32, (8, D), 1) // HALF
    row = lax.broadcasted_iota(jnp.int32, (8, D), 0)
    keep = (col == x) | (row == 2) | (row == 3)
    gvec[...] = jnp.where(keep, gvec[...], 0.0)
    store(gvec, gvec_o)
    wait_all(outs)


def run_second(args):
    any_spec = pl.BlockSpec(memory_space=pl.ANY)
    outs = [
        ((ROWS, D), BF), ((ROWS, D), BF), ((NROWS, D), BF), ((CHUNKS * HALF, D), BF), ((8, D), F32),
    ]
    scratch = [
        ((4 * NROWS, D), BF), ((4, D, D), BF), ((ROWS, D), BF), ((ROWS, D), BF),
        ((2 * D, LAT), BF), ((2, 16, LAT), F32), ((2, 8, HALF), F32), ((ROWS, D), F32),
        ((ROWS, D), F32), ((ROWS, D), F32), ((ROWS, D), BF), ((ROWS, D), BF), ((ROWS, HID), F32),
        ((ROWS, HID), BF), ((3, ROWS, HALF), BF), ((ROWS, HALF), BF), ((NROWS, LAT), BF),
        ((ROWS, D), BF), ((ROWS, D), BF), ((ROWS, D), BF), ((ROWS, D), BF), ((ROWS, HID), BF),
        ((2 * D, LAT), BF), ((3, 2, ROWS, D), BF), ((CHUNKS * HALF, D), BF),
        ((2, HALF, D), BF), ((800, D), F32), ((2, HALF, HALF), BF),
        ((2, HALF, HALF), BF), ((8, D), F32),
    ]
    dma = pltpu.SemaphoreType.DMA
    return pl.pallas_call(
        second_kernel,
        out_shape=[jax.ShapeDtypeStruct(*o) for o in outs],
        in_specs=[any_spec] * len(args),
        out_specs=[any_spec] * len(outs),
        scratch_shapes=[pltpu.VMEM(*s) for s in scratch]
        + [dma((32,)), dma((32,))] + [dma((12,))] * 2,
        compiler_params=pltpu.CompilerParams(
            collective_id=1, has_side_effects=True, vmem_limit_bytes=63 * MIB
        ),
        name="backward",
    )(*args)


def sum_kernel(
    grad_h, vec_h,
    gq_o, gk_o, gv_o, go_o, gup_o, gdown_o, gsq_o, gsk_o, gsv_o, gso_o, gvec_o,
    grad, t0, t1, t2, t3, gvec, gvr, lsem, osem, gs, gr, vs, vr,
):
    me = place()
    c = me["c"]
    xp, yp, cp, ap, bp = me["xp"], me["yp"], me["cp"], me["ap"], me["bp"]
    loads = []
    for k in range(CHUNKS):
        rows = pl.ds(k * HALF, HALF)
        copy = pltpu.make_async_copy(grad_h.at[rows], grad.at[rows], lsem.at[k])
        copy.start()
        loads.append(copy)
    in_vec = pltpu.make_async_copy(vec_h, gvec, lsem.at[CHUNKS])
    in_vec.start()
    greet((xp, yp, cp, ap, bp))

    moves = {}

    def block(k, off, size, core):
        return grad.at[
            pl.ds(pl.multiple_of(k * HALF + off, 16), size),
            pl.ds(pl.multiple_of(core * HALF, HALF), HALF),
        ]

    def add_in(k, off, size, temp):
        cols = pl.ds(pl.multiple_of(c * HALF, HALF), HALF)

        def body(i):
            rows = pl.ds(pl.multiple_of(k * HALF + off + i * 64, 64), 64)
            part = temp[pl.ds(pl.multiple_of(i * 64, 64), 64), :]
            grad[rows, cols] = (grad[rows, cols].astype(F32) + part.astype(F32)).astype(BF)

        loop(size // 64, body)

    def path(k):
        one, two = (me["y"], yp), (me["a"], ap)
        if k % 4 == 3:
            one, two = two, one
        return one, two, (me["b"], bp)

    def slots(k):
        if k % 4 == 3:
            return 6 + (k // 4) % 2, 2, k % 2
        n = k - k // 4
        return n % 6, n % 2, k % 2

    def offsets(k):
        (b1, _), (b2, _), _ = path(k)
        o1 = b1 * 256
        return o1, o1 + b2 * 128

    def result(k, off, size, core):
        rows = pl.ds(pl.multiple_of(core * HALF + off, 16), size)
        if 1 <= k <= 3:
            return (gsq_o, gsk_o, gsv_o)[k - 1].at[rows]
        if 8 <= k <= 11:
            return gup_o.at[rows, pl.ds((k - 8) * HALF, HALF)]
        cols = pl.ds(pl.multiple_of(core * HALF, HALF), HALF)
        if 4 <= k <= 7:
            return gdown_o.at[pl.ds(pl.multiple_of((k - 4) * HALF + off, 16), size), cols]
        target = {0: gso_o, 12: go_o, 13: gq_o, 14: gk_o, 15: gv_o}[k]
        return target.at[pl.ds(pl.multiple_of(off, 16), size), cols]

    def send(k, stage, src, dst, partner):
        move = remote(src, dst, gs.at[k * 8 + stage], gr.at[k * 8 + stage], partner)
        move.start()
        moves[k, stage] = move

    def event(k, s):
        first, second, third = slots(k)
        (b1, p1), (b2, p2), (_, p3) = path(k)
        o1, o2 = offsets(k)
        if s == 0:
            loads[k].wait()
            send(k, 0, block(k, 0, HALF, 1 - c), t0.at[k % 2], cp)
            return
        moves[k, s - 1].wait()
        if s == 1:
            add_in(k, 0, HALF, t0.at[k % 2])
            send(k, 1, block(k, (1 - b1) * 256, 256, c), t1.at[first], p1)
        elif s == 2:
            add_in(k, o1, 256, t1.at[first])
            send(k, 2, block(k, o1 + (1 - b2) * 128, 128, c), t2.at[second], p2)
        elif s == 3:
            add_in(k, o2, 128, t2.at[second])
            send(k, 3, block(k, o2, 128, c), t3.at[third], p3)
        elif s == 4:
            add_in(k, o2, 128, t3.at[third])
            own = block(k, o2, 128, c)
            target = result(k, o2, 128, c)
            send(k, 4, own, target, p2)
            copy = pltpu.make_async_copy(own, target, osem.at[16 + k])
            copy.start()
            moves[k, "own"] = copy
        elif s == 5:
            moves[k, "own"].wait()
            part = result(k, o1, 256, c)
            send(k, 5, part, part, p1)
        elif s == 6:
            part = result(k, 0, HALF, c)
            send(k, 6, part, part, cp)

    clock = [0]
    entered = {}

    def tick(chunk=None):
        now = clock[0]
        clock[0] += 1
        if chunk is not None:
            entered[chunk] = now
        for k in sorted(entered):
            if now - entered[k] in OFFSETS:
                event(k, OFFSETS.index(now - entered[k]))

    v_partners = (xp, cp, yp, ap, bp)
    v_moves = []

    def vec_event(s):
        if s > 0:
            v_moves[s - 1].wait()
            gvec[...] += gvr[s - 1]
        if s < 5:
            move = remote(gvec, gvr.at[s], vs.at[s], vr.at[s], v_partners[s])
            move.start()
            v_moves.append(move)
        else:
            copy = pltpu.make_async_copy(gvec, gvec_o, lsem.at[CHUNKS])
            copy.start()
            copy.wait()

    for k in range(CHUNKS):
        tick(k)
        if k == 2:
            in_vec.wait()
        if k >= 2 and k <= 7:
            vec_event(k - 2)
    for t in range(OFFSETS[-1]):
        tick()


def run_sum(args):
    any_spec = pl.BlockSpec(memory_space=pl.ANY)
    outs = [
        ((HALF, D), BF), ((HALF, D), BF),
        ((HALF, D), BF), ((HALF, D), BF), ((D, HID), BF), ((HID, D), BF), ((D, HALF), BF),
        ((D, HALF), BF), ((D, HALF), BF), ((HALF, D), BF), ((8, D), F32),
    ]
    scratch = [
        ((CHUNKS * HALF, D), BF), ((2, HALF, HALF), BF), ((8, 256, HALF), BF),
        ((3, 128, HALF), BF), ((2, 128, HALF), BF), ((8, D), F32), ((5, 8, D), F32),
    ]
    dma = pltpu.SemaphoreType.DMA
    return pl.pallas_call(
        sum_kernel,
        out_shape=[jax.ShapeDtypeStruct(*o) for o in outs],
        in_specs=[any_spec] * len(args),
        out_specs=[any_spec] * len(outs),
        scratch_shapes=[pltpu.VMEM(*s) for s in scratch]
        + [dma((17,)), dma((32,))] + [dma((CHUNKS * 8,))] * 2 + [dma((5,))] * 2,
        compiler_params=pltpu.CompilerParams(
            collective_id=2, has_side_effects=True, vmem_limit_bytes=62 * MIB
        ),
        name="sum_over_grp",
    )(*args)


def finish_kernel(*refs):
    srcs, refs = refs[:13], refs[13:]
    dsts, (low, wide, insem, outsem, passsem) = refs[:13], refs[13:]
    passes = []
    for i in range(3):
        copy = pltpu.make_async_copy(srcs[i], dsts[i], passsem.at[i])
        copy.start()
        passes.append(copy)
    tiles = []
    for i in range(3, 13):
        rows, cols = srcs[i].shape
        for r in range(0, rows, HALF):
            for q in range(0, cols, HALF):
                tiles.append((i, pl.ds(r, HALF), pl.ds(q, HALF)))
    depth = low.shape[0]
    ins, outs = {}, {}

    def start_in(n):
        i, rows, cols = tiles[n]
        ins[n] = pltpu.make_async_copy(srcs[i].at[rows, cols], low.at[n % depth], insem.at[n % depth])
        ins[n].start()

    for n in range(depth):
        start_in(n)
    for n in range(len(tiles)):
        slot = n % depth
        ins[n].wait()
        if n >= depth:
            outs[n - depth].wait()

        def body(i, slot=slot):
            rows = pl.ds(pl.multiple_of(i * 64, 64), 64)
            wide[slot, rows, :] = low[slot, rows, :].astype(F32)

        loop(HALF // 64, body)
        i, rows, cols = tiles[n]
        outs[n] = pltpu.make_async_copy(wide.at[slot], dsts[i].at[rows, cols], outsem.at[slot])
        outs[n].start()
        if n + depth < len(tiles):
            start_in(n + depth)
    for n in range(len(tiles) - depth, len(tiles)):
        outs[n].wait()
    for copy in passes:
        copy.wait()


def run_finish(args):
    any_spec = pl.BlockSpec(memory_space=pl.ANY)
    depth = 6
    return pl.pallas_call(
        finish_kernel,
        out_shape=[
            jax.ShapeDtypeStruct(a.shape, BF if i < 3 else F32) for i, a in enumerate(args)
        ],
        in_specs=[any_spec] * 13,
        out_specs=[any_spec] * 13,
        scratch_shapes=[
            pltpu.VMEM((depth, HALF, HALF), BF), pltpu.VMEM((depth, HALF, HALF), F32),
            pltpu.SemaphoreType.DMA((depth,)), pltpu.SemaphoreType.DMA((depth,)),
            pltpu.SemaphoreType.DMA((3,)),
        ],
        compiler_params=pltpu.CompilerParams(vmem_limit_bytes=62 * MIB),
        name="finish",
    )(*args)


def per_device_pair(
    latents, inputs, latent_segment, input_segment, cross_query, cross_key, cross_value,
    cross_output, mlp_up, mlp_down, self_query, self_key, self_value, self_output,
    latent_gain, latent_bias, input_gain, input_bias, mlp_gain, mlp_bias, self_gain,
    self_bias, cotangent,
):
    vec = (
        latent_gain, latent_bias, input_gain, input_bias, mlp_gain, mlp_bias, self_gain, self_bias
    )
    lat = latents.reshape(ROWS, D)
    inp = inputs.reshape(NROWS, D)
    cot = cotangent.reshape(ROWS, D)
    kept = run_first((
        lat, inp, latent_segment, input_segment, *vec, cross_key, cross_value, cross_query,
        cross_output, mlp_up, mlp_down, self_query, self_key, self_value, self_output, cot,
    ))
    new, glat, ginp, grad, gvec = run_second(
        tuple(kept) + (
            lat, inp, mlp_up, mlp_down, self_query, self_key, self_value, self_output, cot
        )
    )
    *grads, gvec = run_sum((grad, gvec))
    new, glat, ginp, *grads = run_finish((new, glat, ginp, *grads))
    x = lax.axis_index("shard")
    small = lax.dynamic_slice_in_dim(gvec, x * HALF, HALF, 1)
    return (
        new.reshape(latents.shape), glat.reshape(latents.shape), ginp.reshape(inputs.shape),
        *grads, *[small[i] for i in range(8)],
    )


def norm_forward(values, gain, shift):
    centred = values - jnp.mean(values, axis=-1, keepdims=True)
    inv_std = lax.rsqrt(jnp.mean(centred * centred, axis=-1, keepdims=True) + EPSILON)
    normed = centred * inv_std
    return (normed * gain + shift, normed, inv_std)


def norm_backward(grad_out, normed, inv_std, gain):
    scaled = grad_out * gain
    first_mean = jnp.mean(scaled, axis=-1, keepdims=True)
    second_mean = jnp.mean(scaled * normed, axis=-1, keepdims=True)
    grad_in = inv_std * (scaled - first_mean - normed * second_mean)
    return (grad_in, jnp.sum(grad_out * normed, axis=0), jnp.sum(grad_out, axis=0))


def product(left, right):
    return jnp.dot(left, right, preferred_element_type=jnp.float32)


def inner_rows(left, right):
    return lax.dot_general(
        left, right, (((0,), (0,)), ((), ())), preferred_element_type=jnp.float32
    )


def outer_cols(left, right):
    return lax.dot_general(
        left, right, (((1,), (1,)), ((), ())), preferred_element_type=jnp.float32
    )


def forward_total(term):
    return lax.psum(term.astype(jnp.bfloat16), "shard").astype(jnp.float32)


def backward_total(term):
    return lax.psum(term.astype(jnp.bfloat16), "shard").astype(jnp.float32)


def per_device(
    latents,
    inputs,
    latent_segment,
    input_segment,
    cross_query,
    cross_key,
    cross_value,
    cross_output,
    mlp_up,
    mlp_down,
    self_query,
    self_key,
    self_value,
    self_output,
    latent_gain,
    latent_bias,
    input_gain,
    input_bias,
    mlp_gain,
    mlp_bias,
    self_gain,
    self_bias,
    cotangent,
):
    shards = lax.axis_size("shard")
    groups, lat_len, width = latents.shape
    inp_len = inputs.shape[1]
    width_part = width // shards
    column_start = lax.axis_index("shard") * width_part
    rows = groups * lat_len
    scale = HEAD_DIM ** (-0.5)
    gathered = (
        lax.all_gather(cross_query, "shard", axis=0, tiled=True),
        lax.all_gather(cross_key, "shard", axis=0, tiled=True),
        lax.all_gather(cross_value, "shard", axis=0, tiled=True),
        lax.all_gather(cross_output, "shard", axis=0, tiled=True),
        lax.all_gather(latent_gain, "shard", axis=0, tiled=True),
        lax.all_gather(latent_bias, "shard", axis=0, tiled=True),
        lax.all_gather(input_gain, "shard", axis=0, tiled=True),
        lax.all_gather(input_bias, "shard", axis=0, tiled=True),
        lax.all_gather(mlp_gain, "shard", axis=0, tiled=True),
        lax.all_gather(mlp_bias, "shard", axis=0, tiled=True),
        lax.all_gather(self_gain, "shard", axis=0, tiled=True),
        lax.all_gather(self_bias, "shard", axis=0, tiled=True),
    )
    full_query, full_key, full_value, full_output = (
        gathered[0],
        gathered[1],
        gathered[2],
        gathered[3],
    )
    gain_lat, bias_lat, gain_inp, bias_inp, gain_mlp, bias_mlp, gain_self, bias_self = [
        piece.astype(jnp.float32) for piece in gathered[4:]
    ]
    lat_rows = latents.astype(jnp.float32).reshape(rows, width)
    inp_rows = inputs.astype(jnp.float32).reshape(groups * inp_len, width)
    lat_value, lat_normed, lat_inv = norm_forward(lat_rows, gain_lat, bias_lat)
    lat_in = lat_value.astype(jnp.bfloat16)
    inp_value, inp_normed, inp_inv = norm_forward(inp_rows, gain_inp, bias_inp)
    inp_in = inp_value.astype(jnp.bfloat16)
    cross_q = (
        product(lat_in, full_query).astype(jnp.bfloat16).reshape(groups, lat_len, HEADS, HEAD_DIM)
    )
    cross_k = (
        product(inp_in, full_key).astype(jnp.bfloat16).reshape(groups, inp_len, HEADS, HEAD_DIM)
    )
    cross_v = (
        product(inp_in, full_value).astype(jnp.bfloat16).reshape(groups, inp_len, HEADS, HEAD_DIM)
    )
    allowed = latent_segment[:, None, :, None] == input_segment[:, None, None, :]
    scores = (
        jnp.einsum("glhd,gnhd->ghln", cross_q, cross_k, preferred_element_type=jnp.float32) * scale
    )
    masked = jnp.where(allowed, scores, NEGATIVE)
    part_max = jnp.max(masked, axis=-1)
    top = lax.pmax(part_max, "shard")
    total = lax.psum(
        jnp.sum(jnp.where(allowed, jnp.exp(masked - top[..., None]), 0.0), axis=-1), "shard"
    )
    cross_prob = jnp.where(allowed, jnp.exp(masked - top[..., None]), 0.0) / total[..., None]
    cross_prob_low = cross_prob.astype(jnp.bfloat16)
    part_out = jnp.einsum(
        "ghln,gnhd->glhd", cross_prob_low, cross_v, preferred_element_type=jnp.float32
    )
    attended = lax.psum(part_out.astype(jnp.bfloat16), "shard").astype(jnp.float32)
    attended_in = attended.reshape(rows, width).astype(jnp.bfloat16)
    h_one = lat_rows + product(attended_in, full_output)
    mlp_value, mlp_normed, mlp_inv = norm_forward(h_one, gain_mlp, bias_mlp)
    mlp_in = mlp_value.astype(jnp.bfloat16)
    pre_act = product(mlp_in, mlp_up)
    hidden_in = jax.nn.gelu(pre_act).astype(jnp.bfloat16)
    h_two = h_one + forward_total(product(hidden_in, mlp_down))
    self_value_n, self_normed, self_inv = norm_forward(h_two, gain_self, bias_self)
    self_in = self_value_n.astype(jnp.bfloat16)
    local_heads = self_query.shape[1] // HEAD_DIM
    local_width = local_heads * HEAD_DIM
    self_q = (
        product(self_in, self_query)
        .astype(jnp.bfloat16)
        .reshape(groups, lat_len, local_heads, HEAD_DIM)
    )
    self_k = (
        product(self_in, self_key)
        .astype(jnp.bfloat16)
        .reshape(groups, lat_len, local_heads, HEAD_DIM)
    )
    self_v = (
        product(self_in, self_value)
        .astype(jnp.bfloat16)
        .reshape(groups, lat_len, local_heads, HEAD_DIM)
    )
    self_scores = (
        jnp.einsum("glhd,gmhd->ghlm", self_q, self_k, preferred_element_type=jnp.float32) * scale
    )
    self_prob = jax.nn.softmax(self_scores, axis=-1)
    self_prob_low = self_prob.astype(jnp.bfloat16)
    self_att = jnp.einsum(
        "ghlm,gmhd->glhd", self_prob_low, self_v, preferred_element_type=jnp.float32
    )
    self_att_in = self_att.reshape(rows, local_width).astype(jnp.bfloat16)
    result = h_two + forward_total(product(self_att_in, self_output))
    new_latents = result.reshape(groups, lat_len, width).astype(jnp.bfloat16)
    grad_out = cotangent.astype(jnp.float32).reshape(rows, width)
    grad_branch = grad_out.astype(jnp.bfloat16)
    grad_self_output = inner_rows(self_att_in, grad_branch)
    grad_att = (
        outer_cols(grad_branch, self_output)
        .astype(jnp.bfloat16)
        .reshape(groups, lat_len, local_heads, HEAD_DIM)
    )
    delta = jnp.sum(grad_att.astype(jnp.float32) * self_att, axis=-1).transpose(0, 2, 1)
    grad_prob = jnp.einsum("glhd,gmhd->ghlm", grad_att, self_v, preferred_element_type=jnp.float32)
    grad_sv = jnp.einsum(
        "ghlm,glhd->gmhd", self_prob_low, grad_att, preferred_element_type=jnp.float32
    )
    grad_scores = (self_prob * (grad_prob - delta[..., None])).astype(jnp.bfloat16)
    grad_sq = (
        jnp.einsum("ghlm,gmhd->glhd", grad_scores, self_k, preferred_element_type=jnp.float32)
        * scale
    )
    grad_sk = (
        jnp.einsum("ghlm,glhd->gmhd", grad_scores, self_q, preferred_element_type=jnp.float32)
        * scale
    )
    grad_sq = grad_sq.astype(jnp.bfloat16).reshape(rows, local_width)
    grad_sk = grad_sk.astype(jnp.bfloat16).reshape(rows, local_width)
    grad_sv = grad_sv.astype(jnp.bfloat16).reshape(rows, local_width)
    grad_self_query = inner_rows(self_in, grad_sq)
    grad_self_key = inner_rows(self_in, grad_sk)
    grad_self_value = inner_rows(self_in, grad_sv)
    grad_self_in = backward_total(
        outer_cols(grad_sq, self_query)
        + outer_cols(grad_sk, self_key)
        + outer_cols(grad_sv, self_value)
    )
    grad_norm, gain_full, bias_full = norm_backward(grad_self_in, self_normed, self_inv, gain_self)
    grad_two = grad_out + grad_norm
    grad_self_gain = lax.dynamic_slice_in_dim(gain_full, column_start, width_part)
    grad_self_bias = lax.dynamic_slice_in_dim(bias_full, column_start, width_part)
    grad_mlp_branch = grad_two.astype(jnp.bfloat16)
    grad_mlp_down = inner_rows(hidden_in, grad_mlp_branch)
    grad_hidden = outer_cols(grad_mlp_branch, mlp_down)
    gelu_value, gelu_pull = jax.vjp(jax.nn.gelu, pre_act)
    grad_pre = gelu_pull(grad_hidden)[0].astype(jnp.bfloat16)
    grad_mlp_up = inner_rows(mlp_in, grad_pre)
    grad_mlp_in = backward_total(outer_cols(grad_pre, mlp_up))
    grad_norm, gain_full, bias_full = norm_backward(grad_mlp_in, mlp_normed, mlp_inv, gain_mlp)
    grad_one = grad_two + grad_norm
    grad_mlp_gain = lax.dynamic_slice_in_dim(gain_full, column_start, width_part)
    grad_mlp_bias = lax.dynamic_slice_in_dim(bias_full, column_start, width_part)
    grad_cross_branch = grad_one.astype(jnp.bfloat16)
    grad_cross_output = inner_rows(
        lax.dynamic_slice_in_dim(attended_in, column_start, width_part, 1), grad_cross_branch
    )
    grad_ca = (
        outer_cols(grad_cross_branch, full_output)
        .astype(jnp.bfloat16)
        .reshape(groups, lat_len, HEADS, HEAD_DIM)
    )
    cross_delta = jnp.sum(grad_ca.astype(jnp.float32) * attended, axis=-1).transpose(0, 2, 1)
    grad_cp = jnp.einsum("glhd,gnhd->ghln", grad_ca, cross_v, preferred_element_type=jnp.float32)
    grad_cv = jnp.einsum(
        "ghln,glhd->gnhd", cross_prob_low, grad_ca, preferred_element_type=jnp.float32
    )
    grad_cs = (cross_prob * (grad_cp - cross_delta[..., None])).astype(jnp.bfloat16)
    grad_cq_part = (
        jnp.einsum("ghln,gnhd->glhd", grad_cs, cross_k, preferred_element_type=jnp.float32) * scale
    )
    grad_ck = (
        jnp.einsum("ghln,glhd->gnhd", grad_cs, cross_q, preferred_element_type=jnp.float32) * scale
    )
    grad_cq = backward_total(grad_cq_part.reshape(rows, width)).astype(jnp.bfloat16)
    grad_ck = grad_ck.astype(jnp.bfloat16).reshape(groups * inp_len, width)
    grad_cv = grad_cv.astype(jnp.bfloat16).reshape(groups * inp_len, width)
    grad_cross_query = inner_rows(
        lax.dynamic_slice_in_dim(lat_in, column_start, width_part, 1), grad_cq
    )
    grad_lat_in = outer_cols(grad_cq, full_query)
    grad_norm, gain_full, bias_full = norm_backward(grad_lat_in, lat_normed, lat_inv, gain_lat)
    grad_latents = (grad_one + grad_norm).reshape(groups, lat_len, width).astype(jnp.bfloat16)
    grad_latent_gain = lax.dynamic_slice_in_dim(gain_full, column_start, width_part)
    grad_latent_bias = lax.dynamic_slice_in_dim(bias_full, column_start, width_part)
    key_term = inner_rows(inp_in, grad_ck)
    value_term = inner_rows(inp_in, grad_cv)
    grad_inp_in = outer_cols(grad_ck, full_key) + outer_cols(grad_cv, full_value)
    grad_inp, inp_gain_full, inp_bias_full = norm_backward(
        grad_inp_in, inp_normed, inp_inv, gain_inp
    )
    grad_inputs = grad_inp.reshape(groups, inp_len, width).astype(jnp.bfloat16)
    grad_cross_key, grad_cross_value, grad_input_gain, grad_input_bias = (
        lax.psum_scatter(
            key_term.astype(jnp.bfloat16), "shard", scatter_dimension=0, tiled=True
        ).astype(jnp.float32),
        lax.psum_scatter(
            value_term.astype(jnp.bfloat16), "shard", scatter_dimension=0, tiled=True
        ).astype(jnp.float32),
        lax.psum_scatter(
            inp_gain_full.astype(jnp.bfloat16), "shard", scatter_dimension=0, tiled=True
        ).astype(jnp.float32),
        lax.psum_scatter(
            inp_bias_full.astype(jnp.bfloat16), "shard", scatter_dimension=0, tiled=True
        ).astype(jnp.float32),
    )
    (
        grad_cross_query,
        grad_cross_key,
        grad_cross_value,
        grad_cross_output,
        grad_mlp_up,
        grad_mlp_down,
        grad_self_query,
        grad_self_key,
        grad_self_value,
        grad_self_output,
        grad_latent_gain,
        grad_latent_bias,
        grad_input_gain,
        grad_input_bias,
        grad_mlp_gain,
        grad_mlp_bias,
        grad_self_gain,
        grad_self_bias,
    ) = (
        lax.psum(grad_cross_query.astype(jnp.bfloat16), "grp").astype(jnp.float32),
        lax.psum(grad_cross_key.astype(jnp.bfloat16), "grp").astype(jnp.float32),
        lax.psum(grad_cross_value.astype(jnp.bfloat16), "grp").astype(jnp.float32),
        lax.psum(grad_cross_output.astype(jnp.bfloat16), "grp").astype(jnp.float32),
        lax.psum(grad_mlp_up.astype(jnp.bfloat16), "grp").astype(jnp.float32),
        lax.psum(grad_mlp_down.astype(jnp.bfloat16), "grp").astype(jnp.float32),
        lax.psum(grad_self_query.astype(jnp.bfloat16), "grp").astype(jnp.float32),
        lax.psum(grad_self_key.astype(jnp.bfloat16), "grp").astype(jnp.float32),
        lax.psum(grad_self_value.astype(jnp.bfloat16), "grp").astype(jnp.float32),
        lax.psum(grad_self_output.astype(jnp.bfloat16), "grp").astype(jnp.float32),
        lax.psum(grad_latent_gain.astype(jnp.bfloat16), "grp").astype(jnp.float32),
        lax.psum(grad_latent_bias.astype(jnp.bfloat16), "grp").astype(jnp.float32),
        lax.psum(grad_input_gain.astype(jnp.bfloat16), "grp").astype(jnp.float32),
        lax.psum(grad_input_bias.astype(jnp.bfloat16), "grp").astype(jnp.float32),
        lax.psum(grad_mlp_gain.astype(jnp.bfloat16), "grp").astype(jnp.float32),
        lax.psum(grad_mlp_bias.astype(jnp.bfloat16), "grp").astype(jnp.float32),
        lax.psum(grad_self_gain.astype(jnp.bfloat16), "grp").astype(jnp.float32),
        lax.psum(grad_self_bias.astype(jnp.bfloat16), "grp").astype(jnp.float32),
    )
    return (
        new_latents,
        grad_latents,
        grad_inputs,
        grad_cross_query,
        grad_cross_key,
        grad_cross_value,
        grad_cross_output,
        grad_mlp_up,
        grad_mlp_down,
        grad_self_query,
        grad_self_key,
        grad_self_value,
        grad_self_output,
        grad_latent_gain,
        grad_latent_bias,
        grad_input_gain,
        grad_input_bias,
        grad_mlp_gain,
        grad_mlp_bias,
        grad_self_gain,
        grad_self_bias,
    )


def solution(mesh):
    laid_out = mesh.shape["shard"] == 2 and mesh.shape["grp"] == 16
    return jax.shard_map(
        per_device_pair if laid_out else per_device,
        mesh=mesh,
        in_specs=(
            P("grp", None, None),
            P("grp", "shard", None),
            P("grp", None),
            P("grp", "shard"),
            P("shard", None),
            P("shard", None),
            P("shard", None),
            P("shard", None),
            P(None, "shard"),
            P("shard", None),
            P(None, "shard"),
            P(None, "shard"),
            P(None, "shard"),
            P("shard", None),
            P("shard"),
            P("shard"),
            P("shard"),
            P("shard"),
            P("shard"),
            P("shard"),
            P("shard"),
            P("shard"),
            P("grp", None, None),
        ),
        out_specs=(
            P("grp", None, None),
            P("grp", None, None),
            P("grp", "shard", None),
            P("shard", None),
            P("shard", None),
            P("shard", None),
            P("shard", None),
            P(None, "shard"),
            P("shard", None),
            P(None, "shard"),
            P(None, "shard"),
            P(None, "shard"),
            P("shard", None),
            P("shard"),
            P("shard"),
            P("shard"),
            P("shard"),
            P("shard"),
            P("shard"),
            P("shard"),
            P("shard"),
        ),
        check_vma=False,
    )
```

```python
import jax
import jax.numpy as jnp
from jax import lax
from jax.experimental import pallas as pl
from jax.experimental.pallas import tpu as pltpu
from jax.sharding import PartitionSpec as P

HEADS = 8
HEAD_DIM = 128


EPSILON = 1e-05
NEGATIVE = -1e30

BF = jnp.bfloat16
F32 = jnp.float32
MESH = pl.DeviceIdType.MESH
LAT = 128
INP = 784
D = 1024
HALF = 512
HID = 2048
ROWS = 2 * LAT
NROWS = 2 * INP
SCALE = HEAD_DIM ** (-0.5)
MIB = 1 << 20


def nn(a, b):
    return lax.dot_general(a, b, (((1,), (0,)), ((), ())), preferred_element_type=F32)


def nt(a, b):
    return lax.dot_general(a, b, (((1,), (1,)), ((), ())), preferred_element_type=F32)


def tn(a, b):
    return lax.dot_general(a, b, (((0,), (0,)), ((), ())), preferred_element_type=F32)


def place():
    g = lax.axis_index("grp")
    x = lax.axis_index("shard")
    c = lax.rem(g, 2)
    y = lax.rem(g // 2, 2)
    a = lax.rem(g // 4, 2)
    b = g // 8
    return dict(
        x=x, c=c, y=y, a=a, b=b,
        xp=(g, 1 - x),
        cp=(g + 1 - 2 * c, x),
        yp=(g + 2 - 4 * y, x),
        ap=(g + 4 - 8 * a, x),
        bp=(g + 8 - 16 * b, x),
    )


def greet(partners):
    barrier = pltpu.get_barrier_semaphore()
    for partner in partners:
        pl.semaphore_signal(barrier, inc=1, device_id=partner, device_id_type=MESH)
    pl.semaphore_wait(barrier, len(partners))


def remote(src, dst, send, recv, partner):
    return pltpu.make_async_remote_copy(
        src_ref=src, dst_ref=dst, send_sem=send, recv_sem=recv,
        device_id=partner, device_id_type=MESH,
    )


def norm(v, gain, shift):
    cen = v - jnp.mean(v, axis=-1, keepdims=True)
    inv = lax.rsqrt(jnp.mean(cen * cen, axis=-1, keepdims=True) + EPSILON)
    return cen * inv * gain + shift


def vec_row(vecs, i):
    return jnp.concatenate([vecs[0, i:i + 1, :], vecs[1, i:i + 1, :]], axis=1)


def span(first, last, body):
    lax.fori_loop(first, last, lambda i, carry: (body(i), carry)[1], 0)


def loop(n, body):
    span(0, n, body)


def first_kernel(
    lat_h, inp_h, seglat, seginp, v0, v1, v2, v3, v4, v5, v6, v7, wk_h, wv_h, wq_h, wo_h, up_h, down_h,
    sq_h, sk_h, sv_h, so_h, cot_h,
    wf_o, ck_o, cv_o, inin_o, latin_o, cq_o, att_o, st_o, vec_o, hone_o, htwo_o,
    mlpin_o, selfin_o, pre_o, hid_o, ds_o, slow_o, mask_o,
    wf, inp, inin, ck, cv, lat, latin, cq, mask, segs, axb, stx, att, st, vecs,
    hone, htwo, mlpin, pre, hid, xm, selfin, wup, wdown, wself, wso, cot, qkv, dself,
    ds, slow, lsem, osem, xs, xr, ys, yr, c0s, c0r, c1s, c1r, ms, mr,
):
    me = place()
    x, y, c = me["x"], me["y"], me["c"]
    xp, yp, cp = me["xp"], me["yp"], me["cp"]
    nlocal = [0]
    nout = [0]

    def load(src, dst):
        copy = pltpu.make_async_copy(src, dst, lsem.at[nlocal[0]])
        nlocal[0] += 1
        copy.start()
        return copy

    outs = []

    def store(src, dst):
        copy = pltpu.make_async_copy(src, dst, osem.at[nout[0]])
        nout[0] += 1
        copy.start()
        outs.append(copy)

    own = pl.ds(pl.multiple_of(x * HALF, HALF), HALF)
    in_inp = load(inp_h, inp)
    in_lat = load(lat_h, lat)
    in_cot = load(cot_h, cot)
    in_so = load(so_h, wso)
    greet((xp, yp, cp))
    for i, v in enumerate((v0, v1, v2, v3, v4, v5, v6, v7)):
        vecs[x, i:i + 1, :] = v[...].astype(F32).reshape(1, HALF)
    vec_move = remote(vecs.at[x], vecs.at[x], xs.at[4], xr.at[4], xp)
    vec_move.start()
    weights = (wk_h, wv_h, wq_h, wo_h)
    quarter = 2 * y + c

    def part(w, side, q):
        return wf.at[w, pl.ds(pl.multiple_of(side * HALF + q * 128, 128), 128)]

    x_moves = []
    for w in range(4):
        src = weights[w].at[pl.ds(pl.multiple_of(quarter * 128, 128), 128)]
        move = remote(src, part(w, x, quarter), xs.at[w], xr.at[w], xp)
        move.start()
        x_moves.append(move)
    in_w = [load(weights[w], wf.at[w, own]) for w in range(4)]
    in_self = [load(h, wself.at[i]) for i, h in enumerate((sq_h, sk_h, sv_h))]
    in_up = load(up_h, wup)
    in_down = load(down_h, wdown)
    pending = []

    def forward_x(w):
        x_moves[w].wait()
        for sems, partner in (((ys, yr), yp), ((c0s, c0r), cp)):
            block = part(w, 1 - x, quarter)
            move = remote(block, block, sems[0].at[w], sems[1].at[w], partner)
            move.start()
            pending.append(move)

    def forward_y(w):
        block = part(w, 1 - x, quarter)
        remote(block, block, ys.at[w], yr.at[w], yp).wait_recv()
        block = part(w, 1 - x, 2 * (1 - y) + c)
        move = remote(block, block, c1s.at[w], c1r.at[w], cp)
        move.start()
        pending.append(move)

    def whole(w):
        block = part(w, 1 - x, quarter)
        remote(block, block, c0s.at[w], c0r.at[w], cp).wait_recv()
        remote(block, block, c1s.at[w], c1r.at[w], cp).wait_recv()
        in_w[w].wait()
        store(wf.at[w], wf_o.at[w])

    segs[...] = jnp.zeros_like(segs)
    segs[0:2, 0:INP] = seginp[...].astype(F32)
    for g in range(2):
        lat_row = seglat[g:g + 1, :].astype(F32)
        for j in range(7):
            count = min(128, INP - j * 128)
            col = jnp.broadcast_to(segs[g:g + 1, j * 128:(j + 1) * 128], (128, 128)).T
            mask[g * INP + j * 128:g * INP + j * 128 + count, :] = jnp.where(
                col[:count] == lat_row, 0.0, NEGATIVE
            ).astype(BF)
    store(mask, mask_o)
    in_cot.wait()
    in_so.wait()
    dself[...] = nt(cot[...], wso[...]).astype(BF)
    in_inp.wait()
    vec_move.wait()
    store(vecs, vec_o)
    gain_inp, bias_inp = vec_row(vecs, 2), vec_row(vecs, 3)

    def norm_rows(i):
        rows = pl.ds(pl.multiple_of(i * 32, 32), 32)
        inin[rows, :] = norm(inp[rows, :].astype(F32), gain_inp, bias_inp).astype(BF)

    span(0, 24, norm_rows)
    forward_x(0)
    span(24, 49, norm_rows)
    store(inin, inin_o)
    forward_x(1)
    forward_y(0)
    in_lat.wait()
    latin[...] = norm(lat[...].astype(F32), vec_row(vecs, 0), vec_row(vecs, 1)).astype(BF)
    store(latin, latin_o)

    def project(target, w, half):
        cols = slice(half * HALF, (half + 1) * HALF)

        def body(i):
            rows = pl.ds(pl.multiple_of(i * INP, 16), INP)
            target[rows, cols] = nn(inin[rows, :], wf[w, :, cols]).astype(BF)

        loop(2, body)

    whole(0)
    project(ck, 0, 0)
    forward_x(2)
    forward_y(1)
    project(ck, 0, 1)
    store(ck, ck_o)
    whole(1)
    forward_x(3)
    forward_y(2)
    project(cv, 1, 0)
    project(cv, 1, 1)
    store(cv, cv_o)
    whole(2)
    cq[...] = nn(latin[...], wf[2]).astype(BF)
    store(cq, cq_o)
    forward_y(3)

    def head(g, h):
        cols = pl.ds(pl.multiple_of(h * HEAD_DIM, HEAD_DIM), HEAD_DIM)
        n_rows = slice(g * INP, (g + 1) * INP)
        s = nt(ck[n_rows, cols], cq[g * LAT:(g + 1) * LAT, cols]) * SCALE + mask[n_rows, :].astype(F32)
        top = jnp.maximum(jnp.max(s, axis=0, keepdims=True), 0.1 * NEGATIVE)
        e = jnp.exp(s - top)
        total = jnp.sum(e, axis=0, keepdims=True)
        out = tn(cv[n_rows, cols], e.astype(BF))
        out = out * jnp.where(total > 0.0, 1.0 / total, 0.0)
        axb[x, pl.ds(pl.multiple_of(g * D + h * HEAD_DIM, HEAD_DIM), HEAD_DIM), :] = out.astype(BF)
        stx[x, g, pl.ds(h, 1), :] = top
        stx[x, g, pl.ds(HEADS + h, 1), :] = total

    a_moves = []
    for g in range(2):
        def pair(i, g=g):
            head(g, 2 * i)
            head(g, 2 * i + 1)

        loop(HEADS // 2, pair)
        block = axb.at[x, pl.ds(g * D, D)]
        for src, k in ((block, 0), (stx.at[x, g], 1)):
            move = remote(src, src, ms.at[2 * g + k], mr.at[2 * g + k], xp)
            move.start()
            a_moves.append(move)
    whole(3)
    for g in range(2):
        a_moves[2 * g].wait()
        a_moves[2 * g + 1].wait()
        for h in range(HEADS):
            m0, m1 = stx[0, g, h:h + 1, :], stx[1, g, h:h + 1, :]
            top = jnp.maximum(m0, m1)
            w0 = stx[0, g, HEADS + h:HEADS + h + 1, :] * jnp.exp(m0 - top)
            w1 = stx[1, g, HEADS + h:HEADS + h + 1, :] * jnp.exp(m1 - top)
            inv = 1.0 / (w0 + w1)
            rows = slice(g * D + h * HEAD_DIM, g * D + (h + 1) * HEAD_DIM)
            mixed = axb[0, rows, :].astype(F32) * (w0 * inv) + axb[1, rows, :].astype(F32) * (w1 * inv)
            att[rows, :] = mixed.astype(BF)
            st[g, h:h + 1, :] = top
            st[g, HEADS + h:HEADS + h + 1, :] = inv
        lrows = slice(g * LAT, (g + 1) * LAT)
        hone[lrows, :] = lat[lrows, :].astype(F32) + tn(att[g * D:(g + 1) * D, :], wf[3])
    store(att, att_o)
    store(st, st_o)
    store(hone, hone_o)
    mlpin[...] = norm(hone[...], vec_row(vecs, 4), vec_row(vecs, 5)).astype(BF)
    store(mlpin, mlpin_o)
    in_up.wait()
    for j in range(4):
        cols = slice(j * HALF, (j + 1) * HALF)
        u = nn(mlpin[...], wup[:, cols])
        pre[:, cols] = u
        hid[:, cols] = jax.nn.gelu(u).astype(BF)
    store(pre, pre_o)
    store(hid, hid_o)
    in_down.wait()
    m_moves = []
    for j in range(2):
        xm[x, j] = nn(hid[...], wdown[:, j * HALF:(j + 1) * HALF]).astype(BF)
        move = remote(xm.at[x, j], xm.at[x, j], ms.at[4 + j], mr.at[4 + j], xp)
        move.start()
        m_moves.append(move)
    for copy in in_self:
        copy.wait()
    for j in range(2):
        m_moves[j].wait()
        cols = slice(j * HALF, (j + 1) * HALF)
        htwo[:, cols] = hone[:, cols] + (xm[0, j].astype(F32) + xm[1, j].astype(F32))
    store(htwo, htwo_o)
    selfin[...] = norm(htwo[...], vec_row(vecs, 6), vec_row(vecs, 7)).astype(BF)
    store(selfin, selfin_o)
    for i in range(3):
        qkv[i] = nn(selfin[...], wself[i]).astype(BF)

    def self_group(g):
        rows = pl.ds(pl.multiple_of(g * LAT, LAT), LAT)
        for h in range(4):
            cols = slice(h * HEAD_DIM, (h + 1) * HEAD_DIM)
            q, k, v = qkv[0, rows, cols], qkv[1, rows, cols], qkv[2, rows, cols]
            do = dself[rows, cols]
            s = nt(q, k) * SCALE
            e = jnp.exp(s - jnp.max(s, axis=1, keepdims=True))
            p = e / jnp.sum(e, axis=1, keepdims=True)
            p_low = p.astype(BF)
            o = nn(p_low, v)
            slow[rows, cols] = o.astype(BF)
            delta = jnp.sum(do.astype(F32) * o, axis=1, keepdims=True)
            dp = nt(do, v)
            dsc = (p * (dp - delta)).astype(BF)
            ds[0, rows, cols] = (nn(dsc, k) * SCALE).astype(BF)
            ds[1, rows, cols] = (tn(dsc, q) * SCALE).astype(BF)
            ds[2, rows, cols] = tn(p_low, do).astype(BF)

    loop(2, self_group)
    store(ds, ds_o)
    store(slow, slow_o)
    for move in pending:
        move.wait_send()
    for copy in outs:
        copy.wait()


def run_first(args):
    any_spec = pl.BlockSpec(memory_space=pl.ANY)
    vmem_spec = pl.BlockSpec(memory_space=pltpu.VMEM)
    outs = [
        ((4, D, D), BF), ((NROWS, D), BF), ((NROWS, D), BF), ((NROWS, D), BF),
        ((ROWS, D), BF), ((ROWS, D), BF), ((2 * D, LAT), BF), ((2, 16, LAT), F32),
        ((2, 8, HALF), F32), ((ROWS, D), F32), ((ROWS, D), F32), ((ROWS, D), BF),
        ((ROWS, D), BF), ((ROWS, HID), F32), ((ROWS, HID), BF), ((3, ROWS, HALF), BF),
        ((ROWS, HALF), BF), ((NROWS, LAT), BF),
    ]
    scratch = [
        ((4, D, D), BF), ((NROWS, D), BF), ((NROWS, D), BF), ((NROWS, D), BF), ((NROWS, D), BF),
        ((ROWS, D), BF), ((ROWS, D), BF), ((ROWS, D), BF), ((NROWS, LAT), BF), ((8, 896), F32),
        ((2, 2 * D, LAT), BF), ((2, 2, 16, LAT), F32), ((2 * D, LAT), BF), ((2, 16, LAT), F32),
        ((2, 8, HALF), F32), ((ROWS, D), F32), ((ROWS, D), F32), ((ROWS, D), BF),
        ((ROWS, HID), F32), ((ROWS, HID), BF), ((2, 2, ROWS, HALF), BF), ((ROWS, D), BF),
        ((D, HID), BF), ((HID, D), BF), ((3, D, HALF), BF), ((HALF, D), BF), ((ROWS, D), BF),
        ((3, ROWS, HALF), BF), ((ROWS, HALF), BF), ((3, ROWS, HALF), BF), ((ROWS, HALF), BF),
    ]
    dma = pltpu.SemaphoreType.DMA
    return pl.pallas_call(
        first_kernel,
        out_shape=[jax.ShapeDtypeStruct(*o) for o in outs],
        in_specs=[any_spec] * 2 + [vmem_spec] * 10 + [any_spec] * 11,
        out_specs=[any_spec] * len(outs),
        scratch_shapes=[pltpu.VMEM(*s) for s in scratch]
        + [dma((16,)), dma((24,))] + [dma((5,))] * 2 + [dma((4,))] * 6 + [dma((6,))] * 2,
        compiler_params=pltpu.CompilerParams(
            collective_id=0, has_side_effects=True, vmem_limit_bytes=58 * MIB
        ),
        name="forward",
    )(*args)


def norm_back(v, dy, gain):
    cen = v - jnp.mean(v, axis=-1, keepdims=True)
    inv = lax.rsqrt(jnp.mean(cen * cen, axis=-1, keepdims=True) + EPSILON)
    n = cen * inv
    t = dy * gain
    dv = inv * (t - jnp.mean(t, axis=-1, keepdims=True) - n * jnp.mean(t * n, axis=-1, keepdims=True))
    return (
        dv,
        jnp.sum(dy * n, axis=0, keepdims=True),
        jnp.sum(dy, axis=0, keepdims=True),
    )


def gelu_slope(u):
    root = (2.0 / jnp.pi) ** 0.5
    t = jnp.tanh(root * (u + 0.044715 * u * u * u))
    return 0.5 * (1.0 + t) + 0.5 * u * (1.0 - t * t) * root * (1.0 + 3.0 * 0.044715 * u * u)


CHUNKS = 16
OFFSETS = (0, 1, 4, 5, 6, 7, 10, 11)


def second_kernel(
    wf_h, ck_h, cv_h, inin_h, latin_h, cq_h, att_h, st_h, vec_h, hone_h, htwo_h,
    mlpin_h, selfin_h, pre_h, hid_h, ds_h, slow_h, mask_h,
    lat_h, inp_h, up_h, down_h, sq_h, sk_h, sv_h, so_h, cot_h,
    newlat_o, glat_o, ginp_o, gq_o, gk_o, gv_o, go_o, gup_o, gdown_o, gsq_o, gsk_o,
    gsv_o, gso_o, gvec_o,
    z, wf, latin, cq, att, st, vecs, hone, htwo, etwo, mlpin, selfin, pre, hid, ds,
    slow, mask, lat, cot, elow2, elow1, dpre, dcr, xb, grad, other, t0, t1, t2, t3,
    tk, xk, gvec, gvr,
    lsem, osem, gs, gr, xs, xr, vs, vr, free,
):
    me = place()
    x, c = me["x"], me["c"]
    xp, yp, cp, ap, bp = me["xp"], me["yp"], me["cp"], me["ap"], me["bp"]
    counts = [0, 0]
    outs = []

    def load(src, dst):
        copy = pltpu.make_async_copy(src, dst, lsem.at[counts[0]])
        counts[0] += 1
        copy.start()
        return copy

    def store(src, dst):
        copy = pltpu.make_async_copy(src, dst, osem.at[counts[1]])
        counts[1] += 1
        copy.start()
        outs.append(copy)

    in_ds = load(ds_h, ds)
    in_self = [
        load(sq_h, z.at[pl.ds(4096, D), pl.ds(0, HALF)]),
        load(sk_h, z.at[pl.ds(4096, D), pl.ds(HALF, HALF)]),
        load(sv_h, z.at[pl.ds(5120, D), pl.ds(0, HALF)]),
    ]
    in_early = [load(slow_h, slow), load(cot_h, cot), load(selfin_h, selfin)] + [
        load(so_h.at[:, pl.ds(j * HALF, HALF)], z.at[pl.ds(5120 + j * HALF, HALF), pl.ds(HALF, HALF)])
        for j in range(2)
    ]
    in_two = [load(htwo_h, htwo), load(vec_h, vecs)]
    in_mlp = [
        load(pre_h, pre), load(down_h, z.at[pl.ds(0, HID)]),
        load(up_h.at[:, pl.ds(0, D)], z.at[pl.ds(HID, D)]),
        load(up_h.at[:, pl.ds(D, D)], z.at[pl.ds(HID + D, D)]),
    ]
    in_mid = [load(hid_h, hid), load(mlpin_h, mlpin), load(hone_h, hone)]
    in_cross = [
        load(wf_h, wf), load(att_h, att), load(st_h, st), load(cq_h, cq), load(mask_h, mask),
        load(latin_h, latin), load(lat_h, lat),
    ]
    greet((xp, yp, cp, ap, bp))

    def wait_all(copies):
        for copy in copies:
            copy.wait()

    moves = {}

    def block(k, off, size, core):
        return grad.at[
            pl.ds(pl.multiple_of(k * HALF + off, 16), size),
            pl.ds(pl.multiple_of(core * HALF, HALF), HALF),
        ]

    def add_in(k, off, size, temp):
        cols = pl.ds(pl.multiple_of(c * HALF, HALF), HALF)

        def body(i):
            rows = pl.ds(pl.multiple_of(k * HALF + off + i * 64, 64), 64)
            part = temp[pl.ds(pl.multiple_of(i * 64, 64), 64), :]
            grad[rows, cols] = (grad[rows, cols].astype(F32) + part.astype(F32)).astype(BF)

        loop(size // 64, body)

    def path(k):
        one, two = (me["y"], yp), (me["a"], ap)
        if k % 4 == 3:
            one, two = two, one
        return one, two, (me["b"], bp)

    def slots(k):
        if k % 4 == 3:
            return 6 + (k // 4) % 2, 2, k % 2
        n = k - k // 4
        return n % 6, n % 2, k % 2

    def offsets(k):
        (b1, _), (b2, _), _ = path(k)
        o1 = b1 * 256
        return o1, o1 + b2 * 128

    def send(k, stage, src, dst, partner):
        move = remote(src, dst, gs.at[k * 8 + stage], gr.at[k * 8 + stage], partner)
        move.start()
        moves[k, stage] = move

    def release(k, stage, partner):
        pl.semaphore_signal(
            free.at[k * 3 + stage], inc=1, device_id=partner, device_id_type=MESH
        )

    def claim(k, stage):
        pl.semaphore_wait(free.at[k * 3 + stage], 1)

    def event(k, s):
        first, second, third = slots(k)
        (b1, p1), (b2, p2), (_, p3) = path(k)
        o1, o2 = offsets(k)
        if s == 0:
            send(k, 0, block(k, 0, HALF, 1 - c), t0.at[k % 2], cp)
            return
        moves[k, s - 1].wait()
        if s == 1:
            release(k, 0, cp)
            add_in(k, 0, HALF, t0.at[k % 2])
            if k >= 14:
                finish_x(k - 14)
            send(k, 1, block(k, (1 - b1) * 256, 256, c), t1.at[first], p1)
        elif s == 2:
            release(k, 1, p1)
            add_in(k, o1, 256, t1.at[first])
            send(k, 2, block(k, o1 + (1 - b2) * 128, 128, c), t2.at[second], p2)
        elif s == 3:
            release(k, 2, p2)
            add_in(k, o2, 128, t2.at[second])
            send(k, 3, block(k, o2, 128, c), t3.at[third], p3)
        elif s == 4:
            add_in(k, o2, 128, t3.at[third])
            claim(k, 2)
            part = block(k, o2, 128, c)
            send(k, 4, part, part, p2)
        elif s == 5:
            claim(k, 1)
            part = block(k, o1, 256, c)
            send(k, 5, part, part, p1)
        elif s == 6:
            claim(k, 0)
            part = block(k, 0, HALF, c)
            send(k, 6, part, part, cp)
        else:
            deliver(k)

    def deliver(k):
        rows = pl.ds(k * HALF, HALF)
        left, right = grad.at[rows, pl.ds(0, HALF)], grad.at[rows, pl.ds(HALF, HALF)]
        if 1 <= k <= 3:
            target = (gsq_o, gsk_o, gsv_o)[k - 1]
            store(left, target.at[pl.ds(0, HALF)])
            store(right, target.at[pl.ds(HALF, HALF)])
        elif 8 <= k <= 11:
            cols = pl.ds((k - 8) * HALF, HALF)
            store(left, gup_o.at[pl.ds(0, HALF), cols])
            store(right, gup_o.at[pl.ds(HALF, HALF), cols])
        elif 4 <= k <= 7:
            store(grad.at[rows], gdown_o.at[pl.ds((k - 4) * HALF, HALF)])
        else:
            store(grad.at[rows], {0: gso_o, 12: go_o, 13: gq_o, 14: gk_o, 15: gv_o}[k])

    clock = [0]
    entered = {}

    def tick(chunk=None):
        now = clock[0]
        clock[0] += 1
        if chunk is not None:
            entered[chunk] = now
        for k in sorted(entered):
            if now - entered[k] in OFFSETS:
                event(k, OFFSETS.index(now - entered[k]))

    k_moves = {}

    def start_core(w):
        src = other.at[w, :, pl.ds(pl.multiple_of((1 - c) * HALF, HALF), HALF)]
        move = remote(src, tk.at[w], xs.at[8 + w], xr.at[8 + w], cp)
        move.start()
        k_moves[w, 0] = move

    def start_x(w):
        k_moves[w, 0].wait()
        cols = pl.ds(pl.multiple_of(c * HALF, HALF), HALF)

        def body(i):
            rows = pl.ds(pl.multiple_of(i * 64, 64), 64)
            other[w, rows, cols] = (
                other[w, rows, cols].astype(F32) + tk[w, rows, :].astype(F32)
            ).astype(BF)

        loop(HALF // 64, body)
        move = remote(other.at[w, :, cols], xk.at[w], xs.at[10 + w], xr.at[10 + w], xp)
        move.start()
        k_moves[w, 1] = move

    def finish_x(w):
        k_moves[w, 1].wait()
        add_in(14 + w, 0, HALF, xk.at[w])

    def exchange(n, part, index):
        move = remote(
            xb.at[(n, x) + part], xb.at[(n, x) + part], xs.at[index], xr.at[index], xp
        )
        move.start()
        return move

    def both(n, rows):
        return xb[n, 0, rows, :].astype(F32) + xb[n, 1, rows, :].astype(F32)

    def fill(k, half, value):
        grad[k * HALF:(k + 1) * HALF, half * HALF:(half + 1) * HALF] = value.astype(BF)

    gvec[...] = jnp.zeros_like(gvec)

    in_ds.wait()
    wait_all(in_self)
    m_self = []
    for j in range(2):
        cols = slice(j * HALF, (j + 1) * HALF)
        a_rows = slice(4096 + j * HALF, 4096 + (j + 1) * HALF)
        b_rows = slice(5120 + j * HALF, 5120 + (j + 1) * HALF)
        xb[0, x, :, cols] = (
            nt(ds[0], z[a_rows, 0:HALF]) + nt(ds[1], z[a_rows, HALF:D]) + nt(ds[2], z[b_rows, 0:HALF])
        ).astype(BF)
        m_self.append(exchange(0, (slice(None), pl.ds(j * HALF, HALF)), j))
    wait_all(in_early)
    for j in range(2):
        fill(0, j, tn(slow[...], cot[:, j * HALF:(j + 1) * HALF]))
    tick(0)
    for i in range(3):
        for j in range(2):
            fill(1 + i, j, tn(selfin[:, j * HALF:(j + 1) * HALF], ds[i]))
        tick(1 + i)
    m_new = []
    for j in range(2):
        cols = slice(j * HALF, (j + 1) * HALF)
        xb[1, x, :, cols] = nn(slow[...], z[5120 + j * HALF:5120 + (j + 1) * HALF, HALF:D]).astype(BF)
        m_new.append(exchange(1, (slice(None), pl.ds(j * HALF, HALF)), 2 + j))
    tick()
    wait_all(in_two)
    wait_all(m_self)
    gain_self = vec_row(vecs, 6)

    def two_rows(i):
        rows = pl.ds(pl.multiple_of(i * 32, 32), 32)
        dv, dg, db = norm_back(htwo[rows, :], both(0, rows), gain_self)
        e = cot[rows, :].astype(F32) + dv
        etwo[rows, :] = e
        elow2[rows, :] = e.astype(BF)
        gvec[6:7, :] += dg
        gvec[7:8, :] += db

    loop(8, two_rows)
    tick()
    wait_all(in_mlp)
    for j in range(4):
        cols = slice(j * HALF, (j + 1) * HALF)
        gh = nt(elow2[...], z[cols, :])
        dpre[:, cols] = (gh * gelu_slope(pre[:, cols])).astype(BF)
    m_mlp = []
    for j in range(2):
        cols = slice(j * HALF, (j + 1) * HALF)
        xb[2, x, :, cols] = (
            nt(dpre[:, 0:D], z[HID + j * HALF:HID + (j + 1) * HALF, :])
            + nt(dpre[:, D:HID], z[HID + D + j * HALF:HID + D + (j + 1) * HALF, :])
        ).astype(BF)
        m_mlp.append(exchange(2, (slice(None), pl.ds(j * HALF, HALF)), 4 + j))
    ck, cv = z.at[pl.ds(0, NROWS)], z.at[pl.ds(NROWS, NROWS)]
    inin, inp = z.at[pl.ds(2 * NROWS, NROWS)], z.at[pl.ds(3 * NROWS, NROWS)]
    in_keys = [load(ck_h, ck), load(cv_h, cv)]
    in_late = [load(inin_h, inin), load(inp_h, inp)]
    wait_all(in_mid)

    def fill_down(j):
        for i in range(2):
            fill(4 + j, i, tn(hid[:, j * HALF:(j + 1) * HALF], elow2[:, i * HALF:(i + 1) * HALF]))

    def fill_up(j):
        for i in range(2):
            fill(8 + j, i, tn(mlpin[:, i * HALF:(i + 1) * HALF], dpre[:, j * HALF:(j + 1) * HALF]))

    fill_down(0)
    tick(4)
    fill_down(1)
    tick(5)
    fill_down(2)
    tick(6)
    fill_down(3)
    tick(7)
    wait_all(m_mlp)
    gain_mlp = vec_row(vecs, 4)

    def one_rows(i):
        rows = pl.ds(pl.multiple_of(i * 32, 32), 32)
        dv, dg, db = norm_back(hone[rows, :], both(2, rows), gain_mlp)
        e = etwo[rows, :] + dv
        hone[rows, :] = e
        elow1[rows, :] = e.astype(BF)
        gvec[4:5, :] += dg
        gvec[5:6, :] += db

    loop(8, one_rows)
    wait_all(in_cross)
    for g in range(2):
        dcr[g * D:(g + 1) * D, :] = nt(wf[3], elow1[g * LAT:(g + 1) * LAT, :]).astype(BF)

    wait_all(m_new)

    def new_rows(i):
        rows = pl.ds(pl.multiple_of(i * 64, 64), 64)
        selfin[rows, :] = (htwo[rows, :] + both(1, rows)).astype(BF)

    loop(4, new_rows)
    store(selfin, newlat_o)
    wait_all(in_keys)

    def head(g, h):
        cols = pl.ds(pl.multiple_of(h * HEAD_DIM, HEAD_DIM), HEAD_DIM)
        n_rows = slice(g * INP, (g + 1) * INP)
        l_rows = slice(g * LAT, (g + 1) * LAT)
        t_rows = pl.ds(pl.multiple_of(g * D + h * HEAD_DIM, HEAD_DIM), HEAD_DIM)
        k, v, q = ck[n_rows, cols], cv[n_rows, cols], cq[l_rows, cols]
        s = nt(k, q) * SCALE + mask[n_rows, :].astype(F32)
        p = jnp.exp(s - st[g, pl.ds(h, 1), :]) * st[g, pl.ds(HEADS + h, 1), :]
        do = dcr[t_rows, :]
        delta = jnp.sum(do.astype(F32) * att[t_rows, :].astype(F32), axis=0, keepdims=True)
        dsc = (p * (nn(v, do) - delta)).astype(BF)
        cv[n_rows, cols] = nt(p.astype(BF), do).astype(BF)
        ck[n_rows, cols] = (nn(dsc, q) * SCALE).astype(BF)
        xb[0, x, l_rows, cols] = (tn(dsc, k) * SCALE).astype(BF)

    fills = [lambda j=j: fill_up(j) for j in range(4)]
    m_query = []
    for g in range(2):
        for part in range(2):
            def heads(i, g=g, part=part):
                head(g, 4 * part + 2 * i)
                head(g, 4 * part + 2 * i + 1)

            loop(2, heads)
            fills[2 * g + part]()
            tick(8 + 2 * g + part)
        m_query.append(exchange(0, (pl.ds(g * LAT, LAT),), 6 + g))
    wait_all(in_late)

    def weight_grad(w, source):
        def body(i):
            rows = pl.ds(pl.multiple_of(i * 256, 256), 256)
            mine = pl.ds(pl.multiple_of(x * HALF + i * 256, 256), 256)
            theirs = pl.ds(pl.multiple_of((1 - x) * HALF + i * 256, 256), 256)
            other[w, rows, :] = tn(inin[:, theirs], source[...]).astype(BF)
            grad[pl.ds(pl.multiple_of((14 + w) * HALF + i * 256, 256), 256), :] = tn(
                inin[:, mine], source[...]
            ).astype(BF)

        loop(2, body)

    weight_grad(0, ck)
    start_core(0)
    tick()
    weight_grad(1, cv)
    start_x(0)
    start_core(1)
    for j in range(2):
        value = 0.0
        for g in range(2):
            rows = pl.ds(pl.multiple_of(g * D + x * HALF, HALF), HALF)
            value = value + nn(
                att[rows, :], elow1[g * LAT:(g + 1) * LAT, j * HALF:(j + 1) * HALF]
            )
        fill(12, j, value)
    start_x(1)
    tick(12)
    wait_all(m_query)
    dcq = elow2

    def query_rows(i):
        rows = pl.ds(pl.multiple_of(i * 64, 64), 64)
        dcq[rows, :] = both(0, rows).astype(BF)

    loop(4, query_rows)
    for j in range(2):
        mine = pl.ds(pl.multiple_of(x * HALF, HALF), HALF)
        fill(13, j, tn(latin[:, mine], dcq[:, j * HALF:(j + 1) * HALF]))
    tick(13)
    gain_lat = vec_row(vecs, 0)

    def lat_rows(i):
        rows = pl.ds(pl.multiple_of(i * 128, 128), 128)
        dv, dg, db = norm_back(lat[rows, :].astype(F32), nt(dcq[rows, :], wf[2]), gain_lat)
        lat[rows, :] = (hone[rows, :] + dv).astype(BF)
        gvec[0:1, :] += dg
        gvec[1:2, :] += db

    loop(2, lat_rows)
    store(lat, glat_o)
    gain_inp = vec_row(vecs, 2)

    def inp_rows(i):
        rows = pl.ds(pl.multiple_of(i * 224, 16), 224)
        dy = nt(ck[rows, :], wf[0]) + nt(cv[rows, :], wf[1])
        dv, dg, db = norm_back(inp[rows, :].astype(F32), dy, gain_inp)
        inp[rows, :] = dv.astype(BF)
        gvec[2:3, :] += dg
        gvec[3:4, :] += db

    lax.fori_loop(0, 4, lambda i, carry: (inp_rows(i), carry)[1], 0)
    tick(14)
    lax.fori_loop(4, 7, lambda i, carry: (inp_rows(i), carry)[1], 0)
    store(inp, ginp_o)
    tick(15)
    col = lax.broadcasted_iota(jnp.int32, (8, D), 1) // HALF
    row = lax.broadcasted_iota(jnp.int32, (8, D), 0)
    keep = (col == x) | (row == 2) | (row == 3)
    gvec[...] = jnp.where(keep, gvec[...], 0.0)
    v_partners = (xp, cp, yp, ap, bp)
    v_moves = []

    def vec_event(s):
        if s > 0:
            v_moves[s - 1].wait()
            gvec[...] += gvr[s - 1]
        if s < 5:
            move = remote(gvec, gvr.at[s], vs.at[s], vr.at[s], v_partners[s])
            move.start()
            v_moves.append(move)
        else:
            store(gvec, gvec_o)

    for t in range(OFFSETS[-1]):
        tick()
        if t <= 5:
            vec_event(t)
    wait_all(outs)


def run_second(args):
    any_spec = pl.BlockSpec(memory_space=pl.ANY)
    outs = [
        ((ROWS, D), BF), ((ROWS, D), BF), ((NROWS, D), BF), ((HALF, D), BF), ((HALF, D), BF),
        ((HALF, D), BF), ((HALF, D), BF), ((D, HID), BF), ((HID, D), BF), ((D, HALF), BF),
        ((D, HALF), BF), ((D, HALF), BF), ((HALF, D), BF), ((8, D), F32),
    ]
    scratch = [
        ((4 * NROWS, D), BF), ((4, D, D), BF), ((ROWS, D), BF), ((ROWS, D), BF),
        ((2 * D, LAT), BF), ((2, 16, LAT), F32), ((2, 8, HALF), F32), ((ROWS, D), F32),
        ((ROWS, D), F32), ((ROWS, D), F32), ((ROWS, D), BF), ((ROWS, D), BF), ((ROWS, HID), F32),
        ((ROWS, HID), BF), ((3, ROWS, HALF), BF), ((ROWS, HALF), BF), ((NROWS, LAT), BF),
        ((ROWS, D), BF), ((ROWS, D), BF), ((ROWS, D), BF), ((ROWS, D), BF), ((ROWS, HID), BF),
        ((2 * D, LAT), BF), ((3, 2, ROWS, D), BF), ((CHUNKS * HALF, D), BF),
        ((2, HALF, D), BF), ((2, HALF, HALF), BF), ((8, 256, HALF), BF),
        ((3, 128, HALF), BF), ((2, 128, HALF), BF), ((2, HALF, HALF), BF),
        ((2, HALF, HALF), BF), ((8, D), F32), ((5, 8, D), F32),
    ]
    dma = pltpu.SemaphoreType.DMA
    return pl.pallas_call(
        second_kernel,
        out_shape=[jax.ShapeDtypeStruct(*o) for o in outs],
        in_specs=[any_spec] * len(args),
        out_specs=[any_spec] * len(outs),
        scratch_shapes=[pltpu.VMEM(*s) for s in scratch]
        + [dma((32,)), dma((32,))] + [dma((CHUNKS * 8,))] * 2 + [dma((12,))] * 2 + [dma((5,))] * 2
        + [pltpu.SemaphoreType.REGULAR((CHUNKS * 3,))],
        compiler_params=pltpu.CompilerParams(
            collective_id=1, has_side_effects=True, vmem_limit_bytes=63 * MIB
        ),
        name="backward",
    )(*args)


def finish_kernel(*refs):
    srcs, refs = refs[:13], refs[13:]
    dsts, (low, wide, insem, outsem) = refs[:13], refs[13:]
    tiles = []
    for i in (*range(3, 13), 0, 1, 2):
        rows, cols = srcs[i].shape
        for r in range(0, rows, HALF):
            for q in range(0, cols, HALF):
                count = min(HALF, rows - r)
                tiles.append((i, pl.ds(r, count), pl.ds(q, HALF), pl.ds(0, count)))
    depth = low.shape[0]
    ins, outs, finished = {}, {}, set()

    def finish_out(n):
        if n >= 0 and n not in finished:
            outs[n].wait()
            finished.add(n)

    def start_in(n):
        i, rows, cols, part = tiles[n]
        ins[n] = pltpu.make_async_copy(
            srcs[i].at[rows, cols], low.at[n % depth, part], insem.at[n % depth]
        )
        ins[n].start()

    for n in range(depth):
        start_in(n)
    for n in range(len(tiles)):
        slot = n % depth
        i, rows, cols, part = tiles[n]
        ins[n].wait()
        finish_out(n - depth)
        if i < 3:
            outs[n] = pltpu.make_async_copy(low.at[slot, part], dsts[i].at[rows, cols], outsem.at[slot])
            outs[n].start()
        else:
            def body(i, slot=slot):
                rows = pl.ds(pl.multiple_of(i * 64, 64), 64)
                wide[slot, rows, :] = low[slot, rows, :].astype(F32)

            loop(HALF // 64, body)
            outs[n] = pltpu.make_async_copy(wide.at[slot], dsts[i].at[rows, cols], outsem.at[slot])
            outs[n].start()
        if n + depth < len(tiles):
            if i < 3:
                finish_out(n)
            start_in(n + depth)
    for n in range(len(tiles) - depth, len(tiles)):
        finish_out(n)


def run_finish(args):
    any_spec = pl.BlockSpec(memory_space=pl.ANY)
    depth = 6
    return pl.pallas_call(
        finish_kernel,
        out_shape=[
            jax.ShapeDtypeStruct(a.shape, BF if i < 3 else F32) for i, a in enumerate(args)
        ],
        in_specs=[any_spec] * 13,
        out_specs=[any_spec] * 13,
        scratch_shapes=[
            pltpu.VMEM((depth, HALF, HALF), BF), pltpu.VMEM((depth, HALF, HALF), F32),
            pltpu.SemaphoreType.DMA((depth,)), pltpu.SemaphoreType.DMA((depth,)),
        ],
        compiler_params=pltpu.CompilerParams(vmem_limit_bytes=62 * MIB),
        name="finish",
    )(*args)


def per_device_pair(
    latents, inputs, latent_segment, input_segment, cross_query, cross_key, cross_value,
    cross_output, mlp_up, mlp_down, self_query, self_key, self_value, self_output,
    latent_gain, latent_bias, input_gain, input_bias, mlp_gain, mlp_bias, self_gain,
    self_bias, cotangent,
):
    vec = (
        latent_gain, latent_bias, input_gain, input_bias, mlp_gain, mlp_bias, self_gain, self_bias
    )
    lat = latents.reshape(ROWS, D)
    inp = inputs.reshape(NROWS, D)
    cot = cotangent.reshape(ROWS, D)
    kept = run_first((
        lat, inp, latent_segment, input_segment, *vec, cross_key, cross_value, cross_query,
        cross_output, mlp_up, mlp_down, self_query, self_key, self_value, self_output, cot,
    ))
    (new, glat, ginp, gq, gk, gv, go, gup, gdown, gsq, gsk, gsv, gso, gvec) = run_second(
        tuple(kept) + (
            lat, inp, mlp_up, mlp_down, self_query, self_key, self_value, self_output, cot
        )
    )
    new, glat, ginp, *grads = run_finish(
        (new, glat, ginp, gq, gk, gv, go, gup, gdown, gsq, gsk, gsv, gso)
    )
    x = lax.axis_index("shard")
    small = lax.dynamic_slice_in_dim(gvec, x * HALF, HALF, 1)
    return (
        new.reshape(latents.shape), glat.reshape(latents.shape), ginp.reshape(inputs.shape),
        *grads, *[small[i] for i in range(8)],
    )


def norm_forward(values, gain, shift):
    centred = values - jnp.mean(values, axis=-1, keepdims=True)
    inv_std = lax.rsqrt(jnp.mean(centred * centred, axis=-1, keepdims=True) + EPSILON)
    normed = centred * inv_std
    return (normed * gain + shift, normed, inv_std)


def norm_backward(grad_out, normed, inv_std, gain):
    scaled = grad_out * gain
    first_mean = jnp.mean(scaled, axis=-1, keepdims=True)
    second_mean = jnp.mean(scaled * normed, axis=-1, keepdims=True)
    grad_in = inv_std * (scaled - first_mean - normed * second_mean)
    return (grad_in, jnp.sum(grad_out * normed, axis=0), jnp.sum(grad_out, axis=0))


def product(left, right):
    return jnp.dot(left, right, preferred_element_type=jnp.float32)


def inner_rows(left, right):
    return lax.dot_general(
        left, right, (((0,), (0,)), ((), ())), preferred_element_type=jnp.float32
    )


def outer_cols(left, right):
    return lax.dot_general(
        left, right, (((1,), (1,)), ((), ())), preferred_element_type=jnp.float32
    )


def forward_total(term):
    return lax.psum(term.astype(jnp.bfloat16), "shard").astype(jnp.float32)


def backward_total(term):
    return lax.psum(term.astype(jnp.bfloat16), "shard").astype(jnp.float32)


def per_device(
    latents,
    inputs,
    latent_segment,
    input_segment,
    cross_query,
    cross_key,
    cross_value,
    cross_output,
    mlp_up,
    mlp_down,
    self_query,
    self_key,
    self_value,
    self_output,
    latent_gain,
    latent_bias,
    input_gain,
    input_bias,
    mlp_gain,
    mlp_bias,
    self_gain,
    self_bias,
    cotangent,
):
    shards = lax.axis_size("shard")
    groups, lat_len, width = latents.shape
    inp_len = inputs.shape[1]
    width_part = width // shards
    column_start = lax.axis_index("shard") * width_part
    rows = groups * lat_len
    scale = HEAD_DIM ** (-0.5)
    gathered = (
        lax.all_gather(cross_query, "shard", axis=0, tiled=True),
        lax.all_gather(cross_key, "shard", axis=0, tiled=True),
        lax.all_gather(cross_value, "shard", axis=0, tiled=True),
        lax.all_gather(cross_output, "shard", axis=0, tiled=True),
        lax.all_gather(latent_gain, "shard", axis=0, tiled=True),
        lax.all_gather(latent_bias, "shard", axis=0, tiled=True),
        lax.all_gather(input_gain, "shard", axis=0, tiled=True),
        lax.all_gather(input_bias, "shard", axis=0, tiled=True),
        lax.all_gather(mlp_gain, "shard", axis=0, tiled=True),
        lax.all_gather(mlp_bias, "shard", axis=0, tiled=True),
        lax.all_gather(self_gain, "shard", axis=0, tiled=True),
        lax.all_gather(self_bias, "shard", axis=0, tiled=True),
    )
    full_query, full_key, full_value, full_output = (
        gathered[0],
        gathered[1],
        gathered[2],
        gathered[3],
    )
    gain_lat, bias_lat, gain_inp, bias_inp, gain_mlp, bias_mlp, gain_self, bias_self = [
        piece.astype(jnp.float32) for piece in gathered[4:]
    ]
    lat_rows = latents.astype(jnp.float32).reshape(rows, width)
    inp_rows = inputs.astype(jnp.float32).reshape(groups * inp_len, width)
    lat_value, lat_normed, lat_inv = norm_forward(lat_rows, gain_lat, bias_lat)
    lat_in = lat_value.astype(jnp.bfloat16)
    inp_value, inp_normed, inp_inv = norm_forward(inp_rows, gain_inp, bias_inp)
    inp_in = inp_value.astype(jnp.bfloat16)
    cross_q = (
        product(lat_in, full_query).astype(jnp.bfloat16).reshape(groups, lat_len, HEADS, HEAD_DIM)
    )
    cross_k = (
        product(inp_in, full_key).astype(jnp.bfloat16).reshape(groups, inp_len, HEADS, HEAD_DIM)
    )
    cross_v = (
        product(inp_in, full_value).astype(jnp.bfloat16).reshape(groups, inp_len, HEADS, HEAD_DIM)
    )
    allowed = latent_segment[:, None, :, None] == input_segment[:, None, None, :]
    scores = (
        jnp.einsum("glhd,gnhd->ghln", cross_q, cross_k, preferred_element_type=jnp.float32) * scale
    )
    masked = jnp.where(allowed, scores, NEGATIVE)
    part_max = jnp.max(masked, axis=-1)
    top = lax.pmax(part_max, "shard")
    total = lax.psum(
        jnp.sum(jnp.where(allowed, jnp.exp(masked - top[..., None]), 0.0), axis=-1), "shard"
    )
    cross_prob = jnp.where(allowed, jnp.exp(masked - top[..., None]), 0.0) / total[..., None]
    cross_prob_low = cross_prob.astype(jnp.bfloat16)
    part_out = jnp.einsum(
        "ghln,gnhd->glhd", cross_prob_low, cross_v, preferred_element_type=jnp.float32
    )
    attended = lax.psum(part_out.astype(jnp.bfloat16), "shard").astype(jnp.float32)
    attended_in = attended.reshape(rows, width).astype(jnp.bfloat16)
    h_one = lat_rows + product(attended_in, full_output)
    mlp_value, mlp_normed, mlp_inv = norm_forward(h_one, gain_mlp, bias_mlp)
    mlp_in = mlp_value.astype(jnp.bfloat16)
    pre_act = product(mlp_in, mlp_up)
    hidden_in = jax.nn.gelu(pre_act).astype(jnp.bfloat16)
    h_two = h_one + forward_total(product(hidden_in, mlp_down))
    self_value_n, self_normed, self_inv = norm_forward(h_two, gain_self, bias_self)
    self_in = self_value_n.astype(jnp.bfloat16)
    local_heads = self_query.shape[1] // HEAD_DIM
    local_width = local_heads * HEAD_DIM
    self_q = (
        product(self_in, self_query)
        .astype(jnp.bfloat16)
        .reshape(groups, lat_len, local_heads, HEAD_DIM)
    )
    self_k = (
        product(self_in, self_key)
        .astype(jnp.bfloat16)
        .reshape(groups, lat_len, local_heads, HEAD_DIM)
    )
    self_v = (
        product(self_in, self_value)
        .astype(jnp.bfloat16)
        .reshape(groups, lat_len, local_heads, HEAD_DIM)
    )
    self_scores = (
        jnp.einsum("glhd,gmhd->ghlm", self_q, self_k, preferred_element_type=jnp.float32) * scale
    )
    self_prob = jax.nn.softmax(self_scores, axis=-1)
    self_prob_low = self_prob.astype(jnp.bfloat16)
    self_att = jnp.einsum(
        "ghlm,gmhd->glhd", self_prob_low, self_v, preferred_element_type=jnp.float32
    )
    self_att_in = self_att.reshape(rows, local_width).astype(jnp.bfloat16)
    result = h_two + forward_total(product(self_att_in, self_output))
    new_latents = result.reshape(groups, lat_len, width).astype(jnp.bfloat16)
    grad_out = cotangent.astype(jnp.float32).reshape(rows, width)
    grad_branch = grad_out.astype(jnp.bfloat16)
    grad_self_output = inner_rows(self_att_in, grad_branch)
    grad_att = (
        outer_cols(grad_branch, self_output)
        .astype(jnp.bfloat16)
        .reshape(groups, lat_len, local_heads, HEAD_DIM)
    )
    delta = jnp.sum(grad_att.astype(jnp.float32) * self_att, axis=-1).transpose(0, 2, 1)
    grad_prob = jnp.einsum("glhd,gmhd->ghlm", grad_att, self_v, preferred_element_type=jnp.float32)
    grad_sv = jnp.einsum(
        "ghlm,glhd->gmhd", self_prob_low, grad_att, preferred_element_type=jnp.float32
    )
    grad_scores = (self_prob * (grad_prob - delta[..., None])).astype(jnp.bfloat16)
    grad_sq = (
        jnp.einsum("ghlm,gmhd->glhd", grad_scores, self_k, preferred_element_type=jnp.float32)
        * scale
    )
    grad_sk = (
        jnp.einsum("ghlm,glhd->gmhd", grad_scores, self_q, preferred_element_type=jnp.float32)
        * scale
    )
    grad_sq = grad_sq.astype(jnp.bfloat16).reshape(rows, local_width)
    grad_sk = grad_sk.astype(jnp.bfloat16).reshape(rows, local_width)
    grad_sv = grad_sv.astype(jnp.bfloat16).reshape(rows, local_width)
    grad_self_query = inner_rows(self_in, grad_sq)
    grad_self_key = inner_rows(self_in, grad_sk)
    grad_self_value = inner_rows(self_in, grad_sv)
    grad_self_in = backward_total(
        outer_cols(grad_sq, self_query)
        + outer_cols(grad_sk, self_key)
        + outer_cols(grad_sv, self_value)
    )
    grad_norm, gain_full, bias_full = norm_backward(grad_self_in, self_normed, self_inv, gain_self)
    grad_two = grad_out + grad_norm
    grad_self_gain = lax.dynamic_slice_in_dim(gain_full, column_start, width_part)
    grad_self_bias = lax.dynamic_slice_in_dim(bias_full, column_start, width_part)
    grad_mlp_branch = grad_two.astype(jnp.bfloat16)
    grad_mlp_down = inner_rows(hidden_in, grad_mlp_branch)
    grad_hidden = outer_cols(grad_mlp_branch, mlp_down)
    gelu_value, gelu_pull = jax.vjp(jax.nn.gelu, pre_act)
    grad_pre = gelu_pull(grad_hidden)[0].astype(jnp.bfloat16)
    grad_mlp_up = inner_rows(mlp_in, grad_pre)
    grad_mlp_in = backward_total(outer_cols(grad_pre, mlp_up))
    grad_norm, gain_full, bias_full = norm_backward(grad_mlp_in, mlp_normed, mlp_inv, gain_mlp)
    grad_one = grad_two + grad_norm
    grad_mlp_gain = lax.dynamic_slice_in_dim(gain_full, column_start, width_part)
    grad_mlp_bias = lax.dynamic_slice_in_dim(bias_full, column_start, width_part)
    grad_cross_branch = grad_one.astype(jnp.bfloat16)
    grad_cross_output = inner_rows(
        lax.dynamic_slice_in_dim(attended_in, column_start, width_part, 1), grad_cross_branch
    )
    grad_ca = (
        outer_cols(grad_cross_branch, full_output)
        .astype(jnp.bfloat16)
        .reshape(groups, lat_len, HEADS, HEAD_DIM)
    )
    cross_delta = jnp.sum(grad_ca.astype(jnp.float32) * attended, axis=-1).transpose(0, 2, 1)
    grad_cp = jnp.einsum("glhd,gnhd->ghln", grad_ca, cross_v, preferred_element_type=jnp.float32)
    grad_cv = jnp.einsum(
        "ghln,glhd->gnhd", cross_prob_low, grad_ca, preferred_element_type=jnp.float32
    )
    grad_cs = (cross_prob * (grad_cp - cross_delta[..., None])).astype(jnp.bfloat16)
    grad_cq_part = (
        jnp.einsum("ghln,gnhd->glhd", grad_cs, cross_k, preferred_element_type=jnp.float32) * scale
    )
    grad_ck = (
        jnp.einsum("ghln,glhd->gnhd", grad_cs, cross_q, preferred_element_type=jnp.float32) * scale
    )
    grad_cq = backward_total(grad_cq_part.reshape(rows, width)).astype(jnp.bfloat16)
    grad_ck = grad_ck.astype(jnp.bfloat16).reshape(groups * inp_len, width)
    grad_cv = grad_cv.astype(jnp.bfloat16).reshape(groups * inp_len, width)
    grad_cross_query = inner_rows(
        lax.dynamic_slice_in_dim(lat_in, column_start, width_part, 1), grad_cq
    )
    grad_lat_in = outer_cols(grad_cq, full_query)
    grad_norm, gain_full, bias_full = norm_backward(grad_lat_in, lat_normed, lat_inv, gain_lat)
    grad_latents = (grad_one + grad_norm).reshape(groups, lat_len, width).astype(jnp.bfloat16)
    grad_latent_gain = lax.dynamic_slice_in_dim(gain_full, column_start, width_part)
    grad_latent_bias = lax.dynamic_slice_in_dim(bias_full, column_start, width_part)
    key_term = inner_rows(inp_in, grad_ck)
    value_term = inner_rows(inp_in, grad_cv)
    grad_inp_in = outer_cols(grad_ck, full_key) + outer_cols(grad_cv, full_value)
    grad_inp, inp_gain_full, inp_bias_full = norm_backward(
        grad_inp_in, inp_normed, inp_inv, gain_inp
    )
    grad_inputs = grad_inp.reshape(groups, inp_len, width).astype(jnp.bfloat16)
    grad_cross_key, grad_cross_value, grad_input_gain, grad_input_bias = (
        lax.psum_scatter(
            key_term.astype(jnp.bfloat16), "shard", scatter_dimension=0, tiled=True
        ).astype(jnp.float32),
        lax.psum_scatter(
            value_term.astype(jnp.bfloat16), "shard", scatter_dimension=0, tiled=True
        ).astype(jnp.float32),
        lax.psum_scatter(
            inp_gain_full.astype(jnp.bfloat16), "shard", scatter_dimension=0, tiled=True
        ).astype(jnp.float32),
        lax.psum_scatter(
            inp_bias_full.astype(jnp.bfloat16), "shard", scatter_dimension=0, tiled=True
        ).astype(jnp.float32),
    )
    (
        grad_cross_query,
        grad_cross_key,
        grad_cross_value,
        grad_cross_output,
        grad_mlp_up,
        grad_mlp_down,
        grad_self_query,
        grad_self_key,
        grad_self_value,
        grad_self_output,
        grad_latent_gain,
        grad_latent_bias,
        grad_input_gain,
        grad_input_bias,
        grad_mlp_gain,
        grad_mlp_bias,
        grad_self_gain,
        grad_self_bias,
    ) = (
        lax.psum(grad_cross_query.astype(jnp.bfloat16), "grp").astype(jnp.float32),
        lax.psum(grad_cross_key.astype(jnp.bfloat16), "grp").astype(jnp.float32),
        lax.psum(grad_cross_value.astype(jnp.bfloat16), "grp").astype(jnp.float32),
        lax.psum(grad_cross_output.astype(jnp.bfloat16), "grp").astype(jnp.float32),
        lax.psum(grad_mlp_up.astype(jnp.bfloat16), "grp").astype(jnp.float32),
        lax.psum(grad_mlp_down.astype(jnp.bfloat16), "grp").astype(jnp.float32),
        lax.psum(grad_self_query.astype(jnp.bfloat16), "grp").astype(jnp.float32),
        lax.psum(grad_self_key.astype(jnp.bfloat16), "grp").astype(jnp.float32),
        lax.psum(grad_self_value.astype(jnp.bfloat16), "grp").astype(jnp.float32),
        lax.psum(grad_self_output.astype(jnp.bfloat16), "grp").astype(jnp.float32),
        lax.psum(grad_latent_gain.astype(jnp.bfloat16), "grp").astype(jnp.float32),
        lax.psum(grad_latent_bias.astype(jnp.bfloat16), "grp").astype(jnp.float32),
        lax.psum(grad_input_gain.astype(jnp.bfloat16), "grp").astype(jnp.float32),
        lax.psum(grad_input_bias.astype(jnp.bfloat16), "grp").astype(jnp.float32),
        lax.psum(grad_mlp_gain.astype(jnp.bfloat16), "grp").astype(jnp.float32),
        lax.psum(grad_mlp_bias.astype(jnp.bfloat16), "grp").astype(jnp.float32),
        lax.psum(grad_self_gain.astype(jnp.bfloat16), "grp").astype(jnp.float32),
        lax.psum(grad_self_bias.astype(jnp.bfloat16), "grp").astype(jnp.float32),
    )
    return (
        new_latents,
        grad_latents,
        grad_inputs,
        grad_cross_query,
        grad_cross_key,
        grad_cross_value,
        grad_cross_output,
        grad_mlp_up,
        grad_mlp_down,
        grad_self_query,
        grad_self_key,
        grad_self_value,
        grad_self_output,
        grad_latent_gain,
        grad_latent_bias,
        grad_input_gain,
        grad_input_bias,
        grad_mlp_gain,
        grad_mlp_bias,
        grad_self_gain,
        grad_self_bias,
    )


def solution(mesh):
    laid_out = mesh.shape["shard"] == 2 and mesh.shape["grp"] == 16
    return jax.shard_map(
        per_device_pair if laid_out else per_device,
        mesh=mesh,
        in_specs=(
            P("grp", None, None),
            P("grp", "shard", None),
            P("grp", None),
            P("grp", "shard"),
            P("shard", None),
            P("shard", None),
            P("shard", None),
            P("shard", None),
            P(None, "shard"),
            P("shard", None),
            P(None, "shard"),
            P(None, "shard"),
            P(None, "shard"),
            P("shard", None),
            P("shard"),
            P("shard"),
            P("shard"),
            P("shard"),
            P("shard"),
            P("shard"),
            P("shard"),
            P("shard"),
            P("grp", None, None),
        ),
        out_specs=(
            P("grp", None, None),
            P("grp", None, None),
            P("grp", "shard", None),
            P("shard", None),
            P("shard", None),
            P("shard", None),
            P("shard", None),
            P(None, "shard"),
            P("shard", None),
            P(None, "shard"),
            P(None, "shard"),
            P(None, "shard"),
            P("shard", None),
            P("shard"),
            P("shard"),
            P("shard"),
            P("shard"),
            P("shard"),
            P("shard"),
            P("shard"),
            P("shard"),
        ),
        check_vma=False,
    )
```

```python
import jax
import jax.numpy as jnp
from jax import lax
from jax.experimental import pallas as pl
from jax.experimental.pallas import tpu as pltpu
from jax.sharding import PartitionSpec as P

HEADS = 8
HEAD_DIM = 128


EPSILON = 1e-05
NEGATIVE = -1e30

BF = jnp.bfloat16
F32 = jnp.float32
MESH = pl.DeviceIdType.MESH
LAT = 128
INP = 784
D = 1024
HALF = 512
HID = 2048
ROWS = 2 * LAT
NROWS = 2 * INP
SCALE = HEAD_DIM ** (-0.5)
MIB = 1 << 20


def nn(a, b):
    return lax.dot_general(a, b, (((1,), (0,)), ((), ())), preferred_element_type=F32)


def nt(a, b):
    return lax.dot_general(a, b, (((1,), (1,)), ((), ())), preferred_element_type=F32)


def tn(a, b):
    return lax.dot_general(a, b, (((0,), (0,)), ((), ())), preferred_element_type=F32)


def place():
    g = lax.axis_index("grp")
    x = lax.axis_index("shard")
    c = lax.rem(g, 2)
    y = lax.rem(g // 2, 2)
    a = lax.rem(g // 4, 2)
    b = g // 8
    return dict(
        x=x, c=c, y=y, a=a, b=b,
        xp=(g, 1 - x),
        cp=(g + 1 - 2 * c, x),
        yp=(g + 2 - 4 * y, x),
        ap=(g + 4 - 8 * a, x),
        bp=(g + 8 - 16 * b, x),
        mp=(g + 4 - 8 * b, x),
    )


def greet(partners):
    barrier = pltpu.get_barrier_semaphore()
    for partner in partners:
        pl.semaphore_signal(barrier, inc=1, device_id=partner, device_id_type=MESH)
    pl.semaphore_wait(barrier, len(partners))


def remote(src, dst, send, recv, partner):
    return pltpu.make_async_remote_copy(
        src_ref=src, dst_ref=dst, send_sem=send, recv_sem=recv,
        device_id=partner, device_id_type=MESH,
    )


def norm(v, gain, shift):
    cen = v - jnp.mean(v, axis=-1, keepdims=True)
    inv = lax.rsqrt(jnp.mean(cen * cen, axis=-1, keepdims=True) + EPSILON)
    return cen * inv * gain + shift


def vec_row(vecs, i):
    return jnp.concatenate([vecs[0, i:i + 1, :], vecs[1, i:i + 1, :]], axis=1)


def span(first, last, body):
    lax.fori_loop(first, last, lambda i, carry: (body(i), carry)[1], 0)


def loop(n, body):
    span(0, n, body)


def first_kernel(
    lat_h, inp_h, seglat, seginp, v0, v1, v2, v3, v4, v5, v6, v7, wk_h, wv_h, wq_h, wo_h, up_h, down_h,
    sq_h, sk_h, sv_h, so_h, cot_h,
    wf_o, ck_o, cv_o, inin_o, latin_o, cq_o, att_o, st_o, vec_o, hone_o, htwo_o,
    mlpin_o, selfin_o, pre_o, hid_o, ds_o, slow_o, mask_o,
    wf, inp, inin, ck, cv, lat, latin, cq, mask, segs, axb, stx, att, st, vecs,
    hone, htwo, mlpin, pre, hid, xm, selfin, wup, wdown, wself, wso, cot, qkv, dself,
    ds, slow, lsem, osem, xs, xr, ys, yr, c0s, c0r, c1s, c1r, ms, mr,
):
    me = place()
    x, y, c = me["x"], me["y"], me["c"]
    xp, yp, cp = me["xp"], me["yp"], me["cp"]
    nlocal = [0]
    nout = [0]

    def load(src, dst):
        copy = pltpu.make_async_copy(src, dst, lsem.at[nlocal[0]])
        nlocal[0] += 1
        copy.start()
        return copy

    outs = []

    def store(src, dst):
        copy = pltpu.make_async_copy(src, dst, osem.at[nout[0]])
        nout[0] += 1
        copy.start()
        outs.append(copy)

    own = pl.ds(pl.multiple_of(x * HALF, HALF), HALF)
    in_inp = load(inp_h, inp)
    in_lat = load(lat_h, lat)
    in_cot = load(cot_h, cot)
    in_so = load(so_h, wso)
    greet((xp, yp, cp))
    for i, v in enumerate((v0, v1, v2, v3, v4, v5, v6, v7)):
        vecs[x, i:i + 1, :] = v[...].astype(F32).reshape(1, HALF)
    vec_move = remote(vecs.at[x], vecs.at[x], xs.at[4], xr.at[4], xp)
    vec_move.start()
    weights = (wk_h, wv_h, wq_h, wo_h)
    quarter = 2 * y + c

    def part(w, side, q):
        return wf.at[w, pl.ds(pl.multiple_of(side * HALF + q * 128, 128), 128)]

    x_moves = []
    for w in range(4):
        src = weights[w].at[pl.ds(pl.multiple_of(quarter * 128, 128), 128)]
        move = remote(src, part(w, x, quarter), xs.at[w], xr.at[w], xp)
        move.start()
        x_moves.append(move)
    in_w = [load(weights[w], wf.at[w, own]) for w in range(4)]
    in_self = [load(h, wself.at[i]) for i, h in enumerate((sq_h, sk_h, sv_h))]
    in_up = load(up_h, wup)
    in_down = load(down_h, wdown)
    pending = []

    def forward_x(w):
        x_moves[w].wait()
        for sems, partner in (((ys, yr), yp), ((c0s, c0r), cp)):
            block = part(w, 1 - x, quarter)
            move = remote(block, block, sems[0].at[w], sems[1].at[w], partner)
            move.start()
            pending.append(move)

    def forward_y(w):
        block = part(w, 1 - x, quarter)
        remote(block, block, ys.at[w], yr.at[w], yp).wait_recv()
        block = part(w, 1 - x, 2 * (1 - y) + c)
        move = remote(block, block, c1s.at[w], c1r.at[w], cp)
        move.start()
        pending.append(move)

    def whole(w):
        block = part(w, 1 - x, quarter)
        remote(block, block, c0s.at[w], c0r.at[w], cp).wait_recv()
        remote(block, block, c1s.at[w], c1r.at[w], cp).wait_recv()
        in_w[w].wait()
        store(wf.at[w], wf_o.at[w])

    segs[...] = jnp.zeros_like(segs)
    segs[0:2, 0:INP] = seginp[...].astype(F32)
    for g in range(2):
        lat_row = seglat[g:g + 1, :].astype(F32)
        for j in range(7):
            count = min(128, INP - j * 128)
            col = jnp.broadcast_to(segs[g:g + 1, j * 128:(j + 1) * 128], (128, 128)).T
            mask[g * INP + j * 128:g * INP + j * 128 + count, :] = jnp.where(
                col[:count] == lat_row, 0.0, NEGATIVE
            ).astype(BF)
    store(mask, mask_o)
    in_cot.wait()
    in_so.wait()
    dself[...] = nt(cot[...], wso[...]).astype(BF)
    in_inp.wait()
    vec_move.wait()
    store(vecs, vec_o)
    gain_inp, bias_inp = vec_row(vecs, 2), vec_row(vecs, 3)

    def norm_rows(i):
        rows = pl.ds(pl.multiple_of(i * 32, 32), 32)
        inin[rows, :] = norm(inp[rows, :].astype(F32), gain_inp, bias_inp).astype(BF)

    span(0, 24, norm_rows)
    forward_x(0)
    span(24, 49, norm_rows)
    store(inin, inin_o)
    forward_x(1)
    forward_y(0)
    in_lat.wait()
    latin[...] = norm(lat[...].astype(F32), vec_row(vecs, 0), vec_row(vecs, 1)).astype(BF)
    store(latin, latin_o)

    def project(target, w, half):
        cols = slice(half * HALF, (half + 1) * HALF)

        def body(i):
            rows = pl.ds(pl.multiple_of(i * INP, 16), INP)
            target[rows, cols] = nn(inin[rows, :], wf[w, :, cols]).astype(BF)

        loop(2, body)

    whole(0)
    project(ck, 0, 0)
    forward_x(2)
    forward_y(1)
    project(ck, 0, 1)
    store(ck, ck_o)
    whole(1)
    forward_x(3)
    forward_y(2)
    project(cv, 1, 0)
    project(cv, 1, 1)
    store(cv, cv_o)
    whole(2)
    cq[...] = nn(latin[...], wf[2]).astype(BF)
    store(cq, cq_o)
    forward_y(3)

    def head(g, h):
        cols = pl.ds(pl.multiple_of(h * HEAD_DIM, HEAD_DIM), HEAD_DIM)
        n_rows = slice(g * INP, (g + 1) * INP)
        s = nt(ck[n_rows, cols], cq[g * LAT:(g + 1) * LAT, cols]) * SCALE + mask[n_rows, :].astype(F32)
        top = jnp.maximum(jnp.max(s, axis=0, keepdims=True), 0.1 * NEGATIVE)
        e = jnp.exp(s - top)
        total = jnp.sum(e, axis=0, keepdims=True)
        out = tn(cv[n_rows, cols], e.astype(BF))
        out = out * jnp.where(total > 0.0, 1.0 / total, 0.0)
        axb[x, pl.ds(pl.multiple_of(g * D + h * HEAD_DIM, HEAD_DIM), HEAD_DIM), :] = out.astype(BF)
        stx[x, g, pl.ds(h, 1), :] = top
        stx[x, g, pl.ds(HEADS + h, 1), :] = total

    a_moves = []
    for g in range(2):
        def pair(i, g=g):
            head(g, 2 * i)
            head(g, 2 * i + 1)

        loop(HEADS // 2, pair)
        block = axb.at[x, pl.ds(g * D, D)]
        for src, k in ((block, 0), (stx.at[x, g], 1)):
            move = remote(src, src, ms.at[2 * g + k], mr.at[2 * g + k], xp)
            move.start()
            a_moves.append(move)
    whole(3)
    for g in range(2):
        a_moves[2 * g].wait()
        a_moves[2 * g + 1].wait()
        for h in range(HEADS):
            m0, m1 = stx[0, g, h:h + 1, :], stx[1, g, h:h + 1, :]
            top = jnp.maximum(m0, m1)
            w0 = stx[0, g, HEADS + h:HEADS + h + 1, :] * jnp.exp(m0 - top)
            w1 = stx[1, g, HEADS + h:HEADS + h + 1, :] * jnp.exp(m1 - top)
            inv = 1.0 / (w0 + w1)
            rows = slice(g * D + h * HEAD_DIM, g * D + (h + 1) * HEAD_DIM)
            mixed = axb[0, rows, :].astype(F32) * (w0 * inv) + axb[1, rows, :].astype(F32) * (w1 * inv)
            att[rows, :] = mixed.astype(BF)
            st[g, h:h + 1, :] = top
            st[g, HEADS + h:HEADS + h + 1, :] = inv
        lrows = slice(g * LAT, (g + 1) * LAT)
        hone[lrows, :] = lat[lrows, :].astype(F32) + tn(att[g * D:(g + 1) * D, :], wf[3])
    store(att, att_o)
    store(st, st_o)
    store(hone, hone_o)
    mlpin[...] = norm(hone[...], vec_row(vecs, 4), vec_row(vecs, 5)).astype(BF)
    store(mlpin, mlpin_o)
    in_up.wait()
    for j in range(4):
        cols = slice(j * HALF, (j + 1) * HALF)
        u = nn(mlpin[...], wup[:, cols])
        pre[:, cols] = u
        hid[:, cols] = jax.nn.gelu(u).astype(BF)
    store(pre, pre_o)
    store(hid, hid_o)
    in_down.wait()
    m_moves = []
    for j in range(2):
        xm[x, j] = nn(hid[...], wdown[:, j * HALF:(j + 1) * HALF]).astype(BF)
        move = remote(xm.at[x, j], xm.at[x, j], ms.at[4 + j], mr.at[4 + j], xp)
        move.start()
        m_moves.append(move)
    for copy in in_self:
        copy.wait()
    for j in range(2):
        m_moves[j].wait()
        cols = slice(j * HALF, (j + 1) * HALF)
        htwo[:, cols] = hone[:, cols] + (xm[0, j].astype(F32) + xm[1, j].astype(F32))
    store(htwo, htwo_o)
    selfin[...] = norm(htwo[...], vec_row(vecs, 6), vec_row(vecs, 7)).astype(BF)
    store(selfin, selfin_o)
    for i in range(3):
        qkv[i] = nn(selfin[...], wself[i]).astype(BF)

    def self_group(g):
        rows = pl.ds(pl.multiple_of(g * LAT, LAT), LAT)
        for h in range(4):
            cols = slice(h * HEAD_DIM, (h + 1) * HEAD_DIM)
            q, k, v = qkv[0, rows, cols], qkv[1, rows, cols], qkv[2, rows, cols]
            do = dself[rows, cols]
            s = nt(q, k) * SCALE
            e = jnp.exp(s - jnp.max(s, axis=1, keepdims=True))
            p = e / jnp.sum(e, axis=1, keepdims=True)
            p_low = p.astype(BF)
            o = nn(p_low, v)
            slow[rows, cols] = o.astype(BF)
            delta = jnp.sum(do.astype(F32) * o, axis=1, keepdims=True)
            dp = nt(do, v)
            dsc = (p * (dp - delta)).astype(BF)
            ds[0, rows, cols] = (nn(dsc, k) * SCALE).astype(BF)
            ds[1, rows, cols] = (tn(dsc, q) * SCALE).astype(BF)
            ds[2, rows, cols] = tn(p_low, do).astype(BF)

    loop(2, self_group)
    store(ds, ds_o)
    store(slow, slow_o)
    for move in pending:
        move.wait_send()
    for copy in outs:
        copy.wait()


def run_first(args):
    any_spec = pl.BlockSpec(memory_space=pl.ANY)
    vmem_spec = pl.BlockSpec(memory_space=pltpu.VMEM)
    outs = [
        ((4, D, D), BF), ((NROWS, D), BF), ((NROWS, D), BF), ((NROWS, D), BF),
        ((ROWS, D), BF), ((ROWS, D), BF), ((2 * D, LAT), BF), ((2, 16, LAT), F32),
        ((2, 8, HALF), F32), ((ROWS, D), F32), ((ROWS, D), F32), ((ROWS, D), BF),
        ((ROWS, D), BF), ((ROWS, HID), F32), ((ROWS, HID), BF), ((3, ROWS, HALF), BF),
        ((ROWS, HALF), BF), ((NROWS, LAT), BF),
    ]
    scratch = [
        ((4, D, D), BF), ((NROWS, D), BF), ((NROWS, D), BF), ((NROWS, D), BF), ((NROWS, D), BF),
        ((ROWS, D), BF), ((ROWS, D), BF), ((ROWS, D), BF), ((NROWS, LAT), BF), ((8, 896), F32),
        ((2, 2 * D, LAT), BF), ((2, 2, 16, LAT), F32), ((2 * D, LAT), BF), ((2, 16, LAT), F32),
        ((2, 8, HALF), F32), ((ROWS, D), F32), ((ROWS, D), F32), ((ROWS, D), BF),
        ((ROWS, HID), F32), ((ROWS, HID), BF), ((2, 2, ROWS, HALF), BF), ((ROWS, D), BF),
        ((D, HID), BF), ((HID, D), BF), ((3, D, HALF), BF), ((HALF, D), BF), ((ROWS, D), BF),
        ((3, ROWS, HALF), BF), ((ROWS, HALF), BF), ((3, ROWS, HALF), BF), ((ROWS, HALF), BF),
    ]
    dma = pltpu.SemaphoreType.DMA
    return pl.pallas_call(
        first_kernel,
        out_shape=[jax.ShapeDtypeStruct(*o) for o in outs],
        in_specs=[any_spec] * 2 + [vmem_spec] * 10 + [any_spec] * 11,
        out_specs=[any_spec] * len(outs),
        scratch_shapes=[pltpu.VMEM(*s) for s in scratch]
        + [dma((16,)), dma((24,))] + [dma((5,))] * 2 + [dma((4,))] * 6 + [dma((6,))] * 2,
        compiler_params=pltpu.CompilerParams(
            collective_id=0, has_side_effects=True, vmem_limit_bytes=58 * MIB
        ),
        name="forward",
    )(*args)


def norm_back(v, dy, gain):
    cen = v - jnp.mean(v, axis=-1, keepdims=True)
    inv = lax.rsqrt(jnp.mean(cen * cen, axis=-1, keepdims=True) + EPSILON)
    n = cen * inv
    t = dy * gain
    dv = inv * (t - jnp.mean(t, axis=-1, keepdims=True) - n * jnp.mean(t * n, axis=-1, keepdims=True))
    return (
        dv,
        jnp.sum(dy * n, axis=0, keepdims=True),
        jnp.sum(dy, axis=0, keepdims=True),
    )


def gelu_slope(u):
    root = (2.0 / jnp.pi) ** 0.5
    t = jnp.tanh(root * (u + 0.044715 * u * u * u))
    return 0.5 * (1.0 + t) + 0.5 * u * (1.0 - t * t) * root * (1.0 + 3.0 * 0.044715 * u * u)


OFFSETS = (0, 1, 3, 5, 7, 9, 11, 12)


def second_kernel(
    wf_h, ck_h, cv_h, inin_h, latin_h, cq_h, att_h, st_h, vec_h, hone_h, htwo_h,
    mlpin_h, selfin_h, pre_h, hid_h, ds_h, slow_h, mask_h,
    lat_h, inp_h, up_h, down_h, sq_h, sk_h, sv_h, so_h, cot_h,
    newlat_o, glat_o, ginp_o, gq_o, gk_o, gv_o, go_o, gup_o, gdown_o, gsq_o, gsk_o,
    gsv_o, gso_o, gvec_o,
    z, wf, cq, att, st, vecs, hone, htwo, etwo, mlpin, selfin, pre, hid, ds,
    slow, mask, cot, elow2, elow1, dpre, dcr, xb, grad, other, t0, ty, te, tm, tn_mid, tn_y,
    xk, gvec, gvr,
    lsem, osem, gs, gr, xs, xr, vs, vr, free,
):
    me = place()
    x, c = me["x"], me["c"]
    xp, yp, cp, ap, bp = me["xp"], me["yp"], me["cp"], me["ap"], me["bp"]
    counts = [0, 0]
    outs = []

    def load(src, dst):
        copy = pltpu.make_async_copy(src, dst, lsem.at[counts[0]])
        counts[0] += 1
        copy.start()
        return copy

    def store(src, dst):
        copy = pltpu.make_async_copy(src, dst, osem.at[counts[1]])
        counts[1] += 1
        copy.start()
        outs.append(copy)

    in_ds = load(ds_h, ds)
    in_self = [
        load(sq_h, z.at[pl.ds(4096, D), pl.ds(0, HALF)]),
        load(sk_h, z.at[pl.ds(4096, D), pl.ds(HALF, HALF)]),
        load(sv_h, z.at[pl.ds(5120, D), pl.ds(0, HALF)]),
    ]
    in_early = [load(slow_h, slow), load(cot_h, cot), load(selfin_h, selfin)] + [
        load(so_h.at[:, pl.ds(j * HALF, HALF)], z.at[pl.ds(5120 + j * HALF, HALF), pl.ds(HALF, HALF)])
        for j in range(2)
    ]
    in_two = [load(htwo_h, htwo), load(vec_h, vecs)]
    in_mlp = [
        load(pre_h, pre), load(down_h, z.at[pl.ds(0, HID)]),
        load(up_h.at[:, pl.ds(0, D)], z.at[pl.ds(HID, D)]),
        load(up_h.at[:, pl.ds(D, D)], z.at[pl.ds(HID + D, D)]),
    ]
    in_mid = [
        load(hid_h.at[:, pl.ds(j * D, D)], hid.at[pl.ds(j * ROWS, ROWS)]) for j in range(2)
    ] + [load(mlpin_h, mlpin), load(hone_h, hone)]
    in_cross = [
        load(wf_h, wf), load(att_h, att), load(st_h, st), load(cq_h, cq), load(mask_h, mask),
    ]
    barrier = pltpu.get_barrier_semaphore()
    for partner in (xp, yp, cp, ap, bp):
        pl.semaphore_signal(barrier, inc=1, device_id=partner, device_id_type=MESH)

    @pl.when(me["a"] != me["b"])
    def _():
        pl.semaphore_signal(barrier, inc=1, device_id=me["mp"], device_id_type=MESH)
        pl.semaphore_wait(barrier, 6)

    @pl.when(me["a"] == me["b"])
    def _():
        pl.semaphore_wait(barrier, 5)


    def wait_all(copies):
        for copy in copies:
            copy.wait()

    a_bit, b_bit, y_bit = me["a"], me["b"], me["y"]
    at_end = a_bit == b_bit
    at_middle = a_bit != b_bit
    mp = me["mp"]
    chunks = [(n * HALF, HALF) for n in range(12)] + [(12 * HALF + n * 256, 256) for n in range(8)]

    def cols_of(core):
        return pl.ds(pl.multiple_of(core * HALF, HALF), HALF)

    def block(k, off, size, core):
        return grad.at[pl.ds(pl.multiple_of(chunks[k][0] + off, 16), size), cols_of(core)]

    def add(base, size, part):
        def body(i):
            rows = pl.ds(pl.multiple_of(base + i * 64, 64), 64)
            grad[rows, cols_of(c)] = (
                grad[rows, cols_of(c)].astype(F32)
                + part[pl.ds(pl.multiple_of(i * 64, 64), 64), :].astype(F32)
            ).astype(BF)

        loop(size // 64, body)

    def move(k, stage, src, dst, partner):
        return remote(src, dst, gs.at[k * 7 + stage], gr.at[k * 7 + stage], partner)

    def release(k, n, partner):
        pl.semaphore_signal(free.at[k * 4 + n], inc=1, device_id=partner, device_id_type=MESH)

    def claim(k, n):
        pl.semaphore_wait(free.at[k * 4 + n], 1)

    def event(k, s):
        base, size = chunks[k]
        half = size // 2
        n = k // 2
        kind = "y" if k % 2 == 0 else "z"
        everything = block(k, 0, size, c)
        core_in = t0.at[k % 2, pl.ds(0, size)]
        core_move = move(k, 0, block(k, 0, size, 1 - c), core_in, cp)
        core_back = move(k, 6, everything, everything, cp)
        if s == 0:
            core_move.start()
            return
        if s == 7:
            core_back.wait()
            deliver(k)
            return
        if s == 1:
            core_move.wait()
            if kind == "y":
                release(k, 0, cp)
            else:
                pl.when(at_end)(lambda: release(k, 0, cp))
                pl.when(at_middle)(lambda: release(k, 3, ap))
            add(base, size, core_in)
            if k >= 16:
                finish_x((k - 16) // 2, k % 2)
        if kind == "y":
            off = y_bit * half
            own = block(k, off, half, c)
            y_in, end_in, mid_in = (
                ty.at[n % 2, pl.ds(0, half)], te.at[n % 3, pl.ds(0, half)], tm.at[n % 2, pl.ds(0, half)]
            )
            y_move = move(k, 1, block(k, (1 - y_bit) * half, half, c), y_in, yp)
            end_move = move(k, 2, own, end_in, ap)
            mid_move = move(k, 3, own, mid_in, mp)
            end_back = move(k, 4, own, own, ap)
            y_back = move(k, 5, own, own, yp)
            if s == 1:
                y_move.start()
            elif s == 2:
                y_move.wait()
                release(k, 1, yp)
                add(base + off, half, y_in)
                pl.when(at_end)(end_move.start)
            elif s == 3:
                @pl.when(at_end)
                def _():
                    end_move.wait_send()
                    release(k, 2, ap)

                @pl.when(at_middle)
                def _():
                    end_move.wait_recv()
                    add(base + off, half, end_in)
                    mid_move.start()
            elif s == 4:
                @pl.when(at_middle)
                def _():
                    mid_move.wait()
                    add(base + off, half, mid_in)
                    claim(k, 2)
                    end_back.start()
            elif s == 5:
                pl.when(at_end)(end_back.wait_recv)
                pl.when(at_middle)(end_back.wait_send)
                claim(k, 1)
                y_back.start()
            elif s == 6:
                y_back.wait()
                claim(k, 0)
                core_back.start()
            return
        off = b_bit * half
        own = block(k, off, half, c)
        mid_in, y_in = tn_mid.at[n % 2, pl.ds(0, half)], tn_y.at[n % 2, pl.ds(0, half)]
        end_in = block(k, 0, size, 1 - c)
        end_move = move(k, 1, everything, end_in, ap)
        mid_move = move(k, 2, block(k, (1 - b_bit) * half, half, c), mid_in, mp)
        y_move = move(k, 3, own, y_in, yp)
        mid_back = move(k, 4, own, own, mp)
        end_back = move(k, 5, everything, everything, ap)
        if s == 1:
            @pl.when(at_end)
            def _():
                claim(k, 3)
                end_move.start()
        elif s == 2:
            @pl.when(at_end)
            def _():
                end_move.wait_send()
                release(k, 1, ap)

            @pl.when(at_middle)
            def _():
                end_move.wait_recv()
                add(base, size, end_in)
                release(k, 0, cp)
                mid_move.start()
        elif s == 3:
            @pl.when(at_middle)
            def _():
                mid_move.wait()
                release(k, 2, mp)
                add(base + off, half, mid_in)
                y_move.start()
        elif s == 4:
            @pl.when(at_middle)
            def _():
                y_move.wait()
                add(base + off, half, y_in)
                claim(k, 2)
                mid_back.start()
        elif s == 5:
            @pl.when(at_middle)
            def _():
                mid_back.wait()
                claim(k, 1)
                end_back.start()
        elif s == 6:
            pl.when(at_end)(end_back.wait_recv)
            pl.when(at_middle)(end_back.wait_send)
            claim(k, 0)
            core_back.start()

    def deliver(k):
        base, size = chunks[k]
        rows = pl.ds(base, size)
        left, right = grad.at[rows, pl.ds(0, HALF)], grad.at[rows, pl.ds(HALF, HALF)]
        if 1 <= k <= 3:
            target = (gsq_o, gsk_o, gsv_o)[k - 1]
            store(left, target.at[pl.ds(0, HALF)])
            store(right, target.at[pl.ds(HALF, HALF)])
        elif 8 <= k <= 11:
            cols = pl.ds((k - 8) * HALF, HALF)
            store(left, gup_o.at[pl.ds(0, HALF), cols])
            store(right, gup_o.at[pl.ds(HALF, HALF), cols])
        elif 4 <= k <= 7:
            store(grad.at[rows], gdown_o.at[pl.ds((k - 4) * HALF, HALF)])
        elif k == 0:
            store(grad.at[rows], gso_o)
        else:
            target = (go_o, gq_o, gk_o, gv_o)[(k - 12) // 2]
            store(grad.at[rows], target.at[pl.ds((k % 2) * 256, 256)])

    clock = [0]
    entered = {}

    def tick(chunk=None):
        now = clock[0]
        clock[0] += 1
        if chunk is not None:
            entered[chunk] = now
        for k in sorted(entered):
            if now - entered[k] in OFFSETS:
                event(k, OFFSETS.index(now - entered[k]))

    k_moves = {}

    def start_core(w):
        src = other.at[w, :, pl.ds(pl.multiple_of((1 - c) * HALF, HALF), HALF)]
        move = remote(src, hid.at[:, pl.ds(w * HALF, HALF)], xs.at[8 + w], xr.at[8 + w], cp)
        move.start()
        k_moves[w, 0] = move

    def start_x(w):
        k_moves[w, 0].wait()
        cols = pl.ds(pl.multiple_of(c * HALF, HALF), HALF)

        def body(i):
            rows = pl.ds(pl.multiple_of(i * 64, 64), 64)
            other[w, rows, cols] = (
                other[w, rows, cols].astype(F32) + hid[rows, w * HALF:(w + 1) * HALF].astype(F32)
            ).astype(BF)

        loop(HALF // 64, body)
        move = remote(other.at[w, :, cols], xk.at[w], xs.at[10 + w], xr.at[10 + w], xp)
        move.start()
        k_moves[w, 1] = move

    def finish_x(w, part):
        if part == 0:
            k_moves[w, 1].wait()
        add((14 + w) * HALF + part * 256, 256, xk.at[w, pl.ds(part * 256, 256)])

    def exchange(n, part, index):
        move = remote(
            xb.at[(n, x) + part], xb.at[(n, x) + part], xs.at[index], xr.at[index], xp
        )
        move.start()
        return move

    def both(n, rows):
        return xb[n, 0, rows, :].astype(F32) + xb[n, 1, rows, :].astype(F32)

    def fill(k, half, value):
        grad[k * HALF:(k + 1) * HALF, half * HALF:(half + 1) * HALF] = value.astype(BF)

    gvec[...] = jnp.zeros_like(gvec)

    in_ds.wait()
    wait_all(in_self)
    m_self = []
    for j in range(2):
        cols = slice(j * HALF, (j + 1) * HALF)
        a_rows = slice(4096 + j * HALF, 4096 + (j + 1) * HALF)
        b_rows = slice(5120 + j * HALF, 5120 + (j + 1) * HALF)
        xb[0, x, :, cols] = (
            nt(ds[0], z[a_rows, 0:HALF]) + nt(ds[1], z[a_rows, HALF:D]) + nt(ds[2], z[b_rows, 0:HALF])
        ).astype(BF)
        m_self.append(exchange(0, (slice(None), pl.ds(j * HALF, HALF)), j))
    wait_all(in_early)
    for j in range(2):
        fill(0, j, tn(slow[...], cot[:, j * HALF:(j + 1) * HALF]))
    tick(0)
    for i in range(3):
        for j in range(2):
            fill(1 + i, j, tn(selfin[:, j * HALF:(j + 1) * HALF], ds[i]))
        tick(1 + i)
    m_new = []
    for j in range(2):
        cols = slice(j * HALF, (j + 1) * HALF)
        xb[1, x, :, cols] = nn(slow[...], z[5120 + j * HALF:5120 + (j + 1) * HALF, HALF:D]).astype(BF)
        m_new.append(exchange(1, (slice(None), pl.ds(j * HALF, HALF)), 2 + j))
    tick()
    wait_all(in_two)
    wait_all(m_self)
    gain_self = vec_row(vecs, 6)

    def two_rows(i):
        rows = pl.ds(pl.multiple_of(i * 32, 32), 32)
        dv, dg, db = norm_back(htwo[rows, :], both(0, rows), gain_self)
        e = cot[rows, :].astype(F32) + dv
        etwo[rows, :] = e
        elow2[rows, :] = e.astype(BF)
        gvec[6:7, :] += dg
        gvec[7:8, :] += db

    loop(8, two_rows)
    lat = cot
    in_lat = load(lat_h, lat)
    tick()
    wait_all(in_mlp)
    for j in range(4):
        cols = slice(j * HALF, (j + 1) * HALF)
        gh = nt(elow2[...], z[cols, :])
        dpre[:, cols] = (gh * gelu_slope(pre[:, cols])).astype(BF)
    m_mlp = []
    for j in range(2):
        cols = slice(j * HALF, (j + 1) * HALF)
        xb[2, x, :, cols] = (
            nt(dpre[:, 0:D], z[HID + j * HALF:HID + (j + 1) * HALF, :])
            + nt(dpre[:, D:HID], z[HID + D + j * HALF:HID + D + (j + 1) * HALF, :])
        ).astype(BF)
        m_mlp.append(exchange(2, (slice(None), pl.ds(j * HALF, HALF)), 4 + j))
    ck, cv = z.at[pl.ds(0, NROWS)], z.at[pl.ds(NROWS, NROWS)]
    inin, inp = z.at[pl.ds(2 * NROWS, NROWS)], z.at[pl.ds(3 * NROWS, NROWS)]
    in_keys = [load(ck_h, ck), load(cv_h, cv)]
    in_late = [load(inin_h, inin), load(inp_h, inp)]
    wait_all(in_mid)

    def fill_down(j):
        for i in range(2):
            part = hid[(j // 2) * ROWS:(j // 2 + 1) * ROWS, (j % 2) * HALF:(j % 2 + 1) * HALF]
            fill(4 + j, i, tn(part, elow2[:, i * HALF:(i + 1) * HALF]))

    def fill_up(j):
        for i in range(2):
            fill(8 + j, i, tn(mlpin[:, i * HALF:(i + 1) * HALF], dpre[:, j * HALF:(j + 1) * HALF]))

    fill_down(0)
    tick(4)
    fill_down(1)
    tick(5)
    fill_down(2)
    tick(6)
    fill_down(3)
    tick(7)
    wait_all(m_mlp)
    gain_mlp = vec_row(vecs, 4)

    def one_rows(i):
        rows = pl.ds(pl.multiple_of(i * 32, 32), 32)
        dv, dg, db = norm_back(hone[rows, :], both(2, rows), gain_mlp)
        e = etwo[rows, :] + dv
        hone[rows, :] = e
        elow1[rows, :] = e.astype(BF)
        gvec[4:5, :] += dg
        gvec[5:6, :] += db

    loop(8, one_rows)
    wait_all(in_cross)
    for g in range(2):
        dcr[g * D:(g + 1) * D, :] = nt(wf[3], elow1[g * LAT:(g + 1) * LAT, :]).astype(BF)

    wait_all(m_new)

    def new_rows(i):
        rows = pl.ds(pl.multiple_of(i * 64, 64), 64)
        selfin[rows, :] = (htwo[rows, :] + both(1, rows)).astype(BF)

    loop(4, new_rows)
    store(selfin, newlat_o)
    wait_all(in_keys)

    def head(g, h):
        cols = pl.ds(pl.multiple_of(h * HEAD_DIM, HEAD_DIM), HEAD_DIM)
        n_rows = slice(g * INP, (g + 1) * INP)
        l_rows = slice(g * LAT, (g + 1) * LAT)
        t_rows = pl.ds(pl.multiple_of(g * D + h * HEAD_DIM, HEAD_DIM), HEAD_DIM)
        k, v, q = ck[n_rows, cols], cv[n_rows, cols], cq[l_rows, cols]
        s = nt(k, q) * SCALE + mask[n_rows, :].astype(F32)
        p = jnp.exp(s - st[g, pl.ds(h, 1), :]) * st[g, pl.ds(HEADS + h, 1), :]
        do = dcr[t_rows, :]
        delta = jnp.sum(do.astype(F32) * att[t_rows, :].astype(F32), axis=0, keepdims=True)
        dsc = (p * (nn(v, do) - delta)).astype(BF)
        cv[n_rows, cols] = nt(p.astype(BF), do).astype(BF)
        ck[n_rows, cols] = (nn(dsc, q) * SCALE).astype(BF)
        xb[0, x, l_rows, cols] = (tn(dsc, k) * SCALE).astype(BF)

    fills = [lambda j=j: fill_up(j) for j in range(4)]
    m_query = []
    for g in range(2):
        for part in range(2):
            def heads(i, g=g, part=part):
                head(g, 4 * part + 2 * i)
                head(g, 4 * part + 2 * i + 1)

            loop(2, heads)
            fills[2 * g + part]()
            tick(8 + 2 * g + part)
        m_query.append(exchange(0, (pl.ds(g * LAT, LAT),), 6 + g))
    wait_all(in_late)
    latin = mlpin
    in_latin = load(latin_h, latin)

    def weight_grad(w, source):
        def body(i):
            rows = pl.ds(pl.multiple_of(i * 256, 256), 256)
            mine = pl.ds(pl.multiple_of(x * HALF + i * 256, 256), 256)
            theirs = pl.ds(pl.multiple_of((1 - x) * HALF + i * 256, 256), 256)
            other[w, rows, :] = tn(inin[:, theirs], source[...]).astype(BF)
            grad[pl.ds(pl.multiple_of((14 + w) * HALF + i * 256, 256), 256), :] = tn(
                inin[:, mine], source[...]
            ).astype(BF)

        loop(2, body)

    weight_grad(0, ck)
    start_core(0)
    tick()
    weight_grad(1, cv)
    start_x(0)
    start_core(1)
    for j in range(2):
        value = 0.0
        for g in range(2):
            rows = pl.ds(pl.multiple_of(g * D + x * HALF, HALF), HALF)
            value = value + nn(
                att[rows, :], elow1[g * LAT:(g + 1) * LAT, j * HALF:(j + 1) * HALF]
            )
        fill(12, j, value)
    tick(12)
    start_x(1)
    tick(13)
    wait_all(m_query)
    in_latin.wait()
    dcq = elow2

    def query_rows(i):
        rows = pl.ds(pl.multiple_of(i * 64, 64), 64)
        dcq[rows, :] = both(0, rows).astype(BF)

    loop(4, query_rows)
    for j in range(2):
        mine = pl.ds(pl.multiple_of(x * HALF, HALF), HALF)
        fill(13, j, tn(latin[:, mine], dcq[:, j * HALF:(j + 1) * HALF]))
    tick(14)
    gain_lat = vec_row(vecs, 0)

    def lat_rows(i):
        rows = pl.ds(pl.multiple_of(i * 128, 128), 128)
        dv, dg, db = norm_back(lat[rows, :].astype(F32), nt(dcq[rows, :], wf[2]), gain_lat)
        lat[rows, :] = (hone[rows, :] + dv).astype(BF)
        gvec[0:1, :] += dg
        gvec[1:2, :] += db

    in_lat.wait()
    loop(2, lat_rows)
    store(lat, glat_o)
    tick(15)
    gain_inp = vec_row(vecs, 2)

    def inp_rows(i):
        rows = pl.ds(pl.multiple_of(i * 224, 16), 224)
        dy = nt(ck[rows, :], wf[0]) + nt(cv[rows, :], wf[1])
        dv, dg, db = norm_back(inp[rows, :].astype(F32), dy, gain_inp)
        inp[rows, :] = dv.astype(BF)
        gvec[2:3, :] += dg
        gvec[3:4, :] += db

    span(0, 2, inp_rows)
    tick(16)
    span(2, 4, inp_rows)
    tick(17)
    span(4, 6, inp_rows)
    tick(18)
    span(6, 7, inp_rows)
    store(inp, ginp_o)
    tick(19)
    col = lax.broadcasted_iota(jnp.int32, (8, D), 1) // HALF
    row = lax.broadcasted_iota(jnp.int32, (8, D), 0)
    keep = (col == x) | (row == 2) | (row == 3)
    gvec[...] = jnp.where(keep, gvec[...], 0.0)
    v_partners = (xp, cp, yp, ap, bp)
    v_moves = []

    def vec_event(s):
        if s > 0:
            v_moves[s - 1].wait()
            gvec[...] += gvr[s - 1]
        if s < 5:
            move = remote(gvec, gvr.at[s], vs.at[s], vr.at[s], v_partners[s])
            move.start()
            v_moves.append(move)
        else:
            store(gvec, gvec_o)

    for t in range(OFFSETS[-1]):
        tick()
        if t <= 5:
            vec_event(t)
    wait_all(outs)


def run_second(args):
    any_spec = pl.BlockSpec(memory_space=pl.ANY)
    outs = [
        ((ROWS, D), BF), ((ROWS, D), BF), ((NROWS, D), BF), ((HALF, D), BF), ((HALF, D), BF),
        ((HALF, D), BF), ((HALF, D), BF), ((D, HID), BF), ((HID, D), BF), ((D, HALF), BF),
        ((D, HALF), BF), ((D, HALF), BF), ((HALF, D), BF), ((8, D), F32),
    ]
    scratch = [
        ((4 * NROWS, D), BF), ((4, D, D), BF), ((ROWS, D), BF),
        ((2 * D, LAT), BF), ((2, 16, LAT), F32), ((2, 8, HALF), F32), ((ROWS, D), F32),
        ((ROWS, D), F32), ((ROWS, D), F32), ((ROWS, D), BF), ((ROWS, D), BF), ((ROWS, HID), F32),
        ((2 * ROWS, D), BF), ((3, ROWS, HALF), BF), ((ROWS, HALF), BF), ((NROWS, LAT), BF),
        ((ROWS, D), BF), ((ROWS, D), BF), ((ROWS, D), BF), ((ROWS, HID), BF),
        ((2 * D, LAT), BF), ((3, 2, ROWS, D), BF), ((16 * HALF, D), BF), ((2, HALF, D), BF),
        ((2, HALF, HALF), BF), ((2, 256, HALF), BF), ((3, 256, HALF), BF), ((2, 256, HALF), BF),
        ((2, 256, HALF), BF), ((2, 256, HALF), BF), ((2, HALF, HALF), BF), ((8, D), F32),
        ((5, 8, D), F32),
    ]
    dma = pltpu.SemaphoreType.DMA
    return pl.pallas_call(
        second_kernel,
        out_shape=[jax.ShapeDtypeStruct(*o) for o in outs],
        in_specs=[any_spec] * len(args),
        out_specs=[any_spec] * len(outs),
        scratch_shapes=[pltpu.VMEM(*s) for s in scratch]
        + [dma((32,)), dma((32,))] + [dma((20 * 7,))] * 2 + [dma((12,))] * 2 + [dma((5,))] * 2
        + [pltpu.SemaphoreType.REGULAR((80,))],
        compiler_params=pltpu.CompilerParams(
            collective_id=1, has_side_effects=True, vmem_limit_bytes=63 * MIB
        ),
        name="backward",
    )(*args)


def finish_kernel(*refs):
    srcs, refs = refs[:13], refs[13:]
    dsts, (low, wide, insem, outsem) = refs[:13], refs[13:]
    tiles = []
    for i in (*range(3, 13), 0, 1, 2):
        rows, cols = srcs[i].shape
        for r in range(0, rows, HALF):
            for q in range(0, cols, HALF):
                count = min(HALF, rows - r)
                tiles.append((i, pl.ds(r, count), pl.ds(q, HALF), pl.ds(0, count)))
    depth = low.shape[0]
    ins, outs, finished = {}, {}, set()

    def finish_out(n):
        if n >= 0 and n not in finished:
            outs[n].wait()
            finished.add(n)

    def start_in(n):
        i, rows, cols, part = tiles[n]
        ins[n] = pltpu.make_async_copy(
            srcs[i].at[rows, cols], low.at[n % depth, part], insem.at[n % depth]
        )
        ins[n].start()

    for n in range(depth):
        start_in(n)
    for n in range(len(tiles)):
        slot = n % depth
        i, rows, cols, part = tiles[n]
        ins[n].wait()
        finish_out(n - depth)
        if i < 3:
            outs[n] = pltpu.make_async_copy(low.at[slot, part], dsts[i].at[rows, cols], outsem.at[slot])
            outs[n].start()
        else:
            def body(i, slot=slot):
                rows = pl.ds(pl.multiple_of(i * 64, 64), 64)
                wide[slot, rows, :] = low[slot, rows, :].astype(F32)

            loop(HALF // 64, body)
            outs[n] = pltpu.make_async_copy(wide.at[slot], dsts[i].at[rows, cols], outsem.at[slot])
            outs[n].start()
        if n + depth < len(tiles):
            if i < 3:
                finish_out(n)
            start_in(n + depth)
    for n in range(len(tiles) - depth, len(tiles)):
        finish_out(n)


def run_finish(args):
    any_spec = pl.BlockSpec(memory_space=pl.ANY)
    depth = 6
    return pl.pallas_call(
        finish_kernel,
        out_shape=[
            jax.ShapeDtypeStruct(a.shape, BF if i < 3 else F32) for i, a in enumerate(args)
        ],
        in_specs=[any_spec] * 13,
        out_specs=[any_spec] * 13,
        scratch_shapes=[
            pltpu.VMEM((depth, HALF, HALF), BF), pltpu.VMEM((depth, HALF, HALF), F32),
            pltpu.SemaphoreType.DMA((depth,)), pltpu.SemaphoreType.DMA((depth,)),
        ],
        compiler_params=pltpu.CompilerParams(vmem_limit_bytes=62 * MIB),
        name="finish",
    )(*args)


def per_device_pair(
    latents, inputs, latent_segment, input_segment, cross_query, cross_key, cross_value,
    cross_output, mlp_up, mlp_down, self_query, self_key, self_value, self_output,
    latent_gain, latent_bias, input_gain, input_bias, mlp_gain, mlp_bias, self_gain,
    self_bias, cotangent,
):
    vec = (
        latent_gain, latent_bias, input_gain, input_bias, mlp_gain, mlp_bias, self_gain, self_bias
    )
    lat = latents.reshape(ROWS, D)
    inp = inputs.reshape(NROWS, D)
    cot = cotangent.reshape(ROWS, D)
    kept = run_first((
        lat, inp, latent_segment, input_segment, *vec, cross_key, cross_value, cross_query,
        cross_output, mlp_up, mlp_down, self_query, self_key, self_value, self_output, cot,
    ))
    (new, glat, ginp, gq, gk, gv, go, gup, gdown, gsq, gsk, gsv, gso, gvec) = run_second(
        tuple(kept) + (
            lat, inp, mlp_up, mlp_down, self_query, self_key, self_value, self_output, cot
        )
    )
    new, glat, ginp, *grads = run_finish(
        (new, glat, ginp, gq, gk, gv, go, gup, gdown, gsq, gsk, gsv, gso)
    )
    x = lax.axis_index("shard")
    small = lax.dynamic_slice_in_dim(gvec, x * HALF, HALF, 1)
    return (
        new.reshape(latents.shape), glat.reshape(latents.shape), ginp.reshape(inputs.shape),
        *grads, *[small[i] for i in range(8)],
    )


def norm_forward(values, gain, shift):
    centred = values - jnp.mean(values, axis=-1, keepdims=True)
    inv_std = lax.rsqrt(jnp.mean(centred * centred, axis=-1, keepdims=True) + EPSILON)
    normed = centred * inv_std
    return (normed * gain + shift, normed, inv_std)


def norm_backward(grad_out, normed, inv_std, gain):
    scaled = grad_out * gain
    first_mean = jnp.mean(scaled, axis=-1, keepdims=True)
    second_mean = jnp.mean(scaled * normed, axis=-1, keepdims=True)
    grad_in = inv_std * (scaled - first_mean - normed * second_mean)
    return (grad_in, jnp.sum(grad_out * normed, axis=0), jnp.sum(grad_out, axis=0))


def product(left, right):
    return jnp.dot(left, right, preferred_element_type=jnp.float32)


def inner_rows(left, right):
    return lax.dot_general(
        left, right, (((0,), (0,)), ((), ())), preferred_element_type=jnp.float32
    )


def outer_cols(left, right):
    return lax.dot_general(
        left, right, (((1,), (1,)), ((), ())), preferred_element_type=jnp.float32
    )


def forward_total(term):
    return lax.psum(term.astype(jnp.bfloat16), "shard").astype(jnp.float32)


def backward_total(term):
    return lax.psum(term.astype(jnp.bfloat16), "shard").astype(jnp.float32)


def per_device(
    latents,
    inputs,
    latent_segment,
    input_segment,
    cross_query,
    cross_key,
    cross_value,
    cross_output,
    mlp_up,
    mlp_down,
    self_query,
    self_key,
    self_value,
    self_output,
    latent_gain,
    latent_bias,
    input_gain,
    input_bias,
    mlp_gain,
    mlp_bias,
    self_gain,
    self_bias,
    cotangent,
):
    shards = lax.axis_size("shard")
    groups, lat_len, width = latents.shape
    inp_len = inputs.shape[1]
    width_part = width // shards
    column_start = lax.axis_index("shard") * width_part
    rows = groups * lat_len
    scale = HEAD_DIM ** (-0.5)
    gathered = (
        lax.all_gather(cross_query, "shard", axis=0, tiled=True),
        lax.all_gather(cross_key, "shard", axis=0, tiled=True),
        lax.all_gather(cross_value, "shard", axis=0, tiled=True),
        lax.all_gather(cross_output, "shard", axis=0, tiled=True),
        lax.all_gather(latent_gain, "shard", axis=0, tiled=True),
        lax.all_gather(latent_bias, "shard", axis=0, tiled=True),
        lax.all_gather(input_gain, "shard", axis=0, tiled=True),
        lax.all_gather(input_bias, "shard", axis=0, tiled=True),
        lax.all_gather(mlp_gain, "shard", axis=0, tiled=True),
        lax.all_gather(mlp_bias, "shard", axis=0, tiled=True),
        lax.all_gather(self_gain, "shard", axis=0, tiled=True),
        lax.all_gather(self_bias, "shard", axis=0, tiled=True),
    )
    full_query, full_key, full_value, full_output = (
        gathered[0],
        gathered[1],
        gathered[2],
        gathered[3],
    )
    gain_lat, bias_lat, gain_inp, bias_inp, gain_mlp, bias_mlp, gain_self, bias_self = [
        piece.astype(jnp.float32) for piece in gathered[4:]
    ]
    lat_rows = latents.astype(jnp.float32).reshape(rows, width)
    inp_rows = inputs.astype(jnp.float32).reshape(groups * inp_len, width)
    lat_value, lat_normed, lat_inv = norm_forward(lat_rows, gain_lat, bias_lat)
    lat_in = lat_value.astype(jnp.bfloat16)
    inp_value, inp_normed, inp_inv = norm_forward(inp_rows, gain_inp, bias_inp)
    inp_in = inp_value.astype(jnp.bfloat16)
    cross_q = (
        product(lat_in, full_query).astype(jnp.bfloat16).reshape(groups, lat_len, HEADS, HEAD_DIM)
    )
    cross_k = (
        product(inp_in, full_key).astype(jnp.bfloat16).reshape(groups, inp_len, HEADS, HEAD_DIM)
    )
    cross_v = (
        product(inp_in, full_value).astype(jnp.bfloat16).reshape(groups, inp_len, HEADS, HEAD_DIM)
    )
    allowed = latent_segment[:, None, :, None] == input_segment[:, None, None, :]
    scores = (
        jnp.einsum("glhd,gnhd->ghln", cross_q, cross_k, preferred_element_type=jnp.float32) * scale
    )
    masked = jnp.where(allowed, scores, NEGATIVE)
    part_max = jnp.max(masked, axis=-1)
    top = lax.pmax(part_max, "shard")
    total = lax.psum(
        jnp.sum(jnp.where(allowed, jnp.exp(masked - top[..., None]), 0.0), axis=-1), "shard"
    )
    cross_prob = jnp.where(allowed, jnp.exp(masked - top[..., None]), 0.0) / total[..., None]
    cross_prob_low = cross_prob.astype(jnp.bfloat16)
    part_out = jnp.einsum(
        "ghln,gnhd->glhd", cross_prob_low, cross_v, preferred_element_type=jnp.float32
    )
    attended = lax.psum(part_out.astype(jnp.bfloat16), "shard").astype(jnp.float32)
    attended_in = attended.reshape(rows, width).astype(jnp.bfloat16)
    h_one = lat_rows + product(attended_in, full_output)
    mlp_value, mlp_normed, mlp_inv = norm_forward(h_one, gain_mlp, bias_mlp)
    mlp_in = mlp_value.astype(jnp.bfloat16)
    pre_act = product(mlp_in, mlp_up)
    hidden_in = jax.nn.gelu(pre_act).astype(jnp.bfloat16)
    h_two = h_one + forward_total(product(hidden_in, mlp_down))
    self_value_n, self_normed, self_inv = norm_forward(h_two, gain_self, bias_self)
    self_in = self_value_n.astype(jnp.bfloat16)
    local_heads = self_query.shape[1] // HEAD_DIM
    local_width = local_heads * HEAD_DIM
    self_q = (
        product(self_in, self_query)
        .astype(jnp.bfloat16)
        .reshape(groups, lat_len, local_heads, HEAD_DIM)
    )
    self_k = (
        product(self_in, self_key)
        .astype(jnp.bfloat16)
        .reshape(groups, lat_len, local_heads, HEAD_DIM)
    )
    self_v = (
        product(self_in, self_value)
        .astype(jnp.bfloat16)
        .reshape(groups, lat_len, local_heads, HEAD_DIM)
    )
    self_scores = (
        jnp.einsum("glhd,gmhd->ghlm", self_q, self_k, preferred_element_type=jnp.float32) * scale
    )
    self_prob = jax.nn.softmax(self_scores, axis=-1)
    self_prob_low = self_prob.astype(jnp.bfloat16)
    self_att = jnp.einsum(
        "ghlm,gmhd->glhd", self_prob_low, self_v, preferred_element_type=jnp.float32
    )
    self_att_in = self_att.reshape(rows, local_width).astype(jnp.bfloat16)
    result = h_two + forward_total(product(self_att_in, self_output))
    new_latents = result.reshape(groups, lat_len, width).astype(jnp.bfloat16)
    grad_out = cotangent.astype(jnp.float32).reshape(rows, width)
    grad_branch = grad_out.astype(jnp.bfloat16)
    grad_self_output = inner_rows(self_att_in, grad_branch)
    grad_att = (
        outer_cols(grad_branch, self_output)
        .astype(jnp.bfloat16)
        .reshape(groups, lat_len, local_heads, HEAD_DIM)
    )
    delta = jnp.sum(grad_att.astype(jnp.float32) * self_att, axis=-1).transpose(0, 2, 1)
    grad_prob = jnp.einsum("glhd,gmhd->ghlm", grad_att, self_v, preferred_element_type=jnp.float32)
    grad_sv = jnp.einsum(
        "ghlm,glhd->gmhd", self_prob_low, grad_att, preferred_element_type=jnp.float32
    )
    grad_scores = (self_prob * (grad_prob - delta[..., None])).astype(jnp.bfloat16)
    grad_sq = (
        jnp.einsum("ghlm,gmhd->glhd", grad_scores, self_k, preferred_element_type=jnp.float32)
        * scale
    )
    grad_sk = (
        jnp.einsum("ghlm,glhd->gmhd", grad_scores, self_q, preferred_element_type=jnp.float32)
        * scale
    )
    grad_sq = grad_sq.astype(jnp.bfloat16).reshape(rows, local_width)
    grad_sk = grad_sk.astype(jnp.bfloat16).reshape(rows, local_width)
    grad_sv = grad_sv.astype(jnp.bfloat16).reshape(rows, local_width)
    grad_self_query = inner_rows(self_in, grad_sq)
    grad_self_key = inner_rows(self_in, grad_sk)
    grad_self_value = inner_rows(self_in, grad_sv)
    grad_self_in = backward_total(
        outer_cols(grad_sq, self_query)
        + outer_cols(grad_sk, self_key)
        + outer_cols(grad_sv, self_value)
    )
    grad_norm, gain_full, bias_full = norm_backward(grad_self_in, self_normed, self_inv, gain_self)
    grad_two = grad_out + grad_norm
    grad_self_gain = lax.dynamic_slice_in_dim(gain_full, column_start, width_part)
    grad_self_bias = lax.dynamic_slice_in_dim(bias_full, column_start, width_part)
    grad_mlp_branch = grad_two.astype(jnp.bfloat16)
    grad_mlp_down = inner_rows(hidden_in, grad_mlp_branch)
    grad_hidden = outer_cols(grad_mlp_branch, mlp_down)
    gelu_value, gelu_pull = jax.vjp(jax.nn.gelu, pre_act)
    grad_pre = gelu_pull(grad_hidden)[0].astype(jnp.bfloat16)
    grad_mlp_up = inner_rows(mlp_in, grad_pre)
    grad_mlp_in = backward_total(outer_cols(grad_pre, mlp_up))
    grad_norm, gain_full, bias_full = norm_backward(grad_mlp_in, mlp_normed, mlp_inv, gain_mlp)
    grad_one = grad_two + grad_norm
    grad_mlp_gain = lax.dynamic_slice_in_dim(gain_full, column_start, width_part)
    grad_mlp_bias = lax.dynamic_slice_in_dim(bias_full, column_start, width_part)
    grad_cross_branch = grad_one.astype(jnp.bfloat16)
    grad_cross_output = inner_rows(
        lax.dynamic_slice_in_dim(attended_in, column_start, width_part, 1), grad_cross_branch
    )
    grad_ca = (
        outer_cols(grad_cross_branch, full_output)
        .astype(jnp.bfloat16)
        .reshape(groups, lat_len, HEADS, HEAD_DIM)
    )
    cross_delta = jnp.sum(grad_ca.astype(jnp.float32) * attended, axis=-1).transpose(0, 2, 1)
    grad_cp = jnp.einsum("glhd,gnhd->ghln", grad_ca, cross_v, preferred_element_type=jnp.float32)
    grad_cv = jnp.einsum(
        "ghln,glhd->gnhd", cross_prob_low, grad_ca, preferred_element_type=jnp.float32
    )
    grad_cs = (cross_prob * (grad_cp - cross_delta[..., None])).astype(jnp.bfloat16)
    grad_cq_part = (
        jnp.einsum("ghln,gnhd->glhd", grad_cs, cross_k, preferred_element_type=jnp.float32) * scale
    )
    grad_ck = (
        jnp.einsum("ghln,glhd->gnhd", grad_cs, cross_q, preferred_element_type=jnp.float32) * scale
    )
    grad_cq = backward_total(grad_cq_part.reshape(rows, width)).astype(jnp.bfloat16)
    grad_ck = grad_ck.astype(jnp.bfloat16).reshape(groups * inp_len, width)
    grad_cv = grad_cv.astype(jnp.bfloat16).reshape(groups * inp_len, width)
    grad_cross_query = inner_rows(
        lax.dynamic_slice_in_dim(lat_in, column_start, width_part, 1), grad_cq
    )
    grad_lat_in = outer_cols(grad_cq, full_query)
    grad_norm, gain_full, bias_full = norm_backward(grad_lat_in, lat_normed, lat_inv, gain_lat)
    grad_latents = (grad_one + grad_norm).reshape(groups, lat_len, width).astype(jnp.bfloat16)
    grad_latent_gain = lax.dynamic_slice_in_dim(gain_full, column_start, width_part)
    grad_latent_bias = lax.dynamic_slice_in_dim(bias_full, column_start, width_part)
    key_term = inner_rows(inp_in, grad_ck)
    value_term = inner_rows(inp_in, grad_cv)
    grad_inp_in = outer_cols(grad_ck, full_key) + outer_cols(grad_cv, full_value)
    grad_inp, inp_gain_full, inp_bias_full = norm_backward(
        grad_inp_in, inp_normed, inp_inv, gain_inp
    )
    grad_inputs = grad_inp.reshape(groups, inp_len, width).astype(jnp.bfloat16)
    grad_cross_key, grad_cross_value, grad_input_gain, grad_input_bias = (
        lax.psum_scatter(
            key_term.astype(jnp.bfloat16), "shard", scatter_dimension=0, tiled=True
        ).astype(jnp.float32),
        lax.psum_scatter(
            value_term.astype(jnp.bfloat16), "shard", scatter_dimension=0, tiled=True
        ).astype(jnp.float32),
        lax.psum_scatter(
            inp_gain_full.astype(jnp.bfloat16), "shard", scatter_dimension=0, tiled=True
        ).astype(jnp.float32),
        lax.psum_scatter(
            inp_bias_full.astype(jnp.bfloat16), "shard", scatter_dimension=0, tiled=True
        ).astype(jnp.float32),
    )
    (
        grad_cross_query,
        grad_cross_key,
        grad_cross_value,
        grad_cross_output,
        grad_mlp_up,
        grad_mlp_down,
        grad_self_query,
        grad_self_key,
        grad_self_value,
        grad_self_output,
        grad_latent_gain,
        grad_latent_bias,
        grad_input_gain,
        grad_input_bias,
        grad_mlp_gain,
        grad_mlp_bias,
        grad_self_gain,
        grad_self_bias,
    ) = (
        lax.psum(grad_cross_query.astype(jnp.bfloat16), "grp").astype(jnp.float32),
        lax.psum(grad_cross_key.astype(jnp.bfloat16), "grp").astype(jnp.float32),
        lax.psum(grad_cross_value.astype(jnp.bfloat16), "grp").astype(jnp.float32),
        lax.psum(grad_cross_output.astype(jnp.bfloat16), "grp").astype(jnp.float32),
        lax.psum(grad_mlp_up.astype(jnp.bfloat16), "grp").astype(jnp.float32),
        lax.psum(grad_mlp_down.astype(jnp.bfloat16), "grp").astype(jnp.float32),
        lax.psum(grad_self_query.astype(jnp.bfloat16), "grp").astype(jnp.float32),
        lax.psum(grad_self_key.astype(jnp.bfloat16), "grp").astype(jnp.float32),
        lax.psum(grad_self_value.astype(jnp.bfloat16), "grp").astype(jnp.float32),
        lax.psum(grad_self_output.astype(jnp.bfloat16), "grp").astype(jnp.float32),
        lax.psum(grad_latent_gain.astype(jnp.bfloat16), "grp").astype(jnp.float32),
        lax.psum(grad_latent_bias.astype(jnp.bfloat16), "grp").astype(jnp.float32),
        lax.psum(grad_input_gain.astype(jnp.bfloat16), "grp").astype(jnp.float32),
        lax.psum(grad_input_bias.astype(jnp.bfloat16), "grp").astype(jnp.float32),
        lax.psum(grad_mlp_gain.astype(jnp.bfloat16), "grp").astype(jnp.float32),
        lax.psum(grad_mlp_bias.astype(jnp.bfloat16), "grp").astype(jnp.float32),
        lax.psum(grad_self_gain.astype(jnp.bfloat16), "grp").astype(jnp.float32),
        lax.psum(grad_self_bias.astype(jnp.bfloat16), "grp").astype(jnp.float32),
    )
    return (
        new_latents,
        grad_latents,
        grad_inputs,
        grad_cross_query,
        grad_cross_key,
        grad_cross_value,
        grad_cross_output,
        grad_mlp_up,
        grad_mlp_down,
        grad_self_query,
        grad_self_key,
        grad_self_value,
        grad_self_output,
        grad_latent_gain,
        grad_latent_bias,
        grad_input_gain,
        grad_input_bias,
        grad_mlp_gain,
        grad_mlp_bias,
        grad_self_gain,
        grad_self_bias,
    )


def solution(mesh):
    laid_out = mesh.shape["shard"] == 2 and mesh.shape["grp"] == 16
    return jax.shard_map(
        per_device_pair if laid_out else per_device,
        mesh=mesh,
        in_specs=(
            P("grp", None, None),
            P("grp", "shard", None),
            P("grp", None),
            P("grp", "shard"),
            P("shard", None),
            P("shard", None),
            P("shard", None),
            P("shard", None),
            P(None, "shard"),
            P("shard", None),
            P(None, "shard"),
            P(None, "shard"),
            P(None, "shard"),
            P("shard", None),
            P("shard"),
            P("shard"),
            P("shard"),
            P("shard"),
            P("shard"),
            P("shard"),
            P("shard"),
            P("shard"),
            P("grp", None, None),
        ),
        out_specs=(
            P("grp", None, None),
            P("grp", None, None),
            P("grp", "shard", None),
            P("shard", None),
            P("shard", None),
            P("shard", None),
            P("shard", None),
            P(None, "shard"),
            P("shard", None),
            P(None, "shard"),
            P(None, "shard"),
            P(None, "shard"),
            P("shard", None),
            P("shard"),
            P("shard"),
            P("shard"),
            P("shard"),
            P("shard"),
            P("shard"),
            P("shard"),
            P("shard"),
        ),
        check_vma=False,
    )
```

```python
import jax
import jax.numpy as jnp
from jax import lax
from jax.experimental import pallas as pl
from jax.experimental.pallas import tpu as pltpu
from jax.sharding import PartitionSpec as P

HEADS = 8
HEAD_DIM = 128


EPSILON = 1e-05
NEGATIVE = -1e30

BF = jnp.bfloat16
F32 = jnp.float32
MESH = pl.DeviceIdType.MESH
LAT = 128
INP = 784
D = 1024
HALF = 512
HID = 2048
ROWS = 2 * LAT
NROWS = 2 * INP
SCALE = HEAD_DIM ** (-0.5)
MIB = 1 << 20


def nn(a, b):
    return lax.dot_general(a, b, (((1,), (0,)), ((), ())), preferred_element_type=F32)


def nt(a, b):
    return lax.dot_general(a, b, (((1,), (1,)), ((), ())), preferred_element_type=F32)


def tn(a, b):
    return lax.dot_general(a, b, (((0,), (0,)), ((), ())), preferred_element_type=F32)


def place():
    g = lax.axis_index("grp")
    x = lax.axis_index("shard")
    c = lax.rem(g, 2)
    y = lax.rem(g // 2, 2)
    a = lax.rem(g // 4, 2)
    b = g // 8
    return dict(
        x=x, c=c, y=y, a=a, b=b,
        xp=(g, 1 - x),
        cp=(g + 1 - 2 * c, x),
        yp=(g + 2 - 4 * y, x),
        ap=(g + 4 - 8 * a, x),
        bp=(g + 8 - 16 * b, x),
        mp=(g + 4 - 8 * b, x),
    )


def greet(partners):
    barrier = pltpu.get_barrier_semaphore()
    for partner in partners:
        pl.semaphore_signal(barrier, inc=1, device_id=partner, device_id_type=MESH)
    pl.semaphore_wait(barrier, len(partners))


def remote(src, dst, send, recv, partner):
    return pltpu.make_async_remote_copy(
        src_ref=src, dst_ref=dst, send_sem=send, recv_sem=recv,
        device_id=partner, device_id_type=MESH,
    )


def norm(v, gain, shift):
    cen = v - jnp.mean(v, axis=-1, keepdims=True)
    inv = lax.rsqrt(jnp.mean(cen * cen, axis=-1, keepdims=True) + EPSILON)
    return cen * inv * gain + shift


def vec_row(vecs, i):
    return jnp.concatenate([vecs[0, i:i + 1, :], vecs[1, i:i + 1, :]], axis=1)


def span(first, last, body):
    lax.fori_loop(first, last, lambda i, carry: (body(i), carry)[1], 0)


def loop(n, body):
    span(0, n, body)


def first_kernel(
    lat_h, inp_h, seglat, seginp, v0, v1, v2, v3, v4, v5, v6, v7, wk_h, wv_h, wq_h, wo_h, up_h, down_h,
    sq_h, sk_h, sv_h, so_h, cot_h,
    wf_o, ck_o, cv_o, inin_o, latin_o, cq_o, att_o, st_o, vec_o, hone_o, htwo_o,
    mlpin_o, selfin_o, pre_o, hid_o, ds_o, slow_o, mask_o,
    wf, inp, inin, ck, cv, lat, latin, cq, mask, segs, axb, stx, att, st, vecs,
    hone, htwo, mlpin, pre, hid, xm, selfin, wup, wdown, wself, wso, cot, qkv, dself,
    ds, slow, lsem, osem, xs, xr, ys, yr, c0s, c0r, c1s, c1r, ms, mr,
):
    me = place()
    x, y, c = me["x"], me["y"], me["c"]
    xp, yp, cp = me["xp"], me["yp"], me["cp"]
    nlocal = [0]
    nout = [0]

    def load(src, dst):
        copy = pltpu.make_async_copy(src, dst, lsem.at[nlocal[0]])
        nlocal[0] += 1
        copy.start()
        return copy

    outs = []

    def store(src, dst):
        copy = pltpu.make_async_copy(src, dst, osem.at[nout[0]])
        nout[0] += 1
        copy.start()
        outs.append(copy)

    own = pl.ds(pl.multiple_of(x * HALF, HALF), HALF)
    in_inp = load(inp_h, inp)
    in_lat = load(lat_h, lat)
    in_cot = load(cot_h, cot)
    in_so = load(so_h, wso)
    greet((xp, yp, cp))
    for i, v in enumerate((v0, v1, v2, v3, v4, v5, v6, v7)):
        vecs[x, i:i + 1, :] = v[...].astype(F32).reshape(1, HALF)
    vec_move = remote(vecs.at[x], vecs.at[x], xs.at[4], xr.at[4], xp)
    vec_move.start()
    weights = (wk_h, wv_h, wq_h, wo_h)
    quarter = 2 * y + c

    def part(w, side, q):
        return wf.at[w, pl.ds(pl.multiple_of(side * HALF + q * 128, 128), 128)]

    x_moves = []
    for w in range(4):
        src = weights[w].at[pl.ds(pl.multiple_of(quarter * 128, 128), 128)]
        move = remote(src, part(w, x, quarter), xs.at[w], xr.at[w], xp)
        move.start()
        x_moves.append(move)
    in_w = [load(weights[w], wf.at[w, own]) for w in range(4)]
    in_self = [load(h, wself.at[i]) for i, h in enumerate((sq_h, sk_h, sv_h))]
    in_up = load(up_h, wup)
    in_down = load(down_h, wdown)
    pending = []

    def forward_x(w):
        x_moves[w].wait()
        for sems, partner in (((ys, yr), yp), ((c0s, c0r), cp)):
            block = part(w, 1 - x, quarter)
            move = remote(block, block, sems[0].at[w], sems[1].at[w], partner)
            move.start()
            pending.append(move)

    def forward_y(w):
        block = part(w, 1 - x, quarter)
        remote(block, block, ys.at[w], yr.at[w], yp).wait_recv()
        block = part(w, 1 - x, 2 * (1 - y) + c)
        move = remote(block, block, c1s.at[w], c1r.at[w], cp)
        move.start()
        pending.append(move)

    def whole(w):
        block = part(w, 1 - x, quarter)
        remote(block, block, c0s.at[w], c0r.at[w], cp).wait_recv()
        remote(block, block, c1s.at[w], c1r.at[w], cp).wait_recv()
        in_w[w].wait()
        store(wf.at[w], wf_o.at[w])

    segs[...] = jnp.zeros_like(segs)
    segs[0:2, 0:INP] = seginp[...].astype(F32)
    for g in range(2):
        lat_row = seglat[g:g + 1, :].astype(F32)
        for j in range(7):
            count = min(128, INP - j * 128)
            col = jnp.broadcast_to(segs[g:g + 1, j * 128:(j + 1) * 128], (128, 128)).T
            mask[g * INP + j * 128:g * INP + j * 128 + count, :] = jnp.where(
                col[:count] == lat_row, 0.0, NEGATIVE
            ).astype(BF)
    store(mask, mask_o)
    in_cot.wait()
    in_so.wait()
    dself[...] = nt(cot[...], wso[...]).astype(BF)
    in_inp.wait()
    vec_move.wait()
    store(vecs, vec_o)
    gain_inp, bias_inp = vec_row(vecs, 2), vec_row(vecs, 3)

    def norm_rows(i):
        rows = pl.ds(pl.multiple_of(i * 32, 32), 32)
        inin[rows, :] = norm(inp[rows, :].astype(F32), gain_inp, bias_inp).astype(BF)

    span(0, 24, norm_rows)
    forward_x(0)
    span(24, 49, norm_rows)
    store(inin, inin_o)
    forward_x(1)
    forward_y(0)
    in_lat.wait()
    latin[...] = norm(lat[...].astype(F32), vec_row(vecs, 0), vec_row(vecs, 1)).astype(BF)
    store(latin, latin_o)

    def project(target, w, half):
        cols = slice(half * HALF, (half + 1) * HALF)

        def body(i):
            rows = pl.ds(pl.multiple_of(i * INP, 16), INP)
            target[rows, cols] = nn(inin[rows, :], wf[w, :, cols]).astype(BF)

        loop(2, body)

    whole(0)
    project(ck, 0, 0)
    forward_x(2)
    forward_y(1)
    project(ck, 0, 1)
    store(ck, ck_o)
    whole(1)
    forward_x(3)
    forward_y(2)
    project(cv, 1, 0)
    project(cv, 1, 1)
    store(cv, cv_o)
    whole(2)
    cq[...] = nn(latin[...], wf[2]).astype(BF)
    store(cq, cq_o)
    forward_y(3)

    def head(g, h):
        cols = pl.ds(pl.multiple_of(h * HEAD_DIM, HEAD_DIM), HEAD_DIM)
        n_rows = slice(g * INP, (g + 1) * INP)
        s = nt(ck[n_rows, cols], cq[g * LAT:(g + 1) * LAT, cols]) * SCALE + mask[n_rows, :].astype(F32)
        top = jnp.maximum(jnp.max(s, axis=0, keepdims=True), 0.1 * NEGATIVE)
        e = jnp.exp(s - top)
        total = jnp.sum(e, axis=0, keepdims=True)
        out = tn(cv[n_rows, cols], e.astype(BF))
        out = out * jnp.where(total > 0.0, 1.0 / total, 0.0)
        axb[x, pl.ds(pl.multiple_of(g * D + h * HEAD_DIM, HEAD_DIM), HEAD_DIM), :] = out.astype(BF)
        stx[x, g, pl.ds(h, 1), :] = top
        stx[x, g, pl.ds(HEADS + h, 1), :] = total

    a_moves = []
    for g in range(2):
        def pair(i, g=g):
            head(g, 2 * i)
            head(g, 2 * i + 1)

        loop(HEADS // 2, pair)
        block = axb.at[x, pl.ds(g * D, D)]
        for src, k in ((block, 0), (stx.at[x, g], 1)):
            move = remote(src, src, ms.at[2 * g + k], mr.at[2 * g + k], xp)
            move.start()
            a_moves.append(move)
    whole(3)
    for g in range(2):
        a_moves[2 * g].wait()
        a_moves[2 * g + 1].wait()
        for h in range(HEADS):
            m0, m1 = stx[0, g, h:h + 1, :], stx[1, g, h:h + 1, :]
            top = jnp.maximum(m0, m1)
            w0 = stx[0, g, HEADS + h:HEADS + h + 1, :] * jnp.exp(m0 - top)
            w1 = stx[1, g, HEADS + h:HEADS + h + 1, :] * jnp.exp(m1 - top)
            inv = 1.0 / (w0 + w1)
            rows = slice(g * D + h * HEAD_DIM, g * D + (h + 1) * HEAD_DIM)
            mixed = axb[0, rows, :].astype(F32) * (w0 * inv) + axb[1, rows, :].astype(F32) * (w1 * inv)
            att[rows, :] = mixed.astype(BF)
            st[g, h:h + 1, :] = top
            st[g, HEADS + h:HEADS + h + 1, :] = inv
        lrows = slice(g * LAT, (g + 1) * LAT)
        hone[lrows, :] = lat[lrows, :].astype(F32) + tn(att[g * D:(g + 1) * D, :], wf[3])
    store(att, att_o)
    store(st, st_o)
    store(hone, hone_o)
    mlpin[...] = norm(hone[...], vec_row(vecs, 4), vec_row(vecs, 5)).astype(BF)
    store(mlpin, mlpin_o)
    in_up.wait()
    for j in range(4):
        cols = slice(j * HALF, (j + 1) * HALF)
        u = nn(mlpin[...], wup[:, cols])
        pre[:, cols] = u
        hid[:, cols] = jax.nn.gelu(u).astype(BF)
    store(pre, pre_o)
    store(hid, hid_o)
    in_down.wait()
    m_moves = []
    for j in range(2):
        xm[x, j] = nn(hid[...], wdown[:, j * HALF:(j + 1) * HALF]).astype(BF)
        move = remote(xm.at[x, j], xm.at[x, j], ms.at[4 + j], mr.at[4 + j], xp)
        move.start()
        m_moves.append(move)
    for copy in in_self:
        copy.wait()
    for j in range(2):
        m_moves[j].wait()
        cols = slice(j * HALF, (j + 1) * HALF)
        htwo[:, cols] = hone[:, cols] + (xm[0, j].astype(F32) + xm[1, j].astype(F32))
    store(htwo, htwo_o)
    selfin[...] = norm(htwo[...], vec_row(vecs, 6), vec_row(vecs, 7)).astype(BF)
    store(selfin, selfin_o)
    for i in range(3):
        qkv[i] = nn(selfin[...], wself[i]).astype(BF)

    def self_group(g):
        rows = pl.ds(pl.multiple_of(g * LAT, LAT), LAT)
        for h in range(4):
            cols = slice(h * HEAD_DIM, (h + 1) * HEAD_DIM)
            q, k, v = qkv[0, rows, cols], qkv[1, rows, cols], qkv[2, rows, cols]
            do = dself[rows, cols]
            s = nt(q, k) * SCALE
            e = jnp.exp(s - jnp.max(s, axis=1, keepdims=True))
            p = e / jnp.sum(e, axis=1, keepdims=True)
            p_low = p.astype(BF)
            o = nn(p_low, v)
            slow[rows, cols] = o.astype(BF)
            delta = jnp.sum(do.astype(F32) * o, axis=1, keepdims=True)
            dp = nt(do, v)
            dsc = (p * (dp - delta)).astype(BF)
            ds[0, rows, cols] = (nn(dsc, k) * SCALE).astype(BF)
            ds[1, rows, cols] = (tn(dsc, q) * SCALE).astype(BF)
            ds[2, rows, cols] = tn(p_low, do).astype(BF)

    loop(2, self_group)
    store(ds, ds_o)
    store(slow, slow_o)
    for move in pending:
        move.wait_send()
    for copy in outs:
        copy.wait()


def run_first(args):
    any_spec = pl.BlockSpec(memory_space=pl.ANY)
    vmem_spec = pl.BlockSpec(memory_space=pltpu.VMEM)
    outs = [
        ((4, D, D), BF), ((NROWS, D), BF), ((NROWS, D), BF), ((NROWS, D), BF),
        ((ROWS, D), BF), ((ROWS, D), BF), ((2 * D, LAT), BF), ((2, 16, LAT), F32),
        ((2, 8, HALF), F32), ((ROWS, D), F32), ((ROWS, D), F32), ((ROWS, D), BF),
        ((ROWS, D), BF), ((ROWS, HID), F32), ((ROWS, HID), BF), ((3, ROWS, HALF), BF),
        ((ROWS, HALF), BF), ((NROWS, LAT), BF),
    ]
    scratch = [
        ((4, D, D), BF), ((NROWS, D), BF), ((NROWS, D), BF), ((NROWS, D), BF), ((NROWS, D), BF),
        ((ROWS, D), BF), ((ROWS, D), BF), ((ROWS, D), BF), ((NROWS, LAT), BF), ((8, 896), F32),
        ((2, 2 * D, LAT), BF), ((2, 2, 16, LAT), F32), ((2 * D, LAT), BF), ((2, 16, LAT), F32),
        ((2, 8, HALF), F32), ((ROWS, D), F32), ((ROWS, D), F32), ((ROWS, D), BF),
        ((ROWS, HID), F32), ((ROWS, HID), BF), ((2, 2, ROWS, HALF), BF), ((ROWS, D), BF),
        ((D, HID), BF), ((HID, D), BF), ((3, D, HALF), BF), ((HALF, D), BF), ((ROWS, D), BF),
        ((3, ROWS, HALF), BF), ((ROWS, HALF), BF), ((3, ROWS, HALF), BF), ((ROWS, HALF), BF),
    ]
    dma = pltpu.SemaphoreType.DMA
    return pl.pallas_call(
        first_kernel,
        out_shape=[jax.ShapeDtypeStruct(*o) for o in outs],
        in_specs=[any_spec] * 2 + [vmem_spec] * 10 + [any_spec] * 11,
        out_specs=[any_spec] * len(outs),
        scratch_shapes=[pltpu.VMEM(*s) for s in scratch]
        + [dma((16,)), dma((24,))] + [dma((5,))] * 2 + [dma((4,))] * 6 + [dma((6,))] * 2,
        compiler_params=pltpu.CompilerParams(
            collective_id=0, has_side_effects=True, vmem_limit_bytes=58 * MIB
        ),
        name="forward",
    )(*args)


def norm_back(v, dy, gain):
    cen = v - jnp.mean(v, axis=-1, keepdims=True)
    inv = lax.rsqrt(jnp.mean(cen * cen, axis=-1, keepdims=True) + EPSILON)
    n = cen * inv
    t = dy * gain
    dv = inv * (t - jnp.mean(t, axis=-1, keepdims=True) - n * jnp.mean(t * n, axis=-1, keepdims=True))
    return (
        dv,
        jnp.sum(dy * n, axis=0, keepdims=True),
        jnp.sum(dy, axis=0, keepdims=True),
    )


def gelu_slope(u):
    root = (2.0 / jnp.pi) ** 0.5
    t = jnp.tanh(root * (u + 0.044715 * u * u * u))
    return 0.5 * (1.0 + t) + 0.5 * u * (1.0 - t * t) * root * (1.0 + 3.0 * 0.044715 * u * u)


PART = 256
KINDS = "yzyzyzyzyzyzyzyzyzyzyzyzyzyz" + "yyyy"
SLOTS = (4, 4, 4, 4, 4, 3)
EVENTS = (
    (),
    ((0, 0), (1, 0),),
    (),
    (),
    ((0, 1), (2, 0),),
    ((1, 1), (3, 0), (2, 1), (4, 0), (3, 1), (0, 2), (5, 0), (4, 1), (6, 0), (5, 1), (2, 2), (7, 0),),
    ((1, 2), (6, 1), (4, 2), (7, 1),),
    (),
    (),
    (),
    ((1, 3), (3, 2), (6, 2),),
    ((0, 3), (1, 4), (3, 3),),
    ((8, 0), (9, 0),),
    (),
    ((5, 2),),
    ((0, 4), (3, 4), (8, 1), (2, 3), (9, 1), (10, 0), (11, 0),),
    ((1, 5),),
    ((4, 3),),
    ((0, 5), (10, 1), (5, 3), (8, 2), (11, 1), (12, 0), (13, 0),),
    (),
    ((3, 5), (0, 6), (7, 2), (12, 1), (1, 6), (13, 1), (2, 4), (14, 0), (15, 0),),
    ((0, 7), (6, 3),),
    ((1, 7), (4, 4),),
    (),
    ((3, 6), (5, 4), (7, 3), (9, 2), (15, 1),),
    ((3, 7), (2, 5), (6, 4), (8, 3), (10, 2), (14, 1), (4, 5), (5, 5), (7, 4), (12, 2), (16, 0), (17, 0),),
    ((2, 6), (9, 3), (6, 5), (11, 2), (16, 1), (17, 1), (18, 0), (19, 0), (8, 4),),
    ((2, 7), (14, 2), (7, 5), (18, 1), (19, 1), (4, 6), (5, 6), (13, 2), (20, 0), (21, 0),),
    ((4, 7), (8, 5), (9, 4), (5, 7), (11, 3),),
    ((6, 6), (13, 3), (15, 2), (21, 1),),
    ((6, 7), (7, 6), (9, 5), (10, 3), (16, 2), (20, 1), (22, 0), (23, 0), (12, 3),),
    ((7, 7), (8, 6),),
    ((8, 7), (9, 6), (10, 4), (11, 4), (12, 4), (15, 3), (17, 2), (13, 4), (14, 3), (23, 1),),
    ((9, 7), (10, 5), (11, 5), (18, 2), (22, 1), (15, 4), (19, 2), (12, 5), (17, 3), (20, 2), (24, 0), (25, 0),),
    ((10, 6), (13, 5), (24, 1), (21, 2), (25, 1), (11, 6), (14, 4),),
    (),
    ((10, 7), (11, 7), (12, 6), (15, 5), (16, 3),),
    ((13, 6), (17, 4), (19, 3), (26, 0), (27, 0), (12, 7), (23, 2),),
    ((21, 3),),
    ((13, 7), (14, 5), (18, 3), (16, 4), (22, 2), (26, 1), (19, 4), (27, 1), (28, 0), (29, 0),),
    ((15, 6), (17, 5), (21, 4), (20, 3),),
    ((15, 7), (14, 6), (16, 5), (18, 4), (23, 3), (24, 2), (25, 2), (28, 1), (30, 0),),
    ((14, 7), (16, 6), (17, 6), (19, 5), (22, 3), (21, 5),),
    ((16, 7), (17, 7), (18, 5), (20, 4), (23, 4), (26, 2), (27, 2), (29, 1), (24, 3), (31, 0), (25, 3),),
    ((18, 6), (19, 6), (22, 4), (26, 3),),
    ((18, 7), (19, 7), (23, 5),),
    ((21, 6), (25, 4), (20, 5), (27, 3), (28, 2), (30, 1), (-1, 0), (24, 4), (21, 7), (22, 5), (29, 2), (31, 1),
     (26, 4), (20, 6), (-1, 1), (28, 3), (20, 7), (25, 5), (27, 4), (29, 3), (23, 6), (-1, 2), (28, 4), (23, 7),
     (24, 5), (30, 2), (27, 5), (22, 6), (26, 5), (-1, 3), (22, 7), (29, 4), (30, 3), (31, 2), (24, 6), (25, 6),
     (30, 4), (-1, 4), (31, 3), (24, 7), (26, 6), (25, 7), (28, 5), (26, 7), (-1, 5), (31, 4), (28, 6), (27, 6),
     (28, 7), (27, 7), (29, 5), (30, 5), (29, 6), (31, 5), (29, 7), (30, 6), (30, 7), (31, 6), (31, 7),),
)


def second_kernel(
    wf_h, ck_h, cv_h, inin_h, latin_h, cq_h, att_h, st_h, vec_h, hone_h, htwo_h,
    mlpin_h, selfin_h, pre_h, hid_h, ds_h, slow_h, mask_h,
    lat_h, inp_h, up_h, down_h, sq_h, sk_h, sv_h, so_h, cot_h,
    newlat_o, glat_o, ginp_o, gq_o, gk_o, gv_o, go_o, gup_o, gdown_o, gsq_o, gsk_o,
    gsv_o, gso_o, gvec_o,
    z, wf, cq, att, st, vecs, hone, htwo, etwo, mlpin, selfin, pre, hid, ds,
    slow, mask, cot, elow2, elow1, dpre, dcr, xb, grad, other, t0, ty, te, tm, tn_mid, tn_y,
    xk, gvec, gvr,
    lsem, osem, gs, gr, xs, xr, vs, vr, free,
):
    me = place()
    x, c = me["x"], me["c"]
    xp, yp, cp, ap, bp = me["xp"], me["yp"], me["cp"], me["ap"], me["bp"]
    counts = [0, 0]
    outs = []

    def load(src, dst):
        copy = pltpu.make_async_copy(src, dst, lsem.at[counts[0]])
        counts[0] += 1
        copy.start()
        return copy

    def store(src, dst):
        copy = pltpu.make_async_copy(src, dst, osem.at[counts[1]])
        counts[1] += 1
        copy.start()
        outs.append(copy)

    in_ds = load(ds_h, ds)
    in_self = [
        load(sq_h, z.at[pl.ds(4096, D), pl.ds(0, HALF)]),
        load(sk_h, z.at[pl.ds(4096, D), pl.ds(HALF, HALF)]),
        load(sv_h, z.at[pl.ds(5120, D), pl.ds(0, HALF)]),
    ]
    in_early = [load(slow_h, slow), load(cot_h, cot), load(selfin_h, selfin)] + [
        load(so_h.at[:, pl.ds(j * HALF, HALF)], z.at[pl.ds(5120 + j * HALF, HALF), pl.ds(HALF, HALF)])
        for j in range(2)
    ]
    in_two = [load(htwo_h, htwo), load(vec_h, vecs)]
    in_mlp = [
        load(pre_h, pre), load(down_h, z.at[pl.ds(0, HID)]),
        load(up_h.at[:, pl.ds(0, D)], z.at[pl.ds(HID, D)]),
        load(up_h.at[:, pl.ds(D, D)], z.at[pl.ds(HID + D, D)]),
    ]
    in_mid = [
        load(hid_h.at[:, pl.ds(j * D, D)], hid.at[pl.ds(j * ROWS, ROWS)]) for j in range(2)
    ] + [load(mlpin_h, mlpin), load(hone_h, hone)]
    in_cross = [
        load(wf_h, wf), load(att_h, att), load(st_h, st), load(cq_h, cq), load(mask_h, mask),
    ]
    barrier = pltpu.get_barrier_semaphore()
    for partner in (xp, yp, cp, ap, bp):
        pl.semaphore_signal(barrier, inc=1, device_id=partner, device_id_type=MESH)

    @pl.when(me["a"] != me["b"])
    def _():
        pl.semaphore_signal(barrier, inc=1, device_id=me["mp"], device_id_type=MESH)
        pl.semaphore_wait(barrier, 6)

    @pl.when(me["a"] == me["b"])
    def _():
        pl.semaphore_wait(barrier, 5)


    def wait_all(copies):
        for copy in copies:
            copy.wait()

    a_bit, b_bit, y_bit = me["a"], me["b"], me["y"]
    at_end = a_bit == b_bit
    at_middle = a_bit != b_bit
    mp = me["mp"]

    def cols_of(core):
        return pl.ds(pl.multiple_of(core * HALF, HALF), HALF)

    def block(k, off, size, core):
        return grad.at[pl.ds(pl.multiple_of(k * PART + off, 16), size), cols_of(core)]

    def add(base, size, part):
        def body(i):
            rows = pl.ds(pl.multiple_of(base + i * 64, 64), 64)
            grad[rows, cols_of(c)] = (
                grad[rows, cols_of(c)].astype(F32)
                + part[pl.ds(pl.multiple_of(i * 64, 64), 64), :].astype(F32)
            ).astype(BF)

        loop(size // 64, body)

    def move(k, stage, src, dst, partner):
        return remote(src, dst, gs.at[k * 7 + stage], gr.at[k * 7 + stage], partner)

    def release(k, n, partner):
        pl.semaphore_signal(free.at[k * 4 + n], inc=1, device_id=partner, device_id_type=MESH)

    def claim(k, n):
        pl.semaphore_wait(free.at[k * 4 + n], 1)

    def event(k, s):
        base, size, half = k * PART, PART, PART // 2
        kind = KINDS[k]
        n = KINDS[:k].count(kind)
        everything = block(k, 0, size, c)
        core_in = t0.at[k % t0.shape[0]]
        core_move = move(k, 0, block(k, 0, size, 1 - c), core_in, cp)
        core_back = move(k, 6, everything, everything, cp)
        if s == 0:
            core_move.start()
            return
        if s == 7:
            core_back.wait()
            deliver(k)
            return
        if s == 1:
            core_move.wait()
            if kind == "y":
                release(k, 0, cp)
            else:
                pl.when(at_end)(lambda: release(k, 0, cp))
                pl.when(at_middle)(lambda: release(k, 3, ap))
            add(base, size, core_in)
            if k >= 28:
                finish_x((k - 28) // 2, k % 2)
        if kind == "y":
            off = y_bit * half
            own = block(k, off, half, c)
            y_in, end_in, mid_in = (
                ty.at[n % ty.shape[0]], te.at[n % te.shape[0]], tm.at[n % tm.shape[0]]
            )
            y_move = move(k, 1, block(k, (1 - y_bit) * half, half, c), y_in, yp)
            end_move = move(k, 2, own, end_in, ap)
            mid_move = move(k, 3, own, mid_in, mp)
            end_back = move(k, 4, own, own, ap)
            y_back = move(k, 5, own, own, yp)
            if s == 1:
                y_move.start()
            elif s == 2:
                y_move.wait()
                release(k, 1, yp)
                add(base + off, half, y_in)
                pl.when(at_end)(end_move.start)
            elif s == 3:
                @pl.when(at_end)
                def _():
                    end_move.wait_send()
                    release(k, 2, ap)

                @pl.when(at_middle)
                def _():
                    end_move.wait_recv()
                    add(base + off, half, end_in)
                    mid_move.start()
            elif s == 4:
                @pl.when(at_middle)
                def _():
                    mid_move.wait()
                    add(base + off, half, mid_in)
                    claim(k, 2)
                    end_back.start()
            elif s == 5:
                pl.when(at_end)(end_back.wait_recv)
                pl.when(at_middle)(end_back.wait_send)
                claim(k, 1)
                y_back.start()
            elif s == 6:
                y_back.wait()
                claim(k, 0)
                core_back.start()
            return
        off = b_bit * half
        own = block(k, off, half, c)
        mid_in, y_in = tn_mid.at[n % tn_mid.shape[0]], tn_y.at[n % tn_y.shape[0]]
        end_in = block(k, 0, size, 1 - c)
        end_move = move(k, 1, everything, end_in, ap)
        mid_move = move(k, 2, block(k, (1 - b_bit) * half, half, c), mid_in, mp)
        y_move = move(k, 3, own, y_in, yp)
        mid_back = move(k, 4, own, own, mp)
        end_back = move(k, 5, everything, everything, ap)
        if s == 1:
            @pl.when(at_end)
            def _():
                claim(k, 3)
                end_move.start()
        elif s == 2:
            @pl.when(at_end)
            def _():
                end_move.wait_send()
                release(k, 1, ap)

            @pl.when(at_middle)
            def _():
                end_move.wait_recv()
                add(base, size, end_in)
                release(k, 0, cp)
                mid_move.start()
        elif s == 3:
            @pl.when(at_middle)
            def _():
                mid_move.wait()
                release(k, 2, mp)
                add(base + off, half, mid_in)
                y_move.start()
        elif s == 4:
            @pl.when(at_middle)
            def _():
                y_move.wait()
                add(base + off, half, y_in)
                claim(k, 2)
                mid_back.start()
        elif s == 5:
            @pl.when(at_middle)
            def _():
                mid_back.wait()
                claim(k, 1)
                end_back.start()
        elif s == 6:
            pl.when(at_end)(end_back.wait_recv)
            pl.when(at_middle)(end_back.wait_send)
            claim(k, 0)
            core_back.start()

    def deliver(k):
        n, top = k // 2, (k % 2) * PART
        rows = pl.ds(k * PART, PART)
        left, right = grad.at[rows, pl.ds(0, HALF)], grad.at[rows, pl.ds(HALF, HALF)]
        first, second = pl.ds(top, PART), pl.ds(HALF + top, PART)
        if 1 <= n <= 3:
            target = (gsq_o, gsk_o, gsv_o)[n - 1]
            store(left, target.at[first])
            store(right, target.at[second])
        elif 8 <= n <= 11:
            cols = pl.ds((n - 8) * HALF, HALF)
            store(left, gup_o.at[first, cols])
            store(right, gup_o.at[second, cols])
        elif 4 <= n <= 7:
            store(grad.at[rows], gdown_o.at[pl.ds((n - 4) * HALF + top, PART)])
        else:
            target = {0: gso_o, 12: go_o, 13: gq_o, 14: gk_o, 15: gv_o}[n]
            store(grad.at[rows], target.at[first])

    k_moves = {}

    def start_core(w):
        src = other.at[w, :, pl.ds(pl.multiple_of((1 - c) * HALF, HALF), HALF)]
        move = remote(src, hid.at[:, pl.ds(w * HALF, HALF)], xs.at[8 + w], xr.at[8 + w], cp)
        move.start()
        k_moves[w, 0] = move

    def start_x(w):
        k_moves[w, 0].wait()
        cols = pl.ds(pl.multiple_of(c * HALF, HALF), HALF)

        def body(i):
            rows = pl.ds(pl.multiple_of(i * 64, 64), 64)
            other[w, rows, cols] = (
                other[w, rows, cols].astype(F32) + hid[rows, w * HALF:(w + 1) * HALF].astype(F32)
            ).astype(BF)

        loop(HALF // 64, body)
        move = remote(other.at[w, :, cols], xk.at[w], xs.at[10 + w], xr.at[10 + w], xp)
        move.start()
        k_moves[w, 1] = move

    def finish_x(w, part):
        if part == 0:
            k_moves[w, 1].wait()
        add((14 + w) * HALF + part * 256, 256, xk.at[w, pl.ds(part * 256, 256)])

    def exchange(n, part, index):
        move = remote(
            xb.at[(n, x) + part], xb.at[(n, x) + part], xs.at[index], xr.at[index], xp
        )
        move.start()
        return move

    def both(n, rows):
        return xb[n, 0, rows, :].astype(F32) + xb[n, 1, rows, :].astype(F32)

    def fill(k, half, value):
        grad[k * HALF:(k + 1) * HALF, half * HALF:(half + 1) * HALF] = value.astype(BF)

    gvec[...] = jnp.zeros_like(gvec)
    lat, latin, dcq = cot, mlpin, elow2
    ck, cv = z.at[pl.ds(0, NROWS)], z.at[pl.ds(NROWS, NROWS)]
    inin, inp = z.at[pl.ds(2 * NROWS, NROWS)], z.at[pl.ds(3 * NROWS, NROWS)]
    gain_lat, gain_inp, gain_mlp, gain_self = 0, 2, 4, 6
    m_self, m_new, m_mlp, m_query, later = [], [], [], [], {}

    def self_back():
        in_ds.wait()
        wait_all(in_self)
        for j in range(2):
            cols = slice(j * HALF, (j + 1) * HALF)
            a_rows = slice(4096 + j * HALF, 4096 + (j + 1) * HALF)
            b_rows = slice(5120 + j * HALF, 5120 + (j + 1) * HALF)
            xb[0, x, :, cols] = (
                nt(ds[0], z[a_rows, 0:HALF])
                + nt(ds[1], z[a_rows, HALF:D])
                + nt(ds[2], z[b_rows, 0:HALF])
            ).astype(BF)
            m_self.append(exchange(0, (slice(None), pl.ds(j * HALF, HALF)), j))
        wait_all(in_early)

    def fill_self(n):
        for j in range(2):
            cols = slice(j * HALF, (j + 1) * HALF)
            fill(n, j, tn(slow[...], cot[:, cols]) if n == 0 else tn(selfin[:, cols], ds[n - 1]))

    def new_part():
        for j in range(2):
            cols = slice(j * HALF, (j + 1) * HALF)
            rows = slice(5120 + j * HALF, 5120 + (j + 1) * HALF)
            xb[1, x, :, cols] = nn(slow[...], z[rows, HALF:D]).astype(BF)
            m_new.append(exchange(1, (slice(None), pl.ds(j * HALF, HALF)), 2 + j))

    def two_back():
        wait_all(in_two)
        wait_all(m_self)
        gain = vec_row(vecs, gain_self)

        def body(i):
            rows = pl.ds(pl.multiple_of(i * 32, 32), 32)
            dv, dg, db = norm_back(htwo[rows, :], both(0, rows), gain)
            e = cot[rows, :].astype(F32) + dv
            etwo[rows, :] = e
            elow2[rows, :] = e.astype(BF)
            gvec[6:7, :] += dg
            gvec[7:8, :] += db

        loop(8, body)
        later["lat"] = load(lat_h, lat)

    def hidden_back(j):
        if j == 0:
            wait_all(in_mlp)
        cols = slice(j * HALF, (j + 1) * HALF)
        gh = nt(elow2[...], z[cols, :])
        dpre[:, cols] = (gh * gelu_slope(pre[:, cols])).astype(BF)

    def mlp_back():
        for j in range(2):
            cols = slice(j * HALF, (j + 1) * HALF)
            xb[2, x, :, cols] = (
                nt(dpre[:, 0:D], z[HID + j * HALF:HID + (j + 1) * HALF, :])
                + nt(dpre[:, D:HID], z[HID + D + j * HALF:HID + D + (j + 1) * HALF, :])
            ).astype(BF)
            m_mlp.append(exchange(2, (slice(None), pl.ds(j * HALF, HALF)), 4 + j))
        later["keys"] = [load(ck_h, ck), load(cv_h, cv)]
        later["inputs"] = [load(inin_h, inin), load(inp_h, inp)]
        wait_all(in_mid)

    def fill_down(j):
        for i in range(2):
            part = hid[(j // 2) * ROWS:(j // 2 + 1) * ROWS, (j % 2) * HALF:(j % 2 + 1) * HALF]
            fill(4 + j, i, tn(part, elow2[:, i * HALF:(i + 1) * HALF]))

    def fill_up(j):
        for i in range(2):
            fill(8 + j, i, tn(mlpin[:, i * HALF:(i + 1) * HALF], dpre[:, j * HALF:(j + 1) * HALF]))

    def one_back():
        later["latin"] = load(latin_h, latin)
        wait_all(m_mlp)
        gain = vec_row(vecs, gain_mlp)

        def body(i):
            rows = pl.ds(pl.multiple_of(i * 32, 32), 32)
            dv, dg, db = norm_back(hone[rows, :], both(2, rows), gain)
            e = etwo[rows, :] + dv
            hone[rows, :] = e
            elow1[rows, :] = e.astype(BF)
            gvec[4:5, :] += dg
            gvec[5:6, :] += db

        loop(8, body)

    def cross_back():
        wait_all(in_cross)
        for g in range(2):
            dcr[g * D:(g + 1) * D, :] = nt(wf[3], elow1[g * LAT:(g + 1) * LAT, :]).astype(BF)

    def fill_output():
        for j in range(2):
            value = 0.0
            for g in range(2):
                rows = pl.ds(pl.multiple_of(g * D + x * HALF, HALF), HALF)
                value = value + nn(
                    att[rows, :], elow1[g * LAT:(g + 1) * LAT, j * HALF:(j + 1) * HALF]
                )
            fill(12, j, value)

    def new_latents():
        wait_all(m_new)

        def body(i):
            rows = pl.ds(pl.multiple_of(i * 64, 64), 64)
            selfin[rows, :] = (htwo[rows, :] + both(1, rows)).astype(BF)

        loop(4, body)
        store(selfin, newlat_o)
        wait_all(later["keys"])

    def head(g, h):
        cols = slice(h * HEAD_DIM, (h + 1) * HEAD_DIM)
        n_rows = slice(g * INP, (g + 1) * INP)
        l_rows = slice(g * LAT, (g + 1) * LAT)
        t_rows = slice(g * D + h * HEAD_DIM, g * D + (h + 1) * HEAD_DIM)
        k, v, q = ck[n_rows, cols], cv[n_rows, cols], cq[l_rows, cols]
        s = nt(k, q) * SCALE + mask[n_rows, :].astype(F32)
        p = jnp.exp(s - st[g, h:h + 1, :]) * st[g, HEADS + h:HEADS + h + 1, :]
        do = dcr[t_rows, :]
        delta = jnp.sum(do.astype(F32) * att[t_rows, :].astype(F32), axis=0, keepdims=True)
        dsc = (p * (nn(v, do) - delta)).astype(BF)
        cv[n_rows, cols] = nt(p.astype(BF), do).astype(BF)
        ck[n_rows, cols] = (nn(dsc, q) * SCALE).astype(BF)
        xb[0, x, l_rows, cols] = (tn(dsc, k) * SCALE).astype(BF)

    def heads_back(g, h):
        head(g, h)
        head(g, h + 1)
        if h == HEADS - 2:
            m_query.append(exchange(0, (pl.ds(g * LAT, LAT),), 6 + g))

    def weight_grad(w, i):
        if w == 0 and i == 0:
            wait_all(later["inputs"])
        source = (ck, cv)[w]
        rows = slice(i * 256, (i + 1) * 256)
        mine = pl.ds(pl.multiple_of(x * HALF + i * 256, 256), 256)
        theirs = pl.ds(pl.multiple_of((1 - x) * HALF + i * 256, 256), 256)
        other[w, rows, :] = tn(inin[:, theirs], source[...]).astype(BF)
        grad[(14 + w) * HALF + i * 256:(14 + w) * HALF + (i + 1) * 256, :] = tn(
            inin[:, mine], source[...]
        ).astype(BF)
        if i == 1:
            start_core(w)

    def fill_query():
        wait_all(m_query)
        later["latin"].wait()

        def body(i):
            rows = pl.ds(pl.multiple_of(i * 64, 64), 64)
            dcq[rows, :] = both(0, rows).astype(BF)

        loop(4, body)
        for j in range(2):
            mine = pl.ds(pl.multiple_of(x * HALF, HALF), HALF)
            fill(13, j, tn(latin[:, mine], dcq[:, j * HALF:(j + 1) * HALF]))

    def latents_back():
        gain = vec_row(vecs, gain_lat)
        later["lat"].wait()

        def body(i):
            rows = pl.ds(pl.multiple_of(i * 128, 128), 128)
            dv, dg, db = norm_back(lat[rows, :].astype(F32), nt(dcq[rows, :], wf[2]), gain)
            lat[rows, :] = (hone[rows, :] + dv).astype(BF)
            gvec[0:1, :] += dg
            gvec[1:2, :] += db

        loop(2, body)
        store(lat, glat_o)

    def inputs_back(i):
        rows = slice(i * 224, (i + 1) * 224)
        dy = nt(ck[rows, :], wf[0]) + nt(cv[rows, :], wf[1])
        dv, dg, db = norm_back(inp[rows, :].astype(F32), dy, vec_row(vecs, gain_inp))
        inp[rows, :] = dv.astype(BF)
        gvec[2:3, :] += dg
        gvec[3:4, :] += db
        if i == 6:
            store(inp, ginp_o)
            col = lax.broadcasted_iota(jnp.int32, (8, D), 1) // HALF
            row = lax.broadcasted_iota(jnp.int32, (8, D), 0)
            keep = (col == x) | (row == 2) | (row == 3)
            gvec[...] = jnp.where(keep, gvec[...], 0.0)

    v_partners = (xp, cp, yp, ap, bp)
    v_moves = []

    def vec_event(s):
        if s > 0:
            v_moves[s - 1].wait()
            gvec[...] += gvr[s - 1]
        if s < 5:
            move = remote(gvec, gvr.at[s], vs.at[s], vr.at[s], v_partners[s])
            move.start()
            v_moves.append(move)
        else:
            store(gvec, gvec_o)

    steps = [self_back]
    steps += [lambda n=n: fill_self(n) for n in range(4)]
    steps += [new_part, two_back]
    steps += [lambda j=j: hidden_back(j) for j in range(4)]
    steps += [mlp_back]
    steps += [lambda j=j: fill_down(j) for j in range(4)]
    steps += [lambda j=j: fill_up(j) for j in range(4)]
    steps += [one_back, cross_back, fill_output, new_latents]
    steps += [lambda g=g, h=h: heads_back(g, h) for g in range(2) for h in range(0, HEADS, 2)]
    steps += [lambda i=i: weight_grad(0, i) for i in range(2)]
    steps += [lambda: weight_grad(1, 0), lambda: start_x(0), lambda: weight_grad(1, 1)]
    steps += [fill_query, lambda: start_x(1), latents_back]
    steps += [lambda i=i: inputs_back(i) for i in range(7)]
    for step, events in zip(steps, EVENTS, strict=True):
        step()
        for k, s in events:
            if k < 0:
                vec_event(s)
            else:
                event(k, s)
    wait_all(outs)


def run_second(args):
    any_spec = pl.BlockSpec(memory_space=pl.ANY)
    outs = [
        ((ROWS, D), BF), ((ROWS, D), BF), ((NROWS, D), BF), ((HALF, D), BF), ((HALF, D), BF),
        ((HALF, D), BF), ((HALF, D), BF), ((D, HID), BF), ((HID, D), BF), ((D, HALF), BF),
        ((D, HALF), BF), ((D, HALF), BF), ((HALF, D), BF), ((8, D), F32),
    ]
    scratch = [
        ((4 * NROWS, D), BF), ((4, D, D), BF), ((ROWS, D), BF),
        ((2 * D, LAT), BF), ((2, 16, LAT), F32), ((2, 8, HALF), F32), ((ROWS, D), F32),
        ((ROWS, D), F32), ((ROWS, D), F32), ((ROWS, D), BF), ((ROWS, D), BF), ((ROWS, HID), F32),
        ((2 * ROWS, D), BF), ((3, ROWS, HALF), BF), ((ROWS, HALF), BF), ((NROWS, LAT), BF),
        ((ROWS, D), BF), ((ROWS, D), BF), ((ROWS, D), BF), ((ROWS, HID), BF),
        ((2 * D, LAT), BF), ((3, 2, ROWS, D), BF), ((16 * HALF, D), BF), ((2, HALF, D), BF),
        ((SLOTS[0], PART, HALF), BF), *[((n, PART // 2, HALF), BF) for n in SLOTS[1:]],
        ((2, HALF, HALF), BF), ((8, D), F32),
        ((5, 8, D), F32),
    ]
    dma = pltpu.SemaphoreType.DMA
    return pl.pallas_call(
        second_kernel,
        out_shape=[jax.ShapeDtypeStruct(*o) for o in outs],
        in_specs=[any_spec] * len(args),
        out_specs=[any_spec] * len(outs),
        scratch_shapes=[pltpu.VMEM(*s) for s in scratch]
        + [dma((40,)), dma((64,))] + [dma((32 * 7,))] * 2 + [dma((12,))] * 2 + [dma((5,))] * 2
        + [pltpu.SemaphoreType.REGULAR((128,))],
        compiler_params=pltpu.CompilerParams(
            collective_id=1, has_side_effects=True, vmem_limit_bytes=63 * MIB
        ),
        name="backward",
    )(*args)


def finish_kernel(*refs):
    srcs, refs = refs[:13], refs[13:]
    dsts, (low, wide, insem, outsem) = refs[:13], refs[13:]
    tiles = []
    for i in (*range(3, 13), 0, 1, 2):
        rows, cols = srcs[i].shape
        for r in range(0, rows, HALF):
            for q in range(0, cols, HALF):
                count = min(HALF, rows - r)
                tiles.append((i, pl.ds(r, count), pl.ds(q, HALF), pl.ds(0, count)))
    depth = low.shape[0]
    ins, outs, finished = {}, {}, set()

    def finish_out(n):
        if n >= 0 and n not in finished:
            outs[n].wait()
            finished.add(n)

    def start_in(n):
        i, rows, cols, part = tiles[n]
        ins[n] = pltpu.make_async_copy(
            srcs[i].at[rows, cols], low.at[n % depth, part], insem.at[n % depth]
        )
        ins[n].start()

    for n in range(depth):
        start_in(n)
    for n in range(len(tiles)):
        slot = n % depth
        i, rows, cols, part = tiles[n]
        ins[n].wait()
        finish_out(n - depth)
        if i < 3:
            outs[n] = pltpu.make_async_copy(low.at[slot, part], dsts[i].at[rows, cols], outsem.at[slot])
            outs[n].start()
        else:
            def body(i, slot=slot):
                rows = pl.ds(pl.multiple_of(i * 64, 64), 64)
                wide[slot, rows, :] = low[slot, rows, :].astype(F32)

            loop(HALF // 64, body)
            outs[n] = pltpu.make_async_copy(wide.at[slot], dsts[i].at[rows, cols], outsem.at[slot])
            outs[n].start()
        if n + depth < len(tiles):
            if i < 3:
                finish_out(n)
            start_in(n + depth)
    for n in range(len(tiles) - depth, len(tiles)):
        finish_out(n)


def run_finish(args):
    any_spec = pl.BlockSpec(memory_space=pl.ANY)
    depth = 6
    return pl.pallas_call(
        finish_kernel,
        out_shape=[
            jax.ShapeDtypeStruct(a.shape, BF if i < 3 else F32) for i, a in enumerate(args)
        ],
        in_specs=[any_spec] * 13,
        out_specs=[any_spec] * 13,
        scratch_shapes=[
            pltpu.VMEM((depth, HALF, HALF), BF), pltpu.VMEM((depth, HALF, HALF), F32),
            pltpu.SemaphoreType.DMA((depth,)), pltpu.SemaphoreType.DMA((depth,)),
        ],
        compiler_params=pltpu.CompilerParams(vmem_limit_bytes=62 * MIB),
        name="finish",
    )(*args)


def per_device_pair(
    latents, inputs, latent_segment, input_segment, cross_query, cross_key, cross_value,
    cross_output, mlp_up, mlp_down, self_query, self_key, self_value, self_output,
    latent_gain, latent_bias, input_gain, input_bias, mlp_gain, mlp_bias, self_gain,
    self_bias, cotangent,
):
    vec = (
        latent_gain, latent_bias, input_gain, input_bias, mlp_gain, mlp_bias, self_gain, self_bias
    )
    lat = latents.reshape(ROWS, D)
    inp = inputs.reshape(NROWS, D)
    cot = cotangent.reshape(ROWS, D)
    kept = run_first((
        lat, inp, latent_segment, input_segment, *vec, cross_key, cross_value, cross_query,
        cross_output, mlp_up, mlp_down, self_query, self_key, self_value, self_output, cot,
    ))
    (new, glat, ginp, gq, gk, gv, go, gup, gdown, gsq, gsk, gsv, gso, gvec) = run_second(
        tuple(kept) + (
            lat, inp, mlp_up, mlp_down, self_query, self_key, self_value, self_output, cot
        )
    )
    new, glat, ginp, *grads = run_finish(
        (new, glat, ginp, gq, gk, gv, go, gup, gdown, gsq, gsk, gsv, gso)
    )
    x = lax.axis_index("shard")
    small = lax.dynamic_slice_in_dim(gvec, x * HALF, HALF, 1)
    return (
        new.reshape(latents.shape), glat.reshape(latents.shape), ginp.reshape(inputs.shape),
        *grads, *[small[i] for i in range(8)],
    )


def norm_forward(values, gain, shift):
    centred = values - jnp.mean(values, axis=-1, keepdims=True)
    inv_std = lax.rsqrt(jnp.mean(centred * centred, axis=-1, keepdims=True) + EPSILON)
    normed = centred * inv_std
    return (normed * gain + shift, normed, inv_std)


def norm_backward(grad_out, normed, inv_std, gain):
    scaled = grad_out * gain
    first_mean = jnp.mean(scaled, axis=-1, keepdims=True)
    second_mean = jnp.mean(scaled * normed, axis=-1, keepdims=True)
    grad_in = inv_std * (scaled - first_mean - normed * second_mean)
    return (grad_in, jnp.sum(grad_out * normed, axis=0), jnp.sum(grad_out, axis=0))


def product(left, right):
    return jnp.dot(left, right, preferred_element_type=jnp.float32)


def inner_rows(left, right):
    return lax.dot_general(
        left, right, (((0,), (0,)), ((), ())), preferred_element_type=jnp.float32
    )


def outer_cols(left, right):
    return lax.dot_general(
        left, right, (((1,), (1,)), ((), ())), preferred_element_type=jnp.float32
    )


def forward_total(term):
    return lax.psum(term.astype(jnp.bfloat16), "shard").astype(jnp.float32)


def backward_total(term):
    return lax.psum(term.astype(jnp.bfloat16), "shard").astype(jnp.float32)


def per_device(
    latents,
    inputs,
    latent_segment,
    input_segment,
    cross_query,
    cross_key,
    cross_value,
    cross_output,
    mlp_up,
    mlp_down,
    self_query,
    self_key,
    self_value,
    self_output,
    latent_gain,
    latent_bias,
    input_gain,
    input_bias,
    mlp_gain,
    mlp_bias,
    self_gain,
    self_bias,
    cotangent,
):
    shards = lax.axis_size("shard")
    groups, lat_len, width = latents.shape
    inp_len = inputs.shape[1]
    width_part = width // shards
    column_start = lax.axis_index("shard") * width_part
    rows = groups * lat_len
    scale = HEAD_DIM ** (-0.5)
    gathered = (
        lax.all_gather(cross_query, "shard", axis=0, tiled=True),
        lax.all_gather(cross_key, "shard", axis=0, tiled=True),
        lax.all_gather(cross_value, "shard", axis=0, tiled=True),
        lax.all_gather(cross_output, "shard", axis=0, tiled=True),
        lax.all_gather(latent_gain, "shard", axis=0, tiled=True),
        lax.all_gather(latent_bias, "shard", axis=0, tiled=True),
        lax.all_gather(input_gain, "shard", axis=0, tiled=True),
        lax.all_gather(input_bias, "shard", axis=0, tiled=True),
        lax.all_gather(mlp_gain, "shard", axis=0, tiled=True),
        lax.all_gather(mlp_bias, "shard", axis=0, tiled=True),
        lax.all_gather(self_gain, "shard", axis=0, tiled=True),
        lax.all_gather(self_bias, "shard", axis=0, tiled=True),
    )
    full_query, full_key, full_value, full_output = (
        gathered[0],
        gathered[1],
        gathered[2],
        gathered[3],
    )
    gain_lat, bias_lat, gain_inp, bias_inp, gain_mlp, bias_mlp, gain_self, bias_self = [
        piece.astype(jnp.float32) for piece in gathered[4:]
    ]
    lat_rows = latents.astype(jnp.float32).reshape(rows, width)
    inp_rows = inputs.astype(jnp.float32).reshape(groups * inp_len, width)
    lat_value, lat_normed, lat_inv = norm_forward(lat_rows, gain_lat, bias_lat)
    lat_in = lat_value.astype(jnp.bfloat16)
    inp_value, inp_normed, inp_inv = norm_forward(inp_rows, gain_inp, bias_inp)
    inp_in = inp_value.astype(jnp.bfloat16)
    cross_q = (
        product(lat_in, full_query).astype(jnp.bfloat16).reshape(groups, lat_len, HEADS, HEAD_DIM)
    )
    cross_k = (
        product(inp_in, full_key).astype(jnp.bfloat16).reshape(groups, inp_len, HEADS, HEAD_DIM)
    )
    cross_v = (
        product(inp_in, full_value).astype(jnp.bfloat16).reshape(groups, inp_len, HEADS, HEAD_DIM)
    )
    allowed = latent_segment[:, None, :, None] == input_segment[:, None, None, :]
    scores = (
        jnp.einsum("glhd,gnhd->ghln", cross_q, cross_k, preferred_element_type=jnp.float32) * scale
    )
    masked = jnp.where(allowed, scores, NEGATIVE)
    part_max = jnp.max(masked, axis=-1)
    top = lax.pmax(part_max, "shard")
    total = lax.psum(
        jnp.sum(jnp.where(allowed, jnp.exp(masked - top[..., None]), 0.0), axis=-1), "shard"
    )
    cross_prob = jnp.where(allowed, jnp.exp(masked - top[..., None]), 0.0) / total[..., None]
    cross_prob_low = cross_prob.astype(jnp.bfloat16)
    part_out = jnp.einsum(
        "ghln,gnhd->glhd", cross_prob_low, cross_v, preferred_element_type=jnp.float32
    )
    attended = lax.psum(part_out.astype(jnp.bfloat16), "shard").astype(jnp.float32)
    attended_in = attended.reshape(rows, width).astype(jnp.bfloat16)
    h_one = lat_rows + product(attended_in, full_output)
    mlp_value, mlp_normed, mlp_inv = norm_forward(h_one, gain_mlp, bias_mlp)
    mlp_in = mlp_value.astype(jnp.bfloat16)
    pre_act = product(mlp_in, mlp_up)
    hidden_in = jax.nn.gelu(pre_act).astype(jnp.bfloat16)
    h_two = h_one + forward_total(product(hidden_in, mlp_down))
    self_value_n, self_normed, self_inv = norm_forward(h_two, gain_self, bias_self)
    self_in = self_value_n.astype(jnp.bfloat16)
    local_heads = self_query.shape[1] // HEAD_DIM
    local_width = local_heads * HEAD_DIM
    self_q = (
        product(self_in, self_query)
        .astype(jnp.bfloat16)
        .reshape(groups, lat_len, local_heads, HEAD_DIM)
    )
    self_k = (
        product(self_in, self_key)
        .astype(jnp.bfloat16)
        .reshape(groups, lat_len, local_heads, HEAD_DIM)
    )
    self_v = (
        product(self_in, self_value)
        .astype(jnp.bfloat16)
        .reshape(groups, lat_len, local_heads, HEAD_DIM)
    )
    self_scores = (
        jnp.einsum("glhd,gmhd->ghlm", self_q, self_k, preferred_element_type=jnp.float32) * scale
    )
    self_prob = jax.nn.softmax(self_scores, axis=-1)
    self_prob_low = self_prob.astype(jnp.bfloat16)
    self_att = jnp.einsum(
        "ghlm,gmhd->glhd", self_prob_low, self_v, preferred_element_type=jnp.float32
    )
    self_att_in = self_att.reshape(rows, local_width).astype(jnp.bfloat16)
    result = h_two + forward_total(product(self_att_in, self_output))
    new_latents = result.reshape(groups, lat_len, width).astype(jnp.bfloat16)
    grad_out = cotangent.astype(jnp.float32).reshape(rows, width)
    grad_branch = grad_out.astype(jnp.bfloat16)
    grad_self_output = inner_rows(self_att_in, grad_branch)
    grad_att = (
        outer_cols(grad_branch, self_output)
        .astype(jnp.bfloat16)
        .reshape(groups, lat_len, local_heads, HEAD_DIM)
    )
    delta = jnp.sum(grad_att.astype(jnp.float32) * self_att, axis=-1).transpose(0, 2, 1)
    grad_prob = jnp.einsum("glhd,gmhd->ghlm", grad_att, self_v, preferred_element_type=jnp.float32)
    grad_sv = jnp.einsum(
        "ghlm,glhd->gmhd", self_prob_low, grad_att, preferred_element_type=jnp.float32
    )
    grad_scores = (self_prob * (grad_prob - delta[..., None])).astype(jnp.bfloat16)
    grad_sq = (
        jnp.einsum("ghlm,gmhd->glhd", grad_scores, self_k, preferred_element_type=jnp.float32)
        * scale
    )
    grad_sk = (
        jnp.einsum("ghlm,glhd->gmhd", grad_scores, self_q, preferred_element_type=jnp.float32)
        * scale
    )
    grad_sq = grad_sq.astype(jnp.bfloat16).reshape(rows, local_width)
    grad_sk = grad_sk.astype(jnp.bfloat16).reshape(rows, local_width)
    grad_sv = grad_sv.astype(jnp.bfloat16).reshape(rows, local_width)
    grad_self_query = inner_rows(self_in, grad_sq)
    grad_self_key = inner_rows(self_in, grad_sk)
    grad_self_value = inner_rows(self_in, grad_sv)
    grad_self_in = backward_total(
        outer_cols(grad_sq, self_query)
        + outer_cols(grad_sk, self_key)
        + outer_cols(grad_sv, self_value)
    )
    grad_norm, gain_full, bias_full = norm_backward(grad_self_in, self_normed, self_inv, gain_self)
    grad_two = grad_out + grad_norm
    grad_self_gain = lax.dynamic_slice_in_dim(gain_full, column_start, width_part)
    grad_self_bias = lax.dynamic_slice_in_dim(bias_full, column_start, width_part)
    grad_mlp_branch = grad_two.astype(jnp.bfloat16)
    grad_mlp_down = inner_rows(hidden_in, grad_mlp_branch)
    grad_hidden = outer_cols(grad_mlp_branch, mlp_down)
    gelu_value, gelu_pull = jax.vjp(jax.nn.gelu, pre_act)
    grad_pre = gelu_pull(grad_hidden)[0].astype(jnp.bfloat16)
    grad_mlp_up = inner_rows(mlp_in, grad_pre)
    grad_mlp_in = backward_total(outer_cols(grad_pre, mlp_up))
    grad_norm, gain_full, bias_full = norm_backward(grad_mlp_in, mlp_normed, mlp_inv, gain_mlp)
    grad_one = grad_two + grad_norm
    grad_mlp_gain = lax.dynamic_slice_in_dim(gain_full, column_start, width_part)
    grad_mlp_bias = lax.dynamic_slice_in_dim(bias_full, column_start, width_part)
    grad_cross_branch = grad_one.astype(jnp.bfloat16)
    grad_cross_output = inner_rows(
        lax.dynamic_slice_in_dim(attended_in, column_start, width_part, 1), grad_cross_branch
    )
    grad_ca = (
        outer_cols(grad_cross_branch, full_output)
        .astype(jnp.bfloat16)
        .reshape(groups, lat_len, HEADS, HEAD_DIM)
    )
    cross_delta = jnp.sum(grad_ca.astype(jnp.float32) * attended, axis=-1).transpose(0, 2, 1)
    grad_cp = jnp.einsum("glhd,gnhd->ghln", grad_ca, cross_v, preferred_element_type=jnp.float32)
    grad_cv = jnp.einsum(
        "ghln,glhd->gnhd", cross_prob_low, grad_ca, preferred_element_type=jnp.float32
    )
    grad_cs = (cross_prob * (grad_cp - cross_delta[..., None])).astype(jnp.bfloat16)
    grad_cq_part = (
        jnp.einsum("ghln,gnhd->glhd", grad_cs, cross_k, preferred_element_type=jnp.float32) * scale
    )
    grad_ck = (
        jnp.einsum("ghln,glhd->gnhd", grad_cs, cross_q, preferred_element_type=jnp.float32) * scale
    )
    grad_cq = backward_total(grad_cq_part.reshape(rows, width)).astype(jnp.bfloat16)
    grad_ck = grad_ck.astype(jnp.bfloat16).reshape(groups * inp_len, width)
    grad_cv = grad_cv.astype(jnp.bfloat16).reshape(groups * inp_len, width)
    grad_cross_query = inner_rows(
        lax.dynamic_slice_in_dim(lat_in, column_start, width_part, 1), grad_cq
    )
    grad_lat_in = outer_cols(grad_cq, full_query)
    grad_norm, gain_full, bias_full = norm_backward(grad_lat_in, lat_normed, lat_inv, gain_lat)
    grad_latents = (grad_one + grad_norm).reshape(groups, lat_len, width).astype(jnp.bfloat16)
    grad_latent_gain = lax.dynamic_slice_in_dim(gain_full, column_start, width_part)
    grad_latent_bias = lax.dynamic_slice_in_dim(bias_full, column_start, width_part)
    key_term = inner_rows(inp_in, grad_ck)
    value_term = inner_rows(inp_in, grad_cv)
    grad_inp_in = outer_cols(grad_ck, full_key) + outer_cols(grad_cv, full_value)
    grad_inp, inp_gain_full, inp_bias_full = norm_backward(
        grad_inp_in, inp_normed, inp_inv, gain_inp
    )
    grad_inputs = grad_inp.reshape(groups, inp_len, width).astype(jnp.bfloat16)
    grad_cross_key, grad_cross_value, grad_input_gain, grad_input_bias = (
        lax.psum_scatter(
            key_term.astype(jnp.bfloat16), "shard", scatter_dimension=0, tiled=True
        ).astype(jnp.float32),
        lax.psum_scatter(
            value_term.astype(jnp.bfloat16), "shard", scatter_dimension=0, tiled=True
        ).astype(jnp.float32),
        lax.psum_scatter(
            inp_gain_full.astype(jnp.bfloat16), "shard", scatter_dimension=0, tiled=True
        ).astype(jnp.float32),
        lax.psum_scatter(
            inp_bias_full.astype(jnp.bfloat16), "shard", scatter_dimension=0, tiled=True
        ).astype(jnp.float32),
    )
    (
        grad_cross_query,
        grad_cross_key,
        grad_cross_value,
        grad_cross_output,
        grad_mlp_up,
        grad_mlp_down,
        grad_self_query,
        grad_self_key,
        grad_self_value,
        grad_self_output,
        grad_latent_gain,
        grad_latent_bias,
        grad_input_gain,
        grad_input_bias,
        grad_mlp_gain,
        grad_mlp_bias,
        grad_self_gain,
        grad_self_bias,
    ) = (
        lax.psum(grad_cross_query.astype(jnp.bfloat16), "grp").astype(jnp.float32),
        lax.psum(grad_cross_key.astype(jnp.bfloat16), "grp").astype(jnp.float32),
        lax.psum(grad_cross_value.astype(jnp.bfloat16), "grp").astype(jnp.float32),
        lax.psum(grad_cross_output.astype(jnp.bfloat16), "grp").astype(jnp.float32),
        lax.psum(grad_mlp_up.astype(jnp.bfloat16), "grp").astype(jnp.float32),
        lax.psum(grad_mlp_down.astype(jnp.bfloat16), "grp").astype(jnp.float32),
        lax.psum(grad_self_query.astype(jnp.bfloat16), "grp").astype(jnp.float32),
        lax.psum(grad_self_key.astype(jnp.bfloat16), "grp").astype(jnp.float32),
        lax.psum(grad_self_value.astype(jnp.bfloat16), "grp").astype(jnp.float32),
        lax.psum(grad_self_output.astype(jnp.bfloat16), "grp").astype(jnp.float32),
        lax.psum(grad_latent_gain.astype(jnp.bfloat16), "grp").astype(jnp.float32),
        lax.psum(grad_latent_bias.astype(jnp.bfloat16), "grp").astype(jnp.float32),
        lax.psum(grad_input_gain.astype(jnp.bfloat16), "grp").astype(jnp.float32),
        lax.psum(grad_input_bias.astype(jnp.bfloat16), "grp").astype(jnp.float32),
        lax.psum(grad_mlp_gain.astype(jnp.bfloat16), "grp").astype(jnp.float32),
        lax.psum(grad_mlp_bias.astype(jnp.bfloat16), "grp").astype(jnp.float32),
        lax.psum(grad_self_gain.astype(jnp.bfloat16), "grp").astype(jnp.float32),
        lax.psum(grad_self_bias.astype(jnp.bfloat16), "grp").astype(jnp.float32),
    )
    return (
        new_latents,
        grad_latents,
        grad_inputs,
        grad_cross_query,
        grad_cross_key,
        grad_cross_value,
        grad_cross_output,
        grad_mlp_up,
        grad_mlp_down,
        grad_self_query,
        grad_self_key,
        grad_self_value,
        grad_self_output,
        grad_latent_gain,
        grad_latent_bias,
        grad_input_gain,
        grad_input_bias,
        grad_mlp_gain,
        grad_mlp_bias,
        grad_self_gain,
        grad_self_bias,
    )


def solution(mesh):
    laid_out = mesh.shape["shard"] == 2 and mesh.shape["grp"] == 16
    return jax.shard_map(
        per_device_pair if laid_out else per_device,
        mesh=mesh,
        in_specs=(
            P("grp", None, None),
            P("grp", "shard", None),
            P("grp", None),
            P("grp", "shard"),
            P("shard", None),
            P("shard", None),
            P("shard", None),
            P("shard", None),
            P(None, "shard"),
            P("shard", None),
            P(None, "shard"),
            P(None, "shard"),
            P(None, "shard"),
            P("shard", None),
            P("shard"),
            P("shard"),
            P("shard"),
            P("shard"),
            P("shard"),
            P("shard"),
            P("shard"),
            P("shard"),
            P("grp", None, None),
        ),
        out_specs=(
            P("grp", None, None),
            P("grp", None, None),
            P("grp", "shard", None),
            P("shard", None),
            P("shard", None),
            P("shard", None),
            P("shard", None),
            P(None, "shard"),
            P("shard", None),
            P(None, "shard"),
            P(None, "shard"),
            P(None, "shard"),
            P("shard", None),
            P("shard"),
            P("shard"),
            P("shard"),
            P("shard"),
            P("shard"),
            P("shard"),
            P("shard"),
            P("shard"),
        ),
        check_vma=False,
    )
```

```python
import jax
import jax.numpy as jnp
from jax import lax
from jax.experimental import pallas as pl
from jax.experimental.pallas import tpu as pltpu
from jax.sharding import PartitionSpec as P

HEADS = 8
HEAD_DIM = 128


EPSILON = 1e-05
NEGATIVE = -1e30

BF = jnp.bfloat16
F32 = jnp.float32
MESH = pl.DeviceIdType.MESH
LAT = 128
INP = 784
D = 1024
HALF = 512
HID = 2048
ROWS = 2 * LAT
NROWS = 2 * INP
SCALE = HEAD_DIM ** (-0.5)
MIB = 1 << 20


def nn(a, b):
    return lax.dot_general(a, b, (((1,), (0,)), ((), ())), preferred_element_type=F32)


def nt(a, b):
    return lax.dot_general(a, b, (((1,), (1,)), ((), ())), preferred_element_type=F32)


def tn(a, b):
    return lax.dot_general(a, b, (((0,), (0,)), ((), ())), preferred_element_type=F32)


def place():
    g = lax.axis_index("grp")
    x = lax.axis_index("shard")
    c = lax.rem(g, 2)
    y = lax.rem(g // 2, 2)
    a = lax.rem(g // 4, 2)
    b = g // 8
    return dict(
        x=x, c=c, y=y, a=a, b=b,
        xp=(g, 1 - x),
        cp=(g + 1 - 2 * c, x),
        yp=(g + 2 - 4 * y, x),
        ap=(g + 4 - 8 * a, x),
        bp=(g + 8 - 16 * b, x),
        mp=(g + 4 - 8 * b, x),
    )


def greet(partners):
    barrier = pltpu.get_barrier_semaphore()
    for partner in partners:
        pl.semaphore_signal(barrier, inc=1, device_id=partner, device_id_type=MESH)
    pl.semaphore_wait(barrier, len(partners))


def remote(src, dst, send, recv, partner):
    return pltpu.make_async_remote_copy(
        src_ref=src, dst_ref=dst, send_sem=send, recv_sem=recv,
        device_id=partner, device_id_type=MESH,
    )


def norm(v, gain, shift):
    cen = v - jnp.mean(v, axis=-1, keepdims=True)
    inv = lax.rsqrt(jnp.mean(cen * cen, axis=-1, keepdims=True) + EPSILON)
    return cen * inv * gain + shift


def vec_row(vecs, i):
    return jnp.concatenate([vecs[0, i:i + 1, :], vecs[1, i:i + 1, :]], axis=1)


def span(first, last, body):
    lax.fori_loop(first, last, lambda i, carry: (body(i), carry)[1], 0)


def loop(n, body):
    span(0, n, body)


def first_kernel(
    lat_h, inp_h, seglat, seginp, v0, v1, v2, v3, v4, v5, v6, v7, wk_h, wv_h, wq_h, wo_h, up_h, down_h,
    sq_h, sk_h, sv_h, so_h, cot_h,
    wf_o, ck_o, cv_o, inin_o, latin_o, cq_o, att_o, st_o, vec_o, hone_o, htwo_o,
    mlpin_o, selfin_o, pre_o, hid_o, ds_o, slow_o, mask_o,
    wf, inp, inin, ck, cv, lat, latin, cq, mask, segs, axb, stx, att, st, vecs,
    hone, htwo, mlpin, pre, hid, xm, selfin, wup, wdown, wself, wso, cot, qkv, dself,
    ds, slow, lsem, osem, xs, xr, ys, yr, c0s, c0r, c1s, c1r, ms, mr,
):
    me = place()
    x, y, c = me["x"], me["y"], me["c"]
    xp, yp, cp = me["xp"], me["yp"], me["cp"]
    nlocal = [0]
    nout = [0]

    def load(src, dst):
        copy = pltpu.make_async_copy(src, dst, lsem.at[nlocal[0]])
        nlocal[0] += 1
        copy.start()
        return copy

    outs = []

    def store(src, dst):
        copy = pltpu.make_async_copy(src, dst, osem.at[nout[0]])
        nout[0] += 1
        copy.start()
        outs.append(copy)

    own = pl.ds(pl.multiple_of(x * HALF, HALF), HALF)
    in_inp = load(inp_h, inp)
    in_lat = load(lat_h, lat)
    in_cot = load(cot_h, cot)
    in_so = load(so_h, wso)
    greet((xp, yp, cp))
    for i, v in enumerate((v0, v1, v2, v3, v4, v5, v6, v7)):
        vecs[x, i:i + 1, :] = v[...].astype(F32).reshape(1, HALF)
    vec_move = remote(vecs.at[x], vecs.at[x], xs.at[4], xr.at[4], xp)
    vec_move.start()
    weights = (wk_h, wv_h, wq_h, wo_h)
    quarter = 2 * y + c

    def part(w, side, q):
        return wf.at[w, pl.ds(pl.multiple_of(side * HALF + q * 128, 128), 128)]

    x_moves = []
    for w in range(4):
        src = weights[w].at[pl.ds(pl.multiple_of(quarter * 128, 128), 128)]
        move = remote(src, part(w, x, quarter), xs.at[w], xr.at[w], xp)
        move.start()
        x_moves.append(move)
    in_w = [load(weights[w], wf.at[w, own]) for w in range(4)]
    in_self = [load(h, wself.at[i]) for i, h in enumerate((sq_h, sk_h, sv_h))]
    in_up = load(up_h, wup)
    in_down = load(down_h, wdown)
    pending = []

    def forward_x(w):
        x_moves[w].wait()
        for sems, partner in (((ys, yr), yp), ((c0s, c0r), cp)):
            block = part(w, 1 - x, quarter)
            move = remote(block, block, sems[0].at[w], sems[1].at[w], partner)
            move.start()
            pending.append(move)

    def forward_y(w):
        block = part(w, 1 - x, quarter)
        remote(block, block, ys.at[w], yr.at[w], yp).wait_recv()
        block = part(w, 1 - x, 2 * (1 - y) + c)
        move = remote(block, block, c1s.at[w], c1r.at[w], cp)
        move.start()
        pending.append(move)

    def whole(w):
        block = part(w, 1 - x, quarter)
        remote(block, block, c0s.at[w], c0r.at[w], cp).wait_recv()
        remote(block, block, c1s.at[w], c1r.at[w], cp).wait_recv()
        in_w[w].wait()
        store(wf.at[w], wf_o.at[w])

    segs[...] = jnp.zeros_like(segs)
    segs[0:2, 0:INP] = seginp[...].astype(F32)
    for g in range(2):
        lat_row = seglat[g:g + 1, :].astype(F32)
        for j in range(7):
            count = min(128, INP - j * 128)
            col = jnp.broadcast_to(segs[g:g + 1, j * 128:(j + 1) * 128], (128, 128)).T
            mask[g * INP + j * 128:g * INP + j * 128 + count, :] = jnp.where(
                col[:count] == lat_row, 0.0, NEGATIVE
            ).astype(BF)
    store(mask, mask_o)
    in_cot.wait()
    in_so.wait()
    dself[...] = nt(cot[...], wso[...]).astype(BF)
    in_inp.wait()
    vec_move.wait()
    store(vecs, vec_o)
    gain_inp, bias_inp = vec_row(vecs, 2), vec_row(vecs, 3)

    def norm_rows(i):
        rows = pl.ds(pl.multiple_of(i * 32, 32), 32)
        inin[rows, :] = norm(inp[rows, :].astype(F32), gain_inp, bias_inp).astype(BF)

    span(0, 24, norm_rows)
    forward_x(0)
    span(24, 49, norm_rows)
    store(inin, inin_o)
    forward_x(1)
    forward_y(0)
    in_lat.wait()
    latin[...] = norm(lat[...].astype(F32), vec_row(vecs, 0), vec_row(vecs, 1)).astype(BF)
    store(latin, latin_o)

    def project(target, w, half):
        cols = slice(half * HALF, (half + 1) * HALF)

        def body(i):
            rows = pl.ds(pl.multiple_of(i * INP, 16), INP)
            target[rows, cols] = nn(inin[rows, :], wf[w, :, cols]).astype(BF)

        loop(2, body)

    whole(0)
    project(ck, 0, 0)
    forward_x(2)
    forward_y(1)
    project(ck, 0, 1)
    store(ck, ck_o)
    whole(1)
    forward_x(3)
    forward_y(2)
    project(cv, 1, 0)
    project(cv, 1, 1)
    store(cv, cv_o)
    whole(2)
    cq[...] = nn(latin[...], wf[2]).astype(BF)
    store(cq, cq_o)
    forward_y(3)

    def head(g, h):
        cols = pl.ds(pl.multiple_of(h * HEAD_DIM, HEAD_DIM), HEAD_DIM)
        n_rows = slice(g * INP, (g + 1) * INP)
        s = nt(ck[n_rows, cols], cq[g * LAT:(g + 1) * LAT, cols]) * SCALE + mask[n_rows, :].astype(F32)
        top = jnp.maximum(jnp.max(s, axis=0, keepdims=True), 0.1 * NEGATIVE)
        e = jnp.exp(s - top)
        total = jnp.sum(e, axis=0, keepdims=True)
        out = tn(cv[n_rows, cols], e.astype(BF))
        out = out * jnp.where(total > 0.0, 1.0 / total, 0.0)
        axb[x, pl.ds(pl.multiple_of(g * D + h * HEAD_DIM, HEAD_DIM), HEAD_DIM), :] = out.astype(BF)
        stx[x, g, pl.ds(h, 1), :] = top
        stx[x, g, pl.ds(HEADS + h, 1), :] = total

    a_moves = []
    for g in range(2):
        def pair(i, g=g):
            head(g, 2 * i)
            head(g, 2 * i + 1)

        loop(HEADS // 2, pair)
        block = axb.at[x, pl.ds(g * D, D)]
        for src, k in ((block, 0), (stx.at[x, g], 1)):
            move = remote(src, src, ms.at[2 * g + k], mr.at[2 * g + k], xp)
            move.start()
            a_moves.append(move)
    whole(3)
    for g in range(2):
        a_moves[2 * g].wait()
        a_moves[2 * g + 1].wait()
        for h in range(HEADS):
            m0, m1 = stx[0, g, h:h + 1, :], stx[1, g, h:h + 1, :]
            top = jnp.maximum(m0, m1)
            w0 = stx[0, g, HEADS + h:HEADS + h + 1, :] * jnp.exp(m0 - top)
            w1 = stx[1, g, HEADS + h:HEADS + h + 1, :] * jnp.exp(m1 - top)
            inv = 1.0 / (w0 + w1)
            rows = slice(g * D + h * HEAD_DIM, g * D + (h + 1) * HEAD_DIM)
            mixed = axb[0, rows, :].astype(F32) * (w0 * inv) + axb[1, rows, :].astype(F32) * (w1 * inv)
            att[rows, :] = mixed.astype(BF)
            st[g, h:h + 1, :] = top
            st[g, HEADS + h:HEADS + h + 1, :] = inv
        lrows = slice(g * LAT, (g + 1) * LAT)
        hone[lrows, :] = lat[lrows, :].astype(F32) + tn(att[g * D:(g + 1) * D, :], wf[3])
    store(att, att_o)
    store(st, st_o)
    store(hone, hone_o)
    mlpin[...] = norm(hone[...], vec_row(vecs, 4), vec_row(vecs, 5)).astype(BF)
    store(mlpin, mlpin_o)
    in_up.wait()
    for j in range(4):
        cols = slice(j * HALF, (j + 1) * HALF)
        u = nn(mlpin[...], wup[:, cols])
        pre[:, cols] = u
        hid[:, cols] = jax.nn.gelu(u).astype(BF)
    store(pre, pre_o)
    store(hid, hid_o)
    in_down.wait()
    m_moves = []
    for j in range(2):
        xm[x, j] = nn(hid[...], wdown[:, j * HALF:(j + 1) * HALF]).astype(BF)
        move = remote(xm.at[x, j], xm.at[x, j], ms.at[4 + j], mr.at[4 + j], xp)
        move.start()
        m_moves.append(move)
    for copy in in_self:
        copy.wait()
    for j in range(2):
        m_moves[j].wait()
        cols = slice(j * HALF, (j + 1) * HALF)
        htwo[:, cols] = hone[:, cols] + (xm[0, j].astype(F32) + xm[1, j].astype(F32))
    store(htwo, htwo_o)
    selfin[...] = norm(htwo[...], vec_row(vecs, 6), vec_row(vecs, 7)).astype(BF)
    store(selfin, selfin_o)
    for i in range(3):
        qkv[i] = nn(selfin[...], wself[i]).astype(BF)

    def self_group(g):
        rows = pl.ds(pl.multiple_of(g * LAT, LAT), LAT)
        for h in range(4):
            cols = slice(h * HEAD_DIM, (h + 1) * HEAD_DIM)
            q, k, v = qkv[0, rows, cols], qkv[1, rows, cols], qkv[2, rows, cols]
            do = dself[rows, cols]
            s = nt(q, k) * SCALE
            e = jnp.exp(s - jnp.max(s, axis=1, keepdims=True))
            p = e / jnp.sum(e, axis=1, keepdims=True)
            p_low = p.astype(BF)
            o = nn(p_low, v)
            slow[rows, cols] = o.astype(BF)
            delta = jnp.sum(do.astype(F32) * o, axis=1, keepdims=True)
            dp = nt(do, v)
            dsc = (p * (dp - delta)).astype(BF)
            ds[0, rows, cols] = (nn(dsc, k) * SCALE).astype(BF)
            ds[1, rows, cols] = (tn(dsc, q) * SCALE).astype(BF)
            ds[2, rows, cols] = tn(p_low, do).astype(BF)

    loop(2, self_group)
    store(ds, ds_o)
    store(slow, slow_o)
    for move in pending:
        move.wait_send()
    for copy in outs:
        copy.wait()


def run_first(args):
    any_spec = pl.BlockSpec(memory_space=pl.ANY)
    vmem_spec = pl.BlockSpec(memory_space=pltpu.VMEM)
    outs = [
        ((4, D, D), BF), ((NROWS, D), BF), ((NROWS, D), BF), ((NROWS, D), BF),
        ((ROWS, D), BF), ((ROWS, D), BF), ((2 * D, LAT), BF), ((2, 16, LAT), F32),
        ((2, 8, HALF), F32), ((ROWS, D), F32), ((ROWS, D), F32), ((ROWS, D), BF),
        ((ROWS, D), BF), ((ROWS, HID), F32), ((ROWS, HID), BF), ((3, ROWS, HALF), BF),
        ((ROWS, HALF), BF), ((NROWS, LAT), BF),
    ]
    scratch = [
        ((4, D, D), BF), ((NROWS, D), BF), ((NROWS, D), BF), ((NROWS, D), BF), ((NROWS, D), BF),
        ((ROWS, D), BF), ((ROWS, D), BF), ((ROWS, D), BF), ((NROWS, LAT), BF), ((8, 896), F32),
        ((2, 2 * D, LAT), BF), ((2, 2, 16, LAT), F32), ((2 * D, LAT), BF), ((2, 16, LAT), F32),
        ((2, 8, HALF), F32), ((ROWS, D), F32), ((ROWS, D), F32), ((ROWS, D), BF),
        ((ROWS, HID), F32), ((ROWS, HID), BF), ((2, 2, ROWS, HALF), BF), ((ROWS, D), BF),
        ((D, HID), BF), ((HID, D), BF), ((3, D, HALF), BF), ((HALF, D), BF), ((ROWS, D), BF),
        ((3, ROWS, HALF), BF), ((ROWS, HALF), BF), ((3, ROWS, HALF), BF), ((ROWS, HALF), BF),
    ]
    dma = pltpu.SemaphoreType.DMA
    return pl.pallas_call(
        first_kernel,
        out_shape=[jax.ShapeDtypeStruct(*o) for o in outs],
        in_specs=[any_spec] * 2 + [vmem_spec] * 10 + [any_spec] * 11,
        out_specs=[any_spec] * len(outs),
        scratch_shapes=[pltpu.VMEM(*s) for s in scratch]
        + [dma((16,)), dma((24,))] + [dma((5,))] * 2 + [dma((4,))] * 6 + [dma((6,))] * 2,
        compiler_params=pltpu.CompilerParams(
            collective_id=0, has_side_effects=True, vmem_limit_bytes=58 * MIB
        ),
        name="forward",
    )(*args)


def norm_back(v, dy, gain):
    cen = v - jnp.mean(v, axis=-1, keepdims=True)
    inv = lax.rsqrt(jnp.mean(cen * cen, axis=-1, keepdims=True) + EPSILON)
    n = cen * inv
    t = dy * gain
    dv = inv * (t - jnp.mean(t, axis=-1, keepdims=True) - n * jnp.mean(t * n, axis=-1, keepdims=True))
    return (
        dv,
        jnp.sum(dy * n, axis=0, keepdims=True),
        jnp.sum(dy, axis=0, keepdims=True),
    )


def gelu_slope(u):
    root = (2.0 / jnp.pi) ** 0.5
    t = jnp.tanh(root * (u + 0.044715 * u * u * u))
    return 0.5 * (1.0 + t) + 0.5 * u * (1.0 - t * t) * root * (1.0 + 3.0 * 0.044715 * u * u)


PART = 256
KINDS = "yzyzyzyzyzyzyzyzyzyzyzyzyzyz" + "yyyy"
SLOTS = (4, 4, 4, 4, 4, 4)
EVENTS = (
    ((0, 0), (1, 0),),
    (),
    ((0, 1), (1, 1), (2, 0), (3, 0),),
    (),
    (),
    ((2, 1), (4, 0), (3, 1), (5, 0), (0, 2), (4, 1), (6, 0), (5, 1), (1, 2), (7, 0), (2, 2), (6, 1), (7, 1),
     (4, 2),),
    ((1, 3), (3, 2),),
    ((6, 2),),
    ((0, 3),),
    (),
    (),
    ((0, 4), (1, 4), (3, 3), (5, 2),),
    ((2, 3), (8, 0), (9, 0),),
    (),
    (),
    ((0, 5), (1, 5), (3, 4), (8, 1), (9, 1), (10, 0), (11, 0),),
    ((7, 2),),
    ((5, 3),),
    ((10, 1), (0, 6), (4, 3), (11, 1), (2, 4), (12, 0), (13, 0),),
    (),
    ((0, 7), (1, 6), (3, 5), (6, 3), (8, 2), (12, 1), (13, 1), (5, 4), (2, 5), (14, 0), (7, 3), (15, 0),),
    ((1, 7),),
    ((9, 2), (4, 4), (10, 2), (14, 1), (16, 0),),
    ((15, 1), (17, 0),),
    ((3, 6), (6, 4), (2, 6), (11, 2), (17, 1), (5, 5),),
    ((3, 7), (4, 5), (7, 4), (2, 7), (8, 3), (9, 3), (12, 2), (16, 1), (6, 5), (18, 0), (19, 0),),
    ((11, 3), (14, 2), (18, 1), (4, 6), (13, 2), (20, 0), (7, 5), (19, 1), (21, 0),),
    ((4, 7), (5, 6), (8, 4), (9, 4), (10, 3),),
    ((5, 7), (13, 3), (21, 1),),
    ((6, 6), (7, 6), (9, 5), (15, 2),),
    ((6, 7), (8, 5), (10, 4), (11, 4), (16, 2), (7, 7), (17, 2), (20, 1), (22, 0), (23, 0),),
    ((13, 4), (12, 3), (15, 3), (9, 6),),
    ((9, 7), (8, 6), (10, 5), (11, 5), (14, 3), (17, 3), (18, 2), (22, 1), (23, 1), (24, 0), (25, 0),),
    ((8, 7), (10, 6), (13, 5), (12, 4), (15, 4), (19, 2), (25, 1),),
    ((10, 7), (11, 6), (14, 4), (15, 5), (17, 4), (16, 3), (21, 2),),
    (),
    ((11, 7), (13, 6), (12, 5), (17, 5), (18, 3), (19, 3), (20, 2), (24, 1),),
    ((14, 5), (16, 4), (13, 7), (22, 2), (23, 2), (26, 0), (27, 0),),
    (),
    ((12, 6), (21, 3),),
    ((12, 7), (15, 6), (18, 4), (19, 4), (25, 2), (26, 1), (27, 1), (20, 3), (23, 3), (28, 0), (29, 0),),
    ((15, 7), (14, 6), (17, 6), (19, 5), (22, 3),),
    ((14, 7), (16, 5), (21, 4), (17, 7), (25, 3), (18, 5), (24, 2), (26, 2), (27, 2), (28, 1), (29, 1), (20, 4),
     (30, 0), (31, 0),),
    ((16, 6), (22, 4), (19, 6), (23, 4), (24, 3),),
    ((16, 7), (19, 7), (20, 5), (21, 5), (25, 4), (26, 3), (27, 3),),
    ((18, 6), (22, 5), (23, 5),),
    ((18, 7), (24, 4), (28, 2), (29, 2), (30, 1), (21, 6), (-1, 0), (31, 1), (25, 5), (20, 6), (21, 7), (26, 4),
     (28, 3), (-1, 1), (20, 7), (27, 4), (23, 6), (29, 3), (22, 6), (23, 7), (-1, 2), (24, 5), (28, 4), (22, 7),
     (30, 2), (27, 5), (25, 6), (29, 4), (-1, 3), (30, 3), (24, 6), (25, 7), (26, 5), (31, 2), (24, 7), (-1, 4),
     (30, 4), (28, 5), (26, 6), (31, 3), (26, 7), (28, 6), (-1, 5), (27, 6), (31, 4), (28, 7), (27, 7), (29, 5),
     (30, 5), (29, 6), (31, 5), (29, 7), (30, 6), (30, 7), (31, 6), (31, 7),),
)


def second_kernel(
    wf_h, ck_h, cv_h, inin_h, latin_h, cq_h, att_h, st_h, vec_h, hone_h, htwo_h,
    mlpin_h, selfin_h, pre_h, hid_h, ds_h, slow_h, mask_h,
    lat_h, inp_h, up_h, down_h, sq_h, sk_h, sv_h, so_h, cot_h,
    newlat_o, glat_o, ginp_o, gq_o, gk_o, gv_o, go_o, gup_o, gdown_o, gsq_o, gsk_o,
    gsv_o, gso_o, gvec_o,
    z, wf, cq, att, st, vecs, hone, htwo, etwo, mlpin, selfin, pre, hid, ds,
    slow, mask, cot, elow2, elow1, dpre, dcr, xb, grad, other, t0, ty, te, tm, tn_mid, tn_y,
    xk, gvec, gvr,
    lsem, osem, gs, gr, xs, xr, vs, vr, free,
):
    me = place()
    x, c = me["x"], me["c"]
    xp, yp, cp, ap, bp = me["xp"], me["yp"], me["cp"], me["ap"], me["bp"]
    counts = [0, 0]
    outs = []

    def load(src, dst):
        copy = pltpu.make_async_copy(src, dst, lsem.at[counts[0]])
        counts[0] += 1
        copy.start()
        return copy

    def store(src, dst):
        copy = pltpu.make_async_copy(src, dst, osem.at[counts[1]])
        counts[1] += 1
        copy.start()
        outs.append(copy)

    in_early = [load(slow_h, slow), load(cot_h, cot), load(selfin_h, selfin)]
    in_ds = load(ds_h, ds)
    in_self = [
        load(sq_h, z.at[pl.ds(4096, D), pl.ds(0, HALF)]),
        load(sk_h, z.at[pl.ds(4096, D), pl.ds(HALF, HALF)]),
        load(sv_h, z.at[pl.ds(5120, D), pl.ds(0, HALF)]),
    ]
    in_early += [
        load(so_h.at[:, pl.ds(j * HALF, HALF)], z.at[pl.ds(5120 + j * HALF, HALF), pl.ds(HALF, HALF)])
        for j in range(2)
    ]
    in_two = [load(htwo_h, htwo), load(vec_h, vecs)]
    in_mlp = [
        load(pre_h, pre), load(down_h, z.at[pl.ds(0, HID)]),
        load(up_h.at[:, pl.ds(0, D)], z.at[pl.ds(HID, D)]),
        load(up_h.at[:, pl.ds(D, D)], z.at[pl.ds(HID + D, D)]),
    ]
    in_mid = [
        load(hid_h.at[:, pl.ds(j * D, D)], hid.at[pl.ds(j * ROWS, ROWS)]) for j in range(2)
    ] + [load(mlpin_h, mlpin), load(hone_h, hone)]
    in_cross = [
        load(wf_h, wf), load(att_h, att), load(st_h, st), load(cq_h, cq), load(mask_h, mask),
    ]
    barrier = pltpu.get_barrier_semaphore()
    for partner in (xp, yp, cp, ap, bp):
        pl.semaphore_signal(barrier, inc=1, device_id=partner, device_id_type=MESH)

    @pl.when(me["a"] != me["b"])
    def _():
        pl.semaphore_signal(barrier, inc=1, device_id=me["mp"], device_id_type=MESH)
        pl.semaphore_wait(barrier, 6)

    @pl.when(me["a"] == me["b"])
    def _():
        pl.semaphore_wait(barrier, 5)


    def wait_all(copies):
        for copy in copies:
            copy.wait()

    a_bit, b_bit, y_bit = me["a"], me["b"], me["y"]
    at_end = a_bit == b_bit
    at_middle = a_bit != b_bit
    mp = me["mp"]

    def cols_of(core):
        return pl.ds(pl.multiple_of(core * HALF, HALF), HALF)

    def block(k, off, size, core):
        return grad.at[pl.ds(pl.multiple_of(k * PART + off, 16), size), cols_of(core)]

    def add(base, size, part):
        def body(i):
            rows = pl.ds(pl.multiple_of(base + i * 64, 64), 64)
            grad[rows, cols_of(c)] += part[pl.ds(pl.multiple_of(i * 64, 64), 64), :]

        loop(size // 64, body)

    def move(k, stage, src, dst, partner):
        return remote(src, dst, gs.at[k * 7 + stage], gr.at[k * 7 + stage], partner)

    def release(k, n, partner):
        pl.semaphore_signal(free.at[k * 4 + n], inc=1, device_id=partner, device_id_type=MESH)

    def claim(k, n):
        pl.semaphore_wait(free.at[k * 4 + n], 1)

    def event(k, s):
        base, size, half = k * PART, PART, PART // 2
        kind = KINDS[k]
        n = KINDS[:k].count(kind)
        everything = block(k, 0, size, c)
        core_in = t0.at[k % t0.shape[0]]
        core_move = move(k, 0, block(k, 0, size, 1 - c), core_in, cp)
        core_back = move(k, 6, everything, everything, cp)
        if s == 0:
            core_move.start()
            return
        if s == 7:
            core_back.wait()
            deliver(k)
            return
        if s == 1:
            core_move.wait()
            if kind == "y":
                release(k, 0, cp)
            else:
                pl.when(at_end)(lambda: release(k, 0, cp))
                pl.when(at_middle)(lambda: release(k, 3, ap))
            add(base, size, core_in)
            if k >= 28:
                finish_x((k - 28) // 2, k % 2)
        if kind == "y":
            off = y_bit * half
            own = block(k, off, half, c)
            y_in, end_in, mid_in = (
                ty.at[n % ty.shape[0]], te.at[n % te.shape[0]], tm.at[n % tm.shape[0]]
            )
            y_move = move(k, 1, block(k, (1 - y_bit) * half, half, c), y_in, yp)
            end_move = move(k, 2, own, end_in, ap)
            mid_move = move(k, 3, own, mid_in, mp)
            end_back = move(k, 4, own, own, ap)
            y_back = move(k, 5, own, own, yp)
            if s == 1:
                y_move.start()
            elif s == 2:
                y_move.wait()
                release(k, 1, yp)
                add(base + off, half, y_in)
                pl.when(at_end)(end_move.start)
            elif s == 3:
                @pl.when(at_end)
                def _():
                    end_move.wait_send()
                    release(k, 2, ap)

                @pl.when(at_middle)
                def _():
                    end_move.wait_recv()
                    add(base + off, half, end_in)
                    mid_move.start()
            elif s == 4:
                @pl.when(at_middle)
                def _():
                    mid_move.wait()
                    add(base + off, half, mid_in)
                    claim(k, 2)
                    end_back.start()
            elif s == 5:
                pl.when(at_end)(end_back.wait_recv)
                pl.when(at_middle)(end_back.wait_send)
                claim(k, 1)
                y_back.start()
            elif s == 6:
                y_back.wait()
                claim(k, 0)
                core_back.start()
            return
        off = b_bit * half
        own = block(k, off, half, c)
        mid_in, y_in = tn_mid.at[n % tn_mid.shape[0]], tn_y.at[n % tn_y.shape[0]]
        end_in = block(k, 0, size, 1 - c)
        end_move = move(k, 1, everything, end_in, ap)
        mid_move = move(k, 2, block(k, (1 - b_bit) * half, half, c), mid_in, mp)
        y_move = move(k, 3, own, y_in, yp)
        mid_back = move(k, 4, own, own, mp)
        end_back = move(k, 5, everything, everything, ap)
        if s == 1:
            @pl.when(at_end)
            def _():
                claim(k, 3)
                end_move.start()
        elif s == 2:
            @pl.when(at_end)
            def _():
                end_move.wait_send()
                release(k, 1, ap)

            @pl.when(at_middle)
            def _():
                end_move.wait_recv()
                add(base, size, end_in)
                release(k, 0, cp)
                mid_move.start()
        elif s == 3:
            @pl.when(at_middle)
            def _():
                mid_move.wait()
                release(k, 2, mp)
                add(base + off, half, mid_in)
                y_move.start()
        elif s == 4:
            @pl.when(at_middle)
            def _():
                y_move.wait()
                add(base + off, half, y_in)
                claim(k, 2)
                mid_back.start()
        elif s == 5:
            @pl.when(at_middle)
            def _():
                mid_back.wait()
                claim(k, 1)
                end_back.start()
        elif s == 6:
            pl.when(at_end)(end_back.wait_recv)
            pl.when(at_middle)(end_back.wait_send)
            claim(k, 0)
            core_back.start()

    def deliver(k):
        n, top = k // 2, (k % 2) * PART
        rows = pl.ds(k * PART, PART)
        left, right = grad.at[rows, pl.ds(0, HALF)], grad.at[rows, pl.ds(HALF, HALF)]
        first, second = pl.ds(top, PART), pl.ds(HALF + top, PART)
        if 1 <= n <= 3:
            target = (gsq_o, gsk_o, gsv_o)[n - 1]
            store(left, target.at[first])
            store(right, target.at[second])
        elif 8 <= n <= 11:
            cols = pl.ds((n - 8) * HALF, HALF)
            store(left, gup_o.at[first, cols])
            store(right, gup_o.at[second, cols])
        elif 4 <= n <= 7:
            store(grad.at[rows], gdown_o.at[pl.ds((n - 4) * HALF + top, PART)])
        else:
            target = {0: gso_o, 12: go_o, 13: gq_o, 14: gk_o, 15: gv_o}[n]
            store(grad.at[rows], target.at[first])

    k_moves = {}

    def start_core(w):
        src = other.at[w, :, pl.ds(pl.multiple_of((1 - c) * HALF, HALF), HALF)]
        move = remote(src, hid.at[:, pl.ds(w * HALF, HALF)], xs.at[8 + w], xr.at[8 + w], cp)
        move.start()
        k_moves[w, 0] = move

    def start_x(w):
        k_moves[w, 0].wait()
        cols = pl.ds(pl.multiple_of(c * HALF, HALF), HALF)

        def body(i):
            rows = pl.ds(pl.multiple_of(i * 64, 64), 64)
            other[w, rows, cols] = (
                other[w, rows, cols].astype(F32) + hid[rows, w * HALF:(w + 1) * HALF].astype(F32)
            ).astype(BF)

        loop(HALF // 64, body)
        move = remote(other.at[w, :, cols], xk.at[w], xs.at[10 + w], xr.at[10 + w], xp)
        move.start()
        k_moves[w, 1] = move

    def finish_x(w, part):
        if part == 0:
            k_moves[w, 1].wait()
        add((14 + w) * HALF + part * 256, 256, xk.at[w, pl.ds(part * 256, 256)])

    def exchange(n, part, index):
        move = remote(
            xb.at[(n, x) + part], xb.at[(n, x) + part], xs.at[index], xr.at[index], xp
        )
        move.start()
        return move

    def both(n, rows):
        return xb[n, 0, rows, :].astype(F32) + xb[n, 1, rows, :].astype(F32)

    def fill(k, half, value):
        grad[k * HALF:(k + 1) * HALF, half * HALF:(half + 1) * HALF] = value.astype(BF)

    gvec[...] = jnp.zeros_like(gvec)
    lat, latin, dcq = cot, mlpin, elow2
    ck, cv = z.at[pl.ds(0, NROWS)], z.at[pl.ds(NROWS, NROWS)]
    inin, inp = z.at[pl.ds(2 * NROWS, NROWS)], z.at[pl.ds(3 * NROWS, NROWS)]
    gain_lat, gain_inp, gain_mlp, gain_self = 0, 2, 4, 6
    m_self, m_new, m_mlp, m_query, later = [], [], [], [], {}

    def self_back():
        wait_all(in_self)
        for j in range(2):
            cols = slice(j * HALF, (j + 1) * HALF)
            a_rows = slice(4096 + j * HALF, 4096 + (j + 1) * HALF)
            b_rows = slice(5120 + j * HALF, 5120 + (j + 1) * HALF)
            xb[0, x, :, cols] = (
                nt(ds[0], z[a_rows, 0:HALF])
                + nt(ds[1], z[a_rows, HALF:D])
                + nt(ds[2], z[b_rows, 0:HALF])
            ).astype(BF)
            m_self.append(exchange(0, (slice(None), pl.ds(j * HALF, HALF)), j))

    def fill_self(n):
        if n == 0:
            wait_all(in_early)
            in_ds.wait()
        for j in range(2):
            cols = slice(j * HALF, (j + 1) * HALF)
            fill(n, j, tn(slow[...], cot[:, cols]) if n == 0 else tn(selfin[:, cols], ds[n - 1]))

    def new_part():
        for j in range(2):
            cols = slice(j * HALF, (j + 1) * HALF)
            rows = slice(5120 + j * HALF, 5120 + (j + 1) * HALF)
            xb[1, x, :, cols] = nn(slow[...], z[rows, HALF:D]).astype(BF)
            m_new.append(exchange(1, (slice(None), pl.ds(j * HALF, HALF)), 2 + j))

    def two_back():
        wait_all(in_two)
        wait_all(m_self)
        gain = vec_row(vecs, gain_self)

        def body(i):
            rows = pl.ds(pl.multiple_of(i * 32, 32), 32)
            dv, dg, db = norm_back(htwo[rows, :], both(0, rows), gain)
            e = cot[rows, :].astype(F32) + dv
            etwo[rows, :] = e
            elow2[rows, :] = e.astype(BF)
            gvec[6:7, :] += dg
            gvec[7:8, :] += db

        loop(8, body)
        later["lat"] = load(lat_h, lat)

    def hidden_back(j):
        if j == 0:
            wait_all(in_mlp)
        cols = slice(j * HALF, (j + 1) * HALF)
        gh = nt(elow2[...], z[cols, :])
        dpre[:, cols] = (gh * gelu_slope(pre[:, cols])).astype(BF)

    def mlp_back():
        for j in range(2):
            cols = slice(j * HALF, (j + 1) * HALF)
            xb[2, x, :, cols] = (
                nt(dpre[:, 0:D], z[HID + j * HALF:HID + (j + 1) * HALF, :])
                + nt(dpre[:, D:HID], z[HID + D + j * HALF:HID + D + (j + 1) * HALF, :])
            ).astype(BF)
            m_mlp.append(exchange(2, (slice(None), pl.ds(j * HALF, HALF)), 4 + j))
        later["keys"] = [load(ck_h, ck), load(cv_h, cv)]
        later["inputs"] = [load(inin_h, inin), load(inp_h, inp)]
        wait_all(in_mid)

    def fill_down(j):
        for i in range(2):
            part = hid[(j // 2) * ROWS:(j // 2 + 1) * ROWS, (j % 2) * HALF:(j % 2 + 1) * HALF]
            fill(4 + j, i, tn(part, elow2[:, i * HALF:(i + 1) * HALF]))

    def fill_up(j):
        for i in range(2):
            fill(8 + j, i, tn(mlpin[:, i * HALF:(i + 1) * HALF], dpre[:, j * HALF:(j + 1) * HALF]))

    def one_back():
        later["latin"] = load(latin_h, latin)
        wait_all(m_mlp)
        gain = vec_row(vecs, gain_mlp)

        def body(i):
            rows = pl.ds(pl.multiple_of(i * 32, 32), 32)
            dv, dg, db = norm_back(hone[rows, :], both(2, rows), gain)
            e = etwo[rows, :] + dv
            hone[rows, :] = e
            elow1[rows, :] = e.astype(BF)
            gvec[4:5, :] += dg
            gvec[5:6, :] += db

        loop(8, body)

    def cross_back():
        wait_all(in_cross)
        for g in range(2):
            dcr[g * D:(g + 1) * D, :] = nt(wf[3], elow1[g * LAT:(g + 1) * LAT, :]).astype(BF)

    def fill_output():
        for j in range(2):
            value = 0.0
            for g in range(2):
                rows = pl.ds(pl.multiple_of(g * D + x * HALF, HALF), HALF)
                value = value + nn(
                    att[rows, :], elow1[g * LAT:(g + 1) * LAT, j * HALF:(j + 1) * HALF]
                )
            fill(12, j, value)

    def new_latents():
        wait_all(m_new)

        def body(i):
            rows = pl.ds(pl.multiple_of(i * 64, 64), 64)
            selfin[rows, :] = (htwo[rows, :] + both(1, rows)).astype(BF)

        loop(4, body)
        store(selfin, newlat_o)
        wait_all(later["keys"])

    def head(g, h):
        cols = slice(h * HEAD_DIM, (h + 1) * HEAD_DIM)
        n_rows = slice(g * INP, (g + 1) * INP)
        l_rows = slice(g * LAT, (g + 1) * LAT)
        t_rows = slice(g * D + h * HEAD_DIM, g * D + (h + 1) * HEAD_DIM)
        k, v, q = ck[n_rows, cols], cv[n_rows, cols], cq[l_rows, cols]
        s = nt(k, q) * SCALE + mask[n_rows, :].astype(F32)
        p = jnp.exp(s - st[g, h:h + 1, :]) * st[g, HEADS + h:HEADS + h + 1, :]
        do = dcr[t_rows, :]
        delta = jnp.sum(do.astype(F32) * att[t_rows, :].astype(F32), axis=0, keepdims=True)
        dsc = (p * (nn(v, do) - delta)).astype(BF)
        cv[n_rows, cols] = nt(p.astype(BF), do).astype(BF)
        ck[n_rows, cols] = (nn(dsc, q) * SCALE).astype(BF)
        xb[0, x, l_rows, cols] = (tn(dsc, k) * SCALE).astype(BF)

    def heads_back(g, h):
        head(g, h)
        head(g, h + 1)
        if h == HEADS - 2:
            m_query.append(exchange(0, (pl.ds(g * LAT, LAT),), 6 + g))

    def weight_grad(w, i):
        if w == 0 and i == 0:
            wait_all(later["inputs"])
        source = (ck, cv)[w]
        rows = slice(i * 256, (i + 1) * 256)
        mine = pl.ds(pl.multiple_of(x * HALF + i * 256, 256), 256)
        theirs = pl.ds(pl.multiple_of((1 - x) * HALF + i * 256, 256), 256)
        other[w, rows, :] = tn(inin[:, theirs], source[...]).astype(BF)
        grad[(14 + w) * HALF + i * 256:(14 + w) * HALF + (i + 1) * 256, :] = tn(
            inin[:, mine], source[...]
        ).astype(BF)
        if i == 1:
            start_core(w)

    def fill_query():
        wait_all(m_query)
        later["latin"].wait()

        def body(i):
            rows = pl.ds(pl.multiple_of(i * 64, 64), 64)
            dcq[rows, :] = both(0, rows).astype(BF)

        loop(4, body)
        for j in range(2):
            mine = pl.ds(pl.multiple_of(x * HALF, HALF), HALF)
            fill(13, j, tn(latin[:, mine], dcq[:, j * HALF:(j + 1) * HALF]))

    def latents_back():
        gain = vec_row(vecs, gain_lat)
        later["lat"].wait()

        def body(i):
            rows = pl.ds(pl.multiple_of(i * 128, 128), 128)
            dv, dg, db = norm_back(lat[rows, :].astype(F32), nt(dcq[rows, :], wf[2]), gain)
            lat[rows, :] = (hone[rows, :] + dv).astype(BF)
            gvec[0:1, :] += dg
            gvec[1:2, :] += db

        loop(2, body)
        store(lat, glat_o)

    def inputs_back(i):
        rows = slice(i * 224, (i + 1) * 224)
        dy = nt(ck[rows, :], wf[0]) + nt(cv[rows, :], wf[1])
        dv, dg, db = norm_back(inp[rows, :].astype(F32), dy, vec_row(vecs, gain_inp))
        inp[rows, :] = dv.astype(BF)
        gvec[2:3, :] += dg
        gvec[3:4, :] += db
        if i == 6:
            store(inp, ginp_o)
            col = lax.broadcasted_iota(jnp.int32, (8, D), 1) // HALF
            row = lax.broadcasted_iota(jnp.int32, (8, D), 0)
            keep = (col == x) | (row == 2) | (row == 3)
            gvec[...] = jnp.where(keep, gvec[...], 0.0)

    v_partners = (xp, cp, yp, ap, bp)
    v_moves = []

    def vec_event(s):
        if s > 0:
            v_moves[s - 1].wait()
            gvec[...] += gvr[s - 1]
        if s < 5:
            move = remote(gvec, gvr.at[s], vs.at[s], vr.at[s], v_partners[s])
            move.start()
            v_moves.append(move)
        else:
            store(gvec, gvec_o)

    steps = [lambda: fill_self(0), lambda: fill_self(1), self_back]
    steps += [lambda: fill_self(2), lambda: fill_self(3)]
    steps += [new_part, two_back]
    steps += [lambda j=j: hidden_back(j) for j in range(4)]
    steps += [mlp_back]
    steps += [lambda j=j: fill_down(j) for j in range(4)]
    steps += [lambda j=j: fill_up(j) for j in range(4)]
    steps += [one_back, cross_back, fill_output, new_latents]
    steps += [lambda g=g, h=h: heads_back(g, h) for g in range(2) for h in range(0, HEADS, 2)]
    steps += [lambda i=i: weight_grad(0, i) for i in range(2)]
    steps += [lambda: weight_grad(1, 0), lambda: start_x(0), lambda: weight_grad(1, 1)]
    steps += [fill_query, lambda: start_x(1), latents_back]
    steps += [lambda i=i: inputs_back(i) for i in range(7)]
    for step, events in zip(steps, EVENTS, strict=True):
        step()
        for k, s in events:
            if k < 0:
                vec_event(s)
            else:
                event(k, s)
    wait_all(outs)


def run_second(args):
    any_spec = pl.BlockSpec(memory_space=pl.ANY)
    outs = [
        ((ROWS, D), BF), ((ROWS, D), BF), ((NROWS, D), BF), ((HALF, D), BF), ((HALF, D), BF),
        ((HALF, D), BF), ((HALF, D), BF), ((D, HID), BF), ((HID, D), BF), ((D, HALF), BF),
        ((D, HALF), BF), ((D, HALF), BF), ((HALF, D), BF), ((8, D), F32),
    ]
    scratch = [
        ((4 * NROWS, D), BF), ((4, D, D), BF), ((ROWS, D), BF),
        ((2 * D, LAT), BF), ((2, 16, LAT), F32), ((2, 8, HALF), F32), ((ROWS, D), F32),
        ((ROWS, D), F32), ((ROWS, D), F32), ((ROWS, D), BF), ((ROWS, D), BF), ((ROWS, HID), F32),
        ((2 * ROWS, D), BF), ((3, ROWS, HALF), BF), ((ROWS, HALF), BF), ((NROWS, LAT), BF),
        ((ROWS, D), BF), ((ROWS, D), BF), ((ROWS, D), BF), ((ROWS, HID), BF),
        ((2 * D, LAT), BF), ((3, 2, ROWS, D), BF), ((16 * HALF, D), BF), ((2, HALF, D), BF),
        ((SLOTS[0], PART, HALF), BF), *[((n, PART // 2, HALF), BF) for n in SLOTS[1:]],
        ((2, HALF, HALF), BF), ((8, D), F32),
        ((5, 8, D), F32),
    ]
    dma = pltpu.SemaphoreType.DMA
    return pl.pallas_call(
        second_kernel,
        out_shape=[jax.ShapeDtypeStruct(*o) for o in outs],
        in_specs=[any_spec] * len(args),
        out_specs=[any_spec] * len(outs),
        scratch_shapes=[pltpu.VMEM(*s) for s in scratch]
        + [dma((40,)), dma((64,))] + [dma((32 * 7,))] * 2 + [dma((12,))] * 2 + [dma((5,))] * 2
        + [pltpu.SemaphoreType.REGULAR((128,))],
        compiler_params=pltpu.CompilerParams(
            collective_id=1, has_side_effects=True, vmem_limit_bytes=63 * MIB
        ),
        name="backward",
    )(*args)


def finish_kernel(*refs):
    srcs, refs = refs[:13], refs[13:]
    dsts, (low, wide, insem, outsem) = refs[:13], refs[13:]
    tiles = []
    for i in (*range(3, 13), 0, 1, 2):
        rows, cols = srcs[i].shape
        for r in range(0, rows, 256):
            count = min(256, rows - r)
            tiles.append((i, pl.ds(r, count), (pl.ds(0, count), pl.ds(0, cols))))
    depth = low.shape[0]
    ins, outs, finished = {}, {}, set()

    def finish_out(n):
        if n >= 0 and n not in finished:
            outs[n].wait()
            finished.add(n)

    def start_in(n):
        i, rows, part = tiles[n]
        ins[n] = pltpu.make_async_copy(srcs[i].at[rows], low.at[n % depth, *part], insem.at[n % depth])
        ins[n].start()

    for n in range(depth):
        start_in(n)
    for n in range(len(tiles)):
        slot = n % depth
        i, rows, part = tiles[n]
        ins[n].wait()
        finish_out(n - depth)
        if i < 3:
            outs[n] = pltpu.make_async_copy(low.at[slot, *part], dsts[i].at[rows], outsem.at[slot])
            outs[n].start()
        else:
            cols = part[1]

            def body(i, slot=slot, cols=cols):
                rows = pl.ds(pl.multiple_of(i * 32, 32), 32)
                wide[slot, rows, cols] = low[slot, rows, cols].astype(F32)

            loop(8, body)
            outs[n] = pltpu.make_async_copy(wide.at[slot, *part], dsts[i].at[rows], outsem.at[slot])
            outs[n].start()
        if n + depth < len(tiles):
            if i < 3:
                finish_out(n)
            start_in(n + depth)
    for n in range(len(tiles) - depth, len(tiles)):
        finish_out(n)


def run_finish(args):
    any_spec = pl.BlockSpec(memory_space=pl.ANY)
    depth = 6
    return pl.pallas_call(
        finish_kernel,
        out_shape=[
            jax.ShapeDtypeStruct(a.shape, BF if i < 3 else F32) for i, a in enumerate(args)
        ],
        in_specs=[any_spec] * 13,
        out_specs=[any_spec] * 13,
        scratch_shapes=[
            pltpu.VMEM((depth, 256, HID), BF), pltpu.VMEM((depth, 256, HID), F32),
            pltpu.SemaphoreType.DMA((depth,)), pltpu.SemaphoreType.DMA((depth,)),
        ],
        compiler_params=pltpu.CompilerParams(vmem_limit_bytes=62 * MIB),
        name="finish",
    )(*args)


def per_device_pair(
    latents, inputs, latent_segment, input_segment, cross_query, cross_key, cross_value,
    cross_output, mlp_up, mlp_down, self_query, self_key, self_value, self_output,
    latent_gain, latent_bias, input_gain, input_bias, mlp_gain, mlp_bias, self_gain,
    self_bias, cotangent,
):
    vec = (
        latent_gain, latent_bias, input_gain, input_bias, mlp_gain, mlp_bias, self_gain, self_bias
    )
    lat = latents.reshape(ROWS, D)
    inp = inputs.reshape(NROWS, D)
    cot = cotangent.reshape(ROWS, D)
    kept = run_first((
        lat, inp, latent_segment, input_segment, *vec, cross_key, cross_value, cross_query,
        cross_output, mlp_up, mlp_down, self_query, self_key, self_value, self_output, cot,
    ))
    (new, glat, ginp, gq, gk, gv, go, gup, gdown, gsq, gsk, gsv, gso, gvec) = run_second(
        tuple(kept) + (
            lat, inp, mlp_up, mlp_down, self_query, self_key, self_value, self_output, cot
        )
    )
    new, glat, ginp, *grads = run_finish(
        (new, glat, ginp, gq, gk, gv, go, gup, gdown, gsq, gsk, gsv, gso)
    )
    x = lax.axis_index("shard")
    small = lax.dynamic_slice_in_dim(gvec, x * HALF, HALF, 1)
    return (
        new.reshape(latents.shape), glat.reshape(latents.shape), ginp.reshape(inputs.shape),
        *grads, *[small[i] for i in range(8)],
    )


def norm_forward(values, gain, shift):
    centred = values - jnp.mean(values, axis=-1, keepdims=True)
    inv_std = lax.rsqrt(jnp.mean(centred * centred, axis=-1, keepdims=True) + EPSILON)
    normed = centred * inv_std
    return (normed * gain + shift, normed, inv_std)


def norm_backward(grad_out, normed, inv_std, gain):
    scaled = grad_out * gain
    first_mean = jnp.mean(scaled, axis=-1, keepdims=True)
    second_mean = jnp.mean(scaled * normed, axis=-1, keepdims=True)
    grad_in = inv_std * (scaled - first_mean - normed * second_mean)
    return (grad_in, jnp.sum(grad_out * normed, axis=0), jnp.sum(grad_out, axis=0))


def product(left, right):
    return jnp.dot(left, right, preferred_element_type=jnp.float32)


def inner_rows(left, right):
    return lax.dot_general(
        left, right, (((0,), (0,)), ((), ())), preferred_element_type=jnp.float32
    )


def outer_cols(left, right):
    return lax.dot_general(
        left, right, (((1,), (1,)), ((), ())), preferred_element_type=jnp.float32
    )


def forward_total(term):
    return lax.psum(term.astype(jnp.bfloat16), "shard").astype(jnp.float32)


def backward_total(term):
    return lax.psum(term.astype(jnp.bfloat16), "shard").astype(jnp.float32)


def per_device(
    latents,
    inputs,
    latent_segment,
    input_segment,
    cross_query,
    cross_key,
    cross_value,
    cross_output,
    mlp_up,
    mlp_down,
    self_query,
    self_key,
    self_value,
    self_output,
    latent_gain,
    latent_bias,
    input_gain,
    input_bias,
    mlp_gain,
    mlp_bias,
    self_gain,
    self_bias,
    cotangent,
):
    shards = lax.axis_size("shard")
    groups, lat_len, width = latents.shape
    inp_len = inputs.shape[1]
    width_part = width // shards
    column_start = lax.axis_index("shard") * width_part
    rows = groups * lat_len
    scale = HEAD_DIM ** (-0.5)
    gathered = (
        lax.all_gather(cross_query, "shard", axis=0, tiled=True),
        lax.all_gather(cross_key, "shard", axis=0, tiled=True),
        lax.all_gather(cross_value, "shard", axis=0, tiled=True),
        lax.all_gather(cross_output, "shard", axis=0, tiled=True),
        lax.all_gather(latent_gain, "shard", axis=0, tiled=True),
        lax.all_gather(latent_bias, "shard", axis=0, tiled=True),
        lax.all_gather(input_gain, "shard", axis=0, tiled=True),
        lax.all_gather(input_bias, "shard", axis=0, tiled=True),
        lax.all_gather(mlp_gain, "shard", axis=0, tiled=True),
        lax.all_gather(mlp_bias, "shard", axis=0, tiled=True),
        lax.all_gather(self_gain, "shard", axis=0, tiled=True),
        lax.all_gather(self_bias, "shard", axis=0, tiled=True),
    )
    full_query, full_key, full_value, full_output = (
        gathered[0],
        gathered[1],
        gathered[2],
        gathered[3],
    )
    gain_lat, bias_lat, gain_inp, bias_inp, gain_mlp, bias_mlp, gain_self, bias_self = [
        piece.astype(jnp.float32) for piece in gathered[4:]
    ]
    lat_rows = latents.astype(jnp.float32).reshape(rows, width)
    inp_rows = inputs.astype(jnp.float32).reshape(groups * inp_len, width)
    lat_value, lat_normed, lat_inv = norm_forward(lat_rows, gain_lat, bias_lat)
    lat_in = lat_value.astype(jnp.bfloat16)
    inp_value, inp_normed, inp_inv = norm_forward(inp_rows, gain_inp, bias_inp)
    inp_in = inp_value.astype(jnp.bfloat16)
    cross_q = (
        product(lat_in, full_query).astype(jnp.bfloat16).reshape(groups, lat_len, HEADS, HEAD_DIM)
    )
    cross_k = (
        product(inp_in, full_key).astype(jnp.bfloat16).reshape(groups, inp_len, HEADS, HEAD_DIM)
    )
    cross_v = (
        product(inp_in, full_value).astype(jnp.bfloat16).reshape(groups, inp_len, HEADS, HEAD_DIM)
    )
    allowed = latent_segment[:, None, :, None] == input_segment[:, None, None, :]
    scores = (
        jnp.einsum("glhd,gnhd->ghln", cross_q, cross_k, preferred_element_type=jnp.float32) * scale
    )
    masked = jnp.where(allowed, scores, NEGATIVE)
    part_max = jnp.max(masked, axis=-1)
    top = lax.pmax(part_max, "shard")
    total = lax.psum(
        jnp.sum(jnp.where(allowed, jnp.exp(masked - top[..., None]), 0.0), axis=-1), "shard"
    )
    cross_prob = jnp.where(allowed, jnp.exp(masked - top[..., None]), 0.0) / total[..., None]
    cross_prob_low = cross_prob.astype(jnp.bfloat16)
    part_out = jnp.einsum(
        "ghln,gnhd->glhd", cross_prob_low, cross_v, preferred_element_type=jnp.float32
    )
    attended = lax.psum(part_out.astype(jnp.bfloat16), "shard").astype(jnp.float32)
    attended_in = attended.reshape(rows, width).astype(jnp.bfloat16)
    h_one = lat_rows + product(attended_in, full_output)
    mlp_value, mlp_normed, mlp_inv = norm_forward(h_one, gain_mlp, bias_mlp)
    mlp_in = mlp_value.astype(jnp.bfloat16)
    pre_act = product(mlp_in, mlp_up)
    hidden_in = jax.nn.gelu(pre_act).astype(jnp.bfloat16)
    h_two = h_one + forward_total(product(hidden_in, mlp_down))
    self_value_n, self_normed, self_inv = norm_forward(h_two, gain_self, bias_self)
    self_in = self_value_n.astype(jnp.bfloat16)
    local_heads = self_query.shape[1] // HEAD_DIM
    local_width = local_heads * HEAD_DIM
    self_q = (
        product(self_in, self_query)
        .astype(jnp.bfloat16)
        .reshape(groups, lat_len, local_heads, HEAD_DIM)
    )
    self_k = (
        product(self_in, self_key)
        .astype(jnp.bfloat16)
        .reshape(groups, lat_len, local_heads, HEAD_DIM)
    )
    self_v = (
        product(self_in, self_value)
        .astype(jnp.bfloat16)
        .reshape(groups, lat_len, local_heads, HEAD_DIM)
    )
    self_scores = (
        jnp.einsum("glhd,gmhd->ghlm", self_q, self_k, preferred_element_type=jnp.float32) * scale
    )
    self_prob = jax.nn.softmax(self_scores, axis=-1)
    self_prob_low = self_prob.astype(jnp.bfloat16)
    self_att = jnp.einsum(
        "ghlm,gmhd->glhd", self_prob_low, self_v, preferred_element_type=jnp.float32
    )
    self_att_in = self_att.reshape(rows, local_width).astype(jnp.bfloat16)
    result = h_two + forward_total(product(self_att_in, self_output))
    new_latents = result.reshape(groups, lat_len, width).astype(jnp.bfloat16)
    grad_out = cotangent.astype(jnp.float32).reshape(rows, width)
    grad_branch = grad_out.astype(jnp.bfloat16)
    grad_self_output = inner_rows(self_att_in, grad_branch)
    grad_att = (
        outer_cols(grad_branch, self_output)
        .astype(jnp.bfloat16)
        .reshape(groups, lat_len, local_heads, HEAD_DIM)
    )
    delta = jnp.sum(grad_att.astype(jnp.float32) * self_att, axis=-1).transpose(0, 2, 1)
    grad_prob = jnp.einsum("glhd,gmhd->ghlm", grad_att, self_v, preferred_element_type=jnp.float32)
    grad_sv = jnp.einsum(
        "ghlm,glhd->gmhd", self_prob_low, grad_att, preferred_element_type=jnp.float32
    )
    grad_scores = (self_prob * (grad_prob - delta[..., None])).astype(jnp.bfloat16)
    grad_sq = (
        jnp.einsum("ghlm,gmhd->glhd", grad_scores, self_k, preferred_element_type=jnp.float32)
        * scale
    )
    grad_sk = (
        jnp.einsum("ghlm,glhd->gmhd", grad_scores, self_q, preferred_element_type=jnp.float32)
        * scale
    )
    grad_sq = grad_sq.astype(jnp.bfloat16).reshape(rows, local_width)
    grad_sk = grad_sk.astype(jnp.bfloat16).reshape(rows, local_width)
    grad_sv = grad_sv.astype(jnp.bfloat16).reshape(rows, local_width)
    grad_self_query = inner_rows(self_in, grad_sq)
    grad_self_key = inner_rows(self_in, grad_sk)
    grad_self_value = inner_rows(self_in, grad_sv)
    grad_self_in = backward_total(
        outer_cols(grad_sq, self_query)
        + outer_cols(grad_sk, self_key)
        + outer_cols(grad_sv, self_value)
    )
    grad_norm, gain_full, bias_full = norm_backward(grad_self_in, self_normed, self_inv, gain_self)
    grad_two = grad_out + grad_norm
    grad_self_gain = lax.dynamic_slice_in_dim(gain_full, column_start, width_part)
    grad_self_bias = lax.dynamic_slice_in_dim(bias_full, column_start, width_part)
    grad_mlp_branch = grad_two.astype(jnp.bfloat16)
    grad_mlp_down = inner_rows(hidden_in, grad_mlp_branch)
    grad_hidden = outer_cols(grad_mlp_branch, mlp_down)
    gelu_value, gelu_pull = jax.vjp(jax.nn.gelu, pre_act)
    grad_pre = gelu_pull(grad_hidden)[0].astype(jnp.bfloat16)
    grad_mlp_up = inner_rows(mlp_in, grad_pre)
    grad_mlp_in = backward_total(outer_cols(grad_pre, mlp_up))
    grad_norm, gain_full, bias_full = norm_backward(grad_mlp_in, mlp_normed, mlp_inv, gain_mlp)
    grad_one = grad_two + grad_norm
    grad_mlp_gain = lax.dynamic_slice_in_dim(gain_full, column_start, width_part)
    grad_mlp_bias = lax.dynamic_slice_in_dim(bias_full, column_start, width_part)
    grad_cross_branch = grad_one.astype(jnp.bfloat16)
    grad_cross_output = inner_rows(
        lax.dynamic_slice_in_dim(attended_in, column_start, width_part, 1), grad_cross_branch
    )
    grad_ca = (
        outer_cols(grad_cross_branch, full_output)
        .astype(jnp.bfloat16)
        .reshape(groups, lat_len, HEADS, HEAD_DIM)
    )
    cross_delta = jnp.sum(grad_ca.astype(jnp.float32) * attended, axis=-1).transpose(0, 2, 1)
    grad_cp = jnp.einsum("glhd,gnhd->ghln", grad_ca, cross_v, preferred_element_type=jnp.float32)
    grad_cv = jnp.einsum(
        "ghln,glhd->gnhd", cross_prob_low, grad_ca, preferred_element_type=jnp.float32
    )
    grad_cs = (cross_prob * (grad_cp - cross_delta[..., None])).astype(jnp.bfloat16)
    grad_cq_part = (
        jnp.einsum("ghln,gnhd->glhd", grad_cs, cross_k, preferred_element_type=jnp.float32) * scale
    )
    grad_ck = (
        jnp.einsum("ghln,glhd->gnhd", grad_cs, cross_q, preferred_element_type=jnp.float32) * scale
    )
    grad_cq = backward_total(grad_cq_part.reshape(rows, width)).astype(jnp.bfloat16)
    grad_ck = grad_ck.astype(jnp.bfloat16).reshape(groups * inp_len, width)
    grad_cv = grad_cv.astype(jnp.bfloat16).reshape(groups * inp_len, width)
    grad_cross_query = inner_rows(
        lax.dynamic_slice_in_dim(lat_in, column_start, width_part, 1), grad_cq
    )
    grad_lat_in = outer_cols(grad_cq, full_query)
    grad_norm, gain_full, bias_full = norm_backward(grad_lat_in, lat_normed, lat_inv, gain_lat)
    grad_latents = (grad_one + grad_norm).reshape(groups, lat_len, width).astype(jnp.bfloat16)
    grad_latent_gain = lax.dynamic_slice_in_dim(gain_full, column_start, width_part)
    grad_latent_bias = lax.dynamic_slice_in_dim(bias_full, column_start, width_part)
    key_term = inner_rows(inp_in, grad_ck)
    value_term = inner_rows(inp_in, grad_cv)
    grad_inp_in = outer_cols(grad_ck, full_key) + outer_cols(grad_cv, full_value)
    grad_inp, inp_gain_full, inp_bias_full = norm_backward(
        grad_inp_in, inp_normed, inp_inv, gain_inp
    )
    grad_inputs = grad_inp.reshape(groups, inp_len, width).astype(jnp.bfloat16)
    grad_cross_key, grad_cross_value, grad_input_gain, grad_input_bias = (
        lax.psum_scatter(
            key_term.astype(jnp.bfloat16), "shard", scatter_dimension=0, tiled=True
        ).astype(jnp.float32),
        lax.psum_scatter(
            value_term.astype(jnp.bfloat16), "shard", scatter_dimension=0, tiled=True
        ).astype(jnp.float32),
        lax.psum_scatter(
            inp_gain_full.astype(jnp.bfloat16), "shard", scatter_dimension=0, tiled=True
        ).astype(jnp.float32),
        lax.psum_scatter(
            inp_bias_full.astype(jnp.bfloat16), "shard", scatter_dimension=0, tiled=True
        ).astype(jnp.float32),
    )
    (
        grad_cross_query,
        grad_cross_key,
        grad_cross_value,
        grad_cross_output,
        grad_mlp_up,
        grad_mlp_down,
        grad_self_query,
        grad_self_key,
        grad_self_value,
        grad_self_output,
        grad_latent_gain,
        grad_latent_bias,
        grad_input_gain,
        grad_input_bias,
        grad_mlp_gain,
        grad_mlp_bias,
        grad_self_gain,
        grad_self_bias,
    ) = (
        lax.psum(grad_cross_query.astype(jnp.bfloat16), "grp").astype(jnp.float32),
        lax.psum(grad_cross_key.astype(jnp.bfloat16), "grp").astype(jnp.float32),
        lax.psum(grad_cross_value.astype(jnp.bfloat16), "grp").astype(jnp.float32),
        lax.psum(grad_cross_output.astype(jnp.bfloat16), "grp").astype(jnp.float32),
        lax.psum(grad_mlp_up.astype(jnp.bfloat16), "grp").astype(jnp.float32),
        lax.psum(grad_mlp_down.astype(jnp.bfloat16), "grp").astype(jnp.float32),
        lax.psum(grad_self_query.astype(jnp.bfloat16), "grp").astype(jnp.float32),
        lax.psum(grad_self_key.astype(jnp.bfloat16), "grp").astype(jnp.float32),
        lax.psum(grad_self_value.astype(jnp.bfloat16), "grp").astype(jnp.float32),
        lax.psum(grad_self_output.astype(jnp.bfloat16), "grp").astype(jnp.float32),
        lax.psum(grad_latent_gain.astype(jnp.bfloat16), "grp").astype(jnp.float32),
        lax.psum(grad_latent_bias.astype(jnp.bfloat16), "grp").astype(jnp.float32),
        lax.psum(grad_input_gain.astype(jnp.bfloat16), "grp").astype(jnp.float32),
        lax.psum(grad_input_bias.astype(jnp.bfloat16), "grp").astype(jnp.float32),
        lax.psum(grad_mlp_gain.astype(jnp.bfloat16), "grp").astype(jnp.float32),
        lax.psum(grad_mlp_bias.astype(jnp.bfloat16), "grp").astype(jnp.float32),
        lax.psum(grad_self_gain.astype(jnp.bfloat16), "grp").astype(jnp.float32),
        lax.psum(grad_self_bias.astype(jnp.bfloat16), "grp").astype(jnp.float32),
    )
    return (
        new_latents,
        grad_latents,
        grad_inputs,
        grad_cross_query,
        grad_cross_key,
        grad_cross_value,
        grad_cross_output,
        grad_mlp_up,
        grad_mlp_down,
        grad_self_query,
        grad_self_key,
        grad_self_value,
        grad_self_output,
        grad_latent_gain,
        grad_latent_bias,
        grad_input_gain,
        grad_input_bias,
        grad_mlp_gain,
        grad_mlp_bias,
        grad_self_gain,
        grad_self_bias,
    )


def solution(mesh):
    laid_out = mesh.shape["shard"] == 2 and mesh.shape["grp"] == 16
    return jax.shard_map(
        per_device_pair if laid_out else per_device,
        mesh=mesh,
        in_specs=(
            P("grp", None, None),
            P("grp", "shard", None),
            P("grp", None),
            P("grp", "shard"),
            P("shard", None),
            P("shard", None),
            P("shard", None),
            P("shard", None),
            P(None, "shard"),
            P("shard", None),
            P(None, "shard"),
            P(None, "shard"),
            P(None, "shard"),
            P("shard", None),
            P("shard"),
            P("shard"),
            P("shard"),
            P("shard"),
            P("shard"),
            P("shard"),
            P("shard"),
            P("shard"),
            P("grp", None, None),
        ),
        out_specs=(
            P("grp", None, None),
            P("grp", None, None),
            P("grp", "shard", None),
            P("shard", None),
            P("shard", None),
            P("shard", None),
            P("shard", None),
            P(None, "shard"),
            P("shard", None),
            P(None, "shard"),
            P(None, "shard"),
            P(None, "shard"),
            P("shard", None),
            P("shard"),
            P("shard"),
            P("shard"),
            P("shard"),
            P("shard"),
            P("shard"),
            P("shard"),
            P("shard"),
        ),
        check_vma=False,
    )
```

```python
import jax
import jax.numpy as jnp
from jax import lax
from jax.experimental import pallas as pl
from jax.experimental.pallas import tpu as pltpu
from jax.sharding import PartitionSpec as P

HEADS = 8
HEAD_DIM = 128


EPSILON = 1e-05
NEGATIVE = -1e30

BF = jnp.bfloat16
F32 = jnp.float32
MESH = pl.DeviceIdType.MESH
LAT = 128
INP = 784
D = 1024
HALF = 512
HID = 2048
ROWS = 2 * LAT
NROWS = 2 * INP
SCALE = HEAD_DIM ** (-0.5)
MIB = 1 << 20


def nn(a, b):
    return lax.dot_general(a, b, (((1,), (0,)), ((), ())), preferred_element_type=F32)


def nt(a, b):
    return lax.dot_general(a, b, (((1,), (1,)), ((), ())), preferred_element_type=F32)


def tn(a, b):
    return lax.dot_general(a, b, (((0,), (0,)), ((), ())), preferred_element_type=F32)


def place():
    g = lax.axis_index("grp")
    x = lax.axis_index("shard")
    c = lax.rem(g, 2)
    y = lax.rem(g // 2, 2)
    a = lax.rem(g // 4, 2)
    b = g // 8
    return dict(
        x=x, c=c, y=y, a=a, b=b,
        xp=(g, 1 - x),
        cp=(g + 1 - 2 * c, x),
        yp=(g + 2 - 4 * y, x),
        ap=(g + 4 - 8 * a, x),
        bp=(g + 8 - 16 * b, x),
        mp=(g + 4 - 8 * b, x),
    )


def greet(partners):
    barrier = pltpu.get_barrier_semaphore()
    for partner in partners:
        pl.semaphore_signal(barrier, inc=1, device_id=partner, device_id_type=MESH)
    pl.semaphore_wait(barrier, len(partners))


def remote(src, dst, send, recv, partner):
    return pltpu.make_async_remote_copy(
        src_ref=src, dst_ref=dst, send_sem=send, recv_sem=recv,
        device_id=partner, device_id_type=MESH,
    )


def norm(v, gain, shift):
    cen = v - jnp.mean(v, axis=-1, keepdims=True)
    inv = lax.rsqrt(jnp.mean(cen * cen, axis=-1, keepdims=True) + EPSILON)
    return cen * inv * gain + shift


def vec_row(vecs, i):
    return jnp.concatenate([vecs[0, i:i + 1, :], vecs[1, i:i + 1, :]], axis=1)


def span(first, last, body):
    lax.fori_loop(first, last, lambda i, carry: (body(i), carry)[1], 0)


def loop(n, body):
    span(0, n, body)


def first_kernel(
    lat_h, inp_h, seglat, seginp, v0, v1, v2, v3, v4, v5, v6, v7, wk_h, wv_h, wq_h, wo_h, up_h, down_h,
    sq_h, sk_h, sv_h, so_h, cot_h,
    wf_o, ck_o, cv_o, inin_o, latin_o, cq_o, att_o, st_o, vec_o, hone_o, htwo_o,
    mlpin_o, selfin_o, pre_o, hid_o, ds_o, slow_o, mask_o,
    wf, inp, inin, ck, cv, lat, latin, cq, mask, segs, axb, stx, att, st, vecs,
    hone, htwo, mlpin, pre, hid, xm, selfin, wup, wdown, wself, wso, cot, qkv, dself,
    ds, slow, lsem, osem, xs, xr, ys, yr, c0s, c0r, c1s, c1r, ms, mr,
):
    me = place()
    x, y, c = me["x"], me["y"], me["c"]
    xp, yp, cp = me["xp"], me["yp"], me["cp"]
    nlocal = [0]
    nout = [0]

    def load(src, dst):
        copy = pltpu.make_async_copy(src, dst, lsem.at[nlocal[0]])
        nlocal[0] += 1
        copy.start()
        return copy

    outs = []

    def store(src, dst):
        copy = pltpu.make_async_copy(src, dst, osem.at[nout[0]])
        nout[0] += 1
        copy.start()
        outs.append(copy)

    own = pl.ds(pl.multiple_of(x * HALF, HALF), HALF)
    in_inp = load(inp_h, inp)
    in_lat = load(lat_h, lat)
    in_cot = load(cot_h, cot)
    in_so = load(so_h, wso)
    greet((xp, yp, cp))
    for i, v in enumerate((v0, v1, v2, v3, v4, v5, v6, v7)):
        vecs[x, i:i + 1, :] = v[...].astype(F32).reshape(1, HALF)
    vec_move = remote(vecs.at[x], vecs.at[x], xs.at[4], xr.at[4], xp)
    vec_move.start()
    weights = (wk_h, wv_h, wq_h, wo_h)
    quarter = 2 * y + c

    def part(w, side, q):
        return wf.at[w, pl.ds(pl.multiple_of(side * HALF + q * 128, 128), 128)]

    x_moves = []
    for w in range(4):
        src = weights[w].at[pl.ds(pl.multiple_of(quarter * 128, 128), 128)]
        move = remote(src, part(w, x, quarter), xs.at[w], xr.at[w], xp)
        move.start()
        x_moves.append(move)
    in_w = [load(weights[w], wf.at[w, own]) for w in range(4)]
    in_self = [load(h, wself.at[i]) for i, h in enumerate((sq_h, sk_h, sv_h))]
    in_up = load(up_h, wup)
    in_down = load(down_h, wdown)
    pending = []

    def forward_x(w):
        x_moves[w].wait()
        for sems, partner in (((ys, yr), yp), ((c0s, c0r), cp)):
            block = part(w, 1 - x, quarter)
            move = remote(block, block, sems[0].at[w], sems[1].at[w], partner)
            move.start()
            pending.append(move)

    def forward_y(w):
        block = part(w, 1 - x, quarter)
        remote(block, block, ys.at[w], yr.at[w], yp).wait_recv()
        block = part(w, 1 - x, 2 * (1 - y) + c)
        move = remote(block, block, c1s.at[w], c1r.at[w], cp)
        move.start()
        pending.append(move)

    def whole(w):
        block = part(w, 1 - x, quarter)
        remote(block, block, c0s.at[w], c0r.at[w], cp).wait_recv()
        remote(block, block, c1s.at[w], c1r.at[w], cp).wait_recv()
        in_w[w].wait()
        store(wf.at[w], wf_o.at[w])

    segs[...] = jnp.zeros_like(segs)
    segs[0:2, 0:INP] = seginp[...].astype(F32)
    for g in range(2):
        lat_row = seglat[g:g + 1, :].astype(F32)
        for j in range(7):
            count = min(128, INP - j * 128)
            col = jnp.broadcast_to(segs[g:g + 1, j * 128:(j + 1) * 128], (128, 128)).T
            mask[g * INP + j * 128:g * INP + j * 128 + count, :] = jnp.where(
                col[:count] == lat_row, 0.0, NEGATIVE
            ).astype(BF)
    store(mask, mask_o)
    in_cot.wait()
    in_so.wait()
    dself[...] = nt(cot[...], wso[...]).astype(BF)
    in_inp.wait()
    vec_move.wait()
    store(vecs, vec_o)
    gain_inp, bias_inp = vec_row(vecs, 2), vec_row(vecs, 3)

    def norm_rows(i):
        rows = pl.ds(pl.multiple_of(i * 32, 32), 32)
        inin[rows, :] = norm(inp[rows, :].astype(F32), gain_inp, bias_inp).astype(BF)

    span(0, 24, norm_rows)
    forward_x(0)
    span(24, 49, norm_rows)
    store(inin, inin_o)
    forward_x(1)
    forward_y(0)
    in_lat.wait()
    latin[...] = norm(lat[...].astype(F32), vec_row(vecs, 0), vec_row(vecs, 1)).astype(BF)
    store(latin, latin_o)

    def project(target, w, half):
        cols = slice(half * HALF, (half + 1) * HALF)

        def body(i):
            rows = pl.ds(pl.multiple_of(i * INP, 16), INP)
            target[rows, cols] = nn(inin[rows, :], wf[w, :, cols]).astype(BF)

        loop(2, body)

    whole(0)
    project(ck, 0, 0)
    forward_x(2)
    forward_y(1)
    project(ck, 0, 1)
    store(ck, ck_o)
    whole(1)
    forward_x(3)
    forward_y(2)
    project(cv, 1, 0)
    project(cv, 1, 1)
    store(cv, cv_o)
    whole(2)
    cq[...] = nn(latin[...], wf[2]).astype(BF)
    store(cq, cq_o)
    forward_y(3)

    def head(g, h):
        cols = pl.ds(pl.multiple_of(h * HEAD_DIM, HEAD_DIM), HEAD_DIM)
        n_rows = slice(g * INP, (g + 1) * INP)
        s = nt(ck[n_rows, cols], cq[g * LAT:(g + 1) * LAT, cols]) * SCALE + mask[n_rows, :].astype(F32)
        top = jnp.maximum(jnp.max(s, axis=0, keepdims=True), 0.1 * NEGATIVE)
        e = jnp.exp(s - top)
        total = jnp.sum(e, axis=0, keepdims=True)
        out = tn(cv[n_rows, cols], e.astype(BF))
        out = out * jnp.where(total > 0.0, 1.0 / total, 0.0)
        axb[x, pl.ds(pl.multiple_of(g * D + h * HEAD_DIM, HEAD_DIM), HEAD_DIM), :] = out.astype(BF)
        stx[x, g, pl.ds(h, 1), :] = top
        stx[x, g, pl.ds(HEADS + h, 1), :] = total

    a_moves = []
    for g in range(2):
        def pair(i, g=g):
            head(g, 2 * i)
            head(g, 2 * i + 1)

        loop(HEADS // 2, pair)
        block = axb.at[x, pl.ds(g * D, D)]
        for src, k in ((block, 0), (stx.at[x, g], 1)):
            move = remote(src, src, ms.at[2 * g + k], mr.at[2 * g + k], xp)
            move.start()
            a_moves.append(move)
    whole(3)
    in_up.wait()
    in_down.wait()
    m_moves = []

    def mlp_group(g):
        a_moves[2 * g].wait()
        a_moves[2 * g + 1].wait()
        for h in range(HEADS):
            m0, m1 = stx[0, g, h:h + 1, :], stx[1, g, h:h + 1, :]
            top = jnp.maximum(m0, m1)
            w0 = stx[0, g, HEADS + h:HEADS + h + 1, :] * jnp.exp(m0 - top)
            w1 = stx[1, g, HEADS + h:HEADS + h + 1, :] * jnp.exp(m1 - top)
            inv = 1.0 / (w0 + w1)
            rows = slice(g * D + h * HEAD_DIM, g * D + (h + 1) * HEAD_DIM)
            mixed = axb[0, rows, :].astype(F32) * (w0 * inv) + axb[1, rows, :].astype(F32) * (w1 * inv)
            att[rows, :] = mixed.astype(BF)
            st[g, h:h + 1, :] = top
            st[g, HEADS + h:HEADS + h + 1, :] = inv
        rows = slice(g * LAT, (g + 1) * LAT)
        one = lat[rows, :].astype(F32) + tn(att[g * D:(g + 1) * D, :], wf[3])
        hone[rows, :] = one
        mlpin[rows, :] = norm(one, vec_row(vecs, 4), vec_row(vecs, 5)).astype(BF)
        for j in range(4):
            cols = slice(j * HALF, (j + 1) * HALF)
            u = nn(mlpin[rows, :], wup[:, cols])
            pre[rows, cols] = u
            hid[rows, cols] = jax.nn.gelu(u).astype(BF)
        for j in range(2):
            cols = slice(j * HALF, (j + 1) * HALF)
            xm[x, g, :, cols] = nn(hid[rows, :], wdown[:, cols]).astype(BF)
            part = xm.at[x, g, :, pl.ds(j * HALF, HALF)]
            move = remote(part, part, ms.at[4 + 2 * g + j], mr.at[4 + 2 * g + j], xp)
            move.start()
            m_moves.append(move)

    def self_group(g):
        rows = slice(g * LAT, (g + 1) * LAT)
        m_moves[2 * g].wait()
        m_moves[2 * g + 1].wait()
        two = hone[rows, :] + (xm[0, g].astype(F32) + xm[1, g].astype(F32))
        htwo[rows, :] = two
        selfin[rows, :] = norm(two, vec_row(vecs, 6), vec_row(vecs, 7)).astype(BF)
        for i in range(3):
            qkv[i, rows, :] = nn(selfin[rows, :], wself[i]).astype(BF)
        for h in range(4):
            cols = slice(h * HEAD_DIM, (h + 1) * HEAD_DIM)
            q, k, v = qkv[0, rows, cols], qkv[1, rows, cols], qkv[2, rows, cols]
            do = dself[rows, cols]
            s = nt(q, k) * SCALE
            e = jnp.exp(s - jnp.max(s, axis=1, keepdims=True))
            p = e / jnp.sum(e, axis=1, keepdims=True)
            p_low = p.astype(BF)
            o = nn(p_low, v)
            slow[rows, cols] = o.astype(BF)
            delta = jnp.sum(do.astype(F32) * o, axis=1, keepdims=True)
            dp = nt(do, v)
            dsc = (p * (dp - delta)).astype(BF)
            ds[0, rows, cols] = (nn(dsc, k) * SCALE).astype(BF)
            ds[1, rows, cols] = (tn(dsc, q) * SCALE).astype(BF)
            ds[2, rows, cols] = tn(p_low, do).astype(BF)

    mlp_group(0)
    mlp_group(1)
    store(att, att_o)
    store(st, st_o)
    store(hone, hone_o)
    store(mlpin, mlpin_o)
    store(pre, pre_o)
    store(hid, hid_o)
    for copy in in_self:
        copy.wait()
    self_group(0)
    self_group(1)
    store(ds, ds_o)
    store(slow, slow_o)
    store(htwo, htwo_o)
    store(selfin, selfin_o)
    for move in pending:
        move.wait_send()
    for copy in outs:
        copy.wait()


def run_first(args):
    any_spec = pl.BlockSpec(memory_space=pl.ANY)
    vmem_spec = pl.BlockSpec(memory_space=pltpu.VMEM)
    outs = [
        ((4, D, D), BF), ((NROWS, D), BF), ((NROWS, D), BF), ((NROWS, D), BF),
        ((ROWS, D), BF), ((ROWS, D), BF), ((2 * D, LAT), BF), ((2, 16, LAT), F32),
        ((2, 8, HALF), F32), ((ROWS, D), F32), ((ROWS, D), F32), ((ROWS, D), BF),
        ((ROWS, D), BF), ((ROWS, HID), F32), ((ROWS, HID), BF), ((3, ROWS, HALF), BF),
        ((ROWS, HALF), BF), ((NROWS, LAT), BF),
    ]
    scratch = [
        ((4, D, D), BF), ((NROWS, D), BF), ((NROWS, D), BF), ((NROWS, D), BF), ((NROWS, D), BF),
        ((ROWS, D), BF), ((ROWS, D), BF), ((ROWS, D), BF), ((NROWS, LAT), BF), ((8, 896), F32),
        ((2, 2 * D, LAT), BF), ((2, 2, 16, LAT), F32), ((2 * D, LAT), BF), ((2, 16, LAT), F32),
        ((2, 8, HALF), F32), ((ROWS, D), F32), ((ROWS, D), F32), ((ROWS, D), BF),
        ((ROWS, HID), F32), ((ROWS, HID), BF), ((2, 2, LAT, D), BF), ((ROWS, D), BF),
        ((D, HID), BF), ((HID, D), BF), ((3, D, HALF), BF), ((HALF, D), BF), ((ROWS, D), BF),
        ((3, ROWS, HALF), BF), ((ROWS, HALF), BF), ((3, ROWS, HALF), BF), ((ROWS, HALF), BF),
    ]
    dma = pltpu.SemaphoreType.DMA
    return pl.pallas_call(
        first_kernel,
        out_shape=[jax.ShapeDtypeStruct(*o) for o in outs],
        in_specs=[any_spec] * 2 + [vmem_spec] * 10 + [any_spec] * 11,
        out_specs=[any_spec] * len(outs),
        scratch_shapes=[pltpu.VMEM(*s) for s in scratch]
        + [dma((16,)), dma((24,))] + [dma((5,))] * 2 + [dma((4,))] * 6 + [dma((8,))] * 2,
        compiler_params=pltpu.CompilerParams(
            collective_id=0, has_side_effects=True, vmem_limit_bytes=58 * MIB
        ),
        name="forward",
    )(*args)


def norm_back(v, dy, gain):
    cen = v - jnp.mean(v, axis=-1, keepdims=True)
    inv = lax.rsqrt(jnp.mean(cen * cen, axis=-1, keepdims=True) + EPSILON)
    n = cen * inv
    t = dy * gain
    dv = inv * (t - jnp.mean(t, axis=-1, keepdims=True) - n * jnp.mean(t * n, axis=-1, keepdims=True))
    return (
        dv,
        jnp.sum(dy * n, axis=0, keepdims=True),
        jnp.sum(dy, axis=0, keepdims=True),
    )


def gelu_slope(u):
    root = (2.0 / jnp.pi) ** 0.5
    t = jnp.tanh(root * (u + 0.044715 * u * u * u))
    return 0.5 * (1.0 + t) + 0.5 * u * (1.0 - t * t) * root * (1.0 + 3.0 * 0.044715 * u * u)


PART = 256
KINDS = "zyyyyyyzyzyzyzyy" + "yzyzyzyyyzyyyzzy"
SLOTS = (4, 4, 4, 4, 3, 3)
EVENTS = (
    ((0, 0), (1, 0),),
    (),
    (),
    ((1, 1), (0, 1), (2, 0), (3, 0),),
    (),
    (),
    ((2, 1), (4, 0), (1, 2), (3, 1), (5, 0), (2, 2), (0, 2), (4, 1), (6, 0), (3, 2), (1, 3), (5, 1), (7, 0),),
    ((0, 3),),
    ((2, 3), (4, 2), (6, 1), (7, 1),),
    ((1, 4),),
    (),
    ((3, 3),),
    ((2, 4),),
    ((4, 3), (0, 4), (1, 5), (5, 2),),
    ((3, 4), (8, 0), (9, 0),),
    (),
    ((2, 5), (6, 2),),
    ((8, 1), (10, 0), (4, 4), (7, 2), (1, 6), (9, 1), (11, 0),),
    ((3, 5),),
    ((10, 1), (12, 0), (0, 5), (5, 3), (1, 7), (2, 6),),
    ((11, 1), (13, 0),),
    ((4, 5), (7, 3), (6, 3), (2, 7), (8, 2), (12, 1), (14, 0), (13, 1), (15, 0), (5, 4), (3, 6),),
    ((0, 6),),
    ((6, 4), (3, 7), (9, 2), (10, 2), (14, 1), (16, 0),),
    ((0, 7), (5, 5),),
    (),
    ((4, 6),),
    ((6, 5),),
    ((11, 2), (7, 4), (4, 7), (9, 3),),
    (),
    (),
    ((8, 3), (12, 2), (15, 1), (17, 0),),
    ((11, 3),),
    ((14, 2), (16, 1), (18, 0), (17, 1), (19, 0),),
    ((7, 5),),
    ((5, 6), (13, 2),),
    ((19, 1), (8, 4),),
    ((5, 7), (6, 6), (10, 3),),
    (),
    (),
    ((6, 7), (12, 3), (9, 4), (13, 3), (7, 6),),
    (),
    ((10, 4), (14, 3), (12, 4), (7, 7), (8, 5), (15, 2), (18, 1), (20, 0), (21, 0), (11, 4),),
    ((9, 5), (17, 2), (21, 1), (10, 5), (16, 2), (20, 1), (22, 0), (23, 0),),
    ((14, 4), (11, 5), (13, 4), (12, 5), (19, 2), (8, 6),),
    (),
    ((8, 7), (15, 3), (18, 2), (22, 1), (24, 0), (9, 6), (17, 3),),
    ((13, 5), (10, 6),),
    (),
    ((9, 7), (14, 5),),
    ((10, 7), (21, 2), (20, 2), (23, 1), (25, 0), (15, 4), (19, 3), (12, 6), (16, 3),),
    ((25, 1), (18, 3), (12, 7), (11, 6),),
    (),
    ((16, 4), (20, 3), (17, 4), (11, 7), (13, 6), (21, 3),),
    ((18, 4), (14, 6), (15, 5), (22, 2), (24, 1), (26, 0), (27, 0), (25, 2), (13, 7),),
    ((20, 4), (14, 7), (19, 4), (16, 5), (23, 2), (26, 1), (17, 5), (28, 0), (18, 5), (22, 3),),
    ((21, 4), (25, 3), (20, 5), (23, 3), (15, 6), (19, 5), (15, 7), (24, 2), (27, 1), (29, 0), (-1, 0), (22, 4),
     (17, 6), (29, 1), (16, 6), (21, 5), (17, 7), (24, 3), (16, 7), (26, 2), (28, 1), (-1, 1), (30, 0), (23, 4),
     (31, 0), (19, 6), (18, 6), (30, 1), (24, 4), (22, 5), (19, 7), (29, 2), (-1, 2), (18, 7), (25, 4), (26, 3),
     (20, 6), (29, 3), (21, 6), (20, 7), (27, 2), (31, 1), (25, 5), (21, 7), (-1, 3), (23, 5), (30, 2), (28, 2),
     (26, 4), (24, 5), (27, 3), (22, 6), (30, 3), (28, 3), (22, 7), (-1, 4), (29, 4), (27, 4), (25, 6), (31, 2),
     (28, 4), (25, 7), (26, 5), (23, 6), (29, 5), (27, 5), (-1, 5), (31, 3), (23, 7), (24, 6), (28, 5), (24, 7),
     (30, 4), (31, 4), (26, 6), (29, 6), (30, 5), (26, 7), (27, 6), (29, 7), (31, 5), (27, 7), (28, 6), (28, 7),
     (31, 6), (30, 6), (31, 7), (30, 7),),
)


def second_kernel(
    wf_h, ck_h, cv_h, inin_h, latin_h, cq_h, att_h, st_h, vec_h, hone_h, htwo_h,
    mlpin_h, selfin_h, pre_h, hid_h, ds_h, slow_h, mask_h,
    lat_h, inp_h, up_h, down_h, sq_h, sk_h, sv_h, so_h, cot_h,
    newlat_o, glat_o, ginp_o, gq_o, gk_o, gv_o, go_o, gup_o, gdown_o, gsq_o, gsk_o,
    gsv_o, gso_o, gvec_o,
    z, wf, cq, att, st, vecs, hone, htwo, etwo, mlpin, selfin, pre, hid, ds,
    slow, mask, cot, elow2, elow1, dpre, dcr, xb, grad, other, t0, ty, te, tm, tn_mid, tn_y,
    xk, gvec, gvr,
    lsem, osem, gs, gr, xs, xr, vs, vr, free,
):
    me = place()
    x, c = me["x"], me["c"]
    xp, yp, cp, ap, bp = me["xp"], me["yp"], me["cp"], me["ap"], me["bp"]
    counts = [0, 0]
    outs = []

    def load(src, dst):
        copy = pltpu.make_async_copy(src, dst, lsem.at[counts[0]])
        counts[0] += 1
        copy.start()
        return copy

    def store(src, dst):
        copy = pltpu.make_async_copy(src, dst, osem.at[counts[1]])
        counts[1] += 1
        copy.start()
        outs.append(copy)

    in_early = [load(slow_h, slow), load(cot_h, cot), load(selfin_h, selfin)]
    in_ds = load(ds_h, ds)
    in_self = [
        load(sq_h, z.at[pl.ds(4096, D), pl.ds(0, HALF)]),
        load(sk_h, z.at[pl.ds(4096, D), pl.ds(HALF, HALF)]),
        load(sv_h, z.at[pl.ds(5120, D), pl.ds(0, HALF)]),
    ]
    in_early += [
        load(so_h.at[:, pl.ds(j * HALF, HALF)], z.at[pl.ds(5120 + j * HALF, HALF), pl.ds(HALF, HALF)])
        for j in range(2)
    ]
    in_two = [load(htwo_h, htwo), load(vec_h, vecs)]
    in_mlp = [
        load(pre_h, pre), load(down_h, z.at[pl.ds(0, HID)]),
        load(up_h.at[:, pl.ds(0, D)], z.at[pl.ds(HID, D)]),
        load(up_h.at[:, pl.ds(D, D)], z.at[pl.ds(HID + D, D)]),
    ]
    in_mid = [
        load(hid_h.at[:, pl.ds(j * D, D)], hid.at[pl.ds(j * ROWS, ROWS)]) for j in range(2)
    ] + [load(mlpin_h, mlpin), load(hone_h, hone)]
    in_cross = [
        load(wf_h, wf), load(att_h, att), load(st_h, st), load(cq_h, cq), load(mask_h, mask),
    ]
    barrier = pltpu.get_barrier_semaphore()
    for partner in (xp, yp, cp, ap, bp):
        pl.semaphore_signal(barrier, inc=1, device_id=partner, device_id_type=MESH)

    @pl.when(me["a"] != me["b"])
    def _():
        pl.semaphore_signal(barrier, inc=1, device_id=me["mp"], device_id_type=MESH)
        pl.semaphore_wait(barrier, 6)

    @pl.when(me["a"] == me["b"])
    def _():
        pl.semaphore_wait(barrier, 5)


    def wait_all(copies):
        for copy in copies:
            copy.wait()

    a_bit, b_bit, y_bit = me["a"], me["b"], me["y"]
    at_end = a_bit == b_bit
    at_middle = a_bit != b_bit
    mp = me["mp"]

    def cols_of(core):
        return pl.ds(pl.multiple_of(core * HALF, HALF), HALF)

    def block(k, off, size, core):
        return grad.at[pl.ds(pl.multiple_of(k * PART + off, 16), size), cols_of(core)]

    def add(base, size, part):
        def body(i):
            rows = pl.ds(pl.multiple_of(base + i * 64, 64), 64)
            grad[rows, cols_of(c)] += part[pl.ds(pl.multiple_of(i * 64, 64), 64), :]

        loop(size // 64, body)

    def move(k, stage, src, dst, partner):
        return remote(src, dst, gs.at[k * 7 + stage], gr.at[k * 7 + stage], partner)

    def release(k, n, partner):
        pl.semaphore_signal(free.at[k * 4 + n], inc=1, device_id=partner, device_id_type=MESH)

    def claim(k, n):
        pl.semaphore_wait(free.at[k * 4 + n], 1)

    def event(k, s):
        base, size, half = k * PART, PART, PART // 2
        kind = KINDS[k]
        n = KINDS[:k].count(kind)
        everything = block(k, 0, size, c)
        core_in = t0.at[k % t0.shape[0]]
        core_move = move(k, 0, block(k, 0, size, 1 - c), core_in, cp)
        core_back = move(k, 6, everything, everything, cp)
        if s == 0:
            core_move.start()
            return
        if s == 7:
            core_back.wait()
            deliver(k)
            return
        if s == 1:
            core_move.wait()
            if kind == "y":
                release(k, 0, cp)
            else:
                pl.when(at_end)(lambda: release(k, 0, cp))
                pl.when(at_middle)(lambda: release(k, 3, ap))
            add(base, size, core_in)
            if k >= 28:
                finish_x((k - 28) // 2, k % 2)
        if kind == "y":
            off = y_bit * half
            own = block(k, off, half, c)
            y_in, end_in, mid_in = (
                ty.at[n % ty.shape[0]], te.at[n % te.shape[0]], tm.at[n % tm.shape[0]]
            )
            y_move = move(k, 1, block(k, (1 - y_bit) * half, half, c), y_in, yp)
            end_move = move(k, 2, own, end_in, ap)
            mid_move = move(k, 3, own, mid_in, mp)
            end_back = move(k, 4, own, own, ap)
            y_back = move(k, 5, own, own, yp)
            if s == 1:
                y_move.start()
            elif s == 2:
                y_move.wait()
                release(k, 1, yp)
                add(base + off, half, y_in)
                pl.when(at_end)(end_move.start)
            elif s == 3:
                @pl.when(at_end)
                def _():
                    end_move.wait_send()
                    release(k, 2, ap)

                @pl.when(at_middle)
                def _():
                    end_move.wait_recv()
                    add(base + off, half, end_in)
                    mid_move.start()
            elif s == 4:
                @pl.when(at_middle)
                def _():
                    mid_move.wait()
                    add(base + off, half, mid_in)
                    claim(k, 2)
                    end_back.start()
            elif s == 5:
                pl.when(at_end)(end_back.wait_recv)
                pl.when(at_middle)(end_back.wait_send)
                claim(k, 1)
                y_back.start()
            elif s == 6:
                y_back.wait()
                claim(k, 0)
                core_back.start()
            return
        off = b_bit * half
        own = block(k, off, half, c)
        mid_in, y_in = tn_mid.at[n % tn_mid.shape[0]], tn_y.at[n % tn_y.shape[0]]
        end_in = block(k, 0, size, 1 - c)
        end_move = move(k, 1, everything, end_in, ap)
        mid_move = move(k, 2, block(k, (1 - b_bit) * half, half, c), mid_in, mp)
        y_move = move(k, 3, own, y_in, yp)
        mid_back = move(k, 4, own, own, mp)
        end_back = move(k, 5, everything, everything, ap)
        if s == 1:
            @pl.when(at_end)
            def _():
                claim(k, 3)
                end_move.start()
        elif s == 2:
            @pl.when(at_end)
            def _():
                end_move.wait_send()
                release(k, 1, ap)

            @pl.when(at_middle)
            def _():
                end_move.wait_recv()
                add(base, size, end_in)
                release(k, 0, cp)
                mid_move.start()
        elif s == 3:
            @pl.when(at_middle)
            def _():
                mid_move.wait()
                release(k, 2, mp)
                add(base + off, half, mid_in)
                y_move.start()
        elif s == 4:
            @pl.when(at_middle)
            def _():
                y_move.wait()
                add(base + off, half, y_in)
                claim(k, 2)
                mid_back.start()
        elif s == 5:
            @pl.when(at_middle)
            def _():
                mid_back.wait()
                claim(k, 1)
                end_back.start()
        elif s == 6:
            pl.when(at_end)(end_back.wait_recv)
            pl.when(at_middle)(end_back.wait_send)
            claim(k, 0)
            core_back.start()

    def deliver(k):
        n, top = k // 2, (k % 2) * PART
        rows = pl.ds(k * PART, PART)
        left, right = grad.at[rows, pl.ds(0, HALF)], grad.at[rows, pl.ds(HALF, HALF)]
        first, second = pl.ds(top, PART), pl.ds(HALF + top, PART)
        if 1 <= n <= 3:
            target = (gsq_o, gsk_o, gsv_o)[n - 1]
            store(left, target.at[first])
            store(right, target.at[second])
        elif 8 <= n <= 11:
            cols = pl.ds((n - 8) * HALF, HALF)
            store(left, gup_o.at[first, cols])
            store(right, gup_o.at[second, cols])
        elif 4 <= n <= 7:
            store(grad.at[rows], gdown_o.at[pl.ds((n - 4) * HALF + top, PART)])
        else:
            target = {0: gso_o, 12: go_o, 13: gq_o, 14: gk_o, 15: gv_o}[n]
            store(grad.at[rows], target.at[first])

    k_moves = {}

    def start_core(w):
        src = other.at[w, :, pl.ds(pl.multiple_of((1 - c) * HALF, HALF), HALF)]
        move = remote(src, hid.at[:, pl.ds(w * HALF, HALF)], xs.at[8 + w], xr.at[8 + w], cp)
        move.start()
        k_moves[w, 0] = move

    def start_x(w):
        k_moves[w, 0].wait()
        cols = pl.ds(pl.multiple_of(c * HALF, HALF), HALF)

        def body(i):
            rows = pl.ds(pl.multiple_of(i * 64, 64), 64)
            other[w, rows, cols] = (
                other[w, rows, cols].astype(F32) + hid[rows, w * HALF:(w + 1) * HALF].astype(F32)
            ).astype(BF)

        loop(HALF // 64, body)
        move = remote(other.at[w, :, cols], xk.at[w], xs.at[10 + w], xr.at[10 + w], xp)
        move.start()
        k_moves[w, 1] = move

    def finish_x(w, part):
        if (w, 1) in k_moves:
            k_moves.pop((w, 1)).wait()
        add((14 + w) * HALF + part * 256, 256, xk.at[w, pl.ds(part * 256, 256)])

    def exchange(n, part, index):
        move = remote(
            xb.at[(n, x) + part], xb.at[(n, x) + part], xs.at[index], xr.at[index], xp
        )
        move.start()
        return move

    def both(n, rows):
        return xb[n, 0, rows, :].astype(F32) + xb[n, 1, rows, :].astype(F32)

    def fill(k, half, value):
        grad[k * HALF:(k + 1) * HALF, half * HALF:(half + 1) * HALF] = value.astype(BF)

    gvec[...] = jnp.zeros_like(gvec)
    lat, latin, dcq = cot, mlpin, elow2
    ck, cv = z.at[pl.ds(0, NROWS)], z.at[pl.ds(NROWS, NROWS)]
    inin, inp = z.at[pl.ds(2 * NROWS, NROWS)], z.at[pl.ds(3 * NROWS, NROWS)]
    gain_lat, gain_inp, gain_mlp, gain_self = 0, 2, 4, 6
    m_self, m_new, m_mlp, m_query, later = [], [], [], [], {}

    def self_back(j):
        if j == 0:
            wait_all(in_self)
        cols = slice(j * HALF, (j + 1) * HALF)
        a_rows = slice(4096 + j * HALF, 4096 + (j + 1) * HALF)
        b_rows = slice(5120 + j * HALF, 5120 + (j + 1) * HALF)
        xb[0, x, :, cols] = (
            nt(ds[0], z[a_rows, 0:HALF]) + nt(ds[1], z[a_rows, HALF:D]) + nt(ds[2], z[b_rows, 0:HALF])
        ).astype(BF)
        m_self.append(exchange(0, (slice(None), pl.ds(j * HALF, HALF)), j))

    def fill_self(n):
        if n == 0:
            wait_all(in_early)
            in_ds.wait()
        for j in range(2):
            cols = slice(j * HALF, (j + 1) * HALF)
            fill(n, j, tn(slow[...], cot[:, cols]) if n == 0 else tn(selfin[:, cols], ds[n - 1]))

    def new_part():
        for j in range(2):
            cols = slice(j * HALF, (j + 1) * HALF)
            rows = slice(5120 + j * HALF, 5120 + (j + 1) * HALF)
            xb[1, x, :, cols] = nn(slow[...], z[rows, HALF:D]).astype(BF)
            m_new.append(exchange(1, (slice(None), pl.ds(j * HALF, HALF)), 2 + j))

    def two_back():
        wait_all(in_two)
        wait_all(m_self)
        gain = vec_row(vecs, gain_self)

        def body(i):
            rows = pl.ds(pl.multiple_of(i * 32, 32), 32)
            dv, dg, db = norm_back(htwo[rows, :], both(0, rows), gain)
            e = cot[rows, :].astype(F32) + dv
            etwo[rows, :] = e
            elow2[rows, :] = e.astype(BF)
            gvec[6:7, :] += dg
            gvec[7:8, :] += db

        loop(8, body)
        later["lat"] = load(lat_h, lat)

    def hidden_back(j):
        if j == 0:
            wait_all(in_mlp)
        cols = slice(j * HALF, (j + 1) * HALF)
        gh = nt(elow2[...], z[cols, :])
        dpre[:, cols] = (gh * gelu_slope(pre[:, cols])).astype(BF)

    def mlp_back(j):
        cols = slice(j * HALF, (j + 1) * HALF)
        xb[2, x, :, cols] = (
            nt(dpre[:, 0:D], z[HID + j * HALF:HID + (j + 1) * HALF, :])
            + nt(dpre[:, D:HID], z[HID + D + j * HALF:HID + D + (j + 1) * HALF, :])
        ).astype(BF)
        m_mlp.append(exchange(2, (slice(None), pl.ds(j * HALF, HALF)), 4 + j))
        if j == 0:
            return
        later["keys"] = [load(ck_h, ck), load(cv_h, cv)]
        later["inputs"] = [load(inin_h, inin), load(inp_h, inp)]
        wait_all(in_mid)

    def fill_down(j):
        for i in range(2):
            part = hid[(j // 2) * ROWS:(j // 2 + 1) * ROWS, (j % 2) * HALF:(j % 2 + 1) * HALF]
            fill(4 + j, i, tn(part, elow2[:, i * HALF:(i + 1) * HALF]))

    def fill_up(j):
        for i in range(2):
            fill(8 + j, i, tn(mlpin[:, i * HALF:(i + 1) * HALF], dpre[:, j * HALF:(j + 1) * HALF]))

    def one_back():
        later["latin"] = load(latin_h, latin)
        wait_all(m_mlp)
        gain = vec_row(vecs, gain_mlp)

        def body(i):
            rows = pl.ds(pl.multiple_of(i * 32, 32), 32)
            dv, dg, db = norm_back(hone[rows, :], both(2, rows), gain)
            e = etwo[rows, :] + dv
            hone[rows, :] = e
            elow1[rows, :] = e.astype(BF)
            gvec[4:5, :] += dg
            gvec[5:6, :] += db

        loop(8, body)

    def cross_back():
        wait_all(in_cross)
        for g in range(2):
            dcr[g * D:(g + 1) * D, :] = nt(wf[3], elow1[g * LAT:(g + 1) * LAT, :]).astype(BF)

    def fill_output():
        for j in range(2):
            value = 0.0
            for g in range(2):
                rows = pl.ds(pl.multiple_of(g * D + x * HALF, HALF), HALF)
                value = value + nn(
                    att[rows, :], elow1[g * LAT:(g + 1) * LAT, j * HALF:(j + 1) * HALF]
                )
            fill(12, j, value)

    def new_latents():
        wait_all(m_new)

        def body(i):
            rows = pl.ds(pl.multiple_of(i * 64, 64), 64)
            selfin[rows, :] = (htwo[rows, :] + both(1, rows)).astype(BF)

        loop(4, body)
        store(selfin, newlat_o)
        wait_all(later["keys"])

    def head(g, h):
        cols = slice(h * HEAD_DIM, (h + 1) * HEAD_DIM)
        n_rows = slice(g * INP, (g + 1) * INP)
        l_rows = slice(g * LAT, (g + 1) * LAT)
        t_rows = slice(g * D + h * HEAD_DIM, g * D + (h + 1) * HEAD_DIM)
        k, v, q = ck[n_rows, cols], cv[n_rows, cols], cq[l_rows, cols]
        s = nt(k, q) * SCALE + mask[n_rows, :].astype(F32)
        p = jnp.exp(s - st[g, h:h + 1, :]) * st[g, HEADS + h:HEADS + h + 1, :]
        do = dcr[t_rows, :]
        delta = jnp.sum(do.astype(F32) * att[t_rows, :].astype(F32), axis=0, keepdims=True)
        dsc = (p * (nn(v, do) - delta)).astype(BF)
        cv[n_rows, cols] = nt(p.astype(BF), do).astype(BF)
        ck[n_rows, cols] = (nn(dsc, q) * SCALE).astype(BF)
        xb[0, x, l_rows, cols] = (tn(dsc, k) * SCALE).astype(BF)

    def heads_back(g, h):
        head(g, h)
        if h == HEADS - 1:
            m_query.append(exchange(0, (pl.ds(g * LAT, LAT),), 6 + g))

    def weight_grad(w, i):
        if w == 0 and i == 0:
            wait_all(later["inputs"])
        source = (ck, cv)[w]
        rows = slice(i * 256, (i + 1) * 256)
        mine = pl.ds(pl.multiple_of(x * HALF + i * 256, 256), 256)
        theirs = pl.ds(pl.multiple_of((1 - x) * HALF + i * 256, 256), 256)
        other[w, rows, :] = tn(inin[:, theirs], source[...]).astype(BF)
        grad[(14 + w) * HALF + i * 256:(14 + w) * HALF + (i + 1) * 256, :] = tn(
            inin[:, mine], source[...]
        ).astype(BF)
        if i == 1:
            start_core(w)

    def fill_query():
        wait_all(m_query)
        later["latin"].wait()

        def body(i):
            rows = pl.ds(pl.multiple_of(i * 64, 64), 64)
            dcq[rows, :] = both(0, rows).astype(BF)

        loop(4, body)
        for j in range(2):
            mine = pl.ds(pl.multiple_of(x * HALF, HALF), HALF)
            fill(13, j, tn(latin[:, mine], dcq[:, j * HALF:(j + 1) * HALF]))

    def latents_back():
        gain = vec_row(vecs, gain_lat)
        later["lat"].wait()

        def body(i):
            rows = pl.ds(pl.multiple_of(i * 128, 128), 128)
            dv, dg, db = norm_back(lat[rows, :].astype(F32), nt(dcq[rows, :], wf[2]), gain)
            lat[rows, :] = (hone[rows, :] + dv).astype(BF)
            gvec[0:1, :] += dg
            gvec[1:2, :] += db

        loop(2, body)
        store(lat, glat_o)

    def inputs_back(i):
        rows = slice(i * 224, (i + 1) * 224)
        dy = nt(ck[rows, :], wf[0]) + nt(cv[rows, :], wf[1])
        dv, dg, db = norm_back(inp[rows, :].astype(F32), dy, vec_row(vecs, gain_inp))
        inp[rows, :] = dv.astype(BF)
        gvec[2:3, :] += dg
        gvec[3:4, :] += db
        if i == 6:
            store(inp, ginp_o)
            col = lax.broadcasted_iota(jnp.int32, (8, D), 1) // HALF
            row = lax.broadcasted_iota(jnp.int32, (8, D), 0)
            keep = (col == x) | (row == 2) | (row == 3)
            gvec[...] = jnp.where(keep, gvec[...], 0.0)

    v_partners = (xp, cp, yp, ap, bp)
    v_moves = []

    def vec_event(s):
        if s > 0:
            v_moves[s - 1].wait()
            gvec[...] += gvr[s - 1]
        if s < 5:
            move = remote(gvec, gvr.at[s], vs.at[s], vr.at[s], v_partners[s])
            move.start()
            v_moves.append(move)
        else:
            store(gvec, gvec_o)

    steps = [lambda: fill_self(0), lambda: fill_self(1), lambda: self_back(0), lambda: self_back(1)]
    steps += [lambda: fill_self(2), lambda: fill_self(3)]
    steps += [new_part, two_back]
    steps += [lambda j=j: hidden_back(j) for j in range(4)]
    steps += [lambda: mlp_back(0), lambda: mlp_back(1)]
    steps += [lambda j=j: fill_down(j) for j in range(4)]
    steps += [lambda j=j: fill_up(j) for j in range(4)]
    steps += [one_back, cross_back, fill_output, new_latents]
    steps += [lambda g=g, h=h: heads_back(g, h) for g in range(2) for h in range(HEADS)]
    steps += [lambda i=i: weight_grad(0, i) for i in range(2)]
    steps += [lambda: weight_grad(1, 0), lambda: start_x(0), lambda: weight_grad(1, 1)]
    steps += [fill_query, lambda: start_x(1), latents_back]
    steps += [lambda i=i: inputs_back(i) for i in range(7)]
    for step, events in zip(steps, EVENTS, strict=True):
        step()
        for k, s in events:
            if k < 0:
                vec_event(s)
            else:
                event(k, s)
    wait_all(outs)


def run_second(args):
    any_spec = pl.BlockSpec(memory_space=pl.ANY)
    outs = [
        ((ROWS, D), BF), ((ROWS, D), BF), ((NROWS, D), BF), ((HALF, D), BF), ((HALF, D), BF),
        ((HALF, D), BF), ((HALF, D), BF), ((D, HID), BF), ((HID, D), BF), ((D, HALF), BF),
        ((D, HALF), BF), ((D, HALF), BF), ((HALF, D), BF), ((8, D), F32),
    ]
    scratch = [
        ((4 * NROWS, D), BF), ((4, D, D), BF), ((ROWS, D), BF),
        ((2 * D, LAT), BF), ((2, 16, LAT), F32), ((2, 8, HALF), F32), ((ROWS, D), F32),
        ((ROWS, D), F32), ((ROWS, D), F32), ((ROWS, D), BF), ((ROWS, D), BF), ((ROWS, HID), F32),
        ((2 * ROWS, D), BF), ((3, ROWS, HALF), BF), ((ROWS, HALF), BF), ((NROWS, LAT), BF),
        ((ROWS, D), BF), ((ROWS, D), BF), ((ROWS, D), BF), ((ROWS, HID), BF),
        ((2 * D, LAT), BF), ((3, 2, ROWS, D), BF), ((16 * HALF, D), BF), ((2, HALF, D), BF),
        ((SLOTS[0], PART, HALF), BF), *[((n, PART // 2, HALF), BF) for n in SLOTS[1:]],
        ((2, HALF, HALF), BF), ((8, D), F32),
        ((5, 8, D), F32),
    ]
    dma = pltpu.SemaphoreType.DMA
    return pl.pallas_call(
        second_kernel,
        out_shape=[jax.ShapeDtypeStruct(*o) for o in outs],
        in_specs=[any_spec] * len(args),
        out_specs=[any_spec] * len(outs),
        scratch_shapes=[pltpu.VMEM(*s) for s in scratch]
        + [dma((40,)), dma((64,))] + [dma((32 * 7,))] * 2 + [dma((12,))] * 2 + [dma((5,))] * 2
        + [pltpu.SemaphoreType.REGULAR((128,))],
        compiler_params=pltpu.CompilerParams(
            collective_id=1, has_side_effects=True, vmem_limit_bytes=63 * MIB
        ),
        name="backward",
    )(*args)


def finish_kernel(*refs):
    srcs, gvec, dsts, small = refs[:13], refs[13], refs[14:27], refs[27:35]
    low, wide, insem, outsem = refs[35:]
    tiles = []
    for i in (*range(3, 13), 0, 1, 2):
        rows, cols = srcs[i].shape
        for r in range(0, rows, 256):
            count = min(256, rows - r)
            tiles.append((i, pl.ds(r, count), (pl.ds(0, count), pl.ds(0, cols))))
    depth = low.shape[0]
    ins, outs, finished = {}, {}, set()

    def finish_out(n):
        if n >= 0 and n not in finished:
            outs[n].wait()
            finished.add(n)

    def start_in(n):
        i, rows, part = tiles[n]
        ins[n] = pltpu.make_async_copy(srcs[i].at[rows], low.at[n % depth, *part], insem.at[n % depth])
        ins[n].start()

    for n in range(depth):
        start_in(n)
    first = lax.axis_index("shard") == 0
    mine = jnp.where(first, gvec[:, 0:HALF], gvec[:, HALF:D])
    for i in range(8):
        small[i][...] = mine[i]
    for n in range(len(tiles)):
        slot = n % depth
        i, rows, part = tiles[n]
        ins[n].wait()
        finish_out(n - depth)
        if i < 3:
            outs[n] = pltpu.make_async_copy(low.at[slot, *part], dsts[i].at[rows], outsem.at[slot])
            outs[n].start()
        else:
            cols = part[1]

            def body(i, slot=slot, cols=cols):
                rows = pl.ds(pl.multiple_of(i * 32, 32), 32)
                wide[slot, rows, cols] = low[slot, rows, cols].astype(F32)

            loop(8, body)
            outs[n] = pltpu.make_async_copy(wide.at[slot, *part], dsts[i].at[rows], outsem.at[slot])
            outs[n].start()
        if n + depth < len(tiles):
            if i < 3:
                finish_out(n)
            start_in(n + depth)
    for n in range(len(tiles) - depth, len(tiles)):
        finish_out(n)


def run_finish(args):
    any_spec = pl.BlockSpec(memory_space=pl.ANY)
    vmem_spec = pl.BlockSpec(memory_space=pltpu.VMEM)
    depth = 6
    return pl.pallas_call(
        finish_kernel,
        out_shape=[
            jax.ShapeDtypeStruct(a.shape, BF if i < 3 else F32) for i, a in enumerate(args[:13])
        ] + [jax.ShapeDtypeStruct((HALF,), F32)] * 8,
        in_specs=[any_spec] * 13 + [vmem_spec],
        out_specs=[any_spec] * 13 + [vmem_spec] * 8,
        scratch_shapes=[
            pltpu.VMEM((depth, 256, HID), BF), pltpu.VMEM((depth, 256, HID), F32),
            pltpu.SemaphoreType.DMA((depth,)), pltpu.SemaphoreType.DMA((depth,)),
        ],
        compiler_params=pltpu.CompilerParams(vmem_limit_bytes=62 * MIB),
        name="finish",
    )(*args)


def per_device_pair(
    latents, inputs, latent_segment, input_segment, cross_query, cross_key, cross_value,
    cross_output, mlp_up, mlp_down, self_query, self_key, self_value, self_output,
    latent_gain, latent_bias, input_gain, input_bias, mlp_gain, mlp_bias, self_gain,
    self_bias, cotangent,
):
    vec = (
        latent_gain, latent_bias, input_gain, input_bias, mlp_gain, mlp_bias, self_gain, self_bias
    )
    lat = latents.reshape(ROWS, D)
    inp = inputs.reshape(NROWS, D)
    cot = cotangent.reshape(ROWS, D)
    kept = run_first((
        lat, inp, latent_segment, input_segment, *vec, cross_key, cross_value, cross_query,
        cross_output, mlp_up, mlp_down, self_query, self_key, self_value, self_output, cot,
    ))
    (new, glat, ginp, gq, gk, gv, go, gup, gdown, gsq, gsk, gsv, gso, gvec) = run_second(
        tuple(kept) + (
            lat, inp, mlp_up, mlp_down, self_query, self_key, self_value, self_output, cot
        )
    )
    new, glat, ginp, *grads = run_finish(
        (new, glat, ginp, gq, gk, gv, go, gup, gdown, gsq, gsk, gsv, gso, gvec)
    )
    return (
        new.reshape(latents.shape), glat.reshape(latents.shape), ginp.reshape(inputs.shape), *grads
    )


def norm_forward(values, gain, shift):
    centred = values - jnp.mean(values, axis=-1, keepdims=True)
    inv_std = lax.rsqrt(jnp.mean(centred * centred, axis=-1, keepdims=True) + EPSILON)
    normed = centred * inv_std
    return (normed * gain + shift, normed, inv_std)


def norm_backward(grad_out, normed, inv_std, gain):
    scaled = grad_out * gain
    first_mean = jnp.mean(scaled, axis=-1, keepdims=True)
    second_mean = jnp.mean(scaled * normed, axis=-1, keepdims=True)
    grad_in = inv_std * (scaled - first_mean - normed * second_mean)
    return (grad_in, jnp.sum(grad_out * normed, axis=0), jnp.sum(grad_out, axis=0))


def product(left, right):
    return jnp.dot(left, right, preferred_element_type=jnp.float32)


def inner_rows(left, right):
    return lax.dot_general(
        left, right, (((0,), (0,)), ((), ())), preferred_element_type=jnp.float32
    )


def outer_cols(left, right):
    return lax.dot_general(
        left, right, (((1,), (1,)), ((), ())), preferred_element_type=jnp.float32
    )


def forward_total(term):
    return lax.psum(term.astype(jnp.bfloat16), "shard").astype(jnp.float32)


def backward_total(term):
    return lax.psum(term.astype(jnp.bfloat16), "shard").astype(jnp.float32)


def per_device(
    latents,
    inputs,
    latent_segment,
    input_segment,
    cross_query,
    cross_key,
    cross_value,
    cross_output,
    mlp_up,
    mlp_down,
    self_query,
    self_key,
    self_value,
    self_output,
    latent_gain,
    latent_bias,
    input_gain,
    input_bias,
    mlp_gain,
    mlp_bias,
    self_gain,
    self_bias,
    cotangent,
):
    shards = lax.axis_size("shard")
    groups, lat_len, width = latents.shape
    inp_len = inputs.shape[1]
    width_part = width // shards
    column_start = lax.axis_index("shard") * width_part
    rows = groups * lat_len
    scale = HEAD_DIM ** (-0.5)
    gathered = (
        lax.all_gather(cross_query, "shard", axis=0, tiled=True),
        lax.all_gather(cross_key, "shard", axis=0, tiled=True),
        lax.all_gather(cross_value, "shard", axis=0, tiled=True),
        lax.all_gather(cross_output, "shard", axis=0, tiled=True),
        lax.all_gather(latent_gain, "shard", axis=0, tiled=True),
        lax.all_gather(latent_bias, "shard", axis=0, tiled=True),
        lax.all_gather(input_gain, "shard", axis=0, tiled=True),
        lax.all_gather(input_bias, "shard", axis=0, tiled=True),
        lax.all_gather(mlp_gain, "shard", axis=0, tiled=True),
        lax.all_gather(mlp_bias, "shard", axis=0, tiled=True),
        lax.all_gather(self_gain, "shard", axis=0, tiled=True),
        lax.all_gather(self_bias, "shard", axis=0, tiled=True),
    )
    full_query, full_key, full_value, full_output = (
        gathered[0],
        gathered[1],
        gathered[2],
        gathered[3],
    )
    gain_lat, bias_lat, gain_inp, bias_inp, gain_mlp, bias_mlp, gain_self, bias_self = [
        piece.astype(jnp.float32) for piece in gathered[4:]
    ]
    lat_rows = latents.astype(jnp.float32).reshape(rows, width)
    inp_rows = inputs.astype(jnp.float32).reshape(groups * inp_len, width)
    lat_value, lat_normed, lat_inv = norm_forward(lat_rows, gain_lat, bias_lat)
    lat_in = lat_value.astype(jnp.bfloat16)
    inp_value, inp_normed, inp_inv = norm_forward(inp_rows, gain_inp, bias_inp)
    inp_in = inp_value.astype(jnp.bfloat16)
    cross_q = (
        product(lat_in, full_query).astype(jnp.bfloat16).reshape(groups, lat_len, HEADS, HEAD_DIM)
    )
    cross_k = (
        product(inp_in, full_key).astype(jnp.bfloat16).reshape(groups, inp_len, HEADS, HEAD_DIM)
    )
    cross_v = (
        product(inp_in, full_value).astype(jnp.bfloat16).reshape(groups, inp_len, HEADS, HEAD_DIM)
    )
    allowed = latent_segment[:, None, :, None] == input_segment[:, None, None, :]
    scores = (
        jnp.einsum("glhd,gnhd->ghln", cross_q, cross_k, preferred_element_type=jnp.float32) * scale
    )
    masked = jnp.where(allowed, scores, NEGATIVE)
    part_max = jnp.max(masked, axis=-1)
    top = lax.pmax(part_max, "shard")
    total = lax.psum(
        jnp.sum(jnp.where(allowed, jnp.exp(masked - top[..., None]), 0.0), axis=-1), "shard"
    )
    cross_prob = jnp.where(allowed, jnp.exp(masked - top[..., None]), 0.0) / total[..., None]
    cross_prob_low = cross_prob.astype(jnp.bfloat16)
    part_out = jnp.einsum(
        "ghln,gnhd->glhd", cross_prob_low, cross_v, preferred_element_type=jnp.float32
    )
    attended = lax.psum(part_out.astype(jnp.bfloat16), "shard").astype(jnp.float32)
    attended_in = attended.reshape(rows, width).astype(jnp.bfloat16)
    h_one = lat_rows + product(attended_in, full_output)
    mlp_value, mlp_normed, mlp_inv = norm_forward(h_one, gain_mlp, bias_mlp)
    mlp_in = mlp_value.astype(jnp.bfloat16)
    pre_act = product(mlp_in, mlp_up)
    hidden_in = jax.nn.gelu(pre_act).astype(jnp.bfloat16)
    h_two = h_one + forward_total(product(hidden_in, mlp_down))
    self_value_n, self_normed, self_inv = norm_forward(h_two, gain_self, bias_self)
    self_in = self_value_n.astype(jnp.bfloat16)
    local_heads = self_query.shape[1] // HEAD_DIM
    local_width = local_heads * HEAD_DIM
    self_q = (
        product(self_in, self_query)
        .astype(jnp.bfloat16)
        .reshape(groups, lat_len, local_heads, HEAD_DIM)
    )
    self_k = (
        product(self_in, self_key)
        .astype(jnp.bfloat16)
        .reshape(groups, lat_len, local_heads, HEAD_DIM)
    )
    self_v = (
        product(self_in, self_value)
        .astype(jnp.bfloat16)
        .reshape(groups, lat_len, local_heads, HEAD_DIM)
    )
    self_scores = (
        jnp.einsum("glhd,gmhd->ghlm", self_q, self_k, preferred_element_type=jnp.float32) * scale
    )
    self_prob = jax.nn.softmax(self_scores, axis=-1)
    self_prob_low = self_prob.astype(jnp.bfloat16)
    self_att = jnp.einsum(
        "ghlm,gmhd->glhd", self_prob_low, self_v, preferred_element_type=jnp.float32
    )
    self_att_in = self_att.reshape(rows, local_width).astype(jnp.bfloat16)
    result = h_two + forward_total(product(self_att_in, self_output))
    new_latents = result.reshape(groups, lat_len, width).astype(jnp.bfloat16)
    grad_out = cotangent.astype(jnp.float32).reshape(rows, width)
    grad_branch = grad_out.astype(jnp.bfloat16)
    grad_self_output = inner_rows(self_att_in, grad_branch)
    grad_att = (
        outer_cols(grad_branch, self_output)
        .astype(jnp.bfloat16)
        .reshape(groups, lat_len, local_heads, HEAD_DIM)
    )
    delta = jnp.sum(grad_att.astype(jnp.float32) * self_att, axis=-1).transpose(0, 2, 1)
    grad_prob = jnp.einsum("glhd,gmhd->ghlm", grad_att, self_v, preferred_element_type=jnp.float32)
    grad_sv = jnp.einsum(
        "ghlm,glhd->gmhd", self_prob_low, grad_att, preferred_element_type=jnp.float32
    )
    grad_scores = (self_prob * (grad_prob - delta[..., None])).astype(jnp.bfloat16)
    grad_sq = (
        jnp.einsum("ghlm,gmhd->glhd", grad_scores, self_k, preferred_element_type=jnp.float32)
        * scale
    )
    grad_sk = (
        jnp.einsum("ghlm,glhd->gmhd", grad_scores, self_q, preferred_element_type=jnp.float32)
        * scale
    )
    grad_sq = grad_sq.astype(jnp.bfloat16).reshape(rows, local_width)
    grad_sk = grad_sk.astype(jnp.bfloat16).reshape(rows, local_width)
    grad_sv = grad_sv.astype(jnp.bfloat16).reshape(rows, local_width)
    grad_self_query = inner_rows(self_in, grad_sq)
    grad_self_key = inner_rows(self_in, grad_sk)
    grad_self_value = inner_rows(self_in, grad_sv)
    grad_self_in = backward_total(
        outer_cols(grad_sq, self_query)
        + outer_cols(grad_sk, self_key)
        + outer_cols(grad_sv, self_value)
    )
    grad_norm, gain_full, bias_full = norm_backward(grad_self_in, self_normed, self_inv, gain_self)
    grad_two = grad_out + grad_norm
    grad_self_gain = lax.dynamic_slice_in_dim(gain_full, column_start, width_part)
    grad_self_bias = lax.dynamic_slice_in_dim(bias_full, column_start, width_part)
    grad_mlp_branch = grad_two.astype(jnp.bfloat16)
    grad_mlp_down = inner_rows(hidden_in, grad_mlp_branch)
    grad_hidden = outer_cols(grad_mlp_branch, mlp_down)
    gelu_value, gelu_pull = jax.vjp(jax.nn.gelu, pre_act)
    grad_pre = gelu_pull(grad_hidden)[0].astype(jnp.bfloat16)
    grad_mlp_up = inner_rows(mlp_in, grad_pre)
    grad_mlp_in = backward_total(outer_cols(grad_pre, mlp_up))
    grad_norm, gain_full, bias_full = norm_backward(grad_mlp_in, mlp_normed, mlp_inv, gain_mlp)
    grad_one = grad_two + grad_norm
    grad_mlp_gain = lax.dynamic_slice_in_dim(gain_full, column_start, width_part)
    grad_mlp_bias = lax.dynamic_slice_in_dim(bias_full, column_start, width_part)
    grad_cross_branch = grad_one.astype(jnp.bfloat16)
    grad_cross_output = inner_rows(
        lax.dynamic_slice_in_dim(attended_in, column_start, width_part, 1), grad_cross_branch
    )
    grad_ca = (
        outer_cols(grad_cross_branch, full_output)
        .astype(jnp.bfloat16)
        .reshape(groups, lat_len, HEADS, HEAD_DIM)
    )
    cross_delta = jnp.sum(grad_ca.astype(jnp.float32) * attended, axis=-1).transpose(0, 2, 1)
    grad_cp = jnp.einsum("glhd,gnhd->ghln", grad_ca, cross_v, preferred_element_type=jnp.float32)
    grad_cv = jnp.einsum(
        "ghln,glhd->gnhd", cross_prob_low, grad_ca, preferred_element_type=jnp.float32
    )
    grad_cs = (cross_prob * (grad_cp - cross_delta[..., None])).astype(jnp.bfloat16)
    grad_cq_part = (
        jnp.einsum("ghln,gnhd->glhd", grad_cs, cross_k, preferred_element_type=jnp.float32) * scale
    )
    grad_ck = (
        jnp.einsum("ghln,glhd->gnhd", grad_cs, cross_q, preferred_element_type=jnp.float32) * scale
    )
    grad_cq = backward_total(grad_cq_part.reshape(rows, width)).astype(jnp.bfloat16)
    grad_ck = grad_ck.astype(jnp.bfloat16).reshape(groups * inp_len, width)
    grad_cv = grad_cv.astype(jnp.bfloat16).reshape(groups * inp_len, width)
    grad_cross_query = inner_rows(
        lax.dynamic_slice_in_dim(lat_in, column_start, width_part, 1), grad_cq
    )
    grad_lat_in = outer_cols(grad_cq, full_query)
    grad_norm, gain_full, bias_full = norm_backward(grad_lat_in, lat_normed, lat_inv, gain_lat)
    grad_latents = (grad_one + grad_norm).reshape(groups, lat_len, width).astype(jnp.bfloat16)
    grad_latent_gain = lax.dynamic_slice_in_dim(gain_full, column_start, width_part)
    grad_latent_bias = lax.dynamic_slice_in_dim(bias_full, column_start, width_part)
    key_term = inner_rows(inp_in, grad_ck)
    value_term = inner_rows(inp_in, grad_cv)
    grad_inp_in = outer_cols(grad_ck, full_key) + outer_cols(grad_cv, full_value)
    grad_inp, inp_gain_full, inp_bias_full = norm_backward(
        grad_inp_in, inp_normed, inp_inv, gain_inp
    )
    grad_inputs = grad_inp.reshape(groups, inp_len, width).astype(jnp.bfloat16)
    grad_cross_key, grad_cross_value, grad_input_gain, grad_input_bias = (
        lax.psum_scatter(
            key_term.astype(jnp.bfloat16), "shard", scatter_dimension=0, tiled=True
        ).astype(jnp.float32),
        lax.psum_scatter(
            value_term.astype(jnp.bfloat16), "shard", scatter_dimension=0, tiled=True
        ).astype(jnp.float32),
        lax.psum_scatter(
            inp_gain_full.astype(jnp.bfloat16), "shard", scatter_dimension=0, tiled=True
        ).astype(jnp.float32),
        lax.psum_scatter(
            inp_bias_full.astype(jnp.bfloat16), "shard", scatter_dimension=0, tiled=True
        ).astype(jnp.float32),
    )
    (
        grad_cross_query,
        grad_cross_key,
        grad_cross_value,
        grad_cross_output,
        grad_mlp_up,
        grad_mlp_down,
        grad_self_query,
        grad_self_key,
        grad_self_value,
        grad_self_output,
        grad_latent_gain,
        grad_latent_bias,
        grad_input_gain,
        grad_input_bias,
        grad_mlp_gain,
        grad_mlp_bias,
        grad_self_gain,
        grad_self_bias,
    ) = (
        lax.psum(grad_cross_query.astype(jnp.bfloat16), "grp").astype(jnp.float32),
        lax.psum(grad_cross_key.astype(jnp.bfloat16), "grp").astype(jnp.float32),
        lax.psum(grad_cross_value.astype(jnp.bfloat16), "grp").astype(jnp.float32),
        lax.psum(grad_cross_output.astype(jnp.bfloat16), "grp").astype(jnp.float32),
        lax.psum(grad_mlp_up.astype(jnp.bfloat16), "grp").astype(jnp.float32),
        lax.psum(grad_mlp_down.astype(jnp.bfloat16), "grp").astype(jnp.float32),
        lax.psum(grad_self_query.astype(jnp.bfloat16), "grp").astype(jnp.float32),
        lax.psum(grad_self_key.astype(jnp.bfloat16), "grp").astype(jnp.float32),
        lax.psum(grad_self_value.astype(jnp.bfloat16), "grp").astype(jnp.float32),
        lax.psum(grad_self_output.astype(jnp.bfloat16), "grp").astype(jnp.float32),
        lax.psum(grad_latent_gain.astype(jnp.bfloat16), "grp").astype(jnp.float32),
        lax.psum(grad_latent_bias.astype(jnp.bfloat16), "grp").astype(jnp.float32),
        lax.psum(grad_input_gain.astype(jnp.bfloat16), "grp").astype(jnp.float32),
        lax.psum(grad_input_bias.astype(jnp.bfloat16), "grp").astype(jnp.float32),
        lax.psum(grad_mlp_gain.astype(jnp.bfloat16), "grp").astype(jnp.float32),
        lax.psum(grad_mlp_bias.astype(jnp.bfloat16), "grp").astype(jnp.float32),
        lax.psum(grad_self_gain.astype(jnp.bfloat16), "grp").astype(jnp.float32),
        lax.psum(grad_self_bias.astype(jnp.bfloat16), "grp").astype(jnp.float32),
    )
    return (
        new_latents,
        grad_latents,
        grad_inputs,
        grad_cross_query,
        grad_cross_key,
        grad_cross_value,
        grad_cross_output,
        grad_mlp_up,
        grad_mlp_down,
        grad_self_query,
        grad_self_key,
        grad_self_value,
        grad_self_output,
        grad_latent_gain,
        grad_latent_bias,
        grad_input_gain,
        grad_input_bias,
        grad_mlp_gain,
        grad_mlp_bias,
        grad_self_gain,
        grad_self_bias,
    )


def solution(mesh):
    laid_out = mesh.shape["shard"] == 2 and mesh.shape["grp"] == 16
    return jax.shard_map(
        per_device_pair if laid_out else per_device,
        mesh=mesh,
        in_specs=(
            P("grp", None, None),
            P("grp", "shard", None),
            P("grp", None),
            P("grp", "shard"),
            P("shard", None),
            P("shard", None),
            P("shard", None),
            P("shard", None),
            P(None, "shard"),
            P("shard", None),
            P(None, "shard"),
            P(None, "shard"),
            P(None, "shard"),
            P("shard", None),
            P("shard"),
            P("shard"),
            P("shard"),
            P("shard"),
            P("shard"),
            P("shard"),
            P("shard"),
            P("shard"),
            P("grp", None, None),
        ),
        out_specs=(
            P("grp", None, None),
            P("grp", None, None),
            P("grp", "shard", None),
            P("shard", None),
            P("shard", None),
            P("shard", None),
            P("shard", None),
            P(None, "shard"),
            P("shard", None),
            P(None, "shard"),
            P(None, "shard"),
            P(None, "shard"),
            P("shard", None),
            P("shard"),
            P("shard"),
            P("shard"),
            P("shard"),
            P("shard"),
            P("shard"),
            P("shard"),
            P("shard"),
        ),
        check_vma=False,
    )
```

```python
import jax
import jax.numpy as jnp
from jax import lax
from jax.experimental import pallas as pl
from jax.experimental.pallas import tpu as pltpu
from jax.sharding import PartitionSpec as P

HEADS = 8
HEAD_DIM = 128


EPSILON = 1e-05
NEGATIVE = -1e30

BF = jnp.bfloat16
F32 = jnp.float32
MESH = pl.DeviceIdType.MESH
LAT = 128
INP = 784
D = 1024
HALF = 512
HID = 2048
ROWS = 2 * LAT
NROWS = 2 * INP
SCALE = HEAD_DIM ** (-0.5)
MIB = 1 << 20


def nn(a, b):
    return lax.dot_general(a, b, (((1,), (0,)), ((), ())), preferred_element_type=F32)


def nt(a, b):
    return lax.dot_general(a, b, (((1,), (1,)), ((), ())), preferred_element_type=F32)


def tn(a, b):
    return lax.dot_general(a, b, (((0,), (0,)), ((), ())), preferred_element_type=F32)


def place():
    g = lax.axis_index("grp")
    x = lax.axis_index("shard")
    c = lax.rem(g, 2)
    y = lax.rem(g // 2, 2)
    a = lax.rem(g // 4, 2)
    b = g // 8
    return dict(
        x=x, c=c, y=y, a=a, b=b,
        xp=(g, 1 - x),
        cp=(g + 1 - 2 * c, x),
        yp=(g + 2 - 4 * y, x),
        ap=(g + 4 - 8 * a, x),
        bp=(g + 8 - 16 * b, x),
        mp=(g + 4 - 8 * b, x),
    )


def greet(partners):
    barrier = pltpu.get_barrier_semaphore()
    for partner in partners:
        pl.semaphore_signal(barrier, inc=1, device_id=partner, device_id_type=MESH)
    pl.semaphore_wait(barrier, len(partners))


def remote(src, dst, send, recv, partner):
    return pltpu.make_async_remote_copy(
        src_ref=src, dst_ref=dst, send_sem=send, recv_sem=recv,
        device_id=partner, device_id_type=MESH,
    )


def norm(v, gain, shift):
    cen = v - jnp.mean(v, axis=-1, keepdims=True)
    inv = lax.rsqrt(jnp.mean(cen * cen, axis=-1, keepdims=True) + EPSILON)
    return cen * inv * gain + shift


def vec_row(vecs, i):
    return jnp.concatenate([vecs[0, i:i + 1, :], vecs[1, i:i + 1, :]], axis=1)


def span(first, last, body):
    lax.fori_loop(first, last, lambda i, carry: (body(i), carry)[1], 0)


def loop(n, body):
    span(0, n, body)


def first_kernel(
    lat_h, inp_h, seglat_h, seginp_h, v0, v1, v2, v3, v4, v5, v6, v7, wk_h, wv_h, wq_h, wo_h, up_h, down_h,
    sq_h, sk_h, sv_h, so_h, cot_h,
    wf_o, ck_o, cv_o, inin_o, latin_o, cq_o, att_o, st_o, vec_o, hone_o, htwo_o,
    mlpin_o, selfin_o, pre_o, hid_o, ds_o, slow_o, mask_o,
    wf, inp, inin, ck, cv, lat, latin, cq, mask, segs, axb, stx, att, st, vecs,
    hone, htwo, mlpin, pre, hid, xm, selfin, wup, wdown, wself, wso, cot, qkv, dself,
    ds, slow, seglat, seginp, g0, g1, g2, g3, g4, g5, g6, g7, lsem, osem, xs, xr, ys, yr, c0s, c0r, c1s, c1r, ms, mr,
):
    me = place()
    x, y, c = me["x"], me["y"], me["c"]
    xp, yp, cp = me["xp"], me["yp"], me["cp"]
    nlocal = [0]
    nout = [0]

    def load(src, dst):
        copy = pltpu.make_async_copy(src, dst, lsem.at[nlocal[0]])
        nlocal[0] += 1
        copy.start()
        return copy

    outs = []

    def store(src, dst):
        copy = pltpu.make_async_copy(src, dst, osem.at[nout[0]])
        nout[0] += 1
        copy.start()
        outs.append(copy)

    own = pl.ds(pl.multiple_of(x * HALF, HALF), HALF)
    gains = (g0, g1, g2, g3, g4, g5, g6, g7)
    in_gains = [load(v, g) for v, g in zip((v0, v1, v2, v3, v4, v5, v6, v7), gains)]
    in_seg = [load(seglat_h, seglat), load(seginp_h, seginp)]
    in_inp = load(inp_h, inp)
    in_lat = load(lat_h, lat)
    in_cot = load(cot_h, cot)
    in_so = load(so_h, wso)
    greet((xp, yp, cp))
    weights = (wk_h, wv_h, wq_h, wo_h)
    quarter = 2 * y + c

    def part(w, side, q):
        return wf.at[w, pl.ds(pl.multiple_of(side * HALF + q * 128, 128), 128)]

    x_moves = []
    for w in range(4):
        src = weights[w].at[pl.ds(pl.multiple_of(quarter * 128, 128), 128)]
        move = remote(src, part(w, x, quarter), xs.at[w], xr.at[w], xp)
        move.start()
        x_moves.append(move)
    for i, (copy, g) in enumerate(zip(in_gains, gains)):
        copy.wait()
        vecs[x, i:i + 1, :] = g[...].astype(F32).reshape(1, HALF)
    vec_move = remote(vecs.at[x], vecs.at[x], xs.at[4], xr.at[4], xp)
    vec_move.start()
    in_w = [load(weights[w], wf.at[w, own]) for w in range(4)]
    in_self = [load(h, wself.at[i]) for i, h in enumerate((sq_h, sk_h, sv_h))]
    in_up = load(up_h, wup)
    in_down = load(down_h, wdown)
    pending = []

    def forward_x(w):
        x_moves[w].wait()
        for sems, partner in (((ys, yr), yp), ((c0s, c0r), cp)):
            block = part(w, 1 - x, quarter)
            move = remote(block, block, sems[0].at[w], sems[1].at[w], partner)
            move.start()
            pending.append(move)

    def forward_y(w):
        block = part(w, 1 - x, quarter)
        remote(block, block, ys.at[w], yr.at[w], yp).wait_recv()
        block = part(w, 1 - x, 2 * (1 - y) + c)
        move = remote(block, block, c1s.at[w], c1r.at[w], cp)
        move.start()
        pending.append(move)

    def whole(w):
        block = part(w, 1 - x, quarter)
        remote(block, block, c0s.at[w], c0r.at[w], cp).wait_recv()
        remote(block, block, c1s.at[w], c1r.at[w], cp).wait_recv()
        in_w[w].wait()
        store(wf.at[w], wf_o.at[w])

    for copy in in_seg:
        copy.wait()
    segs[...] = jnp.zeros_like(segs)
    segs[0:2, 0:INP] = seginp[...].astype(F32)
    for g in range(2):
        lat_row = seglat[g:g + 1, :].astype(F32)
        for j in range(7):
            count = min(128, INP - j * 128)
            col = jnp.broadcast_to(segs[g:g + 1, j * 128:(j + 1) * 128], (128, 128)).T
            mask[g * INP + j * 128:g * INP + j * 128 + count, :] = jnp.where(
                col[:count] == lat_row, 0.0, NEGATIVE
            ).astype(BF)
    store(mask, mask_o)
    in_cot.wait()
    in_so.wait()
    dself[...] = nt(cot[...], wso[...]).astype(BF)
    in_inp.wait()
    vec_move.wait()
    store(vecs, vec_o)
    gain_inp, bias_inp = vec_row(vecs, 2), vec_row(vecs, 3)

    def norm_rows(i):
        rows = pl.ds(pl.multiple_of(i * 32, 32), 32)
        inin[rows, :] = norm(inp[rows, :].astype(F32), gain_inp, bias_inp).astype(BF)

    span(0, 24, norm_rows)
    forward_x(0)
    span(24, 49, norm_rows)
    store(inin, inin_o)
    forward_x(1)
    forward_y(0)
    in_lat.wait()
    latin[...] = norm(lat[...].astype(F32), vec_row(vecs, 0), vec_row(vecs, 1)).astype(BF)
    store(latin, latin_o)

    def project(target, w, half):
        cols = slice(half * HALF, (half + 1) * HALF)

        def body(i):
            rows = pl.ds(pl.multiple_of(i * INP, 16), INP)
            target[rows, cols] = nn(inin[rows, :], wf[w, :, cols]).astype(BF)

        loop(2, body)

    whole(0)
    project(ck, 0, 0)
    forward_x(2)
    forward_y(1)
    project(ck, 0, 1)
    store(ck, ck_o)
    whole(1)
    forward_x(3)
    forward_y(2)
    project(cv, 1, 0)
    project(cv, 1, 1)
    store(cv, cv_o)
    whole(2)
    cq[...] = nn(latin[...], wf[2]).astype(BF)
    store(cq, cq_o)
    forward_y(3)

    def head(g, h):
        cols = pl.ds(pl.multiple_of(h * HEAD_DIM, HEAD_DIM), HEAD_DIM)
        n_rows = slice(g * INP, (g + 1) * INP)
        s = nt(ck[n_rows, cols], cq[g * LAT:(g + 1) * LAT, cols]) * SCALE + mask[n_rows, :].astype(F32)
        top = jnp.maximum(jnp.max(s, axis=0, keepdims=True), 0.1 * NEGATIVE)
        e = jnp.exp(s - top)
        total = jnp.sum(e, axis=0, keepdims=True)
        out = tn(cv[n_rows, cols], e.astype(BF))
        out = out * jnp.where(total > 0.0, 1.0 / total, 0.0)
        axb[x, pl.ds(pl.multiple_of(g * D + h * HEAD_DIM, HEAD_DIM), HEAD_DIM), :] = out.astype(BF)
        stx[x, g, pl.ds(h, 1), :] = top
        stx[x, g, pl.ds(HEADS + h, 1), :] = total

    a_moves = []
    for g in range(2):
        def pair(i, g=g):
            head(g, 2 * i)
            head(g, 2 * i + 1)

        loop(HEADS // 2, pair)
        block = axb.at[x, pl.ds(g * D, D)]
        for src, k in ((block, 0), (stx.at[x, g], 1)):
            move = remote(src, src, ms.at[2 * g + k], mr.at[2 * g + k], xp)
            move.start()
            a_moves.append(move)
    whole(3)
    in_up.wait()
    in_down.wait()
    m_moves = []

    def mlp_group(g):
        a_moves[2 * g].wait()
        a_moves[2 * g + 1].wait()
        for h in range(HEADS):
            m0, m1 = stx[0, g, h:h + 1, :], stx[1, g, h:h + 1, :]
            top = jnp.maximum(m0, m1)
            w0 = stx[0, g, HEADS + h:HEADS + h + 1, :] * jnp.exp(m0 - top)
            w1 = stx[1, g, HEADS + h:HEADS + h + 1, :] * jnp.exp(m1 - top)
            inv = 1.0 / (w0 + w1)
            rows = slice(g * D + h * HEAD_DIM, g * D + (h + 1) * HEAD_DIM)
            mixed = axb[0, rows, :].astype(F32) * (w0 * inv) + axb[1, rows, :].astype(F32) * (w1 * inv)
            att[rows, :] = mixed.astype(BF)
            st[g, h:h + 1, :] = top
            st[g, HEADS + h:HEADS + h + 1, :] = inv
        rows = slice(g * LAT, (g + 1) * LAT)
        one = lat[rows, :].astype(F32) + tn(att[g * D:(g + 1) * D, :], wf[3])
        hone[rows, :] = one
        mlpin[rows, :] = norm(one, vec_row(vecs, 4), vec_row(vecs, 5)).astype(BF)
        for j in range(4):
            cols = slice(j * HALF, (j + 1) * HALF)
            u = nn(mlpin[rows, :], wup[:, cols])
            pre[rows, cols] = u
            hid[rows, cols] = jax.nn.gelu(u).astype(BF)
        for j in range(2):
            cols = slice(j * HALF, (j + 1) * HALF)
            xm[x, g, :, cols] = nn(hid[rows, :], wdown[:, cols]).astype(BF)
            part = xm.at[x, g, :, pl.ds(j * HALF, HALF)]
            move = remote(part, part, ms.at[4 + 2 * g + j], mr.at[4 + 2 * g + j], xp)
            move.start()
            m_moves.append(move)

    def self_group(g):
        rows = slice(g * LAT, (g + 1) * LAT)
        m_moves[2 * g].wait()
        m_moves[2 * g + 1].wait()
        two = hone[rows, :] + (xm[0, g].astype(F32) + xm[1, g].astype(F32))
        htwo[rows, :] = two
        selfin[rows, :] = norm(two, vec_row(vecs, 6), vec_row(vecs, 7)).astype(BF)
        for i in range(3):
            qkv[i, rows, :] = nn(selfin[rows, :], wself[i]).astype(BF)
        for h in range(4):
            cols = slice(h * HEAD_DIM, (h + 1) * HEAD_DIM)
            q, k, v = qkv[0, rows, cols], qkv[1, rows, cols], qkv[2, rows, cols]
            do = dself[rows, cols]
            s = nt(q, k) * SCALE
            e = jnp.exp(s - jnp.max(s, axis=1, keepdims=True))
            p = e / jnp.sum(e, axis=1, keepdims=True)
            p_low = p.astype(BF)
            o = nn(p_low, v)
            slow[rows, cols] = o.astype(BF)
            delta = jnp.sum(do.astype(F32) * o, axis=1, keepdims=True)
            dp = nt(do, v)
            dsc = (p * (dp - delta)).astype(BF)
            ds[0, rows, cols] = (nn(dsc, k) * SCALE).astype(BF)
            ds[1, rows, cols] = (tn(dsc, q) * SCALE).astype(BF)
            ds[2, rows, cols] = tn(p_low, do).astype(BF)

    mlp_group(0)
    mlp_group(1)
    store(att, att_o)
    store(st, st_o)
    store(hone, hone_o)
    store(mlpin, mlpin_o)
    store(pre, pre_o)
    store(hid, hid_o)
    for copy in in_self:
        copy.wait()
    self_group(0)
    self_group(1)
    store(ds, ds_o)
    store(slow, slow_o)
    store(htwo, htwo_o)
    store(selfin, selfin_o)
    for move in pending:
        move.wait_send()
    for copy in outs:
        copy.wait()


def run_first(args):
    any_spec = pl.BlockSpec(memory_space=pl.ANY)
    outs = [
        ((4, D, D), BF), ((NROWS, D), BF), ((NROWS, D), BF), ((NROWS, D), BF),
        ((ROWS, D), BF), ((ROWS, D), BF), ((2 * D, LAT), BF), ((2, 16, LAT), F32),
        ((2, 8, HALF), F32), ((ROWS, D), F32), ((ROWS, D), F32), ((ROWS, D), BF),
        ((ROWS, D), BF), ((ROWS, HID), F32), ((ROWS, HID), BF), ((3, ROWS, HALF), BF),
        ((ROWS, HALF), BF), ((NROWS, LAT), BF),
    ]
    scratch = [
        ((4, D, D), BF), ((NROWS, D), BF), ((NROWS, D), BF), ((NROWS, D), BF), ((NROWS, D), BF),
        ((ROWS, D), BF), ((ROWS, D), BF), ((ROWS, D), BF), ((NROWS, LAT), BF), ((8, 896), F32),
        ((2, 2 * D, LAT), BF), ((2, 2, 16, LAT), F32), ((2 * D, LAT), BF), ((2, 16, LAT), F32),
        ((2, 8, HALF), F32), ((ROWS, D), F32), ((ROWS, D), F32), ((ROWS, D), BF),
        ((ROWS, HID), F32), ((ROWS, HID), BF), ((2, 2, LAT, D), BF), ((ROWS, D), BF),
        ((D, HID), BF), ((HID, D), BF), ((3, D, HALF), BF), ((HALF, D), BF), ((ROWS, D), BF),
        ((3, ROWS, HALF), BF), ((ROWS, HALF), BF), ((3, ROWS, HALF), BF), ((ROWS, HALF), BF),
        ((2, LAT), jnp.int32), ((2, INP), jnp.int32), *[((HALF,), BF)] * 8,
    ]
    dma = pltpu.SemaphoreType.DMA
    return pl.pallas_call(
        first_kernel,
        out_shape=[jax.ShapeDtypeStruct(*o) for o in outs],
        in_specs=[any_spec] * len(args),
        out_specs=[any_spec] * len(outs),
        scratch_shapes=[pltpu.VMEM(*s) for s in scratch]
        + [dma((26,)), dma((24,))] + [dma((5,))] * 2 + [dma((4,))] * 6 + [dma((8,))] * 2,
        compiler_params=pltpu.CompilerParams(
            collective_id=0, has_side_effects=True, vmem_limit_bytes=58 * MIB
        ),
        name="forward",
    )(*args)


def norm_back(v, dy, gain):
    cen = v - jnp.mean(v, axis=-1, keepdims=True)
    inv = lax.rsqrt(jnp.mean(cen * cen, axis=-1, keepdims=True) + EPSILON)
    n = cen * inv
    t = dy * gain
    dv = inv * (t - jnp.mean(t, axis=-1, keepdims=True) - n * jnp.mean(t * n, axis=-1, keepdims=True))
    return (
        dv,
        jnp.sum(dy * n, axis=0, keepdims=True),
        jnp.sum(dy, axis=0, keepdims=True),
    )


def gelu_slope(u):
    root = (2.0 / jnp.pi) ** 0.5
    t = jnp.tanh(root * (u + 0.044715 * u * u * u))
    return 0.5 * (1.0 + t) + 0.5 * u * (1.0 - t * t) * root * (1.0 + 3.0 * 0.044715 * u * u)


PART = 256
KINDS = "zyyyzzyyzyyzyyzz" + "yzyyyzyzyyzyyyyz"
SLOTS = (4, 4, 4, 4, 2, 3)
ORDER = (
    0, 1, 2, 3, 4, 5, 6, 7, 8, 14, 9, 10, 11, 12, 15, 25, 13, 18, 17, 16, 19, 21, 22, 23, 26, 27, 28, 20,
    24, 29, 30, 31, 32, 33, 34, 35, 36, 37, 38, 39, 40, 41, 42, 43, 44, 45, 46, 47, 48, 49, 50, 51, 52, 53, 54, 55, 56,
)
EVENTS = (
    ((0, 0), (1, 0),),
    (),
    (),
    ((0, 1), (2, 0), (1, 1), (3, 0),),
    (),
    (),
    ((2, 1), (4, 0), (1, 2), (3, 1), (5, 0), (4, 1), (6, 0), (0, 2), (2, 2), (5, 1), (7, 0), (6, 1), (1, 3),
     (3, 2),),
    ((7, 1),),
    ((0, 3),),
    ((8, 0), (9, 0),),
    ((6, 2),),
    ((1, 4), (4, 2),),
    (),
    ((9, 1), (2, 3), (8, 1),),
    ((10, 0), (11, 0), (0, 4), (1, 5), (7, 2), (4, 3),),
    (),
    ((10, 1), (2, 4), (11, 1), (5, 2),),
    (),
    (),
    ((0, 5), (3, 3), (1, 6), (12, 0), (13, 0),),
    (),
    ((4, 4), (2, 5), (9, 2), (6, 3), (5, 3), (1, 7), (12, 1), (14, 0), (3, 4),),
    ((14, 1),),
    ((0, 6), (4, 5), (2, 6), (8, 2),),
    (),
    ((5, 4), (3, 5), (10, 2), (7, 3), (0, 7), (6, 4), (13, 1), (15, 0), (16, 0), (2, 7),),
    (),
    (),
    ((8, 3),),
    ((15, 1), (17, 0),),
    ((4, 6), (5, 5), (3, 6), (11, 2),),
    (),
    ((6, 5), (12, 2), (16, 1), (9, 3), (18, 0), (4, 7), (7, 4), (17, 1), (19, 0), (3, 7),),
    (),
    ((8, 4), (11, 3),),
    (),
    ((6, 6), (5, 6),),
    ((9, 4), (14, 2),),
    (),
    ((6, 7), (10, 3), (8, 5), (7, 5), (5, 7), (13, 2), (18, 1), (20, 0),),
    (),
    ((11, 4), (9, 5), (14, 3), (16, 2), (19, 1), (21, 0),),
    ((7, 6), (10, 4), (21, 1), (15, 2),),
    ((7, 7), (8, 6), (12, 3), (11, 5),),
    ((15, 3), (14, 4), (9, 6), (8, 7), (10, 5), (18, 2), (20, 1), (22, 0), (23, 0), (17, 2),),
    ((12, 4),),
    ((9, 7), (11, 6), (13, 3), (14, 5), (23, 1),),
    ((15, 4), (16, 3),),
    (),
    ((17, 3), (10, 6), (11, 7), (12, 5), (19, 2), (22, 1), (24, 0), (25, 0),),
    ((10, 7), (13, 4), (21, 2),),
    ((14, 6), (17, 4), (15, 5), (18, 3),),
    ((12, 6), (16, 4), (13, 5), (14, 7), (20, 2), (24, 1), (26, 0),),
    ((12, 7), (21, 3), (23, 2),),
    ((15, 6), (17, 5), (19, 3), (13, 6), (26, 1),),
    ((18, 4), (20, 3), (15, 7), (16, 5), (22, 2), (25, 1), (13, 7), (27, 0), (28, 0),),
    ((21, 4), (23, 3), (19, 4), (17, 6), (16, 6), (26, 2), (20, 4), (17, 7), (18, 5), (24, 2), (-1, 0), (16, 7),
     (22, 3), (27, 1), (29, 0), (21, 5), (19, 5), (25, 2), (23, 4), (28, 1), (30, 0), (24, 3), (-1, 1), (26, 3),
     (20, 5), (18, 6), (22, 4), (25, 3), (18, 7), (27, 2), (29, 1), (31, 0), (23, 5), (-1, 2), (21, 6), (19, 6),
     (31, 1), (24, 4), (27, 3), (21, 7), (22, 5), (28, 2), (19, 7), (30, 1), (25, 4), (-1, 3), (26, 4), (27, 4),
     (31, 2), (23, 6), (20, 6), (26, 5), (28, 3), (23, 7), (24, 5), (29, 2), (20, 7), (-1, 4), (31, 3), (25, 5),
     (22, 6), (29, 3), (28, 4), (22, 7), (27, 5), (30, 2), (24, 6), (29, 4), (-1, 5), (30, 3), (24, 7), (26, 6),
     (31, 4), (26, 7), (28, 5), (25, 6), (30, 4), (25, 7), (29, 5), (27, 6), (31, 5), (27, 7), (30, 5), (28, 6),
     (28, 7), (29, 6), (29, 7), (31, 6), (30, 6), (31, 7), (30, 7),),
)


def second_kernel(
    wf_h, ck_h, cv_h, inin_h, latin_h, cq_h, att_h, st_h, vec_h, hone_h, htwo_h,
    mlpin_h, selfin_h, pre_h, hid_h, ds_h, slow_h, mask_h,
    lat_h, inp_h, up_h, down_h, sq_h, sk_h, sv_h, so_h, cot_h,
    newlat_o, glat_o, ginp_o, gq_o, gk_o, gv_o, go_o, gup_o, gdown_o, gsq_o, gsk_o,
    gsv_o, gso_o, gvec_o,
    z, wf, cq, att, st, vecs, hone, htwo, etwo, mlpin, selfin, pre, hid, ds,
    slow, mask, cot, elow2, elow1, dpre, dcr, xb, grad, other, t0, ty, te, tm, tn_mid, tn_y,
    xk, gvec, gvr,
    lsem, osem, gs, gr, xs, xr, vs, vr, free,
):
    me = place()
    x, c = me["x"], me["c"]
    xp, yp, cp, ap, bp = me["xp"], me["yp"], me["cp"], me["ap"], me["bp"]
    counts = [0, 0]
    outs = []

    def load(src, dst):
        copy = pltpu.make_async_copy(src, dst, lsem.at[counts[0]])
        counts[0] += 1
        copy.start()
        return copy

    def store(src, dst):
        copy = pltpu.make_async_copy(src, dst, osem.at[counts[1]])
        counts[1] += 1
        copy.start()
        outs.append(copy)

    in_early = [load(slow_h, slow), load(cot_h, cot), load(selfin_h, selfin)]
    in_ds = load(ds_h, ds)
    in_self = [
        load(sq_h, z.at[pl.ds(4096, D), pl.ds(0, HALF)]),
        load(sk_h, z.at[pl.ds(4096, D), pl.ds(HALF, HALF)]),
        load(sv_h, z.at[pl.ds(5120, D), pl.ds(0, HALF)]),
    ]
    in_early += [
        load(so_h.at[:, pl.ds(j * HALF, HALF)], z.at[pl.ds(5120 + j * HALF, HALF), pl.ds(HALF, HALF)])
        for j in range(2)
    ]
    in_two = [load(htwo_h, htwo), load(vec_h, vecs)]
    in_mlp = [
        load(pre_h, pre), load(down_h, z.at[pl.ds(0, HID)]),
        load(up_h.at[:, pl.ds(0, D)], z.at[pl.ds(HID, D)]),
        load(up_h.at[:, pl.ds(D, D)], z.at[pl.ds(HID + D, D)]),
    ]
    in_mid = [
        load(hid_h.at[:, pl.ds(j * D, D)], hid.at[pl.ds(j * ROWS, ROWS)]) for j in range(2)
    ] + [load(mlpin_h, mlpin), load(hone_h, hone)]
    in_cross = [
        load(wf_h, wf), load(att_h, att), load(st_h, st), load(cq_h, cq), load(mask_h, mask),
    ]
    barrier = pltpu.get_barrier_semaphore()
    for partner in (xp, yp, cp, ap, bp):
        pl.semaphore_signal(barrier, inc=1, device_id=partner, device_id_type=MESH)

    @pl.when(me["a"] != me["b"])
    def _():
        pl.semaphore_signal(barrier, inc=1, device_id=me["mp"], device_id_type=MESH)
        pl.semaphore_wait(barrier, 6)

    @pl.when(me["a"] == me["b"])
    def _():
        pl.semaphore_wait(barrier, 5)


    def wait_all(copies):
        for copy in copies:
            copy.wait()

    a_bit, b_bit, y_bit = me["a"], me["b"], me["y"]
    at_end = a_bit == b_bit
    at_middle = a_bit != b_bit
    mp = me["mp"]

    def cols_of(core):
        return pl.ds(pl.multiple_of(core * HALF, HALF), HALF)

    def block(k, off, size, core):
        return grad.at[pl.ds(pl.multiple_of(k * PART + off, 16), size), cols_of(core)]

    def add(base, size, part):
        def body(i):
            rows = pl.ds(pl.multiple_of(base + i * 64, 64), 64)
            grad[rows, cols_of(c)] += part[pl.ds(pl.multiple_of(i * 64, 64), 64), :]

        loop(size // 64, body)

    def move(k, stage, src, dst, partner):
        return remote(src, dst, gs.at[k * 7 + stage], gr.at[k * 7 + stage], partner)

    def release(k, n, partner):
        pl.semaphore_signal(free.at[k * 4 + n], inc=1, device_id=partner, device_id_type=MESH)

    def claim(k, n):
        pl.semaphore_wait(free.at[k * 4 + n], 1)

    def event(k, s):
        base, size, half = k * PART, PART, PART // 2
        kind = KINDS[k]
        n = KINDS[:k].count(kind)
        everything = block(k, 0, size, c)
        core_in = t0.at[k % t0.shape[0]]
        core_move = move(k, 0, block(k, 0, size, 1 - c), core_in, cp)
        core_back = move(k, 6, everything, everything, cp)
        if s == 0:
            core_move.start()
            return
        if s == 7:
            core_back.wait()
            deliver(k)
            return
        if s == 1:
            core_move.wait()
            if kind == "y":
                release(k, 0, cp)
            else:
                pl.when(at_end)(lambda: release(k, 0, cp))
                pl.when(at_middle)(lambda: release(k, 3, ap))
            add(base, size, core_in)
            if k >= 28:
                finish_x((k - 28) // 2, k % 2)
        if kind == "y":
            off = y_bit * half
            own = block(k, off, half, c)
            y_in, end_in, mid_in = (
                ty.at[n % ty.shape[0]], te.at[n % te.shape[0]], tm.at[n % tm.shape[0]]
            )
            y_move = move(k, 1, block(k, (1 - y_bit) * half, half, c), y_in, yp)
            end_move = move(k, 2, own, end_in, ap)
            mid_move = move(k, 3, own, mid_in, mp)
            end_back = move(k, 4, own, own, ap)
            y_back = move(k, 5, own, own, yp)
            if s == 1:
                y_move.start()
            elif s == 2:
                y_move.wait()
                release(k, 1, yp)
                add(base + off, half, y_in)
                pl.when(at_end)(end_move.start)
            elif s == 3:
                @pl.when(at_end)
                def _():
                    end_move.wait_send()
                    release(k, 2, ap)

                @pl.when(at_middle)
                def _():
                    end_move.wait_recv()
                    add(base + off, half, end_in)
                    mid_move.start()
            elif s == 4:
                @pl.when(at_middle)
                def _():
                    mid_move.wait()
                    add(base + off, half, mid_in)
                    claim(k, 2)
                    end_back.start()
            elif s == 5:
                pl.when(at_end)(end_back.wait_recv)
                pl.when(at_middle)(end_back.wait_send)
                claim(k, 1)
                y_back.start()
            elif s == 6:
                y_back.wait()
                claim(k, 0)
                core_back.start()
            return
        off = b_bit * half
        own = block(k, off, half, c)
        mid_in, y_in = tn_mid.at[n % tn_mid.shape[0]], tn_y.at[n % tn_y.shape[0]]
        end_in = block(k, 0, size, 1 - c)
        end_move = move(k, 1, everything, end_in, ap)
        mid_move = move(k, 2, block(k, (1 - b_bit) * half, half, c), mid_in, mp)
        y_move = move(k, 3, own, y_in, yp)
        mid_back = move(k, 4, own, own, mp)
        end_back = move(k, 5, everything, everything, ap)
        if s == 1:
            @pl.when(at_end)
            def _():
                claim(k, 3)
                end_move.start()
        elif s == 2:
            @pl.when(at_end)
            def _():
                end_move.wait_send()
                release(k, 1, ap)

            @pl.when(at_middle)
            def _():
                end_move.wait_recv()
                add(base, size, end_in)
                release(k, 0, cp)
                mid_move.start()
        elif s == 3:
            @pl.when(at_middle)
            def _():
                mid_move.wait()
                release(k, 2, mp)
                add(base + off, half, mid_in)
                y_move.start()
        elif s == 4:
            @pl.when(at_middle)
            def _():
                y_move.wait()
                add(base + off, half, y_in)
                claim(k, 2)
                mid_back.start()
        elif s == 5:
            @pl.when(at_middle)
            def _():
                mid_back.wait()
                claim(k, 1)
                end_back.start()
        elif s == 6:
            pl.when(at_end)(end_back.wait_recv)
            pl.when(at_middle)(end_back.wait_send)
            claim(k, 0)
            core_back.start()

    def deliver(k):
        n, top = k // 2, (k % 2) * PART
        rows = pl.ds(k * PART, PART)
        left, right = grad.at[rows, pl.ds(0, HALF)], grad.at[rows, pl.ds(HALF, HALF)]
        first, second = pl.ds(top, PART), pl.ds(HALF + top, PART)
        if 1 <= n <= 3:
            target = (gsq_o, gsk_o, gsv_o)[n - 1]
            store(left, target.at[first])
            store(right, target.at[second])
        elif 8 <= n <= 11:
            cols = pl.ds((n - 8) * HALF, HALF)
            store(left, gup_o.at[first, cols])
            store(right, gup_o.at[second, cols])
        elif 4 <= n <= 7:
            store(grad.at[rows], gdown_o.at[pl.ds((n - 4) * HALF + top, PART)])
        else:
            target = {0: gso_o, 12: go_o, 13: gq_o, 14: gk_o, 15: gv_o}[n]
            store(grad.at[rows], target.at[first])

    k_moves = {}

    def start_core(w):
        src = other.at[w, :, pl.ds(pl.multiple_of((1 - c) * HALF, HALF), HALF)]
        move = remote(src, hid.at[:, pl.ds(w * HALF, HALF)], xs.at[8 + w], xr.at[8 + w], cp)
        move.start()
        k_moves[w, 0] = move

    def start_x(w):
        k_moves[w, 0].wait()
        cols = pl.ds(pl.multiple_of(c * HALF, HALF), HALF)

        def body(i):
            rows = pl.ds(pl.multiple_of(i * 64, 64), 64)
            other[w, rows, cols] = (
                other[w, rows, cols].astype(F32) + hid[rows, w * HALF:(w + 1) * HALF].astype(F32)
            ).astype(BF)

        loop(HALF // 64, body)
        move = remote(other.at[w, :, cols], xk.at[w], xs.at[10 + w], xr.at[10 + w], xp)
        move.start()
        k_moves[w, 1] = move

    def finish_x(w, part):
        if (w, 1) in k_moves:
            k_moves.pop((w, 1)).wait()
        add((14 + w) * HALF + part * 256, 256, xk.at[w, pl.ds(part * 256, 256)])

    def exchange(n, part, index):
        move = remote(
            xb.at[(n, x) + part], xb.at[(n, x) + part], xs.at[index], xr.at[index], xp
        )
        move.start()
        return move

    def both(n, rows):
        return xb[n, 0, rows, :].astype(F32) + xb[n, 1, rows, :].astype(F32)

    def fill(k, half, value):
        grad[k * HALF:(k + 1) * HALF, half * HALF:(half + 1) * HALF] = value.astype(BF)

    gvec[...] = jnp.zeros_like(gvec)
    lat, latin, dcq = cot, mlpin, elow2
    ck, cv = z.at[pl.ds(0, NROWS)], z.at[pl.ds(NROWS, NROWS)]
    inin, inp = z.at[pl.ds(2 * NROWS, NROWS)], z.at[pl.ds(3 * NROWS, NROWS)]
    gain_lat, gain_inp, gain_mlp, gain_self = 0, 2, 4, 6
    m_self, m_new, m_mlp, m_query, later = [], [], [], [], {}

    def self_back(j):
        if j == 0:
            wait_all(in_self)
        cols = slice(j * HALF, (j + 1) * HALF)
        a_rows = slice(4096 + j * HALF, 4096 + (j + 1) * HALF)
        b_rows = slice(5120 + j * HALF, 5120 + (j + 1) * HALF)
        xb[0, x, :, cols] = (
            nt(ds[0], z[a_rows, 0:HALF]) + nt(ds[1], z[a_rows, HALF:D]) + nt(ds[2], z[b_rows, 0:HALF])
        ).astype(BF)
        m_self.append(exchange(0, (slice(None), pl.ds(j * HALF, HALF)), j))

    def fill_self(n):
        if n == 0:
            wait_all(in_early)
            in_ds.wait()
        for j in range(2):
            cols = slice(j * HALF, (j + 1) * HALF)
            fill(n, j, tn(slow[...], cot[:, cols]) if n == 0 else tn(selfin[:, cols], ds[n - 1]))

    def new_part():
        for j in range(2):
            cols = slice(j * HALF, (j + 1) * HALF)
            rows = slice(5120 + j * HALF, 5120 + (j + 1) * HALF)
            xb[1, x, :, cols] = nn(slow[...], z[rows, HALF:D]).astype(BF)
            m_new.append(exchange(1, (slice(None), pl.ds(j * HALF, HALF)), 2 + j))

    def two_back():
        wait_all(in_two)
        wait_all(m_self)
        gain = vec_row(vecs, gain_self)

        def body(i):
            rows = pl.ds(pl.multiple_of(i * 32, 32), 32)
            dv, dg, db = norm_back(htwo[rows, :], both(0, rows), gain)
            e = cot[rows, :].astype(F32) + dv
            etwo[rows, :] = e
            elow2[rows, :] = e.astype(BF)
            gvec[6:7, :] += dg
            gvec[7:8, :] += db

        loop(8, body)
        later["lat"] = load(lat_h, lat)
        wait_all(in_mid)

    def hidden_back(j):
        if j == 0:
            wait_all(in_mlp)
        cols = slice(j * HALF, (j + 1) * HALF)
        gh = nt(elow2[...], z[cols, :])
        dpre[:, cols] = (gh * gelu_slope(pre[:, cols])).astype(BF)

    def mlp_back(j):
        cols = slice(j * HALF, (j + 1) * HALF)
        xb[2, x, :, cols] = (
            nt(dpre[:, 0:D], z[HID + j * HALF:HID + (j + 1) * HALF, :])
            + nt(dpre[:, D:HID], z[HID + D + j * HALF:HID + D + (j + 1) * HALF, :])
        ).astype(BF)
        m_mlp.append(exchange(2, (slice(None), pl.ds(j * HALF, HALF)), 4 + j))
        if j == 0:
            return
        later["keys"] = [load(ck_h, ck), load(cv_h, cv)]
        later["inputs"] = [load(inin_h, inin), load(inp_h, inp)]

    def fill_down(j):
        for i in range(2):
            part = hid[(j // 2) * ROWS:(j // 2 + 1) * ROWS, (j % 2) * HALF:(j % 2 + 1) * HALF]
            fill(4 + j, i, tn(part, elow2[:, i * HALF:(i + 1) * HALF]))

    def fill_up(j):
        for i in range(2):
            fill(8 + j, i, tn(mlpin[:, i * HALF:(i + 1) * HALF], dpre[:, j * HALF:(j + 1) * HALF]))

    def one_back():
        wait_all(m_mlp)
        gain = vec_row(vecs, gain_mlp)

        def body(i):
            rows = pl.ds(pl.multiple_of(i * 32, 32), 32)
            dv, dg, db = norm_back(hone[rows, :], both(2, rows), gain)
            e = etwo[rows, :] + dv
            hone[rows, :] = e
            elow1[rows, :] = e.astype(BF)
            gvec[4:5, :] += dg
            gvec[5:6, :] += db

        loop(8, body)

    def cross_back():
        wait_all(in_cross)
        for g in range(2):
            dcr[g * D:(g + 1) * D, :] = nt(wf[3], elow1[g * LAT:(g + 1) * LAT, :]).astype(BF)

    def fill_output():
        for j in range(2):
            value = 0.0
            for g in range(2):
                rows = pl.ds(pl.multiple_of(g * D + x * HALF, HALF), HALF)
                value = value + nn(
                    att[rows, :], elow1[g * LAT:(g + 1) * LAT, j * HALF:(j + 1) * HALF]
                )
            fill(12, j, value)

    def new_latents():
        wait_all(m_new)

        def body(i):
            rows = pl.ds(pl.multiple_of(i * 64, 64), 64)
            selfin[rows, :] = (htwo[rows, :] + both(1, rows)).astype(BF)

        loop(4, body)
        store(selfin, newlat_o)

    def head(g, h):
        cols = slice(h * HEAD_DIM, (h + 1) * HEAD_DIM)
        n_rows = slice(g * INP, (g + 1) * INP)
        l_rows = slice(g * LAT, (g + 1) * LAT)
        t_rows = slice(g * D + h * HEAD_DIM, g * D + (h + 1) * HEAD_DIM)
        k, v, q = ck[n_rows, cols], cv[n_rows, cols], cq[l_rows, cols]
        s = nt(k, q) * SCALE + mask[n_rows, :].astype(F32)
        p = jnp.exp(s - st[g, h:h + 1, :]) * st[g, HEADS + h:HEADS + h + 1, :]
        do = dcr[t_rows, :]
        delta = jnp.sum(do.astype(F32) * att[t_rows, :].astype(F32), axis=0, keepdims=True)
        dsc = (p * (nn(v, do) - delta)).astype(BF)
        cv[n_rows, cols] = nt(p.astype(BF), do).astype(BF)
        ck[n_rows, cols] = (nn(dsc, q) * SCALE).astype(BF)
        xb[0, x, l_rows, cols] = (tn(dsc, k) * SCALE).astype(BF)

    def heads_back(g, h):
        if g == 0 and h == 0:
            wait_all(later["keys"])
        head(g, h)
        if h == HEADS - 1:
            m_query.append(exchange(0, (pl.ds(g * LAT, LAT),), 6 + g))

    def weight_grad(w, i):
        if w == 0 and i == 0:
            wait_all(later["inputs"])
            later["latin"] = load(latin_h, latin)
        source = (ck, cv)[w]
        rows = slice(i * 256, (i + 1) * 256)
        mine = pl.ds(pl.multiple_of(x * HALF + i * 256, 256), 256)
        theirs = pl.ds(pl.multiple_of((1 - x) * HALF + i * 256, 256), 256)
        other[w, rows, :] = tn(inin[:, theirs], source[...]).astype(BF)
        grad[(14 + w) * HALF + i * 256:(14 + w) * HALF + (i + 1) * 256, :] = tn(
            inin[:, mine], source[...]
        ).astype(BF)
        if i == 1:
            start_core(w)

    def fill_query():
        wait_all(m_query)
        later["latin"].wait()

        def body(i):
            rows = pl.ds(pl.multiple_of(i * 64, 64), 64)
            dcq[rows, :] = both(0, rows).astype(BF)

        loop(4, body)
        for j in range(2):
            mine = pl.ds(pl.multiple_of(x * HALF, HALF), HALF)
            fill(13, j, tn(latin[:, mine], dcq[:, j * HALF:(j + 1) * HALF]))

    def latents_back():
        gain = vec_row(vecs, gain_lat)
        later["lat"].wait()

        def body(i):
            rows = pl.ds(pl.multiple_of(i * 128, 128), 128)
            dv, dg, db = norm_back(lat[rows, :].astype(F32), nt(dcq[rows, :], wf[2]), gain)
            lat[rows, :] = (hone[rows, :] + dv).astype(BF)
            gvec[0:1, :] += dg
            gvec[1:2, :] += db

        loop(2, body)
        store(lat, glat_o)

    def inputs_back(i):
        rows = slice(i * 224, (i + 1) * 224)
        dy = nt(ck[rows, :], wf[0]) + nt(cv[rows, :], wf[1])
        dv, dg, db = norm_back(inp[rows, :].astype(F32), dy, vec_row(vecs, gain_inp))
        inp[rows, :] = dv.astype(BF)
        gvec[2:3, :] += dg
        gvec[3:4, :] += db
        if i == 6:
            store(inp, ginp_o)
            col = lax.broadcasted_iota(jnp.int32, (8, D), 1) // HALF
            row = lax.broadcasted_iota(jnp.int32, (8, D), 0)
            keep = (col == x) | (row == 2) | (row == 3)
            gvec[...] = jnp.where(keep, gvec[...], 0.0)

    v_partners = (xp, cp, yp, ap, bp)
    v_moves = []

    def vec_event(s):
        if s > 0:
            v_moves[s - 1].wait()
            gvec[...] += gvr[s - 1]
        if s < 5:
            move = remote(gvec, gvr.at[s], vs.at[s], vr.at[s], v_partners[s])
            move.start()
            v_moves.append(move)
        else:
            store(gvec, gvec_o)

    steps = [lambda: fill_self(0), lambda: fill_self(1), lambda: self_back(0), lambda: self_back(1)]
    steps += [lambda: fill_self(2), lambda: fill_self(3)]
    steps += [new_part, two_back]
    steps += [lambda j=j: hidden_back(j) for j in range(4)]
    steps += [lambda: mlp_back(0), lambda: mlp_back(1)]
    steps += [lambda j=j: fill_down(j) for j in range(4)]
    steps += [lambda j=j: fill_up(j) for j in range(4)]
    steps += [one_back, cross_back, fill_output, new_latents]
    steps += [lambda g=g, h=h: heads_back(g, h) for g in range(2) for h in range(HEADS)]
    steps += [lambda i=i: weight_grad(0, i) for i in range(2)]
    steps += [lambda: weight_grad(1, 0), lambda: start_x(0), lambda: weight_grad(1, 1)]
    steps += [fill_query, lambda: start_x(1), latents_back]
    steps += [lambda i=i: inputs_back(i) for i in range(7)]
    for at, events in zip(ORDER, EVENTS, strict=True):
        steps[at]()
        for k, s in events:
            if k < 0:
                vec_event(s)
            else:
                event(k, s)
    wait_all(outs)


def run_second(args):
    any_spec = pl.BlockSpec(memory_space=pl.ANY)
    outs = [
        ((ROWS, D), BF), ((ROWS, D), BF), ((NROWS, D), BF), ((HALF, D), BF), ((HALF, D), BF),
        ((HALF, D), BF), ((HALF, D), BF), ((D, HID), BF), ((HID, D), BF), ((D, HALF), BF),
        ((D, HALF), BF), ((D, HALF), BF), ((HALF, D), BF), ((8, D), F32),
    ]
    scratch = [
        ((4 * NROWS, D), BF), ((4, D, D), BF), ((ROWS, D), BF),
        ((2 * D, LAT), BF), ((2, 16, LAT), F32), ((2, 8, HALF), F32), ((ROWS, D), F32),
        ((ROWS, D), F32), ((ROWS, D), F32), ((ROWS, D), BF), ((ROWS, D), BF), ((ROWS, HID), F32),
        ((2 * ROWS, D), BF), ((3, ROWS, HALF), BF), ((ROWS, HALF), BF), ((NROWS, LAT), BF),
        ((ROWS, D), BF), ((ROWS, D), BF), ((ROWS, D), BF), ((ROWS, HID), BF),
        ((2 * D, LAT), BF), ((3, 2, ROWS, D), BF), ((16 * HALF, D), BF), ((2, HALF, D), BF),
        ((SLOTS[0], PART, HALF), BF), *[((n, PART // 2, HALF), BF) for n in SLOTS[1:]],
        ((2, HALF, HALF), BF), ((8, D), F32),
        ((5, 8, D), F32),
    ]
    dma = pltpu.SemaphoreType.DMA
    return pl.pallas_call(
        second_kernel,
        out_shape=[jax.ShapeDtypeStruct(*o) for o in outs],
        in_specs=[any_spec] * len(args),
        out_specs=[any_spec] * len(outs),
        scratch_shapes=[pltpu.VMEM(*s) for s in scratch]
        + [dma((40,)), dma((64,))] + [dma((32 * 7,))] * 2 + [dma((12,))] * 2 + [dma((5,))] * 2
        + [pltpu.SemaphoreType.REGULAR((128,))],
        compiler_params=pltpu.CompilerParams(
            collective_id=1, has_side_effects=True, vmem_limit_bytes=63 * MIB
        ),
        name="backward",
    )(*args)


def finish_kernel(*refs):
    srcs, gvec, dsts, small = refs[:13], refs[13], refs[14:27], refs[27:35]
    low, wide, gains, *pieces, insem, outsem, smallsem = refs[35:]
    in_gains = pltpu.make_async_copy(gvec, gains, smallsem.at[8])
    in_gains.start()
    tiles = []
    for i in (*range(3, 13), 0, 1, 2):
        rows, cols = srcs[i].shape
        for r in range(0, rows, 256):
            count = min(256, rows - r)
            tiles.append((i, pl.ds(r, count), (pl.ds(0, count), pl.ds(0, cols))))
    depth = low.shape[0]
    ins, outs, finished = {}, {}, set()

    def finish_out(n):
        if n >= 0 and n not in finished:
            outs[n].wait()
            finished.add(n)

    def start_in(n):
        i, rows, part = tiles[n]
        ins[n] = pltpu.make_async_copy(srcs[i].at[rows], low.at[n % depth, *part], insem.at[n % depth])
        ins[n].start()

    for n in range(depth):
        start_in(n)
    first = lax.axis_index("shard") == 0
    in_gains.wait()
    mine = jnp.where(first, gains[:, 0:HALF], gains[:, HALF:D])
    out_gains = []
    for i in range(8):
        pieces[i][...] = mine[i]
        copy = pltpu.make_async_copy(pieces[i], small[i], smallsem.at[i])
        copy.start()
        out_gains.append(copy)
    for n in range(len(tiles)):
        slot = n % depth
        i, rows, part = tiles[n]
        ins[n].wait()
        finish_out(n - depth)
        if i < 3:
            outs[n] = pltpu.make_async_copy(low.at[slot, *part], dsts[i].at[rows], outsem.at[slot])
            outs[n].start()
        else:
            cols = part[1]

            def body(i, slot=slot, cols=cols):
                rows = pl.ds(pl.multiple_of(i * 32, 32), 32)
                wide[slot, rows, cols] = low[slot, rows, cols].astype(F32)

            loop(8, body)
            outs[n] = pltpu.make_async_copy(wide.at[slot, *part], dsts[i].at[rows], outsem.at[slot])
            outs[n].start()
        if n + depth < len(tiles):
            if i < 3:
                finish_out(n)
            start_in(n + depth)
    for n in range(len(tiles) - depth, len(tiles)):
        finish_out(n)
    for copy in out_gains:
        copy.wait()


def run_finish(args):
    any_spec = pl.BlockSpec(memory_space=pl.ANY)
    depth = 6
    return pl.pallas_call(
        finish_kernel,
        out_shape=[
            jax.ShapeDtypeStruct(a.shape, BF if i < 3 else F32) for i, a in enumerate(args[:13])
        ] + [jax.ShapeDtypeStruct((HALF,), F32)] * 8,
        in_specs=[any_spec] * 14,
        out_specs=[any_spec] * 21,
        scratch_shapes=[
            pltpu.VMEM((depth, 256, HID), BF), pltpu.VMEM((depth, 256, HID), F32),
            pltpu.VMEM((8, D), F32), *[pltpu.VMEM((HALF,), F32)] * 8,
            pltpu.SemaphoreType.DMA((depth,)), pltpu.SemaphoreType.DMA((depth,)),
            pltpu.SemaphoreType.DMA((9,)),
        ],
        compiler_params=pltpu.CompilerParams(vmem_limit_bytes=62 * MIB),
        name="finish",
    )(*args)


def per_device_pair(
    latents, inputs, latent_segment, input_segment, cross_query, cross_key, cross_value,
    cross_output, mlp_up, mlp_down, self_query, self_key, self_value, self_output,
    latent_gain, latent_bias, input_gain, input_bias, mlp_gain, mlp_bias, self_gain,
    self_bias, cotangent,
):
    vec = (
        latent_gain, latent_bias, input_gain, input_bias, mlp_gain, mlp_bias, self_gain, self_bias
    )
    lat = latents.reshape(ROWS, D)
    inp = inputs.reshape(NROWS, D)
    cot = cotangent.reshape(ROWS, D)
    kept = run_first((
        lat, inp, latent_segment, input_segment, *vec, cross_key, cross_value, cross_query,
        cross_output, mlp_up, mlp_down, self_query, self_key, self_value, self_output, cot,
    ))
    (new, glat, ginp, gq, gk, gv, go, gup, gdown, gsq, gsk, gsv, gso, gvec) = run_second(
        tuple(kept) + (
            lat, inp, mlp_up, mlp_down, self_query, self_key, self_value, self_output, cot
        )
    )
    new, glat, ginp, *grads = run_finish(
        (new, glat, ginp, gq, gk, gv, go, gup, gdown, gsq, gsk, gsv, gso, gvec)
    )
    return (
        new.reshape(latents.shape), glat.reshape(latents.shape), ginp.reshape(inputs.shape), *grads
    )


def norm_forward(values, gain, shift):
    centred = values - jnp.mean(values, axis=-1, keepdims=True)
    inv_std = lax.rsqrt(jnp.mean(centred * centred, axis=-1, keepdims=True) + EPSILON)
    normed = centred * inv_std
    return (normed * gain + shift, normed, inv_std)


def norm_backward(grad_out, normed, inv_std, gain):
    scaled = grad_out * gain
    first_mean = jnp.mean(scaled, axis=-1, keepdims=True)
    second_mean = jnp.mean(scaled * normed, axis=-1, keepdims=True)
    grad_in = inv_std * (scaled - first_mean - normed * second_mean)
    return (grad_in, jnp.sum(grad_out * normed, axis=0), jnp.sum(grad_out, axis=0))


def product(left, right):
    return jnp.dot(left, right, preferred_element_type=jnp.float32)


def inner_rows(left, right):
    return lax.dot_general(
        left, right, (((0,), (0,)), ((), ())), preferred_element_type=jnp.float32
    )


def outer_cols(left, right):
    return lax.dot_general(
        left, right, (((1,), (1,)), ((), ())), preferred_element_type=jnp.float32
    )


def forward_total(term):
    return lax.psum(term.astype(jnp.bfloat16), "shard").astype(jnp.float32)


def backward_total(term):
    return lax.psum(term.astype(jnp.bfloat16), "shard").astype(jnp.float32)


def per_device(
    latents,
    inputs,
    latent_segment,
    input_segment,
    cross_query,
    cross_key,
    cross_value,
    cross_output,
    mlp_up,
    mlp_down,
    self_query,
    self_key,
    self_value,
    self_output,
    latent_gain,
    latent_bias,
    input_gain,
    input_bias,
    mlp_gain,
    mlp_bias,
    self_gain,
    self_bias,
    cotangent,
):
    shards = lax.axis_size("shard")
    groups, lat_len, width = latents.shape
    inp_len = inputs.shape[1]
    width_part = width // shards
    column_start = lax.axis_index("shard") * width_part
    rows = groups * lat_len
    scale = HEAD_DIM ** (-0.5)
    gathered = (
        lax.all_gather(cross_query, "shard", axis=0, tiled=True),
        lax.all_gather(cross_key, "shard", axis=0, tiled=True),
        lax.all_gather(cross_value, "shard", axis=0, tiled=True),
        lax.all_gather(cross_output, "shard", axis=0, tiled=True),
        lax.all_gather(latent_gain, "shard", axis=0, tiled=True),
        lax.all_gather(latent_bias, "shard", axis=0, tiled=True),
        lax.all_gather(input_gain, "shard", axis=0, tiled=True),
        lax.all_gather(input_bias, "shard", axis=0, tiled=True),
        lax.all_gather(mlp_gain, "shard", axis=0, tiled=True),
        lax.all_gather(mlp_bias, "shard", axis=0, tiled=True),
        lax.all_gather(self_gain, "shard", axis=0, tiled=True),
        lax.all_gather(self_bias, "shard", axis=0, tiled=True),
    )
    full_query, full_key, full_value, full_output = (
        gathered[0],
        gathered[1],
        gathered[2],
        gathered[3],
    )
    gain_lat, bias_lat, gain_inp, bias_inp, gain_mlp, bias_mlp, gain_self, bias_self = [
        piece.astype(jnp.float32) for piece in gathered[4:]
    ]
    lat_rows = latents.astype(jnp.float32).reshape(rows, width)
    inp_rows = inputs.astype(jnp.float32).reshape(groups * inp_len, width)
    lat_value, lat_normed, lat_inv = norm_forward(lat_rows, gain_lat, bias_lat)
    lat_in = lat_value.astype(jnp.bfloat16)
    inp_value, inp_normed, inp_inv = norm_forward(inp_rows, gain_inp, bias_inp)
    inp_in = inp_value.astype(jnp.bfloat16)
    cross_q = (
        product(lat_in, full_query).astype(jnp.bfloat16).reshape(groups, lat_len, HEADS, HEAD_DIM)
    )
    cross_k = (
        product(inp_in, full_key).astype(jnp.bfloat16).reshape(groups, inp_len, HEADS, HEAD_DIM)
    )
    cross_v = (
        product(inp_in, full_value).astype(jnp.bfloat16).reshape(groups, inp_len, HEADS, HEAD_DIM)
    )
    allowed = latent_segment[:, None, :, None] == input_segment[:, None, None, :]
    scores = (
        jnp.einsum("glhd,gnhd->ghln", cross_q, cross_k, preferred_element_type=jnp.float32) * scale
    )
    masked = jnp.where(allowed, scores, NEGATIVE)
    part_max = jnp.max(masked, axis=-1)
    top = lax.pmax(part_max, "shard")
    total = lax.psum(
        jnp.sum(jnp.where(allowed, jnp.exp(masked - top[..., None]), 0.0), axis=-1), "shard"
    )
    cross_prob = jnp.where(allowed, jnp.exp(masked - top[..., None]), 0.0) / total[..., None]
    cross_prob_low = cross_prob.astype(jnp.bfloat16)
    part_out = jnp.einsum(
        "ghln,gnhd->glhd", cross_prob_low, cross_v, preferred_element_type=jnp.float32
    )
    attended = lax.psum(part_out.astype(jnp.bfloat16), "shard").astype(jnp.float32)
    attended_in = attended.reshape(rows, width).astype(jnp.bfloat16)
    h_one = lat_rows + product(attended_in, full_output)
    mlp_value, mlp_normed, mlp_inv = norm_forward(h_one, gain_mlp, bias_mlp)
    mlp_in = mlp_value.astype(jnp.bfloat16)
    pre_act = product(mlp_in, mlp_up)
    hidden_in = jax.nn.gelu(pre_act).astype(jnp.bfloat16)
    h_two = h_one + forward_total(product(hidden_in, mlp_down))
    self_value_n, self_normed, self_inv = norm_forward(h_two, gain_self, bias_self)
    self_in = self_value_n.astype(jnp.bfloat16)
    local_heads = self_query.shape[1] // HEAD_DIM
    local_width = local_heads * HEAD_DIM
    self_q = (
        product(self_in, self_query)
        .astype(jnp.bfloat16)
        .reshape(groups, lat_len, local_heads, HEAD_DIM)
    )
    self_k = (
        product(self_in, self_key)
        .astype(jnp.bfloat16)
        .reshape(groups, lat_len, local_heads, HEAD_DIM)
    )
    self_v = (
        product(self_in, self_value)
        .astype(jnp.bfloat16)
        .reshape(groups, lat_len, local_heads, HEAD_DIM)
    )
    self_scores = (
        jnp.einsum("glhd,gmhd->ghlm", self_q, self_k, preferred_element_type=jnp.float32) * scale
    )
    self_prob = jax.nn.softmax(self_scores, axis=-1)
    self_prob_low = self_prob.astype(jnp.bfloat16)
    self_att = jnp.einsum(
        "ghlm,gmhd->glhd", self_prob_low, self_v, preferred_element_type=jnp.float32
    )
    self_att_in = self_att.reshape(rows, local_width).astype(jnp.bfloat16)
    result = h_two + forward_total(product(self_att_in, self_output))
    new_latents = result.reshape(groups, lat_len, width).astype(jnp.bfloat16)
    grad_out = cotangent.astype(jnp.float32).reshape(rows, width)
    grad_branch = grad_out.astype(jnp.bfloat16)
    grad_self_output = inner_rows(self_att_in, grad_branch)
    grad_att = (
        outer_cols(grad_branch, self_output)
        .astype(jnp.bfloat16)
        .reshape(groups, lat_len, local_heads, HEAD_DIM)
    )
    delta = jnp.sum(grad_att.astype(jnp.float32) * self_att, axis=-1).transpose(0, 2, 1)
    grad_prob = jnp.einsum("glhd,gmhd->ghlm", grad_att, self_v, preferred_element_type=jnp.float32)
    grad_sv = jnp.einsum(
        "ghlm,glhd->gmhd", self_prob_low, grad_att, preferred_element_type=jnp.float32
    )
    grad_scores = (self_prob * (grad_prob - delta[..., None])).astype(jnp.bfloat16)
    grad_sq = (
        jnp.einsum("ghlm,gmhd->glhd", grad_scores, self_k, preferred_element_type=jnp.float32)
        * scale
    )
    grad_sk = (
        jnp.einsum("ghlm,glhd->gmhd", grad_scores, self_q, preferred_element_type=jnp.float32)
        * scale
    )
    grad_sq = grad_sq.astype(jnp.bfloat16).reshape(rows, local_width)
    grad_sk = grad_sk.astype(jnp.bfloat16).reshape(rows, local_width)
    grad_sv = grad_sv.astype(jnp.bfloat16).reshape(rows, local_width)
    grad_self_query = inner_rows(self_in, grad_sq)
    grad_self_key = inner_rows(self_in, grad_sk)
    grad_self_value = inner_rows(self_in, grad_sv)
    grad_self_in = backward_total(
        outer_cols(grad_sq, self_query)
        + outer_cols(grad_sk, self_key)
        + outer_cols(grad_sv, self_value)
    )
    grad_norm, gain_full, bias_full = norm_backward(grad_self_in, self_normed, self_inv, gain_self)
    grad_two = grad_out + grad_norm
    grad_self_gain = lax.dynamic_slice_in_dim(gain_full, column_start, width_part)
    grad_self_bias = lax.dynamic_slice_in_dim(bias_full, column_start, width_part)
    grad_mlp_branch = grad_two.astype(jnp.bfloat16)
    grad_mlp_down = inner_rows(hidden_in, grad_mlp_branch)
    grad_hidden = outer_cols(grad_mlp_branch, mlp_down)
    gelu_value, gelu_pull = jax.vjp(jax.nn.gelu, pre_act)
    grad_pre = gelu_pull(grad_hidden)[0].astype(jnp.bfloat16)
    grad_mlp_up = inner_rows(mlp_in, grad_pre)
    grad_mlp_in = backward_total(outer_cols(grad_pre, mlp_up))
    grad_norm, gain_full, bias_full = norm_backward(grad_mlp_in, mlp_normed, mlp_inv, gain_mlp)
    grad_one = grad_two + grad_norm
    grad_mlp_gain = lax.dynamic_slice_in_dim(gain_full, column_start, width_part)
    grad_mlp_bias = lax.dynamic_slice_in_dim(bias_full, column_start, width_part)
    grad_cross_branch = grad_one.astype(jnp.bfloat16)
    grad_cross_output = inner_rows(
        lax.dynamic_slice_in_dim(attended_in, column_start, width_part, 1), grad_cross_branch
    )
    grad_ca = (
        outer_cols(grad_cross_branch, full_output)
        .astype(jnp.bfloat16)
        .reshape(groups, lat_len, HEADS, HEAD_DIM)
    )
    cross_delta = jnp.sum(grad_ca.astype(jnp.float32) * attended, axis=-1).transpose(0, 2, 1)
    grad_cp = jnp.einsum("glhd,gnhd->ghln", grad_ca, cross_v, preferred_element_type=jnp.float32)
    grad_cv = jnp.einsum(
        "ghln,glhd->gnhd", cross_prob_low, grad_ca, preferred_element_type=jnp.float32
    )
    grad_cs = (cross_prob * (grad_cp - cross_delta[..., None])).astype(jnp.bfloat16)
    grad_cq_part = (
        jnp.einsum("ghln,gnhd->glhd", grad_cs, cross_k, preferred_element_type=jnp.float32) * scale
    )
    grad_ck = (
        jnp.einsum("ghln,glhd->gnhd", grad_cs, cross_q, preferred_element_type=jnp.float32) * scale
    )
    grad_cq = backward_total(grad_cq_part.reshape(rows, width)).astype(jnp.bfloat16)
    grad_ck = grad_ck.astype(jnp.bfloat16).reshape(groups * inp_len, width)
    grad_cv = grad_cv.astype(jnp.bfloat16).reshape(groups * inp_len, width)
    grad_cross_query = inner_rows(
        lax.dynamic_slice_in_dim(lat_in, column_start, width_part, 1), grad_cq
    )
    grad_lat_in = outer_cols(grad_cq, full_query)
    grad_norm, gain_full, bias_full = norm_backward(grad_lat_in, lat_normed, lat_inv, gain_lat)
    grad_latents = (grad_one + grad_norm).reshape(groups, lat_len, width).astype(jnp.bfloat16)
    grad_latent_gain = lax.dynamic_slice_in_dim(gain_full, column_start, width_part)
    grad_latent_bias = lax.dynamic_slice_in_dim(bias_full, column_start, width_part)
    key_term = inner_rows(inp_in, grad_ck)
    value_term = inner_rows(inp_in, grad_cv)
    grad_inp_in = outer_cols(grad_ck, full_key) + outer_cols(grad_cv, full_value)
    grad_inp, inp_gain_full, inp_bias_full = norm_backward(
        grad_inp_in, inp_normed, inp_inv, gain_inp
    )
    grad_inputs = grad_inp.reshape(groups, inp_len, width).astype(jnp.bfloat16)
    grad_cross_key, grad_cross_value, grad_input_gain, grad_input_bias = (
        lax.psum_scatter(
            key_term.astype(jnp.bfloat16), "shard", scatter_dimension=0, tiled=True
        ).astype(jnp.float32),
        lax.psum_scatter(
            value_term.astype(jnp.bfloat16), "shard", scatter_dimension=0, tiled=True
        ).astype(jnp.float32),
        lax.psum_scatter(
            inp_gain_full.astype(jnp.bfloat16), "shard", scatter_dimension=0, tiled=True
        ).astype(jnp.float32),
        lax.psum_scatter(
            inp_bias_full.astype(jnp.bfloat16), "shard", scatter_dimension=0, tiled=True
        ).astype(jnp.float32),
    )
    (
        grad_cross_query,
        grad_cross_key,
        grad_cross_value,
        grad_cross_output,
        grad_mlp_up,
        grad_mlp_down,
        grad_self_query,
        grad_self_key,
        grad_self_value,
        grad_self_output,
        grad_latent_gain,
        grad_latent_bias,
        grad_input_gain,
        grad_input_bias,
        grad_mlp_gain,
        grad_mlp_bias,
        grad_self_gain,
        grad_self_bias,
    ) = (
        lax.psum(grad_cross_query.astype(jnp.bfloat16), "grp").astype(jnp.float32),
        lax.psum(grad_cross_key.astype(jnp.bfloat16), "grp").astype(jnp.float32),
        lax.psum(grad_cross_value.astype(jnp.bfloat16), "grp").astype(jnp.float32),
        lax.psum(grad_cross_output.astype(jnp.bfloat16), "grp").astype(jnp.float32),
        lax.psum(grad_mlp_up.astype(jnp.bfloat16), "grp").astype(jnp.float32),
        lax.psum(grad_mlp_down.astype(jnp.bfloat16), "grp").astype(jnp.float32),
        lax.psum(grad_self_query.astype(jnp.bfloat16), "grp").astype(jnp.float32),
        lax.psum(grad_self_key.astype(jnp.bfloat16), "grp").astype(jnp.float32),
        lax.psum(grad_self_value.astype(jnp.bfloat16), "grp").astype(jnp.float32),
        lax.psum(grad_self_output.astype(jnp.bfloat16), "grp").astype(jnp.float32),
        lax.psum(grad_latent_gain.astype(jnp.bfloat16), "grp").astype(jnp.float32),
        lax.psum(grad_latent_bias.astype(jnp.bfloat16), "grp").astype(jnp.float32),
        lax.psum(grad_input_gain.astype(jnp.bfloat16), "grp").astype(jnp.float32),
        lax.psum(grad_input_bias.astype(jnp.bfloat16), "grp").astype(jnp.float32),
        lax.psum(grad_mlp_gain.astype(jnp.bfloat16), "grp").astype(jnp.float32),
        lax.psum(grad_mlp_bias.astype(jnp.bfloat16), "grp").astype(jnp.float32),
        lax.psum(grad_self_gain.astype(jnp.bfloat16), "grp").astype(jnp.float32),
        lax.psum(grad_self_bias.astype(jnp.bfloat16), "grp").astype(jnp.float32),
    )
    return (
        new_latents,
        grad_latents,
        grad_inputs,
        grad_cross_query,
        grad_cross_key,
        grad_cross_value,
        grad_cross_output,
        grad_mlp_up,
        grad_mlp_down,
        grad_self_query,
        grad_self_key,
        grad_self_value,
        grad_self_output,
        grad_latent_gain,
        grad_latent_bias,
        grad_input_gain,
        grad_input_bias,
        grad_mlp_gain,
        grad_mlp_bias,
        grad_self_gain,
        grad_self_bias,
    )


def solution(mesh):
    laid_out = mesh.shape["shard"] == 2 and mesh.shape["grp"] == 16
    return jax.shard_map(
        per_device_pair if laid_out else per_device,
        mesh=mesh,
        in_specs=(
            P("grp", None, None),
            P("grp", "shard", None),
            P("grp", None),
            P("grp", "shard"),
            P("shard", None),
            P("shard", None),
            P("shard", None),
            P("shard", None),
            P(None, "shard"),
            P("shard", None),
            P(None, "shard"),
            P(None, "shard"),
            P(None, "shard"),
            P("shard", None),
            P("shard"),
            P("shard"),
            P("shard"),
            P("shard"),
            P("shard"),
            P("shard"),
            P("shard"),
            P("shard"),
            P("grp", None, None),
        ),
        out_specs=(
            P("grp", None, None),
            P("grp", None, None),
            P("grp", "shard", None),
            P("shard", None),
            P("shard", None),
            P("shard", None),
            P("shard", None),
            P(None, "shard"),
            P("shard", None),
            P(None, "shard"),
            P(None, "shard"),
            P(None, "shard"),
            P("shard", None),
            P("shard"),
            P("shard"),
            P("shard"),
            P("shard"),
            P("shard"),
            P("shard"),
            P("shard"),
            P("shard"),
        ),
        check_vma=False,
    )
```

```python
import jax
import jax.numpy as jnp
from jax import lax
from jax.experimental import pallas as pl
from jax.experimental.pallas import tpu as pltpu
from jax.sharding import PartitionSpec as P

HEADS = 8
HEAD_DIM = 128


EPSILON = 1e-05
NEGATIVE = -1e30

BF = jnp.bfloat16
F32 = jnp.float32
MESH = pl.DeviceIdType.MESH
LAT = 128
INP = 784
D = 1024
HALF = 512
HID = 2048
ROWS = 2 * LAT
NROWS = 2 * INP
SCALE = HEAD_DIM ** (-0.5)
MIB = 1 << 20


def nn(a, b):
    return lax.dot_general(a, b, (((1,), (0,)), ((), ())), preferred_element_type=F32)


def nt(a, b):
    return lax.dot_general(a, b, (((1,), (1,)), ((), ())), preferred_element_type=F32)


def tn(a, b):
    return lax.dot_general(a, b, (((0,), (0,)), ((), ())), preferred_element_type=F32)


def place():
    g = lax.axis_index("grp")
    x = lax.axis_index("shard")
    c = lax.rem(g, 2)
    y = lax.rem(g // 2, 2)
    a = lax.rem(g // 4, 2)
    b = g // 8
    return dict(
        x=x, c=c, y=y, a=a, b=b,
        xp=(g, 1 - x),
        cp=(g + 1 - 2 * c, x),
        yp=(g + 2 - 4 * y, x),
        ap=(g + 4 - 8 * a, x),
        bp=(g + 8 - 16 * b, x),
        mp=(g + 4 - 8 * b, x),
    )


def greet(partners):
    barrier = pltpu.get_barrier_semaphore()
    for partner in partners:
        pl.semaphore_signal(barrier, inc=1, device_id=partner, device_id_type=MESH)
    pl.semaphore_wait(barrier, len(partners))


def remote(src, dst, send, recv, partner):
    return pltpu.make_async_remote_copy(
        src_ref=src, dst_ref=dst, send_sem=send, recv_sem=recv,
        device_id=partner, device_id_type=MESH,
    )


def norm(v, gain, shift):
    cen = v - jnp.mean(v, axis=-1, keepdims=True)
    inv = lax.rsqrt(jnp.mean(cen * cen, axis=-1, keepdims=True) + EPSILON)
    return cen * inv * gain + shift


def vec_row(vecs, i):
    return jnp.concatenate([vecs[0, i:i + 1, :], vecs[1, i:i + 1, :]], axis=1)


def span(first, last, body):
    lax.fori_loop(first, last, lambda i, carry: (body(i), carry)[1], 0)


def loop(n, body):
    span(0, n, body)


def first_kernel(
    lat_h, inp_h, seglat_h, seginp_h, v0, v1, v2, v3, v4, v5, v6, v7, wk_h, wv_h, wq_h, wo_h, up_h, down_h,
    sq_h, sk_h, sv_h, so_h, cot_h,
    wf_o, ck_o, cv_o, inin_o, latin_o, cq_o, att_o, st_o, vec_o, hone_o, htwo_o,
    mlpin_o, selfin_o, pre_o, hid_o, ds_o, slow_o, mask_o,
    wf, inp, inin, ck, cv, lat, latin, cq, mask, segs, axb, stx, att, st, vecs,
    hone, htwo, mlpin, pre, hid, xm, selfin, wup, wdown, wself, wso, cot, qkv, dself,
    ds, slow, seglat, seginp, g0, g1, g2, g3, g4, g5, g6, g7, lsem, osem, xs, xr, ys, yr, c0s, c0r, c1s, c1r, ms, mr,
):
    me = place()
    x, y, c = me["x"], me["y"], me["c"]
    xp, yp, cp = me["xp"], me["yp"], me["cp"]
    nlocal = [0]
    nout = [0]

    def load(src, dst):
        copy = pltpu.make_async_copy(src, dst, lsem.at[nlocal[0]])
        nlocal[0] += 1
        copy.start()
        return copy

    outs = []

    def store(src, dst):
        copy = pltpu.make_async_copy(src, dst, osem.at[nout[0]])
        nout[0] += 1
        copy.start()
        outs.append(copy)

    own = pl.ds(pl.multiple_of(x * HALF, HALF), HALF)
    gains = (g0, g1, g2, g3, g4, g5, g6, g7)
    in_gains = [load(v, g) for v, g in zip((v0, v1, v2, v3, v4, v5, v6, v7), gains)]
    in_seg = [load(seglat_h, seglat), load(seginp_h, seginp)]
    in_inp = load(inp_h, inp)
    in_lat = load(lat_h, lat)
    in_cot = load(cot_h, cot)
    in_so = load(so_h, wso)
    greet((xp, yp, cp))
    for i, (copy, g) in enumerate(zip(in_gains, gains)):
        copy.wait()
        vecs[x, i:i + 1, :] = g[...].astype(F32).reshape(1, HALF)
    vec_move = remote(vecs.at[x], vecs.at[x], xs.at[4], xr.at[4], xp)
    vec_move.start()
    weights = (wk_h, wv_h, wq_h, wo_h)
    quarter = 2 * y + c

    def part(w, side, q):
        return wf.at[w, pl.ds(pl.multiple_of(side * HALF + q * 128, 128), 128)]

    x_moves = []
    for w in range(4):
        src = weights[w].at[pl.ds(pl.multiple_of(quarter * 128, 128), 128)]
        move = remote(src, part(w, x, quarter), xs.at[w], xr.at[w], xp)
        move.start()
        x_moves.append(move)
    in_w = [load(weights[w], wf.at[w, own]) for w in range(4)]
    in_self = [load(h, wself.at[i]) for i, h in enumerate((sq_h, sk_h, sv_h))]
    in_up = load(up_h, wup)
    in_down = load(down_h, wdown)
    pending = []

    def forward_x(w):
        x_moves[w].wait()
        for sems, partner in (((ys, yr), yp), ((c0s, c0r), cp)):
            block = part(w, 1 - x, quarter)
            move = remote(block, block, sems[0].at[w], sems[1].at[w], partner)
            move.start()
            pending.append(move)

    def forward_y(w):
        block = part(w, 1 - x, quarter)
        remote(block, block, ys.at[w], yr.at[w], yp).wait_recv()
        block = part(w, 1 - x, 2 * (1 - y) + c)
        move = remote(block, block, c1s.at[w], c1r.at[w], cp)
        move.start()
        pending.append(move)

    def whole(w):
        block = part(w, 1 - x, quarter)
        remote(block, block, c0s.at[w], c0r.at[w], cp).wait_recv()
        remote(block, block, c1s.at[w], c1r.at[w], cp).wait_recv()
        in_w[w].wait()
        store(wf.at[w], wf_o.at[w])

    for copy in in_seg:
        copy.wait()
    segs[...] = jnp.zeros_like(segs)
    segs[0:2, 0:INP] = seginp[...].astype(F32)
    for g in range(2):
        lat_row = seglat[g:g + 1, :].astype(F32)
        for j in range(7):
            count = min(128, INP - j * 128)
            col = jnp.broadcast_to(segs[g:g + 1, j * 128:(j + 1) * 128], (128, 128)).T
            mask[g * INP + j * 128:g * INP + j * 128 + count, :] = jnp.where(
                col[:count] == lat_row, 0.0, NEGATIVE
            ).astype(BF)
    store(mask, mask_o)
    in_cot.wait()
    in_so.wait()
    dself[...] = nt(cot[...], wso[...]).astype(BF)
    in_inp.wait()
    vec_move.wait()
    store(vecs, vec_o)
    gain_inp, bias_inp = vec_row(vecs, 2), vec_row(vecs, 3)

    def norm_rows(i):
        rows = pl.ds(pl.multiple_of(i * 32, 32), 32)
        inin[rows, :] = norm(inp[rows, :].astype(F32), gain_inp, bias_inp).astype(BF)

    span(0, 24, norm_rows)
    forward_x(0)
    span(24, 49, norm_rows)
    store(inin, inin_o)
    forward_x(1)
    forward_y(0)
    in_lat.wait()
    latin[...] = norm(lat[...].astype(F32), vec_row(vecs, 0), vec_row(vecs, 1)).astype(BF)
    store(latin, latin_o)

    def project(target, w, half):
        cols = slice(half * HALF, (half + 1) * HALF)

        def body(i):
            rows = pl.ds(pl.multiple_of(i * INP, 16), INP)
            target[rows, cols] = nn(inin[rows, :], wf[w, :, cols]).astype(BF)

        loop(2, body)

    whole(0)
    project(ck, 0, 0)
    forward_x(2)
    forward_y(1)
    project(ck, 0, 1)
    store(ck, ck_o)
    whole(1)
    forward_x(3)
    forward_y(2)
    project(cv, 1, 0)
    project(cv, 1, 1)
    store(cv, cv_o)
    whole(2)
    cq[...] = nn(latin[...], wf[2]).astype(BF)
    store(cq, cq_o)
    forward_y(3)

    def head(g, h):
        cols = pl.ds(pl.multiple_of(h * HEAD_DIM, HEAD_DIM), HEAD_DIM)
        n_rows = slice(g * INP, (g + 1) * INP)
        s = nt(ck[n_rows, cols], cq[g * LAT:(g + 1) * LAT, cols]) * SCALE + mask[n_rows, :].astype(F32)
        top = jnp.maximum(jnp.max(s, axis=0, keepdims=True), 0.1 * NEGATIVE)
        e = jnp.exp(s - top)
        total = jnp.sum(e, axis=0, keepdims=True)
        out = tn(cv[n_rows, cols], e.astype(BF))
        out = out * jnp.where(total > 0.0, 1.0 / total, 0.0)
        axb[x, pl.ds(pl.multiple_of(g * D + h * HEAD_DIM, HEAD_DIM), HEAD_DIM), :] = out.astype(BF)
        stx[x, g, pl.ds(h, 1), :] = top
        stx[x, g, pl.ds(HEADS + h, 1), :] = total

    a_moves = []
    for g in range(2):
        def pair(i, g=g):
            head(g, 2 * i)
            head(g, 2 * i + 1)

        loop(HEADS // 2, pair)
        block = axb.at[x, pl.ds(g * D, D)]
        for src, k in ((block, 0), (stx.at[x, g], 1)):
            move = remote(src, src, ms.at[2 * g + k], mr.at[2 * g + k], xp)
            move.start()
            a_moves.append(move)
    whole(3)
    in_up.wait()
    in_down.wait()
    m_moves = []

    def mlp_group(g):
        a_moves[2 * g].wait()
        a_moves[2 * g + 1].wait()
        for h in range(HEADS):
            m0, m1 = stx[0, g, h:h + 1, :], stx[1, g, h:h + 1, :]
            top = jnp.maximum(m0, m1)
            w0 = stx[0, g, HEADS + h:HEADS + h + 1, :] * jnp.exp(m0 - top)
            w1 = stx[1, g, HEADS + h:HEADS + h + 1, :] * jnp.exp(m1 - top)
            inv = 1.0 / (w0 + w1)
            rows = slice(g * D + h * HEAD_DIM, g * D + (h + 1) * HEAD_DIM)
            mixed = axb[0, rows, :].astype(F32) * (w0 * inv) + axb[1, rows, :].astype(F32) * (w1 * inv)
            att[rows, :] = mixed.astype(BF)
            st[g, h:h + 1, :] = top
            st[g, HEADS + h:HEADS + h + 1, :] = inv
        rows = slice(g * LAT, (g + 1) * LAT)
        one = lat[rows, :].astype(F32) + tn(att[g * D:(g + 1) * D, :], wf[3])
        hone[rows, :] = one
        mlpin[rows, :] = norm(one, vec_row(vecs, 4), vec_row(vecs, 5)).astype(BF)
        for j in range(4):
            cols = slice(j * HALF, (j + 1) * HALF)
            u = nn(mlpin[rows, :], wup[:, cols])
            pre[rows, cols] = u
            hid[rows, cols] = jax.nn.gelu(u).astype(BF)
        for j in range(2):
            cols = slice(j * HALF, (j + 1) * HALF)
            xm[x, g, :, cols] = nn(hid[rows, :], wdown[:, cols]).astype(BF)
            part = xm.at[x, g, :, pl.ds(j * HALF, HALF)]
            move = remote(part, part, ms.at[4 + 2 * g + j], mr.at[4 + 2 * g + j], xp)
            move.start()
            m_moves.append(move)

    def self_group(g):
        rows = slice(g * LAT, (g + 1) * LAT)
        m_moves[2 * g].wait()
        m_moves[2 * g + 1].wait()
        two = hone[rows, :] + (xm[0, g].astype(F32) + xm[1, g].astype(F32))
        htwo[rows, :] = two
        selfin[rows, :] = norm(two, vec_row(vecs, 6), vec_row(vecs, 7)).astype(BF)
        for i in range(3):
            qkv[i, rows, :] = nn(selfin[rows, :], wself[i]).astype(BF)
        for h in range(4):
            cols = slice(h * HEAD_DIM, (h + 1) * HEAD_DIM)
            q, k, v = qkv[0, rows, cols], qkv[1, rows, cols], qkv[2, rows, cols]
            do = dself[rows, cols]
            s = nt(q, k) * SCALE
            e = jnp.exp(s - jnp.max(s, axis=1, keepdims=True))
            p = e / jnp.sum(e, axis=1, keepdims=True)
            p_low = p.astype(BF)
            o = nn(p_low, v)
            slow[rows, cols] = o.astype(BF)
            delta = jnp.sum(do.astype(F32) * o, axis=1, keepdims=True)
            dp = nt(do, v)
            dsc = (p * (dp - delta)).astype(BF)
            ds[0, rows, cols] = (nn(dsc, k) * SCALE).astype(BF)
            ds[1, rows, cols] = (tn(dsc, q) * SCALE).astype(BF)
            ds[2, rows, cols] = tn(p_low, do).astype(BF)

    mlp_group(0)
    mlp_group(1)
    store(att, att_o)
    store(st, st_o)
    store(hone, hone_o)
    store(mlpin, mlpin_o)
    store(pre, pre_o)
    store(hid, hid_o)
    for copy in in_self:
        copy.wait()
    for g in range(2):
        self_group(g)
        rows = pl.ds(g * LAT, LAT)
        store(ds.at[:, rows], ds_o.at[:, rows])
        for src, dst in ((slow, slow_o), (htwo, htwo_o), (selfin, selfin_o)):
            store(src.at[rows], dst.at[rows])
    for move in pending:
        move.wait_send()
    for copy in outs:
        copy.wait()


def run_first(args):
    any_spec = pl.BlockSpec(memory_space=pl.ANY)
    outs = [
        ((4, D, D), BF), ((NROWS, D), BF), ((NROWS, D), BF), ((NROWS, D), BF),
        ((ROWS, D), BF), ((ROWS, D), BF), ((2 * D, LAT), BF), ((2, 16, LAT), F32),
        ((2, 8, HALF), F32), ((ROWS, D), F32), ((ROWS, D), F32), ((ROWS, D), BF),
        ((ROWS, D), BF), ((ROWS, HID), F32), ((ROWS, HID), BF), ((3, ROWS, HALF), BF),
        ((ROWS, HALF), BF), ((NROWS, LAT), BF),
    ]
    scratch = [
        ((4, D, D), BF), ((NROWS, D), BF), ((NROWS, D), BF), ((NROWS, D), BF), ((NROWS, D), BF),
        ((ROWS, D), BF), ((ROWS, D), BF), ((ROWS, D), BF), ((NROWS, LAT), BF), ((8, 896), F32),
        ((2, 2 * D, LAT), BF), ((2, 2, 16, LAT), F32), ((2 * D, LAT), BF), ((2, 16, LAT), F32),
        ((2, 8, HALF), F32), ((ROWS, D), F32), ((ROWS, D), F32), ((ROWS, D), BF),
        ((ROWS, HID), F32), ((ROWS, HID), BF), ((2, 2, LAT, D), BF), ((ROWS, D), BF),
        ((D, HID), BF), ((HID, D), BF), ((3, D, HALF), BF), ((HALF, D), BF), ((ROWS, D), BF),
        ((3, ROWS, HALF), BF), ((ROWS, HALF), BF), ((3, ROWS, HALF), BF), ((ROWS, HALF), BF),
        ((2, LAT), jnp.int32), ((2, INP), jnp.int32), *[((HALF,), BF)] * 8,
    ]
    dma = pltpu.SemaphoreType.DMA
    return pl.pallas_call(
        first_kernel,
        out_shape=[jax.ShapeDtypeStruct(*o) for o in outs],
        in_specs=[any_spec] * len(args),
        out_specs=[any_spec] * len(outs),
        scratch_shapes=[pltpu.VMEM(*s) for s in scratch]
        + [dma((26,)), dma((28,))] + [dma((5,))] * 2 + [dma((4,))] * 6 + [dma((8,))] * 2,
        compiler_params=pltpu.CompilerParams(
            collective_id=0, has_side_effects=True, vmem_limit_bytes=58 * MIB
        ),
        name="forward",
    )(*args)


def norm_back(v, dy, gain):
    cen = v - jnp.mean(v, axis=-1, keepdims=True)
    inv = lax.rsqrt(jnp.mean(cen * cen, axis=-1, keepdims=True) + EPSILON)
    n = cen * inv
    t = dy * gain
    dv = inv * (t - jnp.mean(t, axis=-1, keepdims=True) - n * jnp.mean(t * n, axis=-1, keepdims=True))
    return (
        dv,
        jnp.sum(dy * n, axis=0, keepdims=True),
        jnp.sum(dy, axis=0, keepdims=True),
    )


def gelu_slope(u):
    root = (2.0 / jnp.pi) ** 0.5
    t = jnp.tanh(root * (u + 0.044715 * u * u * u))
    return 0.5 * (1.0 + t) + 0.5 * u * (1.0 - t * t) * root * (1.0 + 3.0 * 0.044715 * u * u)


PART = 256
KINDS = "zyyyzzyyzyyzyyzz" + "yzyyyzyzyyzyyyyz"
SLOTS = (4, 4, 4, 4, 2, 3)
ORDER = (
    0, 1, 2, 3, 4, 5, 6, 7, 8, 14, 9, 10, 11, 12, 15, 25, 13, 18, 17, 16, 19, 21, 22, 23, 26, 27, 28, 20,
    24, 29, 30, 31, 32, 33, 34, 35, 36, 37, 38, 39, 40, 41, 42, 43, 44, 45, 46, 47, 48, 49, 50, 51, 52, 53, 54, 55, 56,
)
EVENTS = (
    ((0, 0), (1, 0),),
    (),
    (),
    ((0, 1), (2, 0), (1, 1), (3, 0),),
    (),
    (),
    ((2, 1), (4, 0), (1, 2), (3, 1), (5, 0), (4, 1), (6, 0), (0, 2), (2, 2), (5, 1), (7, 0), (6, 1), (1, 3),
     (3, 2),),
    ((7, 1),),
    ((0, 3),),
    ((8, 0), (9, 0),),
    ((6, 2),),
    ((1, 4), (4, 2),),
    (),
    ((9, 1), (2, 3), (8, 1),),
    ((10, 0), (11, 0), (0, 4), (1, 5), (7, 2), (4, 3),),
    (),
    ((10, 1), (2, 4), (11, 1), (5, 2),),
    (),
    (),
    ((0, 5), (3, 3), (1, 6), (12, 0), (13, 0),),
    (),
    ((4, 4), (2, 5), (9, 2), (6, 3), (5, 3), (1, 7), (12, 1), (14, 0), (3, 4),),
    ((14, 1),),
    ((0, 6), (4, 5), (2, 6), (8, 2),),
    (),
    ((5, 4), (3, 5), (10, 2), (7, 3), (0, 7), (6, 4), (13, 1), (15, 0), (16, 0), (2, 7),),
    (),
    (),
    ((8, 3),),
    ((15, 1), (17, 0),),
    ((4, 6), (5, 5), (3, 6), (11, 2),),
    (),
    ((6, 5), (12, 2), (16, 1), (9, 3), (18, 0), (4, 7), (7, 4), (17, 1), (19, 0), (3, 7),),
    (),
    ((8, 4), (11, 3),),
    (),
    ((6, 6), (5, 6),),
    ((9, 4), (14, 2),),
    (),
    ((6, 7), (10, 3), (8, 5), (7, 5), (5, 7), (13, 2), (18, 1), (20, 0),),
    (),
    ((11, 4), (9, 5), (14, 3), (16, 2), (19, 1), (21, 0),),
    ((7, 6), (10, 4), (21, 1), (15, 2),),
    ((7, 7), (8, 6), (12, 3), (11, 5),),
    ((15, 3), (14, 4), (9, 6), (8, 7), (10, 5), (18, 2), (20, 1), (22, 0), (23, 0), (17, 2),),
    ((12, 4),),
    ((9, 7), (11, 6), (13, 3), (14, 5), (23, 1),),
    ((15, 4), (16, 3),),
    (),
    ((17, 3), (10, 6), (11, 7), (12, 5), (19, 2), (22, 1), (24, 0), (25, 0),),
    ((10, 7), (13, 4), (21, 2),),
    ((14, 6), (17, 4), (15, 5), (18, 3),),
    ((12, 6), (16, 4), (13, 5), (14, 7), (20, 2), (24, 1), (26, 0),),
    ((12, 7), (21, 3), (23, 2),),
    ((15, 6), (17, 5), (19, 3), (13, 6), (26, 1),),
    ((18, 4), (20, 3), (15, 7), (16, 5), (22, 2), (25, 1), (13, 7), (27, 0), (28, 0),),
    ((21, 4), (23, 3), (19, 4), (17, 6), (16, 6), (26, 2), (20, 4), (17, 7), (18, 5), (24, 2), (-1, 0), (16, 7),
     (22, 3), (27, 1), (29, 0), (21, 5), (19, 5), (25, 2), (23, 4), (28, 1), (30, 0), (24, 3), (-1, 1), (26, 3),
     (20, 5), (18, 6), (22, 4), (25, 3), (18, 7), (27, 2), (29, 1), (31, 0), (23, 5), (-1, 2), (21, 6), (19, 6),
     (31, 1), (24, 4), (27, 3), (21, 7), (22, 5), (28, 2), (19, 7), (30, 1), (25, 4), (-1, 3), (26, 4), (27, 4),
     (31, 2), (23, 6), (20, 6), (26, 5), (28, 3), (23, 7), (24, 5), (29, 2), (20, 7), (-1, 4), (31, 3), (25, 5),
     (22, 6), (29, 3), (28, 4), (22, 7), (27, 5), (30, 2), (24, 6), (29, 4), (-1, 5), (30, 3), (24, 7), (26, 6),
     (31, 4), (26, 7), (28, 5), (25, 6), (30, 4), (25, 7), (29, 5), (27, 6), (31, 5), (27, 7), (30, 5), (28, 6),
     (28, 7), (29, 6), (29, 7), (31, 6), (30, 6), (31, 7), (30, 7),),
)


def second_kernel(
    wf_h, ck_h, cv_h, inin_h, latin_h, cq_h, att_h, st_h, vec_h, hone_h, htwo_h,
    mlpin_h, selfin_h, pre_h, hid_h, ds_h, slow_h, mask_h,
    lat_h, inp_h, up_h, down_h, sq_h, sk_h, sv_h, so_h, cot_h,
    newlat_o, glat_o, ginp_o, gq_o, gk_o, gv_o, go_o, gup_o, gdown_o, gsq_o, gsk_o,
    gsv_o, gso_o, gvec_o,
    z, wf, cq, att, st, vecs, hone, htwo, etwo, mlpin, selfin, pre, hid, ds,
    slow, mask, cot, elow2, elow1, dpre, dcr, xb, grad, other, t0, ty, te, tm, tn_mid, tn_y,
    xk, gvec, gvr,
    lsem, osem, gs, gr, xs, xr, vs, vr, free,
):
    me = place()
    x, c = me["x"], me["c"]
    xp, yp, cp, ap, bp = me["xp"], me["yp"], me["cp"], me["ap"], me["bp"]
    counts = [0, 0]
    outs = []

    def load(src, dst):
        copy = pltpu.make_async_copy(src, dst, lsem.at[counts[0]])
        counts[0] += 1
        copy.start()
        return copy

    def store(src, dst):
        copy = pltpu.make_async_copy(src, dst, osem.at[counts[1]])
        counts[1] += 1
        copy.start()
        outs.append(copy)

    in_early = [load(slow_h, slow), load(cot_h, cot), load(selfin_h, selfin)]
    in_ds = load(ds_h, ds)
    in_self = [
        load(sq_h, z.at[pl.ds(4096, D), pl.ds(0, HALF)]),
        load(sk_h, z.at[pl.ds(4096, D), pl.ds(HALF, HALF)]),
        load(sv_h, z.at[pl.ds(5120, D), pl.ds(0, HALF)]),
    ]
    in_early += [
        load(so_h.at[:, pl.ds(j * HALF, HALF)], z.at[pl.ds(5120 + j * HALF, HALF), pl.ds(HALF, HALF)])
        for j in range(2)
    ]
    in_two = [load(htwo_h, htwo), load(vec_h, vecs)]
    in_mlp = [
        load(pre_h, pre), load(down_h, z.at[pl.ds(0, HID)]),
        load(up_h.at[:, pl.ds(0, D)], z.at[pl.ds(HID, D)]),
        load(up_h.at[:, pl.ds(D, D)], z.at[pl.ds(HID + D, D)]),
    ]
    in_mid = [
        load(hid_h.at[:, pl.ds(j * D, D)], hid.at[pl.ds(j * ROWS, ROWS)]) for j in range(2)
    ] + [load(mlpin_h, mlpin), load(hone_h, hone)]
    in_cross = [
        load(wf_h, wf), load(att_h, att), load(st_h, st), load(cq_h, cq), load(mask_h, mask),
    ]
    barrier = pltpu.get_barrier_semaphore()
    for partner in (xp, yp, cp, ap, bp):
        pl.semaphore_signal(barrier, inc=1, device_id=partner, device_id_type=MESH)

    @pl.when(me["a"] != me["b"])
    def _():
        pl.semaphore_signal(barrier, inc=1, device_id=me["mp"], device_id_type=MESH)
        pl.semaphore_wait(barrier, 6)

    @pl.when(me["a"] == me["b"])
    def _():
        pl.semaphore_wait(barrier, 5)


    def wait_all(copies):
        for copy in copies:
            copy.wait()

    a_bit, b_bit, y_bit = me["a"], me["b"], me["y"]
    at_end = a_bit == b_bit
    at_middle = a_bit != b_bit
    mp = me["mp"]

    def cols_of(core):
        return pl.ds(pl.multiple_of(core * HALF, HALF), HALF)

    def block(k, off, size, core):
        return grad.at[pl.ds(pl.multiple_of(k * PART + off, 16), size), cols_of(core)]

    def add(base, size, part):
        def body(i):
            rows = pl.ds(pl.multiple_of(base + i * 64, 64), 64)
            grad[rows, cols_of(c)] += part[pl.ds(pl.multiple_of(i * 64, 64), 64), :]

        loop(size // 64, body)

    def move(k, stage, src, dst, partner):
        return remote(src, dst, gs.at[k * 7 + stage], gr.at[k * 7 + stage], partner)

    def release(k, n, partner):
        pl.semaphore_signal(free.at[k * 4 + n], inc=1, device_id=partner, device_id_type=MESH)

    def claim(k, n):
        pl.semaphore_wait(free.at[k * 4 + n], 1)

    def event(k, s):
        base, size, half = k * PART, PART, PART // 2
        kind = KINDS[k]
        n = KINDS[:k].count(kind)
        everything = block(k, 0, size, c)
        core_in = t0.at[k % t0.shape[0]]
        core_move = move(k, 0, block(k, 0, size, 1 - c), core_in, cp)
        core_back = move(k, 6, everything, everything, cp)
        if s == 0:
            core_move.start()
            return
        if s == 7:
            core_back.wait()
            deliver(k)
            return
        if s == 1:
            core_move.wait()
            if kind == "y":
                release(k, 0, cp)
            else:
                pl.when(at_end)(lambda: release(k, 0, cp))
                pl.when(at_middle)(lambda: release(k, 3, ap))
            add(base, size, core_in)
            if k >= 28:
                finish_x((k - 28) // 2, k % 2)
        if kind == "y":
            off = y_bit * half
            own = block(k, off, half, c)
            y_in, end_in, mid_in = (
                ty.at[n % ty.shape[0]], te.at[n % te.shape[0]], tm.at[n % tm.shape[0]]
            )
            y_move = move(k, 1, block(k, (1 - y_bit) * half, half, c), y_in, yp)
            end_move = move(k, 2, own, end_in, ap)
            mid_move = move(k, 3, own, mid_in, mp)
            end_back = move(k, 4, own, own, ap)
            y_back = move(k, 5, own, own, yp)
            if s == 1:
                y_move.start()
            elif s == 2:
                y_move.wait()
                release(k, 1, yp)
                add(base + off, half, y_in)
                pl.when(at_end)(end_move.start)
            elif s == 3:
                @pl.when(at_end)
                def _():
                    end_move.wait_send()
                    release(k, 2, ap)

                @pl.when(at_middle)
                def _():
                    end_move.wait_recv()
                    add(base + off, half, end_in)
                    mid_move.start()
            elif s == 4:
                @pl.when(at_middle)
                def _():
                    mid_move.wait()
                    add(base + off, half, mid_in)
                    claim(k, 2)
                    end_back.start()
            elif s == 5:
                pl.when(at_end)(end_back.wait_recv)
                pl.when(at_middle)(end_back.wait_send)
                claim(k, 1)
                y_back.start()
            elif s == 6:
                y_back.wait()
                claim(k, 0)
                core_back.start()
            return
        off = b_bit * half
        own = block(k, off, half, c)
        mid_in, y_in = tn_mid.at[n % tn_mid.shape[0]], tn_y.at[n % tn_y.shape[0]]
        end_in = block(k, 0, size, 1 - c)
        end_move = move(k, 1, everything, end_in, ap)
        mid_move = move(k, 2, block(k, (1 - b_bit) * half, half, c), mid_in, mp)
        y_move = move(k, 3, own, y_in, yp)
        mid_back = move(k, 4, own, own, mp)
        end_back = move(k, 5, everything, everything, ap)
        if s == 1:
            @pl.when(at_end)
            def _():
                claim(k, 3)
                end_move.start()
        elif s == 2:
            @pl.when(at_end)
            def _():
                end_move.wait_send()
                release(k, 1, ap)

            @pl.when(at_middle)
            def _():
                end_move.wait_recv()
                add(base, size, end_in)
                release(k, 0, cp)
                mid_move.start()
        elif s == 3:
            @pl.when(at_middle)
            def _():
                mid_move.wait()
                release(k, 2, mp)
                add(base + off, half, mid_in)
                y_move.start()
        elif s == 4:
            @pl.when(at_middle)
            def _():
                y_move.wait()
                add(base + off, half, y_in)
                claim(k, 2)
                mid_back.start()
        elif s == 5:
            @pl.when(at_middle)
            def _():
                mid_back.wait()
                claim(k, 1)
                end_back.start()
        elif s == 6:
            pl.when(at_end)(end_back.wait_recv)
            pl.when(at_middle)(end_back.wait_send)
            claim(k, 0)
            core_back.start()

    def deliver(k):
        n, top = k // 2, (k % 2) * PART
        rows = pl.ds(k * PART, PART)
        left, right = grad.at[rows, pl.ds(0, HALF)], grad.at[rows, pl.ds(HALF, HALF)]
        first, second = pl.ds(top, PART), pl.ds(HALF + top, PART)
        if 1 <= n <= 3:
            target = (gsq_o, gsk_o, gsv_o)[n - 1]
            store(left, target.at[first])
            store(right, target.at[second])
        elif 8 <= n <= 11:
            cols = pl.ds((n - 8) * HALF, HALF)
            store(left, gup_o.at[first, cols])
            store(right, gup_o.at[second, cols])
        elif 4 <= n <= 7:
            store(grad.at[rows], gdown_o.at[pl.ds((n - 4) * HALF + top, PART)])
        else:
            target = {0: gso_o, 12: go_o, 13: gq_o, 14: gk_o, 15: gv_o}[n]
            store(grad.at[rows], target.at[first])

    k_moves = {}

    def start_core(w):
        src = other.at[w, :, pl.ds(pl.multiple_of((1 - c) * HALF, HALF), HALF)]
        move = remote(src, hid.at[:, pl.ds(w * HALF, HALF)], xs.at[8 + w], xr.at[8 + w], cp)
        move.start()
        k_moves[w, 0] = move

    def start_x(w):
        k_moves[w, 0].wait()
        cols = pl.ds(pl.multiple_of(c * HALF, HALF), HALF)

        def body(i):
            rows = pl.ds(pl.multiple_of(i * 64, 64), 64)
            other[w, rows, cols] = (
                other[w, rows, cols].astype(F32) + hid[rows, w * HALF:(w + 1) * HALF].astype(F32)
            ).astype(BF)

        loop(HALF // 64, body)
        move = remote(other.at[w, :, cols], xk.at[w], xs.at[10 + w], xr.at[10 + w], xp)
        move.start()
        k_moves[w, 1] = move

    def finish_x(w, part):
        if (w, 1) in k_moves:
            k_moves.pop((w, 1)).wait()
        add((14 + w) * HALF + part * 256, 256, xk.at[w, pl.ds(part * 256, 256)])

    def exchange(n, part, index):
        move = remote(
            xb.at[(n, x) + part], xb.at[(n, x) + part], xs.at[index], xr.at[index], xp
        )
        move.start()
        return move

    def both(n, rows):
        return xb[n, 0, rows, :].astype(F32) + xb[n, 1, rows, :].astype(F32)

    def fill(k, half, value):
        grad[k * HALF:(k + 1) * HALF, half * HALF:(half + 1) * HALF] = value.astype(BF)

    gvec[...] = jnp.zeros_like(gvec)
    lat, latin, dcq = cot, mlpin, elow2
    ck, cv = z.at[pl.ds(0, NROWS)], z.at[pl.ds(NROWS, NROWS)]
    inin, inp = z.at[pl.ds(2 * NROWS, NROWS)], z.at[pl.ds(3 * NROWS, NROWS)]
    gain_lat, gain_inp, gain_mlp, gain_self = 0, 2, 4, 6
    m_self, m_new, m_mlp, m_query, later = [], [], [], [], {}

    def self_back(j):
        if j == 0:
            wait_all(in_self)
        cols = slice(j * HALF, (j + 1) * HALF)
        a_rows = slice(4096 + j * HALF, 4096 + (j + 1) * HALF)
        b_rows = slice(5120 + j * HALF, 5120 + (j + 1) * HALF)
        xb[0, x, :, cols] = (
            nt(ds[0], z[a_rows, 0:HALF]) + nt(ds[1], z[a_rows, HALF:D]) + nt(ds[2], z[b_rows, 0:HALF])
        ).astype(BF)
        m_self.append(exchange(0, (slice(None), pl.ds(j * HALF, HALF)), j))

    def fill_self(n):
        if n == 0:
            wait_all(in_early)
            in_ds.wait()
        for j in range(2):
            cols = slice(j * HALF, (j + 1) * HALF)
            fill(n, j, tn(slow[...], cot[:, cols]) if n == 0 else tn(selfin[:, cols], ds[n - 1]))

    def new_part():
        for j in range(2):
            cols = slice(j * HALF, (j + 1) * HALF)
            rows = slice(5120 + j * HALF, 5120 + (j + 1) * HALF)
            xb[1, x, :, cols] = nn(slow[...], z[rows, HALF:D]).astype(BF)
            m_new.append(exchange(1, (slice(None), pl.ds(j * HALF, HALF)), 2 + j))

    def two_back():
        wait_all(in_two)
        wait_all(m_self)
        gain = vec_row(vecs, gain_self)

        def body(i):
            rows = pl.ds(pl.multiple_of(i * 32, 32), 32)
            dv, dg, db = norm_back(htwo[rows, :], both(0, rows), gain)
            e = cot[rows, :].astype(F32) + dv
            etwo[rows, :] = e
            elow2[rows, :] = e.astype(BF)
            gvec[6:7, :] += dg
            gvec[7:8, :] += db

        loop(8, body)
        later["lat"] = load(lat_h, lat)
        wait_all(in_mid)

    def hidden_back(j):
        if j == 0:
            wait_all(in_mlp)
        cols = slice(j * HALF, (j + 1) * HALF)
        gh = nt(elow2[...], z[cols, :])
        dpre[:, cols] = (gh * gelu_slope(pre[:, cols])).astype(BF)

    def mlp_back(j):
        cols = slice(j * HALF, (j + 1) * HALF)
        xb[2, x, :, cols] = (
            nt(dpre[:, 0:D], z[HID + j * HALF:HID + (j + 1) * HALF, :])
            + nt(dpre[:, D:HID], z[HID + D + j * HALF:HID + D + (j + 1) * HALF, :])
        ).astype(BF)
        m_mlp.append(exchange(2, (slice(None), pl.ds(j * HALF, HALF)), 4 + j))
        if j == 0:
            return
        later["keys"] = [load(ck_h, ck), load(cv_h, cv)]
        later["inputs"] = [load(inin_h, inin), load(inp_h, inp)]

    def fill_down(j):
        for i in range(2):
            part = hid[(j // 2) * ROWS:(j // 2 + 1) * ROWS, (j % 2) * HALF:(j % 2 + 1) * HALF]
            fill(4 + j, i, tn(part, elow2[:, i * HALF:(i + 1) * HALF]))

    def fill_up(j):
        for i in range(2):
            fill(8 + j, i, tn(mlpin[:, i * HALF:(i + 1) * HALF], dpre[:, j * HALF:(j + 1) * HALF]))

    def one_back():
        wait_all(m_mlp)
        gain = vec_row(vecs, gain_mlp)

        def body(i):
            rows = pl.ds(pl.multiple_of(i * 32, 32), 32)
            dv, dg, db = norm_back(hone[rows, :], both(2, rows), gain)
            e = etwo[rows, :] + dv
            hone[rows, :] = e
            elow1[rows, :] = e.astype(BF)
            gvec[4:5, :] += dg
            gvec[5:6, :] += db

        loop(8, body)

    def cross_back():
        wait_all(in_cross)
        for g in range(2):
            dcr[g * D:(g + 1) * D, :] = nt(wf[3], elow1[g * LAT:(g + 1) * LAT, :]).astype(BF)

    def fill_output():
        for j in range(2):
            value = 0.0
            for g in range(2):
                rows = pl.ds(pl.multiple_of(g * D + x * HALF, HALF), HALF)
                value = value + nn(
                    att[rows, :], elow1[g * LAT:(g + 1) * LAT, j * HALF:(j + 1) * HALF]
                )
            fill(12, j, value)

    def new_latents():
        wait_all(m_new)

        def body(i):
            rows = pl.ds(pl.multiple_of(i * 64, 64), 64)
            selfin[rows, :] = (htwo[rows, :] + both(1, rows)).astype(BF)

        loop(4, body)
        store(selfin, newlat_o)

    def head(g, h):
        cols = slice(h * HEAD_DIM, (h + 1) * HEAD_DIM)
        n_rows = slice(g * INP, (g + 1) * INP)
        l_rows = slice(g * LAT, (g + 1) * LAT)
        t_rows = slice(g * D + h * HEAD_DIM, g * D + (h + 1) * HEAD_DIM)
        k, v, q = ck[n_rows, cols], cv[n_rows, cols], cq[l_rows, cols]
        s = nt(k, q) * SCALE + mask[n_rows, :].astype(F32)
        p = jnp.exp(s - st[g, h:h + 1, :]) * st[g, HEADS + h:HEADS + h + 1, :]
        do = dcr[t_rows, :]
        delta = jnp.sum(do.astype(F32) * att[t_rows, :].astype(F32), axis=0, keepdims=True)
        dsc = (p * (nn(v, do) - delta)).astype(BF)
        cv[n_rows, cols] = nt(p.astype(BF), do).astype(BF)
        ck[n_rows, cols] = (nn(dsc, q) * SCALE).astype(BF)
        xb[0, x, l_rows, cols] = (tn(dsc, k) * SCALE).astype(BF)

    def heads_back(g, h):
        if g == 0 and h == 0:
            wait_all(later["keys"])
        head(g, h)
        if h == HEADS - 1:
            m_query.append(exchange(0, (pl.ds(g * LAT, LAT),), 6 + g))

    def weight_grad(w, i):
        if w == 0 and i == 0:
            wait_all(later["inputs"])
            later["latin"] = load(latin_h, latin)
        source = (ck, cv)[w]
        rows = slice(i * 256, (i + 1) * 256)
        mine = pl.ds(pl.multiple_of(x * HALF + i * 256, 256), 256)
        theirs = pl.ds(pl.multiple_of((1 - x) * HALF + i * 256, 256), 256)
        other[w, rows, :] = tn(inin[:, theirs], source[...]).astype(BF)
        grad[(14 + w) * HALF + i * 256:(14 + w) * HALF + (i + 1) * 256, :] = tn(
            inin[:, mine], source[...]
        ).astype(BF)
        if i == 1:
            start_core(w)

    def fill_query():
        wait_all(m_query)
        later["latin"].wait()

        def body(i):
            rows = pl.ds(pl.multiple_of(i * 64, 64), 64)
            dcq[rows, :] = both(0, rows).astype(BF)

        loop(4, body)
        for j in range(2):
            mine = pl.ds(pl.multiple_of(x * HALF, HALF), HALF)
            fill(13, j, tn(latin[:, mine], dcq[:, j * HALF:(j + 1) * HALF]))

    def latents_back():
        gain = vec_row(vecs, gain_lat)
        later["lat"].wait()

        def body(i):
            rows = pl.ds(pl.multiple_of(i * 128, 128), 128)
            dv, dg, db = norm_back(lat[rows, :].astype(F32), nt(dcq[rows, :], wf[2]), gain)
            lat[rows, :] = (hone[rows, :] + dv).astype(BF)
            gvec[0:1, :] += dg
            gvec[1:2, :] += db

        loop(2, body)
        store(lat, glat_o)

    def inputs_back(i):
        rows = slice(i * 224, (i + 1) * 224)
        dy = nt(ck[rows, :], wf[0]) + nt(cv[rows, :], wf[1])
        dv, dg, db = norm_back(inp[rows, :].astype(F32), dy, vec_row(vecs, gain_inp))
        inp[rows, :] = dv.astype(BF)
        gvec[2:3, :] += dg
        gvec[3:4, :] += db
        if i == 6:
            store(inp, ginp_o)
            col = lax.broadcasted_iota(jnp.int32, (8, D), 1) // HALF
            row = lax.broadcasted_iota(jnp.int32, (8, D), 0)
            keep = (col == x) | (row == 2) | (row == 3)
            gvec[...] = jnp.where(keep, gvec[...], 0.0)

    v_partners = (xp, cp, yp, ap, bp)
    v_moves = []

    def vec_event(s):
        if s > 0:
            v_moves[s - 1].wait()
            gvec[...] += gvr[s - 1]
        if s < 5:
            move = remote(gvec, gvr.at[s], vs.at[s], vr.at[s], v_partners[s])
            move.start()
            v_moves.append(move)
        else:
            store(gvec, gvec_o)

    steps = [lambda: fill_self(0), lambda: fill_self(1), lambda: self_back(0), lambda: self_back(1)]
    steps += [lambda: fill_self(2), lambda: fill_self(3)]
    steps += [new_part, two_back]
    steps += [lambda j=j: hidden_back(j) for j in range(4)]
    steps += [lambda: mlp_back(0), lambda: mlp_back(1)]
    steps += [lambda j=j: fill_down(j) for j in range(4)]
    steps += [lambda j=j: fill_up(j) for j in range(4)]
    steps += [one_back, cross_back, fill_output, new_latents]
    steps += [lambda g=g, h=h: heads_back(g, h) for g in range(2) for h in range(HEADS)]
    steps += [lambda i=i: weight_grad(0, i) for i in range(2)]
    steps += [lambda: weight_grad(1, 0), lambda: start_x(0), lambda: weight_grad(1, 1)]
    steps += [fill_query, lambda: start_x(1), latents_back]
    steps += [lambda i=i: inputs_back(i) for i in range(7)]
    for at, events in zip(ORDER, EVENTS, strict=True):
        steps[at]()
        for k, s in events:
            if k < 0:
                vec_event(s)
            else:
                event(k, s)
    wait_all(outs)


def run_second(args):
    any_spec = pl.BlockSpec(memory_space=pl.ANY)
    outs = [
        ((ROWS, D), BF), ((ROWS, D), BF), ((NROWS, D), BF), ((HALF, D), BF), ((HALF, D), BF),
        ((HALF, D), BF), ((HALF, D), BF), ((D, HID), BF), ((HID, D), BF), ((D, HALF), BF),
        ((D, HALF), BF), ((D, HALF), BF), ((HALF, D), BF), ((8, D), F32),
    ]
    scratch = [
        ((4 * NROWS, D), BF), ((4, D, D), BF), ((ROWS, D), BF),
        ((2 * D, LAT), BF), ((2, 16, LAT), F32), ((2, 8, HALF), F32), ((ROWS, D), F32),
        ((ROWS, D), F32), ((ROWS, D), F32), ((ROWS, D), BF), ((ROWS, D), BF), ((ROWS, HID), F32),
        ((2 * ROWS, D), BF), ((3, ROWS, HALF), BF), ((ROWS, HALF), BF), ((NROWS, LAT), BF),
        ((ROWS, D), BF), ((ROWS, D), BF), ((ROWS, D), BF), ((ROWS, HID), BF),
        ((2 * D, LAT), BF), ((3, 2, ROWS, D), BF), ((16 * HALF, D), BF), ((2, HALF, D), BF),
        ((SLOTS[0], PART, HALF), BF), *[((n, PART // 2, HALF), BF) for n in SLOTS[1:]],
        ((2, HALF, HALF), BF), ((8, D), F32),
        ((5, 8, D), F32),
    ]
    dma = pltpu.SemaphoreType.DMA
    return pl.pallas_call(
        second_kernel,
        out_shape=[jax.ShapeDtypeStruct(*o) for o in outs],
        in_specs=[any_spec] * len(args),
        out_specs=[any_spec] * len(outs),
        scratch_shapes=[pltpu.VMEM(*s) for s in scratch]
        + [dma((40,)), dma((64,))] + [dma((32 * 7,))] * 2 + [dma((12,))] * 2 + [dma((5,))] * 2
        + [pltpu.SemaphoreType.REGULAR((128,))],
        compiler_params=pltpu.CompilerParams(
            collective_id=1, has_side_effects=True, vmem_limit_bytes=63 * MIB
        ),
        name="backward",
    )(*args)


def finish_kernel(*refs):
    srcs, gvec, dsts, small = refs[:13], refs[13], refs[14:27], refs[27:35]
    low, wide, gains, *pieces, insem, outsem, smallsem = refs[35:]
    in_gains = pltpu.make_async_copy(gvec, gains, smallsem.at[8])
    in_gains.start()
    tiles = []
    for i in (*range(3, 13), 0, 1, 2):
        rows, cols = srcs[i].shape
        for r in range(0, rows, 256):
            count = min(256, rows - r)
            tiles.append((i, pl.ds(r, count), (pl.ds(0, count), pl.ds(0, cols))))
    depth = low.shape[0]
    ins, outs, finished = {}, {}, set()

    def finish_out(n):
        if n >= 0 and n not in finished:
            outs[n].wait()
            finished.add(n)

    def start_in(n):
        i, rows, part = tiles[n]
        ins[n] = pltpu.make_async_copy(srcs[i].at[rows], low.at[n % depth, *part], insem.at[n % depth])
        ins[n].start()

    for n in range(depth):
        start_in(n)
    first = lax.axis_index("shard") == 0
    in_gains.wait()
    mine = jnp.where(first, gains[:, 0:HALF], gains[:, HALF:D])
    out_gains = []
    for i in range(8):
        pieces[i][...] = mine[i]
        copy = pltpu.make_async_copy(pieces[i], small[i], smallsem.at[i])
        copy.start()
        out_gains.append(copy)
    for n in range(len(tiles)):
        slot = n % depth
        i, rows, part = tiles[n]
        ins[n].wait()
        finish_out(n - depth)
        if i < 3:
            outs[n] = pltpu.make_async_copy(low.at[slot, *part], dsts[i].at[rows], outsem.at[slot])
            outs[n].start()
        else:
            cols = part[1]

            def body(i, slot=slot, cols=cols):
                rows = pl.ds(pl.multiple_of(i * 32, 32), 32)
                wide[slot, rows, cols] = low[slot, rows, cols].astype(F32)

            loop(8, body)
            outs[n] = pltpu.make_async_copy(wide.at[slot, *part], dsts[i].at[rows], outsem.at[slot])
            outs[n].start()
        if n + depth < len(tiles):
            if i < 3:
                finish_out(n)
            start_in(n + depth)
    for n in range(len(tiles) - depth, len(tiles)):
        finish_out(n)
    for copy in out_gains:
        copy.wait()


def run_finish(args):
    any_spec = pl.BlockSpec(memory_space=pl.ANY)
    depth = 6
    return pl.pallas_call(
        finish_kernel,
        out_shape=[
            jax.ShapeDtypeStruct(a.shape, BF if i < 3 else F32) for i, a in enumerate(args[:13])
        ] + [jax.ShapeDtypeStruct((HALF,), F32)] * 8,
        in_specs=[any_spec] * 14,
        out_specs=[any_spec] * 21,
        scratch_shapes=[
            pltpu.VMEM((depth, 256, HID), BF), pltpu.VMEM((depth, 256, HID), F32),
            pltpu.VMEM((8, D), F32), *[pltpu.VMEM((HALF,), F32)] * 8,
            pltpu.SemaphoreType.DMA((depth,)), pltpu.SemaphoreType.DMA((depth,)),
            pltpu.SemaphoreType.DMA((9,)),
        ],
        compiler_params=pltpu.CompilerParams(vmem_limit_bytes=62 * MIB),
        name="finish",
    )(*args)


def per_device_pair(
    latents, inputs, latent_segment, input_segment, cross_query, cross_key, cross_value,
    cross_output, mlp_up, mlp_down, self_query, self_key, self_value, self_output,
    latent_gain, latent_bias, input_gain, input_bias, mlp_gain, mlp_bias, self_gain,
    self_bias, cotangent,
):
    vec = (
        latent_gain, latent_bias, input_gain, input_bias, mlp_gain, mlp_bias, self_gain, self_bias
    )
    lat = latents.reshape(ROWS, D)
    inp = inputs.reshape(NROWS, D)
    cot = cotangent.reshape(ROWS, D)
    kept = run_first((
        lat, inp, latent_segment, input_segment, *vec, cross_key, cross_value, cross_query,
        cross_output, mlp_up, mlp_down, self_query, self_key, self_value, self_output, cot,
    ))
    (new, glat, ginp, gq, gk, gv, go, gup, gdown, gsq, gsk, gsv, gso, gvec) = run_second(
        tuple(kept) + (
            lat, inp, mlp_up, mlp_down, self_query, self_key, self_value, self_output, cot
        )
    )
    new, glat, ginp, *grads = run_finish(
        (new, glat, ginp, gq, gk, gv, go, gup, gdown, gsq, gsk, gsv, gso, gvec)
    )
    return (
        new.reshape(latents.shape), glat.reshape(latents.shape), ginp.reshape(inputs.shape), *grads
    )


def norm_forward(values, gain, shift):
    centred = values - jnp.mean(values, axis=-1, keepdims=True)
    inv_std = lax.rsqrt(jnp.mean(centred * centred, axis=-1, keepdims=True) + EPSILON)
    normed = centred * inv_std
    return (normed * gain + shift, normed, inv_std)


def norm_backward(grad_out, normed, inv_std, gain):
    scaled = grad_out * gain
    first_mean = jnp.mean(scaled, axis=-1, keepdims=True)
    second_mean = jnp.mean(scaled * normed, axis=-1, keepdims=True)
    grad_in = inv_std * (scaled - first_mean - normed * second_mean)
    return (grad_in, jnp.sum(grad_out * normed, axis=0), jnp.sum(grad_out, axis=0))


def product(left, right):
    return jnp.dot(left, right, preferred_element_type=jnp.float32)


def inner_rows(left, right):
    return lax.dot_general(
        left, right, (((0,), (0,)), ((), ())), preferred_element_type=jnp.float32
    )


def outer_cols(left, right):
    return lax.dot_general(
        left, right, (((1,), (1,)), ((), ())), preferred_element_type=jnp.float32
    )


def forward_total(term):
    return lax.psum(term.astype(jnp.bfloat16), "shard").astype(jnp.float32)


def backward_total(term):
    return lax.psum(term.astype(jnp.bfloat16), "shard").astype(jnp.float32)


def per_device(
    latents,
    inputs,
    latent_segment,
    input_segment,
    cross_query,
    cross_key,
    cross_value,
    cross_output,
    mlp_up,
    mlp_down,
    self_query,
    self_key,
    self_value,
    self_output,
    latent_gain,
    latent_bias,
    input_gain,
    input_bias,
    mlp_gain,
    mlp_bias,
    self_gain,
    self_bias,
    cotangent,
):
    shards = lax.axis_size("shard")
    groups, lat_len, width = latents.shape
    inp_len = inputs.shape[1]
    width_part = width // shards
    column_start = lax.axis_index("shard") * width_part
    rows = groups * lat_len
    scale = HEAD_DIM ** (-0.5)
    gathered = (
        lax.all_gather(cross_query, "shard", axis=0, tiled=True),
        lax.all_gather(cross_key, "shard", axis=0, tiled=True),
        lax.all_gather(cross_value, "shard", axis=0, tiled=True),
        lax.all_gather(cross_output, "shard", axis=0, tiled=True),
        lax.all_gather(latent_gain, "shard", axis=0, tiled=True),
        lax.all_gather(latent_bias, "shard", axis=0, tiled=True),
        lax.all_gather(input_gain, "shard", axis=0, tiled=True),
        lax.all_gather(input_bias, "shard", axis=0, tiled=True),
        lax.all_gather(mlp_gain, "shard", axis=0, tiled=True),
        lax.all_gather(mlp_bias, "shard", axis=0, tiled=True),
        lax.all_gather(self_gain, "shard", axis=0, tiled=True),
        lax.all_gather(self_bias, "shard", axis=0, tiled=True),
    )
    full_query, full_key, full_value, full_output = (
        gathered[0],
        gathered[1],
        gathered[2],
        gathered[3],
    )
    gain_lat, bias_lat, gain_inp, bias_inp, gain_mlp, bias_mlp, gain_self, bias_self = [
        piece.astype(jnp.float32) for piece in gathered[4:]
    ]
    lat_rows = latents.astype(jnp.float32).reshape(rows, width)
    inp_rows = inputs.astype(jnp.float32).reshape(groups * inp_len, width)
    lat_value, lat_normed, lat_inv = norm_forward(lat_rows, gain_lat, bias_lat)
    lat_in = lat_value.astype(jnp.bfloat16)
    inp_value, inp_normed, inp_inv = norm_forward(inp_rows, gain_inp, bias_inp)
    inp_in = inp_value.astype(jnp.bfloat16)
    cross_q = (
        product(lat_in, full_query).astype(jnp.bfloat16).reshape(groups, lat_len, HEADS, HEAD_DIM)
    )
    cross_k = (
        product(inp_in, full_key).astype(jnp.bfloat16).reshape(groups, inp_len, HEADS, HEAD_DIM)
    )
    cross_v = (
        product(inp_in, full_value).astype(jnp.bfloat16).reshape(groups, inp_len, HEADS, HEAD_DIM)
    )
    allowed = latent_segment[:, None, :, None] == input_segment[:, None, None, :]
    scores = (
        jnp.einsum("glhd,gnhd->ghln", cross_q, cross_k, preferred_element_type=jnp.float32) * scale
    )
    masked = jnp.where(allowed, scores, NEGATIVE)
    part_max = jnp.max(masked, axis=-1)
    top = lax.pmax(part_max, "shard")
    total = lax.psum(
        jnp.sum(jnp.where(allowed, jnp.exp(masked - top[..., None]), 0.0), axis=-1), "shard"
    )
    cross_prob = jnp.where(allowed, jnp.exp(masked - top[..., None]), 0.0) / total[..., None]
    cross_prob_low = cross_prob.astype(jnp.bfloat16)
    part_out = jnp.einsum(
        "ghln,gnhd->glhd", cross_prob_low, cross_v, preferred_element_type=jnp.float32
    )
    attended = lax.psum(part_out.astype(jnp.bfloat16), "shard").astype(jnp.float32)
    attended_in = attended.reshape(rows, width).astype(jnp.bfloat16)
    h_one = lat_rows + product(attended_in, full_output)
    mlp_value, mlp_normed, mlp_inv = norm_forward(h_one, gain_mlp, bias_mlp)
    mlp_in = mlp_value.astype(jnp.bfloat16)
    pre_act = product(mlp_in, mlp_up)
    hidden_in = jax.nn.gelu(pre_act).astype(jnp.bfloat16)
    h_two = h_one + forward_total(product(hidden_in, mlp_down))
    self_value_n, self_normed, self_inv = norm_forward(h_two, gain_self, bias_self)
    self_in = self_value_n.astype(jnp.bfloat16)
    local_heads = self_query.shape[1] // HEAD_DIM
    local_width = local_heads * HEAD_DIM
    self_q = (
        product(self_in, self_query)
        .astype(jnp.bfloat16)
        .reshape(groups, lat_len, local_heads, HEAD_DIM)
    )
    self_k = (
        product(self_in, self_key)
        .astype(jnp.bfloat16)
        .reshape(groups, lat_len, local_heads, HEAD_DIM)
    )
    self_v = (
        product(self_in, self_value)
        .astype(jnp.bfloat16)
        .reshape(groups, lat_len, local_heads, HEAD_DIM)
    )
    self_scores = (
        jnp.einsum("glhd,gmhd->ghlm", self_q, self_k, preferred_element_type=jnp.float32) * scale
    )
    self_prob = jax.nn.softmax(self_scores, axis=-1)
    self_prob_low = self_prob.astype(jnp.bfloat16)
    self_att = jnp.einsum(
        "ghlm,gmhd->glhd", self_prob_low, self_v, preferred_element_type=jnp.float32
    )
    self_att_in = self_att.reshape(rows, local_width).astype(jnp.bfloat16)
    result = h_two + forward_total(product(self_att_in, self_output))
    new_latents = result.reshape(groups, lat_len, width).astype(jnp.bfloat16)
    grad_out = cotangent.astype(jnp.float32).reshape(rows, width)
    grad_branch = grad_out.astype(jnp.bfloat16)
    grad_self_output = inner_rows(self_att_in, grad_branch)
    grad_att = (
        outer_cols(grad_branch, self_output)
        .astype(jnp.bfloat16)
        .reshape(groups, lat_len, local_heads, HEAD_DIM)
    )
    delta = jnp.sum(grad_att.astype(jnp.float32) * self_att, axis=-1).transpose(0, 2, 1)
    grad_prob = jnp.einsum("glhd,gmhd->ghlm", grad_att, self_v, preferred_element_type=jnp.float32)
    grad_sv = jnp.einsum(
        "ghlm,glhd->gmhd", self_prob_low, grad_att, preferred_element_type=jnp.float32
    )
    grad_scores = (self_prob * (grad_prob - delta[..., None])).astype(jnp.bfloat16)
    grad_sq = (
        jnp.einsum("ghlm,gmhd->glhd", grad_scores, self_k, preferred_element_type=jnp.float32)
        * scale
    )
    grad_sk = (
        jnp.einsum("ghlm,glhd->gmhd", grad_scores, self_q, preferred_element_type=jnp.float32)
        * scale
    )
    grad_sq = grad_sq.astype(jnp.bfloat16).reshape(rows, local_width)
    grad_sk = grad_sk.astype(jnp.bfloat16).reshape(rows, local_width)
    grad_sv = grad_sv.astype(jnp.bfloat16).reshape(rows, local_width)
    grad_self_query = inner_rows(self_in, grad_sq)
    grad_self_key = inner_rows(self_in, grad_sk)
    grad_self_value = inner_rows(self_in, grad_sv)
    grad_self_in = backward_total(
        outer_cols(grad_sq, self_query)
        + outer_cols(grad_sk, self_key)
        + outer_cols(grad_sv, self_value)
    )
    grad_norm, gain_full, bias_full = norm_backward(grad_self_in, self_normed, self_inv, gain_self)
    grad_two = grad_out + grad_norm
    grad_self_gain = lax.dynamic_slice_in_dim(gain_full, column_start, width_part)
    grad_self_bias = lax.dynamic_slice_in_dim(bias_full, column_start, width_part)
    grad_mlp_branch = grad_two.astype(jnp.bfloat16)
    grad_mlp_down = inner_rows(hidden_in, grad_mlp_branch)
    grad_hidden = outer_cols(grad_mlp_branch, mlp_down)
    gelu_value, gelu_pull = jax.vjp(jax.nn.gelu, pre_act)
    grad_pre = gelu_pull(grad_hidden)[0].astype(jnp.bfloat16)
    grad_mlp_up = inner_rows(mlp_in, grad_pre)
    grad_mlp_in = backward_total(outer_cols(grad_pre, mlp_up))
    grad_norm, gain_full, bias_full = norm_backward(grad_mlp_in, mlp_normed, mlp_inv, gain_mlp)
    grad_one = grad_two + grad_norm
    grad_mlp_gain = lax.dynamic_slice_in_dim(gain_full, column_start, width_part)
    grad_mlp_bias = lax.dynamic_slice_in_dim(bias_full, column_start, width_part)
    grad_cross_branch = grad_one.astype(jnp.bfloat16)
    grad_cross_output = inner_rows(
        lax.dynamic_slice_in_dim(attended_in, column_start, width_part, 1), grad_cross_branch
    )
    grad_ca = (
        outer_cols(grad_cross_branch, full_output)
        .astype(jnp.bfloat16)
        .reshape(groups, lat_len, HEADS, HEAD_DIM)
    )
    cross_delta = jnp.sum(grad_ca.astype(jnp.float32) * attended, axis=-1).transpose(0, 2, 1)
    grad_cp = jnp.einsum("glhd,gnhd->ghln", grad_ca, cross_v, preferred_element_type=jnp.float32)
    grad_cv = jnp.einsum(
        "ghln,glhd->gnhd", cross_prob_low, grad_ca, preferred_element_type=jnp.float32
    )
    grad_cs = (cross_prob * (grad_cp - cross_delta[..., None])).astype(jnp.bfloat16)
    grad_cq_part = (
        jnp.einsum("ghln,gnhd->glhd", grad_cs, cross_k, preferred_element_type=jnp.float32) * scale
    )
    grad_ck = (
        jnp.einsum("ghln,glhd->gnhd", grad_cs, cross_q, preferred_element_type=jnp.float32) * scale
    )
    grad_cq = backward_total(grad_cq_part.reshape(rows, width)).astype(jnp.bfloat16)
    grad_ck = grad_ck.astype(jnp.bfloat16).reshape(groups * inp_len, width)
    grad_cv = grad_cv.astype(jnp.bfloat16).reshape(groups * inp_len, width)
    grad_cross_query = inner_rows(
        lax.dynamic_slice_in_dim(lat_in, column_start, width_part, 1), grad_cq
    )
    grad_lat_in = outer_cols(grad_cq, full_query)
    grad_norm, gain_full, bias_full = norm_backward(grad_lat_in, lat_normed, lat_inv, gain_lat)
    grad_latents = (grad_one + grad_norm).reshape(groups, lat_len, width).astype(jnp.bfloat16)
    grad_latent_gain = lax.dynamic_slice_in_dim(gain_full, column_start, width_part)
    grad_latent_bias = lax.dynamic_slice_in_dim(bias_full, column_start, width_part)
    key_term = inner_rows(inp_in, grad_ck)
    value_term = inner_rows(inp_in, grad_cv)
    grad_inp_in = outer_cols(grad_ck, full_key) + outer_cols(grad_cv, full_value)
    grad_inp, inp_gain_full, inp_bias_full = norm_backward(
        grad_inp_in, inp_normed, inp_inv, gain_inp
    )
    grad_inputs = grad_inp.reshape(groups, inp_len, width).astype(jnp.bfloat16)
    grad_cross_key, grad_cross_value, grad_input_gain, grad_input_bias = (
        lax.psum_scatter(
            key_term.astype(jnp.bfloat16), "shard", scatter_dimension=0, tiled=True
        ).astype(jnp.float32),
        lax.psum_scatter(
            value_term.astype(jnp.bfloat16), "shard", scatter_dimension=0, tiled=True
        ).astype(jnp.float32),
        lax.psum_scatter(
            inp_gain_full.astype(jnp.bfloat16), "shard", scatter_dimension=0, tiled=True
        ).astype(jnp.float32),
        lax.psum_scatter(
            inp_bias_full.astype(jnp.bfloat16), "shard", scatter_dimension=0, tiled=True
        ).astype(jnp.float32),
    )
    (
        grad_cross_query,
        grad_cross_key,
        grad_cross_value,
        grad_cross_output,
        grad_mlp_up,
        grad_mlp_down,
        grad_self_query,
        grad_self_key,
        grad_self_value,
        grad_self_output,
        grad_latent_gain,
        grad_latent_bias,
        grad_input_gain,
        grad_input_bias,
        grad_mlp_gain,
        grad_mlp_bias,
        grad_self_gain,
        grad_self_bias,
    ) = (
        lax.psum(grad_cross_query.astype(jnp.bfloat16), "grp").astype(jnp.float32),
        lax.psum(grad_cross_key.astype(jnp.bfloat16), "grp").astype(jnp.float32),
        lax.psum(grad_cross_value.astype(jnp.bfloat16), "grp").astype(jnp.float32),
        lax.psum(grad_cross_output.astype(jnp.bfloat16), "grp").astype(jnp.float32),
        lax.psum(grad_mlp_up.astype(jnp.bfloat16), "grp").astype(jnp.float32),
        lax.psum(grad_mlp_down.astype(jnp.bfloat16), "grp").astype(jnp.float32),
        lax.psum(grad_self_query.astype(jnp.bfloat16), "grp").astype(jnp.float32),
        lax.psum(grad_self_key.astype(jnp.bfloat16), "grp").astype(jnp.float32),
        lax.psum(grad_self_value.astype(jnp.bfloat16), "grp").astype(jnp.float32),
        lax.psum(grad_self_output.astype(jnp.bfloat16), "grp").astype(jnp.float32),
        lax.psum(grad_latent_gain.astype(jnp.bfloat16), "grp").astype(jnp.float32),
        lax.psum(grad_latent_bias.astype(jnp.bfloat16), "grp").astype(jnp.float32),
        lax.psum(grad_input_gain.astype(jnp.bfloat16), "grp").astype(jnp.float32),
        lax.psum(grad_input_bias.astype(jnp.bfloat16), "grp").astype(jnp.float32),
        lax.psum(grad_mlp_gain.astype(jnp.bfloat16), "grp").astype(jnp.float32),
        lax.psum(grad_mlp_bias.astype(jnp.bfloat16), "grp").astype(jnp.float32),
        lax.psum(grad_self_gain.astype(jnp.bfloat16), "grp").astype(jnp.float32),
        lax.psum(grad_self_bias.astype(jnp.bfloat16), "grp").astype(jnp.float32),
    )
    return (
        new_latents,
        grad_latents,
        grad_inputs,
        grad_cross_query,
        grad_cross_key,
        grad_cross_value,
        grad_cross_output,
        grad_mlp_up,
        grad_mlp_down,
        grad_self_query,
        grad_self_key,
        grad_self_value,
        grad_self_output,
        grad_latent_gain,
        grad_latent_bias,
        grad_input_gain,
        grad_input_bias,
        grad_mlp_gain,
        grad_mlp_bias,
        grad_self_gain,
        grad_self_bias,
    )


def solution(mesh):
    laid_out = mesh.shape["shard"] == 2 and mesh.shape["grp"] == 16
    return jax.shard_map(
        per_device_pair if laid_out else per_device,
        mesh=mesh,
        in_specs=(
            P("grp", None, None),
            P("grp", "shard", None),
            P("grp", None),
            P("grp", "shard"),
            P("shard", None),
            P("shard", None),
            P("shard", None),
            P("shard", None),
            P(None, "shard"),
            P("shard", None),
            P(None, "shard"),
            P(None, "shard"),
            P(None, "shard"),
            P("shard", None),
            P("shard"),
            P("shard"),
            P("shard"),
            P("shard"),
            P("shard"),
            P("shard"),
            P("shard"),
            P("shard"),
            P("grp", None, None),
        ),
        out_specs=(
            P("grp", None, None),
            P("grp", None, None),
            P("grp", "shard", None),
            P("shard", None),
            P("shard", None),
            P("shard", None),
            P("shard", None),
            P(None, "shard"),
            P("shard", None),
            P(None, "shard"),
            P(None, "shard"),
            P(None, "shard"),
            P("shard", None),
            P("shard"),
            P("shard"),
            P("shard"),
            P("shard"),
            P("shard"),
            P("shard"),
            P("shard"),
            P("shard"),
        ),
        check_vma=False,
    )
```
